32 devices in a mesh: cells: 4 (over y, x), sensors: 8 (over z, core).
Axes of the slice: x: 2, y: 2, z: 4, core: 2. Of those that a mesh axis runs over, the one named last changes fastest.
Arguments:
- rhs: float32 [256, 6, 128, 128], P('sensors', None, 'cells'), may hold values from -18 to 18
- forward_map: bfloat16 [2, 128, 128, 16384], P(None, None, 'sensors', 'cells'), may hold values from -0.125 to 0.125
- stiffness: float32 [128, 128], P('cells'), may hold values from 0.5 to 1.5
- reaction: float32 [128, 128], P('cells'), may hold values from 0.25 to 2
- noise_weight: float32 [128], replicated, may hold values from 0.3 to 3
- sensor_cell: int32 [128], replicated, may hold values from 0 to 16383, as said below
Outputs:
- solution: float32 [256, 6, 128, 128], P('sensors', None, 'cells')
- residual: float32 [256, 6, 128, 128], P('sensors', None, 'cells')
The draws below stay inside these ranges and needn't reach their ends.
Inputs may be any that keep to these rules, and one draw needn't show every extreme that they name: `sensor_cell`: row-major index over the 128 x 128 grid of the cell under each sensor; several sensors may share a cell.
All inputs are finite; a program needn't handle non-finite values.
Results may differ from the reference program's by a relative error of at most 0.0073.
Values may be sent and summed in bfloat16 or wider, within the bound.
No kernel may reach another device: no remote copies, remote signals or barrier semaphores. Data moves between devices by JAX's collectives and lax.ppermute only.
A program may use at most 192 MiB of HBM per device.

```python
import math
import jax
import jax.numpy as jnp
from jax import lax

SAMPLES = 6
NF = 128
NT = 256
NS = 128
GX = 128
GY = 128
NC = 16384
SWEEPS = 4
ITERS = 2


def draw_sensor_cell(key, part):
    key_cells, key_upper, key_lower = jax.random.split(jax.random.fold_in(key, 17), 3)
    chosen = jax.random.randint(key_cells, (NS,), 0, NC, dtype=jnp.int32)
    upper_slot = jax.random.randint(key_upper, (), 0, NS, dtype=jnp.int32)
    lower_slot = (upper_slot + 1 + jax.random.randint(key_lower, (), 0, NS - 1, dtype=jnp.int32)) % NS
    positions = jnp.arange(NS, dtype=jnp.int32)
    chosen = jnp.where(positions == upper_slot, NC - 1, chosen)
    return jnp.where(positions == lower_slot, 0, chosen).astype(jnp.int32)


def shard_levels(stream_key, extent, pieces, low, largest):
    loudness = 1.0
    for position, parts in pieces:
        heights = jax.random.uniform(jax.random.fold_in(jax.random.fold_in(stream_key, 6), position), (parts,), jnp.float32, low / len(pieces), largest / len(pieces))
        loudness = loudness * jnp.repeat(jnp.exp(heights), extent[position] // parts).reshape((-1,) + (1,) * (len(extent) - 1 - position))
    return loudness


def normal_values(rng, extent, deviation, most, pieces=(), kind=jnp.bfloat16):
    loudness = shard_levels(rng, extent, pieces, -0.22, 0.18) if pieces else 1.0
    drawn = jax.random.normal(rng, extent, jnp.float32) * deviation * loudness
    return jnp.minimum(jnp.maximum(drawn, -most), most).astype(kind)


def setup_inputs(seed: int = 0) -> dict:
    key_list = jax.random.split(jax.random.key(seed), 7)
    return {
        "rhs": normal_values(key_list[0], (NT, SAMPLES, GX, GY), 3.0, 18.0, ((0, 8), (2, 4)), jnp.float32),
        "forward_map": normal_values(key_list[1], (2, NF, NS, NC), (NC // 8) ** -0.5, 0.125, ((2, 8), (3, 4))),
        "stiffness": jnp.clip(jnp.exp(math.log(1.5) - 1.0986123 * jax.random.uniform(key_list[2], (GX, GY), jnp.float32) ** shard_levels(key_list[2], (GX, GY), ((0, 4),), -0.2, 0.2)), 0.5, 1.5),
        "reaction": jnp.clip(jnp.exp(math.log(2.0) - 2.0794415 * jax.random.uniform(key_list[3], (GX, GY), jnp.float32) ** shard_levels(key_list[3], (GX, GY), ((0, 4),), -0.2, 0.2)), 0.25, 2.0),
        "noise_weight": jnp.clip(jnp.exp(jax.random.uniform(key_list[4], (NS,), jnp.float32, math.log(0.3), math.log(3.0))), 0.3, 3.0),
        "sensor_cell": draw_sensor_cell(jax.random.fold_in(key_list[6], 71), 0),
    }


DAMPING = 0.8

def neighbour_sum(field):
    padded = jnp.pad(field, ((0, 0), (0, 0), (1, 1), (1, 1)))
    return padded[:, :, 2:, 1:-1] + padded[:, :, :-2, 1:-1] + padded[:, :, 1:-1, 2:] + padded[:, :, 1:-1, :-2]

def transform_table(freqs, period):
    wave = jnp.arange(freqs, dtype=jnp.int32)[:, None]
    moment = jnp.arange(period, dtype=jnp.int32)[None, :]
    phase = (wave * moment % period).astype(jnp.float32) * (2.0 * math.pi / period)
    factor = 1.0 / math.sqrt(period)
    return jnp.concatenate([jnp.cos(phase) * factor, -jnp.sin(phase) * factor], axis=0).astype(jnp.bfloat16)

def prior_apply(field, stiffness, diagonal):
    return diagonal * field - stiffness * neighbour_sum(stiffness * field)

def precondition(residual, stiffness, diagonal, inverse):
    update = DAMPING * inverse * residual
    for sweep in range(SWEEPS - 1):
        update = update + DAMPING * inverse * (residual - prior_apply(update, stiffness, diagonal))
    return update

def misfit_apply(field, forward_map, noise_weight, sensor_cell, table):
    period = field.shape[0]
    spectrum = jnp.dot(table, field.astype(jnp.bfloat16).reshape(period, -1), preferred_element_type=jnp.float32)
    spectrum = spectrum.astype(jnp.bfloat16).reshape(2 * NF, SAMPLES, NC)
    real_part = spectrum[:NF]
    imag_part = spectrum[NF:]

    def observe(items):
        map_real, map_imag, field_real, field_imag = items
        obs_real = jnp.dot(field_real, map_real.T, preferred_element_type=jnp.float32) - jnp.dot(field_imag, map_imag.T, preferred_element_type=jnp.float32)
        obs_imag = jnp.dot(field_imag, map_real.T, preferred_element_type=jnp.float32) + jnp.dot(field_real, map_imag.T, preferred_element_type=jnp.float32)
        return (obs_real, obs_imag)
    obs_real, obs_imag = lax.map(observe, (forward_map[0], forward_map[1], real_part, imag_part))
    obs_real = obs_real + real_part[:, :, sensor_cell].astype(jnp.float32)
    obs_imag = obs_imag + imag_part[:, :, sensor_cell].astype(jnp.float32)
    weighted_real = (noise_weight * obs_real).astype(jnp.bfloat16)
    weighted_imag = (noise_weight * obs_imag).astype(jnp.bfloat16)

    def spread(items):
        map_real, map_imag, data_real, data_imag = items
        back_real = jnp.dot(data_real, map_real, preferred_element_type=jnp.float32) + jnp.dot(data_imag, map_imag, preferred_element_type=jnp.float32)
        back_imag = jnp.dot(data_imag, map_real, preferred_element_type=jnp.float32) - jnp.dot(data_real, map_imag, preferred_element_type=jnp.float32)
        return (back_real, back_imag)
    back_real, back_imag = lax.map(spread, (forward_map[0], forward_map[1], weighted_real, weighted_imag))
    back_real = back_real.at[:, :, sensor_cell].add(weighted_real.astype(jnp.float32))
    back_imag = back_imag.at[:, :, sensor_cell].add(weighted_imag.astype(jnp.float32))
    adjoint = jnp.concatenate([back_real, back_imag], axis=0).reshape(2 * NF, -1)
    time_terms = jnp.dot(table.astype(jnp.float32).T, adjoint, precision=lax.Precision.HIGHEST, preferred_element_type=jnp.float32)
    return time_terms.reshape(field.shape)

def reference(rhs, forward_map, stiffness, reaction, noise_weight, sensor_cell):
    diagonal = reaction + 4.0 * stiffness * stiffness
    inverse = 1.0 / diagonal
    table = transform_table(NF, NT)
    solution = precondition(rhs, stiffness, diagonal, inverse)
    residual = rhs
    for iteration in range(ITERS):
        hessian = prior_apply(solution, stiffness, diagonal) + misfit_apply(solution, forward_map, noise_weight, sensor_cell, table)
        residual = rhs - hessian
        solution = solution + precondition(residual, stiffness, diagonal, inverse)
    return (solution, residual)
```

```python
import math

import jax
import jax.numpy as jnp
from jax import lax
from jax.experimental import pallas as pl
from jax.experimental.pallas import tpu as pltpu
from jax.sharding import PartitionSpec as P

SWEEPS = 4
ITERS = 2
DAMPING = 0.8
HALO = SWEEPS
LANES = 128
SUBLANES = 8
GROUPS = 2
CHUNK_ROWS = 4
VMEM_BYTES = 40 * 2**20


def transform_table(freqs, period):
    wave = jnp.arange(freqs, dtype=jnp.int32)[:, None]
    moment = jnp.arange(period, dtype=jnp.int32)[None, :]
    phase = (wave * moment % period).astype(jnp.float32) * (2.0 * math.pi / period)
    factor = 1.0 / math.sqrt(period)
    return jnp.concatenate([jnp.cos(phase) * factor, -jnp.sin(phase) * factor], axis=0).astype(
        jnp.bfloat16
    )


def params(**kwargs):
    return pltpu.CompilerParams(vmem_limit_bytes=VMEM_BYTES, **kwargs)


def whole_block(array):
    return pl.BlockSpec(array.shape, lambda *_: (0,) * array.ndim)


def dot(left, right):
    return jnp.dot(left, right, preferred_element_type=jnp.float32)


def dot_lanes(left, right):
    return lax.dot_general(left, right, (((1,), (1,)), ((), ())), preferred_element_type=jnp.float32)


def neighbours(field):
    inner = field[1:-1]
    lane = lax.broadcasted_iota(jnp.int32, inner.shape, 2)
    before = jnp.where(lane == 0, 0.0, pltpu.roll(inner, 1, 2))
    after = jnp.where(lane == LANES - 1, 0.0, pltpu.roll(inner, LANES - 1, 2))
    return (field[2:] + field[:-2]) + (before + after)


def trim(array, width):
    return array[width : array.shape[0] - width]


def precondition(residual, coeff_ref):
    extra = (coeff_ref.shape[1] - residual.shape[0]) // 2
    coeff = [trim(coeff_ref[k], extra) for k in range(3)]
    first = coeff[0] * residual
    scaled = first
    for sweep in range(1, SWEEPS):
        scaled = (
            (1.0 - DAMPING) * scaled[1:-1]
            + trim(first, sweep)
            + trim(coeff[1], sweep) * neighbours(scaled)
        )
    return trim(coeff[2], SWEEPS - 1) * scaled


def prior(field, coeff_ref):
    extra = (coeff_ref.shape[1] - field.shape[0]) // 2
    stiffness = trim(coeff_ref[3], extra)
    diagonal = trim(coeff_ref[4], extra + 1)
    return diagonal * field[1:-1] - stiffness[1:-1] * neighbours(stiffness * field)


def time_chunks(steps, body):
    def run(index, carry):
        body(pl.ds(pl.multiple_of(index * SUBLANES, SUBLANES), SUBLANES))
        return carry

    lax.fori_loop(0, steps // SUBLANES, run, 0)


def start_kernel(rhs_ref, up_ref, down_ref, coeff_ref, iter_ref, low_ref, rest_ref, top_ref, bottom_ref):
    rows = iter_ref.shape[1]

    def body(times):
        here = jnp.swapaxes(rhs_ref[times], 0, 1)
        update = precondition(
            jnp.concatenate([up_ref[0, :, times], here, down_ref[0, :, times]], axis=0), coeff_ref
        )
        iter_ref[0, :, times] = update[1:-1]
        rest = here - prior(update, coeff_ref)
        rest_ref[0, :, times] = rest
        top_ref[0, :, times] = rest[:HALO]
        bottom_ref[0, :, times] = rest[rows - HALO :]

    time_chunks(iter_ref.shape[2], body)
    low_ref[...] = iter_ref[...].astype(low_ref.dtype)


def start(group, members, rhs, up, down, coeff):
    steps, _, rows, cols = rhs.shape
    flat = rhs.reshape(steps, -1, cols)
    field = pl.BlockSpec((1, rows, steps, cols), lambda b: (b, 0, 0, 0))
    rim = pl.BlockSpec((1, HALO, steps, cols), lambda b: (b, 0, 0, 0))
    whole_rim = pl.BlockSpec((1, HALO, steps, cols), lambda b: (b + group * members, 0, 0, 0))
    shape = (members, rows, steps, cols)
    rim_shape = (members, HALO, steps, cols)
    return pl.pallas_call(
        start_kernel,
        grid=(members,),
        in_specs=[
            pl.BlockSpec((steps, rows, cols), lambda b: (0, b + group * members, 0)),
            whole_rim,
            whole_rim,
            whole_block(coeff),
        ],
        out_specs=[field, field, field, rim, rim],
        out_shape=[
            jax.ShapeDtypeStruct(shape, jnp.float32),
            jax.ShapeDtypeStruct(shape, jnp.bfloat16),
            jax.ShapeDtypeStruct(shape, jnp.float32),
            jax.ShapeDtypeStruct(rim_shape, jnp.float32),
            jax.ShapeDtypeStruct(rim_shape, jnp.float32),
        ],
        compiler_params=params(),
        name="start",
    )(flat, up, down, coeff)


def residual_of(times, rest_refs, misfit_refs):
    parts = [
        rest[0, :, times] - misfit[0, :, times].astype(jnp.float32)
        for rest, misfit in zip(rest_refs, misfit_refs)
    ]
    return jnp.concatenate(parts, axis=0)


def step_kernel(
    up_ref, rest_ref, down_ref, mup_ref, misfit_ref, mdown_ref, iter_ref, coeff_ref,
    next_ref, low_ref, later_ref, top_ref, bottom_ref,
):
    rows = iter_ref.shape[1]

    def body(times):
        residual = residual_of(times, (up_ref, rest_ref, down_ref), (mup_ref, misfit_ref, mdown_ref))
        update = precondition(residual, coeff_ref)
        next_ref[0, :, times] = iter_ref[0, :, times] + update[1:-1]
        rest = rest_ref[0, :, times] - prior(update, coeff_ref)
        later_ref[0, :, times] = rest
        top_ref[0, :, times] = rest[:HALO]
        bottom_ref[0, :, times] = rest[rows - HALO :]

    time_chunks(iter_ref.shape[2], body)
    low_ref[...] = next_ref[...].astype(low_ref.dtype)


def step(rests, misfits, iterate, coeff):
    members, rows, steps, cols = iterate.shape
    field = pl.BlockSpec((1, rows, steps, cols), lambda b: (b, 0, 0, 0))
    rim = pl.BlockSpec((1, HALO, steps, cols), lambda b: (b, 0, 0, 0))
    rim_shape = (members, HALO, steps, cols)
    return pl.pallas_call(
        step_kernel,
        grid=(members,),
        in_specs=[rim, field, rim] * 2 + [field, whole_block(coeff)],
        out_specs=[field, field, field, rim, rim],
        out_shape=[
            jax.ShapeDtypeStruct(iterate.shape, jnp.float32),
            jax.ShapeDtypeStruct(iterate.shape, jnp.bfloat16),
            jax.ShapeDtypeStruct(iterate.shape, jnp.float32),
            jax.ShapeDtypeStruct(rim_shape, jnp.float32),
            jax.ShapeDtypeStruct(rim_shape, jnp.float32),
        ],
        compiler_params=params(),
        name="step",
    )(*rests, *misfits, iterate, coeff)


def finish_kernel(
    up_ref, rest_ref, down_ref, mup_ref, misfit_ref, mdown_ref, iter_ref, coeff_ref, *refs
):
    solution_ref, residual_ref = refs[-2:]

    def body(times):
        residual = residual_of(times, (up_ref, rest_ref, down_ref), (mup_ref, misfit_ref, mdown_ref))
        update = precondition(residual, coeff_ref)
        solution_ref[times] = jnp.swapaxes(iter_ref[0, :, times] + update[1:-1], 0, 1)
        residual_ref[times] = jnp.swapaxes(trim(residual, HALO), 0, 1)

    time_chunks(iter_ref.shape[2], body)


def finish(group, samples, rests, misfits, iterate, coeff, previous):
    members, rows, steps, cols = iterate.shape
    field = pl.BlockSpec((1, rows, steps, cols), lambda b: (b, 0, 0, 0))
    rim = pl.BlockSpec((1, HALO, steps, cols), lambda b: (b, 0, 0, 0))
    result = pl.BlockSpec((steps, rows, cols), lambda b: (0, b + group * members, 0))
    shape = jax.ShapeDtypeStruct((steps, samples * rows, cols), jnp.float32)
    first = 8
    return pl.pallas_call(
        finish_kernel,
        grid=(members,),
        in_specs=[rim, field, rim] * 2
        + [field, whole_block(coeff)]
        + [pl.BlockSpec(memory_space=pl.ANY)] * len(previous),
        out_specs=[result, result],
        out_shape=[shape, shape],
        input_output_aliases={first + k: k for k in range(len(previous))},
        compiler_params=params(),
        name="finish",
    )(*rests, *misfits, iterate, coeff, *previous)


def same_frequency(near, sensors):
    shape = (near, LANES)
    return lax.broadcasted_iota(jnp.int32, shape, 0) == (
        lax.broadcasted_iota(jnp.int32, shape, 1) // sensors
    )


def marks_of(cell_ref, width):
    first = pl.program_id(0) * width
    parts = []
    for start_lane in range(0, width, LANES):
        lane = lax.broadcasted_iota(jnp.int32, cell_ref.shape, 1) + (first + start_lane)
        parts.append(jnp.where(cell_ref[...] == lane, 1.0, 0.0).astype(jnp.bfloat16))
    return jnp.concatenate(parts, axis=1)


def observe_kernel(field_ref, map_ref, table_ref, cell_ref, real_ref, imag_ref, spec, acc, picked):
    devices, members, rows, steps, lanes = field_ref.shape
    freqs, sensors, width = map_ref.shape[1:]
    near = lanes // sensors
    chunk = pl.program_id(0)

    @pl.when(chunk == 0)
    def _():
        acc[...] = jnp.zeros_like(acc)
        picked[...] = jnp.zeros_like(picked)

    marks = marks_of(cell_ref, width)
    for b in range(members):
        history = jnp.concatenate(
            [field_ref[:, b, r].reshape(devices * steps, lanes) for r in range(rows)], axis=1
        )
        spectrum = dot(table_ref[...], history)
        spec[2 * b] = spectrum[:freqs]
        spec[2 * b + 1] = spectrum[freqs:]
    for m in range(2 * members):
        picked[m] += dot_lanes(spec[m].astype(jnp.bfloat16), marks)
    for q in range(freqs // near):
        here = slice(q * near, (q + 1) * near)
        left = spec[:, here].reshape(2 * members * near, width).astype(jnp.bfloat16)
        acc[q] += dot_lanes(left, map_ref[:, here].reshape(2 * near * sensors, width))

    @pl.when(chunk == pl.num_programs(0) - 1)
    def _():
        mask = same_frequency(near, sensors)
        for q in range(freqs // near):
            here = slice(q * near, (q + 1) * near)
            for b in range(members):
                real = acc[q, 2 * b * near : (2 * b + 1) * near]
                imag = acc[q, (2 * b + 1) * near : (2 * b + 2) * near]
                obs_real = real[:, :lanes] - imag[:, lanes:] + picked[2 * b, here]
                obs_imag = imag[:, :lanes] + real[:, lanes:] + picked[2 * b + 1, here]
                real_ref[b, q : q + 1] = jnp.sum(jnp.where(mask, obs_real, 0.0), 0, keepdims=True)
                imag_ref[b, q : q + 1] = jnp.sum(jnp.where(mask, obs_imag, 0.0), 0, keepdims=True)


def map_spec(forward_map, width):
    return pl.BlockSpec(forward_map.shape[:3] + (width,), lambda c: (0, 0, 0, c))


def observe(field, forward_map, table, local_cells):
    devices, members, rows, steps, lanes = field.shape
    _, freqs, sensors, cells = forward_map.shape
    width = CHUNK_ROWS * lanes
    near = lanes // sensors
    shape = (members, freqs // near, lanes)
    return pl.pallas_call(
        observe_kernel,
        grid=(rows // CHUNK_ROWS,),
        in_specs=[
            pl.BlockSpec((devices, members, CHUNK_ROWS, steps, lanes), lambda c: (0, 0, c, 0, 0)),
            map_spec(forward_map, width),
            whole_block(table),
            whole_block(local_cells),
        ],
        out_specs=[pl.BlockSpec(shape, lambda c: (0, 0, 0))] * 2,
        out_shape=[jax.ShapeDtypeStruct(shape, jnp.float32)] * 2,
        scratch_shapes=[
            pltpu.VMEM((2 * members, freqs, width), jnp.float32),
            pltpu.VMEM((freqs // near, 2 * members * near, 2 * lanes), jnp.float32),
            pltpu.VMEM((2 * members, freqs, lanes), jnp.float32),
        ],
        compiler_params=params(),
        cost_estimate=pl.CostEstimate(
            flops=8 * members * freqs * sensors * cells,
            bytes_accessed=2 * forward_map.size + 2 * field.size,
            transcendentals=0,
        ),
        name="observe",
    )(field, forward_map, table, local_cells)


def pull_kernel(*refs):
    reals, imags = refs[: len(refs) // 2 - 3], refs[len(refs) // 2 - 3 : -7]
    noise_ref, map_ref, back_ref, cell_ref, out_ref, weights, adjoint = refs[-7:]
    devices, members, rows, steps, lanes = out_ref.shape
    freqs, sensors, width = map_ref.shape[1:]
    near = lanes // sensors

    def total(parts, b):
        values = [part[b] for part in parts]
        while len(values) > 1:
            values = [values[k] + values[k + 1] for k in range(0, len(values), 2)]
        return (noise_ref[...] * values[0]).astype(jnp.bfloat16).astype(jnp.float32)

    @pl.when(pl.program_id(0) == 0)
    def _():
        mask = same_frequency(near, sensors)
        for b in range(members):
            real, imag = total(reals, b), total(imags, b)
            for q in range(freqs // near):
                here = slice(q * near, (q + 1) * near)
                w_real = jnp.where(mask, real[q : q + 1], 0.0)
                w_imag = jnp.where(mask, imag[q : q + 1], 0.0)
                weights[2 * b, here, :lanes] = w_real
                weights[2 * b, here, lanes:] = w_imag
                weights[2 * b + 1, here, :lanes] = w_imag
                weights[2 * b + 1, here, lanes:] = -w_real

    marks = marks_of(cell_ref, width)
    for m in range(2 * members):
        adjoint[m] = dot(weights[m, :, :lanes].astype(jnp.bfloat16), marks)
    for q in range(freqs // near):
        here = slice(q * near, (q + 1) * near)
        left = weights[:, here].reshape(2 * members * near, 2 * lanes).astype(jnp.bfloat16)
        part = dot(left, map_ref[:, here].reshape(2 * near * sensors, width))
        adjoint[:, here] += part.reshape(2 * members, near, width)
    for b in range(members):
        whole = adjoint[2 * b : 2 * b + 2].reshape(2 * freqs, width)
        high = whole.astype(jnp.bfloat16)
        low = (whole - high.astype(jnp.float32)).astype(jnp.bfloat16)
        misfit = (dot(back_ref[...], high) + dot(back_ref[...], low)).astype(out_ref.dtype)
        for r in range(rows):
            part = misfit[:, r * lanes : (r + 1) * lanes]
            out_ref[:, b, r] = part.reshape(devices, steps, lanes)


def pull_back(reals, imags, noise, forward_map, back, local_cells, shape):
    devices, members, rows, steps, lanes = shape
    _, freqs, sensors, cells = forward_map.shape
    width = CHUNK_ROWS * lanes
    small = [*reals, *imags, noise]
    return pl.pallas_call(
        pull_kernel,
        grid=(rows // CHUNK_ROWS,),
        in_specs=[whole_block(array) for array in small]
        + [map_spec(forward_map, width), whole_block(back), whole_block(local_cells)],
        out_specs=pl.BlockSpec(
            (devices, members, CHUNK_ROWS, steps, lanes), lambda c: (0, 0, c, 0, 0)
        ),
        out_shape=jax.ShapeDtypeStruct(shape, jnp.bfloat16),
        scratch_shapes=[
            pltpu.VMEM((2 * members, freqs, 2 * lanes), jnp.float32),
            pltpu.VMEM((2 * members, freqs, width), jnp.float32),
        ],
        compiler_params=params(),
        cost_estimate=pl.CostEstimate(
            flops=8 * members * freqs * sensors * cells,
            bytes_accessed=2 * forward_map.size + 2 * math.prod(shape),
            transcendentals=0,
        ),
        name="pull_back",
    )(*small, forward_map, back, local_cells)


def rims(top, bottom):
    size = lax.axis_size("cells")
    onward = [(k, k + 1) for k in range(size - 1)]
    backward = [(k + 1, k) for k in range(size - 1)]
    return lax.ppermute(bottom, "cells", onward), lax.ppermute(top, "cells", backward)


def from_all_cells(value):
    size = lax.axis_size("cells")
    if size & (size - 1):
        return [lax.psum(value, "cells")]
    return [value] + [
        lax.ppermute(value, "cells", [(k, k ^ other) for k in range(size)])
        for other in range(1, size)
    ]


def shards(rhs, forward_map, stiffness, reaction, noise_weight, sensor_cell):
    steps, samples, rows, cols = rhs.shape
    _, freqs, sensors, cells = forward_map.shape
    times_over = lax.axis_size("sensors")
    table = transform_table(freqs, 2 * freqs)
    back = table.T
    near = LANES // sensors

    diagonal = reaction + 4.0 * stiffness * stiffness
    local = jnp.stack([stiffness, diagonal])
    up, down = rims(local[:, :HALO], local[:, rows - HALO :])
    stiff, diag = jnp.concatenate([up, local, down], axis=1)
    inside = diag > 0.0
    inverse = jnp.where(inside, 1.0 / jnp.where(inside, diag, 1.0), 0.0)
    unscale = jnp.where(inside, 1.0 / jnp.where(inside, stiff, 1.0), 0.0)
    scaled = DAMPING * inverse * stiff
    coeff = jnp.stack([scaled, scaled * stiff, unscale, stiff, diag])
    coeff = jnp.broadcast_to(coeff[:, :, None, :], coeff.shape[:2] + (SUBLANES, cols))

    cell_index = lax.axis_index("cells")
    sensor_index = lax.axis_index("sensors")
    local_cells = lax.dynamic_slice_in_dim(sensor_cell, sensor_index * sensors, sensors)
    local_cells = jnp.tile(local_cells - cell_index * cells, near)[:, None]
    local_cells = jnp.broadcast_to(local_cells, (LANES, LANES))
    noise = lax.dynamic_slice_in_dim(noise_weight, sensor_index * sensors, sensors)
    noise = jnp.tile(noise, near)[None, :]

    up, down = rims(
        jnp.transpose(rhs[:, :, :HALO], (1, 2, 0, 3)),
        jnp.transpose(rhs[:, :, rows - HALO :], (1, 2, 0, 3)),
    )
    members = samples // GROUPS
    states = []
    for group in range(GROUPS):
        states.append(start(group, members, rhs, up, down, coeff))

    outputs = ()
    for iteration in range(ITERS):
        for group in range(GROUPS):
            iterate, low, rest, top, bottom = states[group]
            above, below = rims(top, bottom)
            field = lax.all_gather(low, "sensors", axis=0, tiled=False)
            real, imag = observe(field, forward_map, table, local_cells)
            misfit = pull_back(
                from_all_cells(real),
                from_all_cells(imag),
                noise,
                forward_map,
                back,
                local_cells,
                (times_over, members, rows, steps, cols),
            )
            misfit = lax.psum_scatter(misfit, "sensors", scatter_dimension=0, tiled=False)
            m_above, m_below = rims(misfit[:, :HALO], misfit[:, rows - HALO :])
            rests, misfits = (above, rest, below), (m_above, misfit, m_below)
            if iteration < ITERS - 1:
                states[group] = step(rests, misfits, iterate, coeff)
            else:
                outputs = finish(group, samples, rests, misfits, iterate, coeff, outputs)
    return tuple(out.reshape(rhs.shape) for out in outputs)


def solution(mesh):
    placed = (
        P("sensors", None, "cells", None),
        P(None, None, "sensors", "cells"),
        P("cells", None),
        P("cells", None),
        P(),
        P(),
    )
    return jax.shard_map(
        shards,
        mesh=mesh,
        in_specs=placed,
        out_specs=(P("sensors", None, "cells", None), P("sensors", None, "cells", None)),
        check_vma=False,
    )
```

```python
import math

import jax
import jax.numpy as jnp
from jax import lax
from jax.experimental import pallas as pl
from jax.experimental.pallas import tpu as pltpu
from jax.sharding import PartitionSpec as P

SWEEPS = 4
ITERS = 2
DAMPING = 0.8
HALO = SWEEPS
LANES = 128
SUBLANES = 8
GROUPS = 3
CHUNK_ROWS = 4
VMEM_BYTES = 40 * 2**20


def transform_table(freqs, moments):
    period = moments.size
    wave = jnp.arange(freqs, dtype=jnp.int32)[:, None]
    moment = moments.reshape(1, period)
    phase = (wave * moment % period).astype(jnp.float32) * (2.0 * math.pi / period)
    factor = 1.0 / math.sqrt(period)
    return jnp.concatenate([jnp.cos(phase) * factor, -jnp.sin(phase) * factor], axis=0).astype(
        jnp.bfloat16
    )


def whole_block(array):
    return pl.BlockSpec(array.shape, lambda *_: (0,) * array.ndim)


def call(kernel, core, grid, in_specs, out_specs, out_shape, scratch=(), aliases=None, **kwargs):
    grid_spec = pltpu.PrefetchScalarGridSpec(
        num_scalar_prefetch=1,
        grid=grid,
        in_specs=in_specs,
        out_specs=out_specs,
        scratch_shapes=list(scratch),
    )
    return pl.pallas_call(
        kernel,
        grid_spec=grid_spec,
        out_shape=out_shape,
        input_output_aliases=aliases or {},
        compiler_params=pltpu.CompilerParams(vmem_limit_bytes=VMEM_BYTES),
        **kwargs,
    )


def dot(left, right):
    return jnp.dot(left, right, preferred_element_type=jnp.float32)


def dot_lanes(left, right):
    return lax.dot_general(left, right, (((1,), (1,)), ((), ())), preferred_element_type=jnp.float32)


def neighbours(field):
    inner = field[1:-1]
    lane = lax.broadcasted_iota(jnp.int32, inner.shape, 2)
    before = jnp.where(lane == 0, 0.0, pltpu.roll(inner, 1, 2))
    after = jnp.where(lane == LANES - 1, 0.0, pltpu.roll(inner, LANES - 1, 2))
    return (field[2:] + field[:-2]) + (before + after)


def trim(array, width):
    return array[width : array.shape[0] - width]


def precondition(residual, coeff_ref):
    extra = (coeff_ref.shape[1] - residual.shape[0]) // 2
    coeff = [trim(coeff_ref[k], extra) for k in range(3)]
    first = coeff[0] * residual
    scaled = first
    for sweep in range(1, SWEEPS):
        scaled = (
            (1.0 - DAMPING) * scaled[1:-1]
            + trim(first, sweep)
            + trim(coeff[1], sweep) * neighbours(scaled)
        )
    return trim(coeff[2], SWEEPS - 1) * scaled


def prior(field, coeff_ref):
    extra = (coeff_ref.shape[1] - field.shape[0]) // 2
    stiffness = trim(coeff_ref[3], extra)
    diagonal = trim(coeff_ref[4], extra + 1)
    return diagonal * field[1:-1] - stiffness[1:-1] * neighbours(stiffness * field)


def time_chunks(steps, body):
    def run(index, carry):
        body(pl.ds(pl.multiple_of(index * SUBLANES, SUBLANES), SUBLANES))
        return carry

    lax.fori_loop(0, steps // SUBLANES, run, 0)


def fields(members, rows, steps, cols):
    field = pl.BlockSpec((1, rows, steps, cols), lambda b, core: (b, 0, 0, 0))
    half = pl.BlockSpec((1, rows // 2, steps, cols), lambda b, core: (b, 0, 0, 0))
    rim = pl.BlockSpec((1, HALO, steps, cols), lambda b, core: (b, 0, 0, 0))

    def shape(count, dtype):
        return jax.ShapeDtypeStruct((members, count, steps, cols), dtype)

    specs = [field, half, half, field, rim, rim]
    shapes = [
        shape(rows, jnp.float32),
        shape(rows // 2, jnp.bfloat16),
        shape(rows // 2, jnp.bfloat16),
        shape(rows, jnp.float32),
        shape(HALO, jnp.bfloat16),
        shape(HALO, jnp.bfloat16),
    ]
    return field, half, rim, specs, shapes


def put_rest(rest, times, rest_ref, top_ref, bottom_ref):
    rest_ref[0, :, times] = rest
    top_ref[0, :, times] = rest[:HALO].astype(top_ref.dtype)
    bottom_ref[0, :, times] = rest[rest.shape[0] - HALO :].astype(bottom_ref.dtype)


def put_low(core, iter_ref, keep_ref, give_ref):
    half = keep_ref.shape[1]
    keep_ref[0] = iter_ref[0, pl.ds(core * half, half)].astype(keep_ref.dtype)
    give_ref[0] = iter_ref[0, pl.ds((1 - core) * half, half)].astype(give_ref.dtype)


def start_kernel(
    core_ref, rhs_ref, up_ref, down_ref, coeff_ref,
    iter_ref, keep_ref, give_ref, rest_ref, top_ref, bottom_ref,
):
    def body(times):
        here = jnp.swapaxes(rhs_ref[times], 0, 1)
        rims_here = [ref[0, :, times].astype(jnp.float32) for ref in (up_ref, down_ref)]
        update = precondition(jnp.concatenate([rims_here[0], here, rims_here[1]], axis=0), coeff_ref)
        iter_ref[0, :, times] = update[1:-1]
        put_rest(here - prior(update, coeff_ref), times, rest_ref, top_ref, bottom_ref)

    time_chunks(iter_ref.shape[2], body)
    put_low(core_ref[0], iter_ref, keep_ref, give_ref)


def start(group, members, core, rhs, up, down, coeff):
    steps, _, rows, cols = rhs.shape
    flat = rhs.reshape(steps, -1, cols)
    field, half, rim, specs, shapes = fields(members, rows, steps, cols)
    return call(
        start_kernel,
        core,
        (members,),
        [
            pl.BlockSpec((steps, rows, cols), lambda b, core: (0, b + group * members, 0)),
            rim,
            rim,
            whole_block(coeff),
        ],
        specs,
        shapes,
        name="start",
    )(core, flat, up, down, coeff)


def residual_of(core, times, rest_refs, misfit_refs, whole_ref):
    own_ref, other_ref, same_ref, cross_ref = misfit_refs
    half = own_ref.shape[1]
    whole_ref[pl.ds(core * half, half)] = own_ref[0, :, times].astype(jnp.float32)
    whole_ref[pl.ds((1 - core) * half, half)] = other_ref[0, :, times].astype(jnp.float32)
    same = same_ref[0, :, times].astype(jnp.float32)
    cross = cross_ref[0, :, times].astype(jnp.float32)
    first = core == 0
    parts = [jnp.where(first, cross, same), whole_ref[...], jnp.where(first, same, cross)]
    rests = [ref[0, :, times].astype(jnp.float32) for ref in rest_refs]
    return jnp.concatenate([rest - part for rest, part in zip(rests, parts)], axis=0)


def step_kernel(
    core_ref, up_ref, rest_ref, down_ref, own_ref, other_ref, same_ref, cross_ref, iter_ref, coeff_ref,
    next_ref, keep_ref, give_ref, later_ref, top_ref, bottom_ref, whole_ref,
):
    def body(times):
        residual = residual_of(
            core_ref[0],
            times,
            (up_ref, rest_ref, down_ref),
            (own_ref, other_ref, same_ref, cross_ref),
            whole_ref,
        )
        update = precondition(residual, coeff_ref)
        next_ref[0, :, times] = iter_ref[0, :, times] + update[1:-1]
        put_rest(rest_ref[0, :, times] - prior(update, coeff_ref), times, later_ref, top_ref, bottom_ref)

    time_chunks(iter_ref.shape[2], body)
    put_low(core_ref[0], next_ref, keep_ref, give_ref)


def step(core, rests, misfits, iterate, coeff):
    members, rows, steps, cols = iterate.shape
    field, half, rim, specs, shapes = fields(members, rows, steps, cols)
    return call(
        step_kernel,
        core,
        (members,),
        [rim, field, rim, half, half, rim, rim, field, whole_block(coeff)],
        specs,
        shapes,
        [pltpu.VMEM((rows, SUBLANES, cols), jnp.float32)],
        name="step",
    )(core, *rests, *misfits, iterate, coeff)


def finish_kernel(
    core_ref, up_ref, rest_ref, down_ref, own_ref, other_ref, same_ref, cross_ref, iter_ref, coeff_ref,
    *refs,
):
    solution_ref, residual_ref, whole_ref = refs[-3:]

    def body(times):
        residual = residual_of(
            core_ref[0],
            times,
            (up_ref, rest_ref, down_ref),
            (own_ref, other_ref, same_ref, cross_ref),
            whole_ref,
        )
        update = precondition(residual, coeff_ref)
        solution_ref[times] = jnp.swapaxes(iter_ref[0, :, times] + update[1:-1], 0, 1)
        residual_ref[times] = jnp.swapaxes(trim(residual, HALO), 0, 1)

    time_chunks(iter_ref.shape[2], body)


def finish(group, samples, core, rests, misfits, iterate, coeff, previous):
    members, rows, steps, cols = iterate.shape
    field, half, rim, _, _ = fields(members, rows, steps, cols)
    result = pl.BlockSpec((steps, rows, cols), lambda b, core: (0, b + group * members, 0))
    shape = jax.ShapeDtypeStruct((steps, samples * rows, cols), jnp.float32)
    in_specs = [rim, field, rim, half, half, rim, rim, field, whole_block(coeff)]
    first = 1 + len(in_specs)
    return call(
        finish_kernel,
        core,
        (members,),
        in_specs + [pl.BlockSpec(memory_space=pl.ANY)] * len(previous),
        [result, result],
        [shape, shape],
        [pltpu.VMEM((rows, SUBLANES, cols), jnp.float32)],
        {first + k: k for k in range(len(previous))},
        name="finish",
    )(core, *rests, *misfits, iterate, coeff, *previous)


def same_frequency(near, sensors, lanes):
    shape = (near, lanes)
    return lax.broadcasted_iota(jnp.int32, shape, 0) == (
        lax.broadcasted_iota(jnp.int32, shape, 1) % LANES // sensors
    )


def marks_of(cell_ref, width):
    first = pl.program_id(0) * width
    parts = []
    for start_lane in range(0, width, LANES):
        lane = lax.broadcasted_iota(jnp.int32, cell_ref.shape, 1) + (first + start_lane)
        parts.append(jnp.where(cell_ref[...] == lane, 1.0, 0.0).astype(jnp.bfloat16))
    return jnp.concatenate(parts, axis=1)


def near_map(own_ref, other_ref, here):
    _, freqs, sensors, width = own_ref.shape
    parts = [
        ref[part, here].reshape(LANES, width) for part in range(2) for ref in (own_ref, other_ref)
    ]
    return jnp.concatenate(parts, axis=0)


def observe_kernel(core_ref, *refs):
    *field_refs, own_ref, other_ref, table_ref, cell_ref, out_ref, spec, acc, picked = refs
    _, members, rows, steps, lanes = field_refs[0].shape
    freqs, sensors, width = own_ref.shape[1:]
    near = lanes // sensors
    wide = 2 * lanes
    count = len(field_refs) // 2 + 1
    chunk = pl.program_id(0)

    @pl.when(chunk == 0)
    def _():
        acc[...] = jnp.zeros_like(acc)
        picked[...] = jnp.zeros_like(picked)

    marks = marks_of(cell_ref, width)

    def history(b, r):
        slots = [field_refs[0][:, b, r]]
        for k in range(1, count):
            slots.append(field_refs[k][:, b, r] + field_refs[2 * count - 1 - k][:, b, r])
        return jnp.concatenate([slot.reshape(2 * steps, lanes) for slot in slots], axis=0)

    for b in range(members):
        spectrum = dot(
            table_ref[...], jnp.concatenate([history(b, r) for r in range(rows)], axis=1)
        )
        spec[2 * b] = spectrum[:freqs]
        spec[2 * b + 1] = spectrum[freqs:]
    for m in range(2 * members):
        picked[m] += dot_lanes(spec[m].astype(jnp.bfloat16), marks)
    for q in range(freqs // near):
        here = slice(q * near, (q + 1) * near)
        left = spec[:, here].reshape(2 * members * near, width).astype(jnp.bfloat16)
        acc[q] += dot_lanes(left, near_map(own_ref, other_ref, here))

    @pl.when(chunk == pl.num_programs(0) - 1)
    def _():
        mask = same_frequency(near, sensors, wide)
        for q in range(freqs // near):
            here = slice(q * near, (q + 1) * near)
            for b in range(members):
                real = acc[q, 2 * b * near : (2 * b + 1) * near]
                imag = acc[q, (2 * b + 1) * near : (2 * b + 2) * near]
                sums = (
                    real[:, :wide] - imag[:, wide:] + picked[2 * b, here],
                    imag[:, :wide] + real[:, wide:] + picked[2 * b + 1, here],
                )
                for part, value in enumerate(sums):
                    line = jnp.sum(jnp.where(mask, value, 0.0), 0, keepdims=True)
                    out_ref[0, part, b, q : q + 1] = line[:, :lanes]
                    out_ref[1, part, b, q : q + 1] = line[:, lanes:]


def map_specs(own, other, width):
    chunks = other.shape[3] // width
    return [
        pl.BlockSpec(own.shape[:3] + (width,), lambda c, core: (0, 0, 0, core[0] * chunks + c)),
        pl.BlockSpec(other.shape[:3] + (width,), lambda c, core: (0, 0, 0, c)),
    ]


def map_cost(members, own, other, moved):
    return pl.CostEstimate(
        flops=16 * members * other.size,
        bytes_accessed=4 * other.size + 2 * moved,
        transcendentals=0,
    )


def observe(core, slots, own, other, table, local_cells):
    _, members, rows, steps, lanes = slots[0].shape
    _, freqs, sensors, cells = other.shape
    width = CHUNK_ROWS * lanes
    near = lanes // sensors
    shape = (2, 2, members, freqs // near, lanes)
    slot = pl.BlockSpec((2, members, CHUNK_ROWS, steps, lanes), lambda c, core: (0, 0, c, 0, 0))
    return call(
        observe_kernel,
        core,
        (rows // CHUNK_ROWS,),
        [slot] * len(slots)
        + map_specs(own, other, width)
        + [whole_block(table), whole_block(local_cells)],
        pl.BlockSpec(shape, lambda c, core: (0, 0, 0, 0, 0)),
        jax.ShapeDtypeStruct(shape, jnp.float32),
        [
            pltpu.VMEM((2 * members, freqs, width), jnp.float32),
            pltpu.VMEM((freqs // near, 2 * members * near, 4 * lanes), jnp.float32),
            pltpu.VMEM((2 * members, freqs, 2 * lanes), jnp.float32),
        ],
        cost_estimate=map_cost(members, own, other, len(slots) * slots[0].size),
        name="observe",
    )(core, *slots, own, other, table, local_cells)


def pull_kernel(core_ref, *refs):
    *sums, noise_ref, own_ref, other_ref, back_ref, cell_ref, out_ref, weights, adjoint = refs
    devices, _, members, rows, steps, lanes = out_ref.shape
    freqs, sensors, width = own_ref.shape[1:]
    near = lanes // sensors
    wide = 2 * lanes

    def total(part, b, which):
        values = [ref[which, part, b] for ref in sums]
        while len(values) > 1:
            values = [values[k] + values[k + 1] for k in range(0, len(values), 2)]
        noise = noise_ref[which : which + 1]
        return (noise * values[0]).astype(jnp.bfloat16).astype(jnp.float32)

    @pl.when(pl.program_id(0) == 0)
    def _():
        mask = same_frequency(near, sensors, wide)
        for b in range(members):
            real, imag = (
                jnp.concatenate([total(part, b, 0), total(part, b, 1)], axis=1) for part in range(2)
            )
            for q in range(freqs // near):
                here = slice(q * near, (q + 1) * near)
                w_real = jnp.where(mask, real[q : q + 1], 0.0)
                w_imag = jnp.where(mask, imag[q : q + 1], 0.0)
                weights[2 * b, here, :wide] = w_real
                weights[2 * b, here, wide:] = w_imag
                weights[2 * b + 1, here, :wide] = w_imag
                weights[2 * b + 1, here, wide:] = -w_real

    marks = marks_of(cell_ref, width)
    for m in range(2 * members):
        adjoint[m] = dot(weights[m, :, :wide].astype(jnp.bfloat16), marks)
    for q in range(freqs // near):
        here = slice(q * near, (q + 1) * near)
        left = weights[:, here].reshape(2 * members * near, 2 * wide).astype(jnp.bfloat16)
        part = dot(left, near_map(own_ref, other_ref, here))
        adjoint[:, here] += part.reshape(2 * members, near, width)
    for b in range(members):
        whole = adjoint[2 * b : 2 * b + 2].reshape(2 * freqs, width)
        high = whole.astype(jnp.bfloat16)
        low = (whole - high.astype(jnp.float32)).astype(jnp.bfloat16)
        misfit = (dot(back_ref[...], high) + dot(back_ref[...], low)).astype(out_ref.dtype)
        for r in range(rows):
            part = misfit[:, r * lanes : (r + 1) * lanes]
            out_ref[:, :, b, r] = part.reshape(devices, 2, steps, lanes)


def pull_back(core, sums, noise, own, other, back, local_cells, shape):
    devices, _, members, rows, steps, lanes = shape
    _, freqs, sensors, cells = other.shape
    width = CHUNK_ROWS * lanes
    small = [*sums, noise]
    return call(
        pull_kernel,
        core,
        (rows // CHUNK_ROWS,),
        [whole_block(array) for array in small]
        + map_specs(own, other, width)
        + [whole_block(back), whole_block(local_cells)],
        pl.BlockSpec(
            (devices, 2, members, CHUNK_ROWS, steps, lanes), lambda c, core: (0, 0, 0, c, 0, 0)
        ),
        jax.ShapeDtypeStruct(shape, jnp.bfloat16),
        [
            pltpu.VMEM((2 * members, freqs, 4 * lanes), jnp.float32),
            pltpu.VMEM((2 * members, freqs, width), jnp.float32),
        ],
        cost_estimate=map_cost(members, own, other, math.prod(shape)),
        name="pull_back",
    )(core, *small, own, other, back, local_cells)


def rims(top, bottom):
    size = lax.axis_size("cells")
    onward = [(k, k + 1) for k in range(size - 1)]
    backward = [(k + 1, k) for k in range(size - 1)]
    return lax.ppermute(bottom, "cells", onward), lax.ppermute(top, "cells", backward)


def misfit_rims(edge):
    size, width = lax.axis_size("cells"), lax.axis_size("sensors")
    same, cross = [], []
    for cell in range(size):
        for sensor in range(width):
            there = cell + 2 * (sensor % 2) - 1
            if 0 <= there < size:
                same.append((cell * width + sensor, there * width + sensor))
                cross.append((cell * width + sensor, there * width + (sensor ^ 1)))
    both = ("cells", "sensors")
    return lax.ppermute(edge, both, same), lax.ppermute(edge, both, cross)


def swap_cores(value):
    size = lax.axis_size("sensors")
    return lax.ppermute(value, "sensors", [(k, k ^ 1) for k in range(size)])


def from_all_cells(value):
    size = lax.axis_size("cells")
    if size & (size - 1):
        return [lax.psum(value, "cells")]
    return [value] + [
        lax.ppermute(value, "cells", [(k, k ^ other) for k in range(size)])
        for other in range(1, size)
    ]


def gather_line(value):
    size = lax.axis_size("sensors")
    chips = size // 2
    ups, downs = [value], [value]
    for hop in range(1, chips):
        onward = [(k, k + 2) for k in range(2 * hop - 2, size - 2)]
        backward = [(size - 1 - k, size - 1 - there) for k, there in onward]
        ups.append(lax.ppermute(ups[-1], "sensors", onward))
        downs.append(lax.ppermute(downs[-1], "sensors", backward))
    return [value, *ups[1:], *downs[1:]]


def shards(rhs, forward_map, stiffness, reaction, noise_weight, sensor_cell):
    steps, samples, rows, cols = rhs.shape
    _, freqs, sensors, cells = forward_map.shape
    size = lax.axis_size("sensors")
    chips = size // 2
    cell_index = lax.axis_index("cells")
    sensor_index = lax.axis_index("sensors")
    core = sensor_index % 2
    chip = sensor_index // 2
    near = LANES // sensors
    half = cells // 2

    away = lax.dynamic_slice_in_dim(forward_map, (1 - core) * half, half, axis=3)
    other_map = swap_cores(away)

    cores = jnp.stack([core, 1 - core])
    offsets = cores[None, :, None] * steps + jnp.arange(steps, dtype=jnp.int32)
    chip_steps = 2 * steps
    places = (chip - jnp.arange(chips, dtype=jnp.int32)) % chips
    table = transform_table(freqs, places[:, None, None] * chip_steps + offsets)
    places = jnp.arange(chips, dtype=jnp.int32)
    back = transform_table(freqs, places[:, None, None] * chip_steps + offsets).T

    diagonal = reaction + 4.0 * stiffness * stiffness
    local = jnp.stack([stiffness, diagonal])
    up, down = rims(local[:, :HALO], local[:, rows - HALO :])
    stiff, diag = jnp.concatenate([up, local, down], axis=1)
    inside = diag > 0.0
    inverse = jnp.where(inside, 1.0 / jnp.where(inside, diag, 1.0), 0.0)
    unscale = jnp.where(inside, 1.0 / jnp.where(inside, stiff, 1.0), 0.0)
    scaled = DAMPING * inverse * stiff
    coeff = jnp.stack([scaled, scaled * stiff, unscale, stiff, diag])
    coeff = jnp.broadcast_to(coeff[:, :, None, :], coeff.shape[:2] + (SUBLANES, cols))

    def per_lane(values):
        own = lax.dynamic_slice_in_dim(values, sensor_index * sensors, sensors)
        other = lax.dynamic_slice_in_dim(values, (sensor_index ^ 1) * sensors, sensors)
        return jnp.stack([jnp.tile(own, near), jnp.tile(other, near)])

    noise = per_lane(noise_weight)
    local_cells = per_lane(sensor_cell) - (cell_index * cells + core * half)
    local_cells = jnp.broadcast_to(local_cells.reshape(2 * LANES, 1), (2 * LANES, LANES))
    core = core.reshape(1)

    members = samples // GROUPS
    states = []
    for group in range(GROUPS):
        group_rhs = rhs[:, group * members : (group + 1) * members]
        up, down = rims(
            *(
                jnp.transpose(rim, (1, 2, 0, 3)).astype(jnp.bfloat16)
                for rim in (group_rhs[:, :, :HALO], group_rhs[:, :, rows - HALO :])
            )
        )
        states.append(start(group, members, core, rhs, up, down, coeff))

    lines = [[k for k in range(size) if k % 2 == parity] for parity in range(2)]
    outputs = ()
    for iteration in range(ITERS):
        for group in range(GROUPS):
            iterate, keep, give, rest, top, bottom = states[group]
            above, below = rims(top, bottom)
            slots = gather_line(jnp.stack([keep, swap_cores(give)]))
            sums = observe(core, slots, forward_map, other_map, table, local_cells)
            sums = from_all_cells(sums + swap_cores(sums)[::-1])
            shape = (chips, 2, members, rows // 2, steps, cols)
            misfit = pull_back(core, sums, noise, forward_map, other_map, back, local_cells, shape)
            misfit = lax.psum_scatter(
                misfit, "sensors", scatter_dimension=0, axis_index_groups=lines, tiled=False
            )
            first = (rows // 2 - HALO) * core[0]
            edge = lax.dynamic_slice_in_dim(misfit, first, HALO, axis=2)
            same, _ = misfit_rims(edge[0])
            _, cross = misfit_rims(edge[1])
            misfits = (misfit[0], swap_cores(misfit[1]), same, cross)
            rests = (above, rest, below)
            if iteration < ITERS - 1:
                states[group] = step(core, rests, misfits, iterate, coeff)
            else:
                outputs = finish(group, samples, core, rests, misfits, iterate, coeff, outputs)
    return tuple(out.reshape(rhs.shape) for out in outputs)


def solution(mesh):
    placed = (
        P("sensors", None, "cells", None),
        P(None, None, "sensors", "cells"),
        P("cells", None),
        P("cells", None),
        P(),
        P(),
    )
    return jax.shard_map(
        shards,
        mesh=mesh,
        in_specs=placed,
        out_specs=(P("sensors", None, "cells", None), P("sensors", None, "cells", None)),
        check_vma=False,
    )
```

```python
import math

import jax
import jax.numpy as jnp
from jax import lax
from jax.experimental import pallas as pl
from jax.experimental.pallas import tpu as pltpu
from jax.sharding import PartitionSpec as P

SWEEPS = 4
ITERS = 2
DAMPING = 0.8
HALO = SWEEPS
LANES = 128
SUBLANES = 8
GROUPS = 2
CHUNK_ROWS = 4
VMEM_BYTES = 40 * 2**20


def transform_table(freqs, moments):
    period = moments.size
    wave = jnp.arange(freqs, dtype=jnp.int32)[:, None]
    moment = moments.reshape(1, period)
    phase = (wave * moment % period).astype(jnp.float32) * (2.0 * math.pi / period)
    factor = 1.0 / math.sqrt(period)
    return jnp.concatenate([jnp.cos(phase) * factor, -jnp.sin(phase) * factor], axis=0).astype(
        jnp.bfloat16
    )


def whole_block(array):
    return pl.BlockSpec(array.shape, lambda *_: (0,) * array.ndim)


def call(kernel, core, grid, in_specs, out_specs, out_shape, scratch=(), aliases=None, **kwargs):
    grid_spec = pltpu.PrefetchScalarGridSpec(
        num_scalar_prefetch=1,
        grid=grid,
        in_specs=in_specs,
        out_specs=out_specs,
        scratch_shapes=list(scratch),
    )
    return pl.pallas_call(
        kernel,
        grid_spec=grid_spec,
        out_shape=out_shape,
        input_output_aliases=aliases or {},
        compiler_params=pltpu.CompilerParams(vmem_limit_bytes=VMEM_BYTES),
        **kwargs,
    )


def dot(left, right):
    return jnp.dot(left, right, preferred_element_type=jnp.float32)


def dot_lanes(left, right):
    return lax.dot_general(left, right, (((1,), (1,)), ((), ())), preferred_element_type=jnp.float32)


def neighbours(field):
    inner = field[1:-1]
    lane = lax.broadcasted_iota(jnp.int32, inner.shape, 2)
    before = jnp.where(lane == 0, 0.0, pltpu.roll(inner, 1, 2))
    after = jnp.where(lane == LANES - 1, 0.0, pltpu.roll(inner, LANES - 1, 2))
    return (field[2:] + field[:-2]) + (before + after)


def trim(array, width):
    return array[width : array.shape[0] - width]


def precondition(residual, coeff_ref):
    extra = (coeff_ref.shape[1] - residual.shape[0]) // 2
    coeff = [trim(coeff_ref[k], extra) for k in range(3)]
    first = coeff[0] * residual
    scaled = first
    for sweep in range(1, SWEEPS):
        scaled = (
            (1.0 - DAMPING) * scaled[1:-1]
            + trim(first, sweep)
            + trim(coeff[1], sweep) * neighbours(scaled)
        )
    return trim(coeff[2], SWEEPS - 1) * scaled


def prior(field, coeff_ref):
    extra = (coeff_ref.shape[1] - field.shape[0]) // 2
    stiffness = trim(coeff_ref[3], extra)
    diagonal = trim(coeff_ref[4], extra + 1)
    return diagonal * field[1:-1] - stiffness[1:-1] * neighbours(stiffness * field)


def time_chunks(steps, body):
    def run(index, carry):
        body(pl.ds(pl.multiple_of(index * SUBLANES, SUBLANES), SUBLANES))
        return carry

    lax.fori_loop(0, steps // SUBLANES, run, 0)


def fields(members, rows, steps, cols):
    field = pl.BlockSpec((1, rows, steps, cols), lambda b, core: (b, 0, 0, 0))
    half = pl.BlockSpec((1, rows // 2, steps, cols), lambda b, core: (b, 0, 0, 0))
    rim = pl.BlockSpec((1, HALO, steps, cols), lambda b, core: (b, 0, 0, 0))

    def shape(count, dtype):
        return jax.ShapeDtypeStruct((members, count, steps, cols), dtype)

    specs = [field, half, half, field, rim, rim]
    shapes = [
        shape(rows, jnp.float32),
        shape(rows // 2, jnp.bfloat16),
        shape(rows // 2, jnp.bfloat16),
        shape(rows, jnp.float32),
        shape(HALO, jnp.bfloat16),
        shape(HALO, jnp.bfloat16),
    ]
    return field, half, rim, specs, shapes


def put_rest(rest, times, rest_ref, top_ref, bottom_ref):
    rest_ref[0, :, times] = rest
    top_ref[0, :, times] = rest[:HALO].astype(top_ref.dtype)
    bottom_ref[0, :, times] = rest[rest.shape[0] - HALO :].astype(bottom_ref.dtype)


def put_low(core, iter_ref, keep_ref, give_ref):
    half = keep_ref.shape[1]
    keep_ref[0] = iter_ref[0, pl.ds(core * half, half)].astype(keep_ref.dtype)
    give_ref[0] = iter_ref[0, pl.ds((1 - core) * half, half)].astype(give_ref.dtype)


def start_kernel(
    core_ref, rhs_ref, up_ref, down_ref, coeff_ref,
    iter_ref, keep_ref, give_ref, rest_ref, top_ref, bottom_ref,
):
    def body(times):
        here = jnp.swapaxes(rhs_ref[times], 0, 1)
        rims_here = [ref[0, :, times].astype(jnp.float32) for ref in (up_ref, down_ref)]
        update = precondition(jnp.concatenate([rims_here[0], here, rims_here[1]], axis=0), coeff_ref)
        iter_ref[0, :, times] = update[1:-1]
        put_rest(here - prior(update, coeff_ref), times, rest_ref, top_ref, bottom_ref)

    time_chunks(iter_ref.shape[2], body)
    put_low(core_ref[0], iter_ref, keep_ref, give_ref)


def start(group, members, core, rhs, up, down, coeff):
    steps, _, rows, cols = rhs.shape
    flat = rhs.reshape(steps, -1, cols)
    field, half, rim, specs, shapes = fields(members, rows, steps, cols)
    return call(
        start_kernel,
        core,
        (members,),
        [
            pl.BlockSpec((steps, rows, cols), lambda b, core: (0, b + group * members, 0)),
            rim,
            rim,
            whole_block(coeff),
        ],
        specs,
        shapes,
        name="start",
    )(core, flat, up, down, coeff)


def residual_of(core, times, rest_refs, misfit_refs, whole_ref):
    own_ref, other_ref, same_ref, cross_ref = misfit_refs
    half = own_ref.shape[1]
    whole_ref[pl.ds(core * half, half)] = own_ref[0, :, times].astype(jnp.float32)
    whole_ref[pl.ds((1 - core) * half, half)] = other_ref[0, :, times].astype(jnp.float32)
    same = same_ref[0, :, times].astype(jnp.float32)
    cross = cross_ref[0, :, times].astype(jnp.float32)
    first = core == 0
    parts = [jnp.where(first, cross, same), whole_ref[...], jnp.where(first, same, cross)]
    rests = [ref[0, :, times].astype(jnp.float32) for ref in rest_refs]
    return jnp.concatenate([rest - part for rest, part in zip(rests, parts)], axis=0)


def step_kernel(
    core_ref, up_ref, rest_ref, down_ref, own_ref, other_ref, same_ref, cross_ref, iter_ref, coeff_ref,
    next_ref, keep_ref, give_ref, later_ref, top_ref, bottom_ref, whole_ref,
):
    def body(times):
        residual = residual_of(
            core_ref[0],
            times,
            (up_ref, rest_ref, down_ref),
            (own_ref, other_ref, same_ref, cross_ref),
            whole_ref,
        )
        update = precondition(residual, coeff_ref)
        next_ref[0, :, times] = iter_ref[0, :, times] + update[1:-1]
        put_rest(rest_ref[0, :, times] - prior(update, coeff_ref), times, later_ref, top_ref, bottom_ref)

    time_chunks(iter_ref.shape[2], body)
    put_low(core_ref[0], next_ref, keep_ref, give_ref)


def step(core, rests, misfits, iterate, coeff):
    members, rows, steps, cols = iterate.shape
    field, half, rim, specs, shapes = fields(members, rows, steps, cols)
    return call(
        step_kernel,
        core,
        (members,),
        [rim, field, rim, half, half, rim, rim, field, whole_block(coeff)],
        specs,
        shapes,
        [pltpu.VMEM((rows, SUBLANES, cols), jnp.float32)],
        name="step",
    )(core, *rests, *misfits, iterate, coeff)


def finish_kernel(
    core_ref, up_ref, rest_ref, down_ref, own_ref, other_ref, same_ref, cross_ref, iter_ref, coeff_ref,
    *refs,
):
    solution_ref, residual_ref, whole_ref = refs[-3:]

    def body(times):
        residual = residual_of(
            core_ref[0],
            times,
            (up_ref, rest_ref, down_ref),
            (own_ref, other_ref, same_ref, cross_ref),
            whole_ref,
        )
        update = precondition(residual, coeff_ref)
        solution_ref[times] = jnp.swapaxes(iter_ref[0, :, times] + update[1:-1], 0, 1)
        residual_ref[times] = jnp.swapaxes(trim(residual, HALO), 0, 1)

    time_chunks(iter_ref.shape[2], body)


def finish(group, samples, core, rests, misfits, iterate, coeff, previous):
    members, rows, steps, cols = iterate.shape
    field, half, rim, _, _ = fields(members, rows, steps, cols)
    result = pl.BlockSpec((steps, rows, cols), lambda b, core: (0, b + group * members, 0))
    shape = jax.ShapeDtypeStruct((steps, samples * rows, cols), jnp.float32)
    in_specs = [rim, field, rim, half, half, rim, rim, field, whole_block(coeff)]
    first = 1 + len(in_specs)
    return call(
        finish_kernel,
        core,
        (members,),
        in_specs + [pl.BlockSpec(memory_space=pl.ANY)] * len(previous),
        [result, result],
        [shape, shape],
        [pltpu.VMEM((rows, SUBLANES, cols), jnp.float32)],
        {first + k: k for k in range(len(previous))},
        name="finish",
    )(core, *rests, *misfits, iterate, coeff, *previous)


def same_frequency(near, sensors, lanes):
    shape = (near, lanes)
    return lax.broadcasted_iota(jnp.int32, shape, 0) == (
        lax.broadcasted_iota(jnp.int32, shape, 1) % LANES // sensors
    )


def marks_of(cell_ref, width):
    first = pl.program_id(0) * width
    parts = []
    for start_lane in range(0, width, LANES):
        lane = lax.broadcasted_iota(jnp.int32, cell_ref.shape, 1) + (first + start_lane)
        parts.append(jnp.where(cell_ref[...] == lane, 1.0, 0.0).astype(jnp.bfloat16))
    return jnp.concatenate(parts, axis=1)


def near_map(own_ref, other_ref, here):
    _, freqs, sensors, width = own_ref.shape
    parts = [
        ref[part, here].reshape(LANES, width) for part in range(2) for ref in (own_ref, other_ref)
    ]
    return jnp.concatenate(parts, axis=0)


def observe_kernel(core_ref, *refs):
    field_ref, own_ref, other_ref, table_ref, cell_ref, out_ref, spec, acc, picked = refs
    chips, _, members, rows, steps, lanes = field_ref.shape
    freqs, sensors, width = own_ref.shape[1:]
    near = lanes // sensors
    wide = 2 * lanes
    chunk = pl.program_id(0)

    @pl.when(chunk == 0)
    def _():
        acc[...] = jnp.zeros_like(acc)
        picked[...] = jnp.zeros_like(picked)

    marks = marks_of(cell_ref, width)

    def history(b, r):
        return field_ref[:, :, b, r].reshape(2 * chips * steps, lanes)

    for b in range(members):
        spectrum = dot(
            table_ref[...], jnp.concatenate([history(b, r) for r in range(rows)], axis=1)
        )
        spec[2 * b] = spectrum[:freqs]
        spec[2 * b + 1] = spectrum[freqs:]
    for m in range(2 * members):
        picked[m] += dot_lanes(spec[m].astype(jnp.bfloat16), marks)
    for q in range(freqs // near):
        here = slice(q * near, (q + 1) * near)
        left = spec[:, here].reshape(2 * members * near, width).astype(jnp.bfloat16)
        acc[q] += dot_lanes(left, near_map(own_ref, other_ref, here))

    @pl.when(chunk == pl.num_programs(0) - 1)
    def _():
        mask = same_frequency(near, sensors, wide)
        for q in range(freqs // near):
            here = slice(q * near, (q + 1) * near)
            for b in range(members):
                real = acc[q, 2 * b * near : (2 * b + 1) * near]
                imag = acc[q, (2 * b + 1) * near : (2 * b + 2) * near]
                sums = (
                    real[:, :wide] - imag[:, wide:] + picked[2 * b, here],
                    imag[:, :wide] + real[:, wide:] + picked[2 * b + 1, here],
                )
                for part, value in enumerate(sums):
                    line = jnp.sum(jnp.where(mask, value, 0.0), 0, keepdims=True)
                    out_ref[0, part, b, q : q + 1] = line[:, :lanes]
                    out_ref[1, part, b, q : q + 1] = line[:, lanes:]


def map_specs(own, other, width):
    chunks = other.shape[3] // width
    return [
        pl.BlockSpec(own.shape[:3] + (width,), lambda c, core: (0, 0, 0, core[0] * chunks + c)),
        pl.BlockSpec(other.shape[:3] + (width,), lambda c, core: (0, 0, 0, c)),
    ]


def map_cost(members, own, other, moved):
    return pl.CostEstimate(
        flops=16 * members * other.size,
        bytes_accessed=4 * other.size + 2 * moved,
        transcendentals=0,
    )


def observe(core, field, own, other, table, local_cells):
    chips, _, members, rows, steps, lanes = field.shape
    _, freqs, sensors, cells = other.shape
    width = CHUNK_ROWS * lanes
    near = lanes // sensors
    shape = (2, 2, members, freqs // near, lanes)
    block = (chips, 2, members, CHUNK_ROWS, steps, lanes)
    return call(
        observe_kernel,
        core,
        (rows // CHUNK_ROWS,),
        [pl.BlockSpec(block, lambda c, core: (0, 0, 0, c, 0, 0))]
        + map_specs(own, other, width)
        + [whole_block(table), whole_block(local_cells)],
        pl.BlockSpec(shape, lambda c, core: (0, 0, 0, 0, 0)),
        jax.ShapeDtypeStruct(shape, jnp.float32),
        [
            pltpu.VMEM((2 * members, freqs, width), jnp.float32),
            pltpu.VMEM((freqs // near, 2 * members * near, 4 * lanes), jnp.float32),
            pltpu.VMEM((2 * members, freqs, 2 * lanes), jnp.float32),
        ],
        cost_estimate=map_cost(members, own, other, field.size),
        name="observe",
    )(core, field, own, other, table, local_cells)


def pull_kernel(core_ref, *refs):
    *sums, noise_ref, own_ref, other_ref, back_ref, cell_ref, out_ref, weights, adjoint = refs
    devices, _, members, rows, steps, lanes = out_ref.shape
    freqs, sensors, width = own_ref.shape[1:]
    near = lanes // sensors
    wide = 2 * lanes

    def total(part, b, which):
        values = [ref[which, part, b] for ref in sums]
        while len(values) > 1:
            values = [values[k] + values[k + 1] for k in range(0, len(values), 2)]
        noise = noise_ref[which : which + 1]
        return (noise * values[0]).astype(jnp.bfloat16).astype(jnp.float32)

    @pl.when(pl.program_id(0) == 0)
    def _():
        mask = same_frequency(near, sensors, wide)
        for b in range(members):
            real, imag = (
                jnp.concatenate([total(part, b, 0), total(part, b, 1)], axis=1) for part in range(2)
            )
            for q in range(freqs // near):
                here = slice(q * near, (q + 1) * near)
                w_real = jnp.where(mask, real[q : q + 1], 0.0)
                w_imag = jnp.where(mask, imag[q : q + 1], 0.0)
                weights[2 * b, here, :wide] = w_real
                weights[2 * b, here, wide:] = w_imag
                weights[2 * b + 1, here, :wide] = w_imag
                weights[2 * b + 1, here, wide:] = -w_real

    marks = marks_of(cell_ref, width)
    for m in range(2 * members):
        adjoint[m] = dot(weights[m, :, :wide].astype(jnp.bfloat16), marks)
    for q in range(freqs // near):
        here = slice(q * near, (q + 1) * near)
        left = weights[:, here].reshape(2 * members * near, 2 * wide).astype(jnp.bfloat16)
        part = dot(left, near_map(own_ref, other_ref, here))
        adjoint[:, here] += part.reshape(2 * members, near, width)
    for b in range(members):
        whole = adjoint[2 * b : 2 * b + 2].reshape(2 * freqs, width)
        high = whole.astype(jnp.bfloat16)
        low = (whole - high.astype(jnp.float32)).astype(jnp.bfloat16)
        misfit = (dot(back_ref[...], high) + dot(back_ref[...], low)).astype(out_ref.dtype)
        for r in range(rows):
            part = misfit[:, r * lanes : (r + 1) * lanes]
            out_ref[:, :, b, r] = part.reshape(devices, 2, steps, lanes)


def pull_back(core, sums, noise, own, other, back, local_cells, shape):
    devices, _, members, rows, steps, lanes = shape
    _, freqs, sensors, cells = other.shape
    width = CHUNK_ROWS * lanes
    small = [*sums, noise]
    return call(
        pull_kernel,
        core,
        (rows // CHUNK_ROWS,),
        [whole_block(array) for array in small]
        + map_specs(own, other, width)
        + [whole_block(back), whole_block(local_cells)],
        pl.BlockSpec(
            (devices, 2, members, CHUNK_ROWS, steps, lanes), lambda c, core: (0, 0, 0, c, 0, 0)
        ),
        jax.ShapeDtypeStruct(shape, jnp.bfloat16),
        [
            pltpu.VMEM((2 * members, freqs, 4 * lanes), jnp.float32),
            pltpu.VMEM((2 * members, freqs, width), jnp.float32),
        ],
        cost_estimate=map_cost(members, own, other, math.prod(shape)),
        name="pull_back",
    )(core, *small, own, other, back, local_cells)


def rims(top, bottom):
    size = lax.axis_size("cells")
    onward = [(k, k + 1) for k in range(size - 1)]
    backward = [(k + 1, k) for k in range(size - 1)]
    return lax.ppermute(bottom, "cells", onward), lax.ppermute(top, "cells", backward)


def misfit_rims(edge):
    size, width = lax.axis_size("cells"), lax.axis_size("sensors")
    same, cross = [], []
    for cell in range(size):
        for sensor in range(width):
            there = cell + 2 * (sensor % 2) - 1
            if 0 <= there < size:
                same.append((cell * width + sensor, there * width + sensor))
                cross.append((cell * width + sensor, there * width + (sensor ^ 1)))
    both = ("cells", "sensors")
    return lax.ppermute(edge, both, same), lax.ppermute(edge, both, cross)


def swap_cores(value):
    size = lax.axis_size("sensors")
    return lax.ppermute(value, "sensors", [(k, k ^ 1) for k in range(size)])


def from_all_cells(value):
    size = lax.axis_size("cells")
    if size & (size - 1):
        return [lax.psum(value, "cells")]
    return [value] + [
        lax.ppermute(value, "cells", [(k, k ^ other) for k in range(size)])
        for other in range(1, size)
    ]


def shards(rhs, forward_map, stiffness, reaction, noise_weight, sensor_cell):
    steps, samples, rows, cols = rhs.shape
    _, freqs, sensors, cells = forward_map.shape
    size = lax.axis_size("sensors")
    chips = size // 2
    cell_index = lax.axis_index("cells")
    sensor_index = lax.axis_index("sensors")
    core = sensor_index % 2
    near = LANES // sensors
    half = cells // 2

    away = lax.dynamic_slice_in_dim(forward_map, (1 - core) * half, half, axis=3)
    other_map = swap_cores(away)

    cores = jnp.stack([core, 1 - core])
    offsets = cores[None, :, None] * steps + jnp.arange(steps, dtype=jnp.int32)
    chip_steps = 2 * steps
    places = jnp.arange(chips, dtype=jnp.int32)[:, None, None] * chip_steps
    table = transform_table(freqs, places + offsets)
    back = table.T

    diagonal = reaction + 4.0 * stiffness * stiffness
    local = jnp.stack([stiffness, diagonal])
    up, down = rims(local[:, :HALO], local[:, rows - HALO :])
    stiff, diag = jnp.concatenate([up, local, down], axis=1)
    inside = diag > 0.0
    inverse = jnp.where(inside, 1.0 / jnp.where(inside, diag, 1.0), 0.0)
    unscale = jnp.where(inside, 1.0 / jnp.where(inside, stiff, 1.0), 0.0)
    scaled = DAMPING * inverse * stiff
    coeff = jnp.stack([scaled, scaled * stiff, unscale, stiff, diag])
    coeff = jnp.broadcast_to(coeff[:, :, None, :], coeff.shape[:2] + (SUBLANES, cols))

    def per_lane(values):
        own = lax.dynamic_slice_in_dim(values, sensor_index * sensors, sensors)
        other = lax.dynamic_slice_in_dim(values, (sensor_index ^ 1) * sensors, sensors)
        return jnp.stack([jnp.tile(own, near), jnp.tile(other, near)])

    noise = per_lane(noise_weight)
    local_cells = per_lane(sensor_cell) - (cell_index * cells + core * half)
    local_cells = jnp.broadcast_to(local_cells.reshape(2 * LANES, 1), (2 * LANES, LANES))
    core = core.reshape(1)

    members = samples // GROUPS
    states = []
    for group in range(GROUPS):
        group_rhs = rhs[:, group * members : (group + 1) * members]
        up, down = rims(
            *(
                jnp.transpose(rim, (1, 2, 0, 3)).astype(jnp.bfloat16)
                for rim in (group_rhs[:, :, :HALO], group_rhs[:, :, rows - HALO :])
            )
        )
        states.append(start(group, members, core, rhs, up, down, coeff))

    lines = [[k for k in range(size) if k % 2 == parity] for parity in range(2)]
    outputs = ()
    for iteration in range(ITERS):
        for group in range(GROUPS):
            iterate, keep, give, rest, top, bottom = states[group]
            above, below = rims(top, bottom)
            field = lax.all_gather(
                jnp.stack([keep, swap_cores(give)]), "sensors", axis_index_groups=lines
            )
            sums = observe(core, field, forward_map, other_map, table, local_cells)
            sums = from_all_cells(sums + swap_cores(sums)[::-1])
            shape = (chips, 2, members, rows // 2, steps, cols)
            misfit = pull_back(core, sums, noise, forward_map, other_map, back, local_cells, shape)
            misfit = lax.psum_scatter(
                misfit, "sensors", scatter_dimension=0, axis_index_groups=lines, tiled=False
            )
            first = (rows // 2 - HALO) * core[0]
            edge = lax.dynamic_slice_in_dim(misfit, first, HALO, axis=2)
            same, _ = misfit_rims(edge[0])
            _, cross = misfit_rims(edge[1])
            misfits = (misfit[0], swap_cores(misfit[1]), same, cross)
            rests = (above, rest, below)
            if iteration < ITERS - 1:
                states[group] = step(core, rests, misfits, iterate, coeff)
            else:
                outputs = finish(group, samples, core, rests, misfits, iterate, coeff, outputs)
    return tuple(out.reshape(rhs.shape) for out in outputs)


def solution(mesh):
    placed = (
        P("sensors", None, "cells", None),
        P(None, None, "sensors", "cells"),
        P("cells", None),
        P("cells", None),
        P(),
        P(),
    )
    return jax.shard_map(
        shards,
        mesh=mesh,
        in_specs=placed,
        out_specs=(P("sensors", None, "cells", None), P("sensors", None, "cells", None)),
        check_vma=False,
    )
```

```python
import math

import jax
import jax.numpy as jnp
from jax import lax
from jax.experimental import pallas as pl
from jax.experimental.pallas import tpu as pltpu
from jax.sharding import PartitionSpec as P

SWEEPS = 4
ITERS = 2
DAMPING = 0.8
HALO = SWEEPS
LANES = 128
SUBLANES = 8
GROUPS = 3
CHUNK_ROWS = 4
VMEM_BYTES = 40 * 2**20


def transform_table(freqs, moments):
    period = moments.size
    wave = jnp.arange(freqs, dtype=jnp.int32)[:, None]
    moment = moments.reshape(1, period)
    phase = (wave * moment % period).astype(jnp.float32) * (2.0 * math.pi / period)
    factor = 1.0 / math.sqrt(period)
    return jnp.concatenate([jnp.cos(phase) * factor, -jnp.sin(phase) * factor], axis=0).astype(
        jnp.bfloat16
    )


def whole_block(array):
    return pl.BlockSpec(array.shape, lambda *_: (0,) * array.ndim)


def call(kernel, core, grid, in_specs, out_specs, out_shape, scratch=(), aliases=None, **kwargs):
    grid_spec = pltpu.PrefetchScalarGridSpec(
        num_scalar_prefetch=1,
        grid=grid,
        in_specs=in_specs,
        out_specs=out_specs,
        scratch_shapes=list(scratch),
    )
    return pl.pallas_call(
        kernel,
        grid_spec=grid_spec,
        out_shape=out_shape,
        input_output_aliases=aliases or {},
        compiler_params=pltpu.CompilerParams(vmem_limit_bytes=VMEM_BYTES),
        **kwargs,
    )


def dot(left, right):
    return jnp.dot(left, right, preferred_element_type=jnp.float32)


def dot_lanes(left, right):
    return lax.dot_general(left, right, (((1,), (1,)), ((), ())), preferred_element_type=jnp.float32)


def neighbours(field):
    inner = field[1:-1]
    lane = lax.broadcasted_iota(jnp.int32, inner.shape, 2)
    before = jnp.where(lane == 0, 0.0, pltpu.roll(inner, 1, 2))
    after = jnp.where(lane == LANES - 1, 0.0, pltpu.roll(inner, LANES - 1, 2))
    return (field[2:] + field[:-2]) + (before + after)


def trim(array, width):
    return array[width : array.shape[0] - width]


def precondition(residual, coeff_ref):
    extra = (coeff_ref.shape[1] - residual.shape[0]) // 2
    coeff = [trim(coeff_ref[k], extra) for k in range(3)]
    first = coeff[0] * residual
    scaled = first
    for sweep in range(1, SWEEPS):
        scaled = (
            (1.0 - DAMPING) * scaled[1:-1]
            + trim(first, sweep)
            + trim(coeff[1], sweep) * neighbours(scaled)
        )
    return trim(coeff[2], SWEEPS - 1) * scaled


def prior(field, coeff_ref):
    extra = (coeff_ref.shape[1] - field.shape[0]) // 2
    stiffness = trim(coeff_ref[3], extra)
    diagonal = trim(coeff_ref[4], extra + 1)
    return diagonal * field[1:-1] - stiffness[1:-1] * neighbours(stiffness * field)


def time_chunks(steps, body):
    def run(index, carry):
        body(pl.ds(pl.multiple_of(index * SUBLANES, SUBLANES), SUBLANES))
        return carry

    lax.fori_loop(0, steps // SUBLANES, run, 0)


def fields(members, rows, steps, cols):
    field = pl.BlockSpec((1, rows, steps, cols), lambda b, core: (b, 0, 0, 0))
    half = pl.BlockSpec((1, rows // 2, steps, cols), lambda b, core: (b, 0, 0, 0))
    rim = pl.BlockSpec((1, HALO, steps, cols), lambda b, core: (b, 0, 0, 0))

    def shape(count, dtype):
        return jax.ShapeDtypeStruct((members, count, steps, cols), dtype)

    specs = [field, half, half, field, rim, rim]
    shapes = [
        shape(rows, jnp.float32),
        shape(rows // 2, jnp.bfloat16),
        shape(rows // 2, jnp.bfloat16),
        shape(rows, jnp.float32),
        shape(HALO, jnp.bfloat16),
        shape(HALO, jnp.bfloat16),
    ]
    return field, half, rim, specs, shapes


def put_rest(rest, times, rest_ref, top_ref, bottom_ref):
    rest_ref[0, :, times] = rest
    top_ref[0, :, times] = rest[:HALO].astype(top_ref.dtype)
    bottom_ref[0, :, times] = rest[rest.shape[0] - HALO :].astype(bottom_ref.dtype)


def put_low(core, iter_ref, keep_ref, give_ref):
    half = keep_ref.shape[1]
    keep_ref[0] = iter_ref[0, pl.ds(core * half, half)].astype(keep_ref.dtype)
    give_ref[0] = iter_ref[0, pl.ds((1 - core) * half, half)].astype(give_ref.dtype)


def start_kernel(
    core_ref, rhs_ref, up_ref, down_ref, coeff_ref,
    iter_ref, keep_ref, give_ref, rest_ref, top_ref, bottom_ref,
):
    def body(times):
        here = jnp.swapaxes(rhs_ref[times], 0, 1)
        rims_here = [ref[0, :, times].astype(jnp.float32) for ref in (up_ref, down_ref)]
        update = precondition(jnp.concatenate([rims_here[0], here, rims_here[1]], axis=0), coeff_ref)
        iter_ref[0, :, times] = update[1:-1]
        put_rest(here - prior(update, coeff_ref), times, rest_ref, top_ref, bottom_ref)

    time_chunks(iter_ref.shape[2], body)
    put_low(core_ref[0], iter_ref, keep_ref, give_ref)


def start(group, members, core, rhs, up, down, coeff):
    steps, _, rows, cols = rhs.shape
    flat = rhs.reshape(steps, -1, cols)
    field, half, rim, specs, shapes = fields(members, rows, steps, cols)
    return call(
        start_kernel,
        core,
        (members,),
        [
            pl.BlockSpec((steps, rows, cols), lambda b, core: (0, b + group * members, 0)),
            rim,
            rim,
            whole_block(coeff),
        ],
        specs,
        shapes,
        name="start",
    )(core, flat, up, down, coeff)


def residual_of(core, times, rest_refs, misfit_refs, whole_ref):
    own_ref, other_ref, same_ref, cross_ref = misfit_refs
    half = own_ref.shape[1]
    whole_ref[pl.ds(core * half, half)] = own_ref[0, :, times].astype(jnp.float32)
    whole_ref[pl.ds((1 - core) * half, half)] = other_ref[0, :, times].astype(jnp.float32)
    same = same_ref[0, :, times].astype(jnp.float32)
    cross = cross_ref[0, :, times].astype(jnp.float32)
    first = core == 0
    parts = [jnp.where(first, cross, same), whole_ref[...], jnp.where(first, same, cross)]
    rests = [ref[0, :, times].astype(jnp.float32) for ref in rest_refs]
    return jnp.concatenate([rest - part for rest, part in zip(rests, parts)], axis=0)


def step_kernel(
    core_ref, up_ref, rest_ref, down_ref, own_ref, other_ref, same_ref, cross_ref, iter_ref, coeff_ref,
    next_ref, keep_ref, give_ref, later_ref, top_ref, bottom_ref, whole_ref,
):
    def body(times):
        residual = residual_of(
            core_ref[0],
            times,
            (up_ref, rest_ref, down_ref),
            (own_ref, other_ref, same_ref, cross_ref),
            whole_ref,
        )
        update = precondition(residual, coeff_ref)
        next_ref[0, :, times] = iter_ref[0, :, times] + update[1:-1]
        put_rest(rest_ref[0, :, times] - prior(update, coeff_ref), times, later_ref, top_ref, bottom_ref)

    time_chunks(iter_ref.shape[2], body)
    put_low(core_ref[0], next_ref, keep_ref, give_ref)


def step(core, rests, misfits, iterate, coeff):
    members, rows, steps, cols = iterate.shape
    field, half, rim, specs, shapes = fields(members, rows, steps, cols)
    return call(
        step_kernel,
        core,
        (members,),
        [rim, field, rim, half, half, rim, rim, field, whole_block(coeff)],
        specs,
        shapes,
        [pltpu.VMEM((rows, SUBLANES, cols), jnp.float32)],
        name="step",
    )(core, *rests, *misfits, iterate, coeff)


def finish_kernel(
    core_ref, up_ref, rest_ref, down_ref, own_ref, other_ref, same_ref, cross_ref, iter_ref, coeff_ref,
    *refs,
):
    solution_ref, residual_ref, whole_ref = refs[-3:]

    def body(times):
        residual = residual_of(
            core_ref[0],
            times,
            (up_ref, rest_ref, down_ref),
            (own_ref, other_ref, same_ref, cross_ref),
            whole_ref,
        )
        update = precondition(residual, coeff_ref)
        solution_ref[times] = jnp.swapaxes(iter_ref[0, :, times] + update[1:-1], 0, 1)
        residual_ref[times] = jnp.swapaxes(trim(residual, HALO), 0, 1)

    time_chunks(iter_ref.shape[2], body)


def finish(group, samples, core, rests, misfits, iterate, coeff, previous):
    members, rows, steps, cols = iterate.shape
    field, half, rim, _, _ = fields(members, rows, steps, cols)
    result = pl.BlockSpec((steps, rows, cols), lambda b, core: (0, b + group * members, 0))
    shape = jax.ShapeDtypeStruct((steps, samples * rows, cols), jnp.float32)
    in_specs = [rim, field, rim, half, half, rim, rim, field, whole_block(coeff)]
    first = 1 + len(in_specs)
    return call(
        finish_kernel,
        core,
        (members,),
        in_specs + [pl.BlockSpec(memory_space=pl.ANY)] * len(previous),
        [result, result],
        [shape, shape],
        [pltpu.VMEM((rows, SUBLANES, cols), jnp.float32)],
        {first + k: k for k in range(len(previous))},
        name="finish",
    )(core, *rests, *misfits, iterate, coeff, *previous)


def same_frequency(near, sensors, lanes):
    shape = (near, lanes)
    return lax.broadcasted_iota(jnp.int32, shape, 0) == (
        lax.broadcasted_iota(jnp.int32, shape, 1) % LANES // sensors
    )


def marks_of(cell_ref, width):
    first = pl.program_id(0) * width
    parts = []
    for start_lane in range(0, width, LANES):
        lane = lax.broadcasted_iota(jnp.int32, cell_ref.shape, 1) + (first + start_lane)
        parts.append(jnp.where(cell_ref[...] == lane, 1.0, 0.0).astype(jnp.bfloat16))
    return jnp.concatenate(parts, axis=1)


def near_map(own_ref, other_ref, here):
    _, freqs, sensors, width = own_ref.shape
    parts = [
        ref[part, here].reshape(LANES, width) for part in range(2) for ref in (own_ref, other_ref)
    ]
    return jnp.concatenate(parts, axis=0)


def observe_kernel(core_ref, *refs):
    *field_refs, own_ref, other_ref, table_ref, cell_ref, out_ref, spec, acc, picked = refs
    _, members, rows, steps, lanes = field_refs[0].shape
    freqs, sensors, width = own_ref.shape[1:]
    near = lanes // sensors
    wide = 2 * lanes
    count = len(field_refs) // 2 + 1
    chunk = pl.program_id(0)

    @pl.when(chunk == 0)
    def _():
        acc[...] = jnp.zeros_like(acc)
        picked[...] = jnp.zeros_like(picked)

    marks = marks_of(cell_ref, width)

    def history(b, r):
        slots = [field_refs[0][:, b, r]]
        for k in range(1, count):
            slots.append(field_refs[k][:, b, r] + field_refs[2 * count - 1 - k][:, b, r])
        return jnp.concatenate([slot.reshape(2 * steps, lanes) for slot in slots], axis=0)

    for b in range(members):
        spectrum = dot(
            table_ref[...], jnp.concatenate([history(b, r) for r in range(rows)], axis=1)
        )
        spec[2 * b] = spectrum[:freqs]
        spec[2 * b + 1] = spectrum[freqs:]
    for m in range(2 * members):
        picked[m] += dot_lanes(spec[m].astype(jnp.bfloat16), marks)
    for q in range(freqs // near):
        here = slice(q * near, (q + 1) * near)
        left = spec[:, here].reshape(2 * members * near, width).astype(jnp.bfloat16)
        acc[q] += dot_lanes(left, near_map(own_ref, other_ref, here))

    @pl.when(chunk == pl.num_programs(0) - 1)
    def _():
        mask = same_frequency(near, sensors, wide)
        for q in range(freqs // near):
            here = slice(q * near, (q + 1) * near)
            for b in range(members):
                real = acc[q, 2 * b * near : (2 * b + 1) * near]
                imag = acc[q, (2 * b + 1) * near : (2 * b + 2) * near]
                sums = (
                    real[:, :wide] - imag[:, wide:] + picked[2 * b, here],
                    imag[:, :wide] + real[:, wide:] + picked[2 * b + 1, here],
                )
                for part, value in enumerate(sums):
                    line = jnp.sum(jnp.where(mask, value, 0.0), 0, keepdims=True)
                    out_ref[0, part, b, q : q + 1] = line[:, :lanes]
                    out_ref[1, part, b, q : q + 1] = line[:, lanes:]


def map_specs(own, other, width):
    chunks = other.shape[3] // width
    return [
        pl.BlockSpec(own.shape[:3] + (width,), lambda c, core: (0, 0, 0, core[0] * chunks + c)),
        pl.BlockSpec(other.shape[:3] + (width,), lambda c, core: (0, 0, 0, c)),
    ]


def map_cost(members, own, other, moved):
    return pl.CostEstimate(
        flops=16 * members * other.size,
        bytes_accessed=4 * other.size + 2 * moved,
        transcendentals=0,
    )


def observe(core, slots, own, other, table, local_cells):
    _, members, rows, steps, lanes = slots[0].shape
    _, freqs, sensors, cells = other.shape
    width = CHUNK_ROWS * lanes
    near = lanes // sensors
    shape = (2, 2, members, freqs // near, lanes)
    slot = pl.BlockSpec((2, members, CHUNK_ROWS, steps, lanes), lambda c, core: (0, 0, c, 0, 0))
    return call(
        observe_kernel,
        core,
        (rows // CHUNK_ROWS,),
        [slot] * len(slots)
        + map_specs(own, other, width)
        + [whole_block(table), whole_block(local_cells)],
        pl.BlockSpec(shape, lambda c, core: (0, 0, 0, 0, 0)),
        jax.ShapeDtypeStruct(shape, jnp.float32),
        [
            pltpu.VMEM((2 * members, freqs, width), jnp.float32),
            pltpu.VMEM((freqs // near, 2 * members * near, 4 * lanes), jnp.float32),
            pltpu.VMEM((2 * members, freqs, 2 * lanes), jnp.float32),
        ],
        cost_estimate=map_cost(members, own, other, len(slots) * slots[0].size),
        name="observe",
    )(core, *slots, own, other, table, local_cells)


def pull_kernel(core_ref, *refs):
    *sums, noise_ref, own_ref, other_ref, back_ref, cell_ref, out_ref, weights, adjoint = refs
    devices, _, members, rows, steps, lanes = out_ref.shape
    freqs, sensors, width = own_ref.shape[1:]
    near = lanes // sensors
    wide = 2 * lanes

    def total(part, b, which):
        values = [ref[which, part, b] for ref in sums]
        while len(values) > 1:
            values = [values[k] + values[k + 1] for k in range(0, len(values), 2)]
        noise = noise_ref[which : which + 1]
        return (noise * values[0]).astype(jnp.bfloat16).astype(jnp.float32)

    @pl.when(pl.program_id(0) == 0)
    def _():
        mask = same_frequency(near, sensors, wide)
        for b in range(members):
            real, imag = (
                jnp.concatenate([total(part, b, 0), total(part, b, 1)], axis=1) for part in range(2)
            )
            for q in range(freqs // near):
                here = slice(q * near, (q + 1) * near)
                w_real = jnp.where(mask, real[q : q + 1], 0.0)
                w_imag = jnp.where(mask, imag[q : q + 1], 0.0)
                weights[2 * b, here, :wide] = w_real
                weights[2 * b, here, wide:] = w_imag
                weights[2 * b + 1, here, :wide] = w_imag
                weights[2 * b + 1, here, wide:] = -w_real

    marks = marks_of(cell_ref, width)
    for m in range(2 * members):
        adjoint[m] = dot(weights[m, :, :wide].astype(jnp.bfloat16), marks)
    for q in range(freqs // near):
        here = slice(q * near, (q + 1) * near)
        left = weights[:, here].reshape(2 * members * near, 2 * wide).astype(jnp.bfloat16)
        part = dot(left, near_map(own_ref, other_ref, here))
        adjoint[:, here] += part.reshape(2 * members, near, width)
    for b in range(members):
        whole = adjoint[2 * b : 2 * b + 2].reshape(2 * freqs, width)
        high = whole.astype(jnp.bfloat16)
        low = (whole - high.astype(jnp.float32)).astype(jnp.bfloat16)
        misfit = (dot(back_ref[...], high) + dot(back_ref[...], low)).astype(out_ref.dtype)
        for r in range(rows):
            part = misfit[:, r * lanes : (r + 1) * lanes]
            out_ref[:, :, b, r] = part.reshape(devices, 2, steps, lanes)


def pull_back(core, sums, noise, own, other, back, local_cells, shape):
    devices, _, members, rows, steps, lanes = shape
    _, freqs, sensors, cells = other.shape
    width = CHUNK_ROWS * lanes
    small = [*sums, noise]
    return call(
        pull_kernel,
        core,
        (rows // CHUNK_ROWS,),
        [whole_block(array) for array in small]
        + map_specs(own, other, width)
        + [whole_block(back), whole_block(local_cells)],
        pl.BlockSpec(
            (devices, 2, members, CHUNK_ROWS, steps, lanes), lambda c, core: (0, 0, 0, c, 0, 0)
        ),
        jax.ShapeDtypeStruct(shape, jnp.bfloat16),
        [
            pltpu.VMEM((2 * members, freqs, 4 * lanes), jnp.float32),
            pltpu.VMEM((2 * members, freqs, width), jnp.float32),
        ],
        cost_estimate=map_cost(members, own, other, math.prod(shape)),
        name="pull_back",
    )(core, *small, own, other, back, local_cells)


def rims(top, bottom):
    size = lax.axis_size("cells")
    onward = [(k, k + 1) for k in range(size - 1)]
    backward = [(k + 1, k) for k in range(size - 1)]
    return lax.ppermute(bottom, "cells", onward), lax.ppermute(top, "cells", backward)


def misfit_rims(edge):
    size, width = lax.axis_size("cells"), lax.axis_size("sensors")
    same, cross = [], []
    for cell in range(size):
        for sensor in range(width):
            there = cell + 2 * (sensor % 2) - 1
            if 0 <= there < size:
                same.append((cell * width + sensor, there * width + sensor))
                cross.append((cell * width + sensor, there * width + (sensor ^ 1)))
    both = ("cells", "sensors")
    return lax.ppermute(edge, both, same), lax.ppermute(edge, both, cross)


def swap_cores(value):
    size = lax.axis_size("sensors")
    return lax.ppermute(value, "sensors", [(k, k ^ 1) for k in range(size)])


def from_all_cells(value):
    size = lax.axis_size("cells")
    if size & (size - 1):
        return [lax.psum(value, "cells")]
    return [value] + [
        lax.ppermute(value, "cells", [(k, k ^ other) for k in range(size)])
        for other in range(1, size)
    ]


class Line:
    def __init__(self, value):
        self.size = lax.axis_size("sensors")
        self.value, self.ups, self.downs = value, [], []
        self.ends = (value, value)

    def hop(self, last=False):
        while len(self.ups) < self.size // 2 - 1:
            start = 2 * len(self.ups)
            onward = [(k, k + 2) for k in range(start, self.size - 2)]
            backward = [(self.size - 1 - k, self.size - 1 - there) for k, there in onward]
            self.sent = self.ends
            up = lax.ppermute(self.ends[0], "sensors", onward)
            down = lax.ppermute(self.ends[1], "sensors", backward)
            self.ups.append(up)
            self.downs.append(down)
            self.ends = (up, down)
            if not last:
                break

    def after(self, other):
        if other is not None and self.ups:
            self.ends, other = lax.optimization_barrier((self.ends, other))
            self.ups[-1], self.downs[-1] = self.ends
        return other

    def mark(self):
        return self.sent

    def slots(self):
        return [self.value, *self.ups, *self.downs]


def shards(rhs, forward_map, stiffness, reaction, noise_weight, sensor_cell):
    steps, samples, rows, cols = rhs.shape
    _, freqs, sensors, cells = forward_map.shape
    size = lax.axis_size("sensors")
    chips = size // 2
    cell_index = lax.axis_index("cells")
    sensor_index = lax.axis_index("sensors")
    core = sensor_index % 2
    chip = sensor_index // 2
    near = LANES // sensors
    half = cells // 2

    cores = jnp.stack([core, 1 - core])
    offsets = cores[None, :, None] * steps + jnp.arange(steps, dtype=jnp.int32)
    chip_steps = 2 * steps
    places = (chip - jnp.arange(chips, dtype=jnp.int32)) % chips
    table = transform_table(freqs, places[:, None, None] * chip_steps + offsets)
    places = jnp.arange(chips, dtype=jnp.int32)
    back = transform_table(freqs, places[:, None, None] * chip_steps + offsets).T

    diagonal = reaction + 4.0 * stiffness * stiffness
    local = jnp.stack([stiffness, diagonal])
    up, down = rims(local[:, :HALO], local[:, rows - HALO :])
    stiff, diag = jnp.concatenate([up, local, down], axis=1)
    inside = diag > 0.0
    inverse = jnp.where(inside, 1.0 / jnp.where(inside, diag, 1.0), 0.0)
    unscale = jnp.where(inside, 1.0 / jnp.where(inside, stiff, 1.0), 0.0)
    scaled = DAMPING * inverse * stiff
    coeff = jnp.stack([scaled, scaled * stiff, unscale, stiff, diag])
    coeff = jnp.broadcast_to(coeff[:, :, None, :], coeff.shape[:2] + (SUBLANES, cols))

    def per_lane(values):
        own = lax.dynamic_slice_in_dim(values, sensor_index * sensors, sensors)
        other = lax.dynamic_slice_in_dim(values, (sensor_index ^ 1) * sensors, sensors)
        return jnp.stack([jnp.tile(own, near), jnp.tile(other, near)])

    noise = per_lane(noise_weight)
    local_cells = per_lane(sensor_cell) - (cell_index * cells + core * half)
    local_cells = jnp.broadcast_to(local_cells.reshape(2 * LANES, 1), (2 * LANES, LANES))
    core = core.reshape(1)

    members = samples // GROUPS
    top, bottom = (
        jnp.transpose(rim, (1, 2, 0, 3)).astype(jnp.bfloat16)
        for rim in (rhs[:, :, :HALO], rhs[:, :, rows - HALO :])
    )
    states = []
    for group in range(GROUPS):
        here = slice(group * members, (group + 1) * members)
        up, down = rims(top[here], bottom[here])
        states.append(start(group, members, core, rhs, up, down, coeff))
    there, *states[0] = lax.optimization_barrier(((1 - core[0]) * half, *states[0]))
    other_map = swap_cores(lax.dynamic_slice_in_dim(forward_map, there, half, axis=3))

    lines = [[k for k in range(size) if k % 2 == parity] for parity in range(2)]
    shape = (chips, 2, members, rows // 2, steps, cols)

    def ready(state):
        iterate, keep, give, rest, top, bottom = state
        above, below = rims(top, bottom)
        return iterate, jnp.stack([keep, swap_cores(give)]), (above, rest, below)

    def edges(misfit):
        first = (rows // 2 - HALO) * core[0]
        edge = lax.dynamic_slice_in_dim(misfit, first, HALO, axis=2)
        same, _ = misfit_rims(edge[0])
        _, cross = misfit_rims(edge[1])
        return misfit[0], swap_cores(misfit[1]), same, cross

    items = [(iteration, group) for iteration in range(ITERS) for group in range(GROUPS)]
    states = {k: ready(state) for k, state in enumerate(states)}
    scattered = {}
    outputs = ()
    slots = None
    for i in range(len(items) + 2):
        line = None
        if i < len(items):
            here = states[i][1]
            if slots is not None:
                here, slots = lax.optimization_barrier((here, slots))
            line = Line(here)
            line.hop()
        sums = None
        if slots is not None:
            sums = observe(core, slots, forward_map, other_map, table, local_cells)
        if line is not None:
            sums = line.after(sums)
            line.hop()
        misfit = None
        if sums is not None:
            sums = from_all_cells(sums + swap_cores(sums)[::-1])
            misfit = pull_back(core, sums, noise, forward_map, other_map, back, local_cells, shape)
        if line is not None:
            misfit = line.after(misfit)
            line.hop(last=True)
        if misfit is not None:
            scattered[i - 1] = lax.psum_scatter(
                misfit, "sensors", scatter_dimension=0, axis_index_groups=lines, tiled=False
            )
        done = i - 2
        if done in scattered:
            total = scattered.pop(done)
            if line is not None:
                total, _ = lax.optimization_barrier((total, line.mark()))
            iteration, group = items[done]
            iterate, _, rests = states.pop(done)
            if iteration < ITERS - 1:
                states[done + GROUPS] = ready(step(core, rests, edges(total), iterate, coeff))
            else:
                outputs = finish(
                    group, samples, core, rests, edges(total), iterate, coeff, outputs
                )
        slots = line.slots() if line is not None else None
    return tuple(out.reshape(rhs.shape) for out in outputs)


def solution(mesh):
    placed = (
        P("sensors", None, "cells", None),
        P(None, None, "sensors", "cells"),
        P("cells", None),
        P("cells", None),
        P(),
        P(),
    )
    return jax.shard_map(
        shards,
        mesh=mesh,
        in_specs=placed,
        out_specs=(P("sensors", None, "cells", None), P("sensors", None, "cells", None)),
        check_vma=False,
    )
```

```python
import math

import jax
import jax.numpy as jnp
from jax import lax
from jax.experimental import pallas as pl
from jax.experimental.pallas import tpu as pltpu
from jax.sharding import PartitionSpec as P

SWEEPS = 4
ITERS = 2
DAMPING = 0.8
HALO = SWEEPS
LANES = 128
SUBLANES = 8
GROUPS = 3
CHUNK_ROWS = 4
VMEM_BYTES = 20 * 2**20


def transform_table(freqs, moments):
    period = moments.size
    wave = jnp.arange(freqs, dtype=jnp.int32)[:, None]
    moment = moments.reshape(1, period)
    phase = (wave * moment % period).astype(jnp.float32) * (2.0 * math.pi / period)
    factor = 1.0 / math.sqrt(period)
    return jnp.concatenate([jnp.cos(phase) * factor, -jnp.sin(phase) * factor], axis=0).astype(
        jnp.bfloat16
    )


def whole_block(array):
    return pl.BlockSpec(array.shape, lambda *_: (0,) * array.ndim)


def call(kernel, core, grid, in_specs, out_specs, out_shape, scratch=(), aliases=None, **kwargs):
    grid_spec = pltpu.PrefetchScalarGridSpec(
        num_scalar_prefetch=1,
        grid=grid,
        in_specs=in_specs,
        out_specs=out_specs,
        scratch_shapes=list(scratch),
    )
    return pl.pallas_call(
        kernel,
        grid_spec=grid_spec,
        out_shape=out_shape,
        input_output_aliases=aliases or {},
        compiler_params=pltpu.CompilerParams(vmem_limit_bytes=VMEM_BYTES),
        **kwargs,
    )


def dot(left, right):
    return jnp.dot(left, right, preferred_element_type=jnp.float32)


def dot_lanes(left, right):
    return lax.dot_general(left, right, (((1,), (1,)), ((), ())), preferred_element_type=jnp.float32)


def neighbours(field):
    inner = field[1:-1]
    lane = lax.broadcasted_iota(jnp.int32, inner.shape, 2)
    before = jnp.where(lane == 0, 0.0, pltpu.roll(inner, 1, 2))
    after = jnp.where(lane == LANES - 1, 0.0, pltpu.roll(inner, LANES - 1, 2))
    return (field[2:] + field[:-2]) + (before + after)


def trim(array, width):
    return array[width : array.shape[0] - width]


def precondition(residual, coeff_ref):
    extra = (coeff_ref.shape[1] - residual.shape[0]) // 2
    coeff = [trim(coeff_ref[k], extra) for k in range(3)]
    first = coeff[0] * residual
    scaled = first
    for sweep in range(1, SWEEPS):
        scaled = (
            (1.0 - DAMPING) * scaled[1:-1]
            + trim(first, sweep)
            + trim(coeff[1], sweep) * neighbours(scaled)
        )
    return trim(coeff[2], SWEEPS - 1) * scaled


def prior(field, coeff_ref):
    extra = (coeff_ref.shape[1] - field.shape[0]) // 2
    stiffness = trim(coeff_ref[3], extra)
    diagonal = trim(coeff_ref[4], extra + 1)
    return diagonal * field[1:-1] - stiffness[1:-1] * neighbours(stiffness * field)


def time_chunks(steps, body):
    def run(index, carry):
        body(pl.ds(pl.multiple_of(index * SUBLANES, SUBLANES), SUBLANES))
        return carry

    lax.fori_loop(0, steps // SUBLANES, run, 0)


def fields(members, rows, steps, cols):
    field = pl.BlockSpec((1, rows, steps, cols), lambda b, core: (b, 0, 0, 0))
    half = pl.BlockSpec((1, rows // 2, steps, cols), lambda b, core: (b, 0, 0, 0))
    rim = pl.BlockSpec((1, HALO, steps, cols), lambda b, core: (b, 0, 0, 0))

    def shape(count, dtype):
        return jax.ShapeDtypeStruct((members, count, steps, cols), dtype)

    specs = [field, half, half, field, rim, rim]
    shapes = [
        shape(rows, jnp.float32),
        shape(rows // 2, jnp.bfloat16),
        shape(rows // 2, jnp.bfloat16),
        shape(rows, jnp.float32),
        shape(HALO, jnp.bfloat16),
        shape(HALO, jnp.bfloat16),
    ]
    return field, half, rim, specs, shapes


def put_rest(rest, times, rest_ref, top_ref, bottom_ref):
    rest_ref[0, :, times] = rest
    top_ref[0, :, times] = rest[:HALO].astype(top_ref.dtype)
    bottom_ref[0, :, times] = rest[rest.shape[0] - HALO :].astype(bottom_ref.dtype)


def put_low(core, iter_ref, keep_ref, give_ref):
    half = keep_ref.shape[1]
    keep_ref[0] = iter_ref[0, pl.ds(core * half, half)].astype(keep_ref.dtype)
    give_ref[0] = iter_ref[0, pl.ds((1 - core) * half, half)].astype(give_ref.dtype)


def start_kernel(
    core_ref, rhs_ref, up_ref, down_ref, coeff_ref,
    iter_ref, keep_ref, give_ref, rest_ref, top_ref, bottom_ref,
):
    def body(times):
        here = jnp.swapaxes(rhs_ref[times], 0, 1)
        rims_here = [ref[0, :, times].astype(jnp.float32) for ref in (up_ref, down_ref)]
        update = precondition(jnp.concatenate([rims_here[0], here, rims_here[1]], axis=0), coeff_ref)
        iter_ref[0, :, times] = update[1:-1]
        put_rest(here - prior(update, coeff_ref), times, rest_ref, top_ref, bottom_ref)

    time_chunks(iter_ref.shape[2], body)
    put_low(core_ref[0], iter_ref, keep_ref, give_ref)


def start(group, members, core, rhs, up, down, coeff):
    steps, _, rows, cols = rhs.shape
    flat = rhs.reshape(steps, -1, cols)
    field, half, rim, specs, shapes = fields(members, rows, steps, cols)
    return call(
        start_kernel,
        core,
        (members,),
        [
            pl.BlockSpec((steps, rows, cols), lambda b, core: (0, b + group * members, 0)),
            rim,
            rim,
            whole_block(coeff),
        ],
        specs,
        shapes,
        name="start",
    )(core, flat, up, down, coeff)


def residual_of(core, times, rest_refs, misfit_refs, whole_ref):
    own_ref, other_ref, same_ref, cross_ref = misfit_refs
    half = own_ref.shape[1]
    whole_ref[pl.ds(core * half, half)] = own_ref[0, :, times].astype(jnp.float32)
    whole_ref[pl.ds((1 - core) * half, half)] = other_ref[0, :, times].astype(jnp.float32)
    same = same_ref[0, :, times].astype(jnp.float32)
    cross = cross_ref[0, :, times].astype(jnp.float32)
    first = core == 0
    parts = [jnp.where(first, cross, same), whole_ref[...], jnp.where(first, same, cross)]
    rests = [ref[0, :, times].astype(jnp.float32) for ref in rest_refs]
    return jnp.concatenate([rest - part for rest, part in zip(rests, parts)], axis=0)


def step_kernel(
    core_ref, up_ref, rest_ref, down_ref, own_ref, other_ref, same_ref, cross_ref, iter_ref, coeff_ref,
    next_ref, keep_ref, give_ref, later_ref, top_ref, bottom_ref, whole_ref,
):
    def body(times):
        residual = residual_of(
            core_ref[0],
            times,
            (up_ref, rest_ref, down_ref),
            (own_ref, other_ref, same_ref, cross_ref),
            whole_ref,
        )
        update = precondition(residual, coeff_ref)
        next_ref[0, :, times] = iter_ref[0, :, times] + update[1:-1]
        put_rest(rest_ref[0, :, times] - prior(update, coeff_ref), times, later_ref, top_ref, bottom_ref)

    time_chunks(iter_ref.shape[2], body)
    put_low(core_ref[0], next_ref, keep_ref, give_ref)


def step(core, rests, misfits, iterate, coeff):
    members, rows, steps, cols = iterate.shape
    field, half, rim, specs, shapes = fields(members, rows, steps, cols)
    return call(
        step_kernel,
        core,
        (members,),
        [rim, field, rim, half, half, rim, rim, field, whole_block(coeff)],
        specs,
        shapes,
        [pltpu.VMEM((rows, SUBLANES, cols), jnp.float32)],
        name="step",
    )(core, *rests, *misfits, iterate, coeff)


def finish_kernel(
    core_ref, up_ref, rest_ref, down_ref, own_ref, other_ref, same_ref, cross_ref, iter_ref, coeff_ref,
    *refs,
):
    solution_ref, residual_ref, whole_ref = refs[-3:]

    def body(times):
        residual = residual_of(
            core_ref[0],
            times,
            (up_ref, rest_ref, down_ref),
            (own_ref, other_ref, same_ref, cross_ref),
            whole_ref,
        )
        update = precondition(residual, coeff_ref)
        solution_ref[times] = jnp.swapaxes(iter_ref[0, :, times] + update[1:-1], 0, 1)
        residual_ref[times] = jnp.swapaxes(trim(residual, HALO), 0, 1)

    time_chunks(iter_ref.shape[2], body)


def finish(group, samples, core, rests, misfits, iterate, coeff, previous):
    members, rows, steps, cols = iterate.shape
    field, half, rim, _, _ = fields(members, rows, steps, cols)
    result = pl.BlockSpec((steps, rows, cols), lambda b, core: (0, b + group * members, 0))
    shape = jax.ShapeDtypeStruct((steps, samples * rows, cols), jnp.float32)
    in_specs = [rim, field, rim, half, half, rim, rim, field, whole_block(coeff)]
    first = 1 + len(in_specs)
    return call(
        finish_kernel,
        core,
        (members,),
        in_specs + [pl.BlockSpec(memory_space=pl.ANY)] * len(previous),
        [result, result],
        [shape, shape],
        [pltpu.VMEM((rows, SUBLANES, cols), jnp.float32)],
        {first + k: k for k in range(len(previous))},
        name="finish",
    )(core, *rests, *misfits, iterate, coeff, *previous)


def same_frequency(near, sensors, lanes):
    shape = (near, lanes)
    return lax.broadcasted_iota(jnp.int32, shape, 0) == (
        lax.broadcasted_iota(jnp.int32, shape, 1) % LANES // sensors
    )


def marks_of(cell_ref, width):
    first = pl.program_id(0) * width
    parts = []
    for start_lane in range(0, width, LANES):
        lane = lax.broadcasted_iota(jnp.int32, cell_ref.shape, 1) + (first + start_lane)
        parts.append(jnp.where(cell_ref[...] == lane, 1.0, 0.0).astype(jnp.bfloat16))
    return jnp.concatenate(parts, axis=1)


def near_map(own_ref, other_ref, here, width):
    cells = pl.ds(pl.multiple_of(pl.program_id(0) * width, LANES), width)
    parts = [
        ref[part, here, :, cells].reshape(LANES, width)
        for part in range(2)
        for ref in (own_ref, other_ref)
    ]
    return jnp.concatenate(parts, axis=0)


def keep_kernel(core_ref, map_ref, out_ref, sem):
    cells = pl.ds(pl.multiple_of(core_ref[0], LANES), out_ref.shape[3])
    copy = pltpu.make_async_copy(map_ref.at[:, :, :, cells], out_ref, sem)
    copy.start()
    copy.wait()


def keep(first, forward_map, cells):
    return call(
        keep_kernel,
        first,
        (1,),
        [pl.BlockSpec(memory_space=pl.ANY)],
        pl.BlockSpec(memory_space=pltpu.VMEM),
        pltpu.VMEM(forward_map.shape[:3] + (cells,), forward_map.dtype),
        [pltpu.SemaphoreType.DMA],
        name="keep",
    )(first.reshape(1), forward_map)


def resident(*maps):
    return [pltpu.with_memory_space_constraint(part, pltpu.VMEM) for part in maps]


def observe_kernel(core_ref, *refs):
    field_ref, own_ref, other_ref, table_ref, cell_ref, out_ref, spec, acc, picked = refs
    chips, _, members, rows, steps, lanes = field_ref.shape
    freqs, sensors, _ = own_ref.shape[1:]
    width = rows * lanes
    near = lanes // sensors
    wide = 2 * lanes
    chunk = pl.program_id(0)

    @pl.when(chunk == 0)
    def _():
        acc[...] = jnp.zeros_like(acc)
        picked[...] = jnp.zeros_like(picked)

    marks = marks_of(cell_ref, width)

    def history(b, r):
        return field_ref[:, :, b, r].reshape(2 * chips * steps, lanes)

    for b in range(members):
        spectrum = dot(
            table_ref[...], jnp.concatenate([history(b, r) for r in range(rows)], axis=1)
        )
        spec[2 * b] = spectrum[:freqs]
        spec[2 * b + 1] = spectrum[freqs:]
    for m in range(2 * members):
        picked[m] += dot_lanes(spec[m].astype(jnp.bfloat16), marks)
    for q in range(freqs // near):
        here = slice(q * near, (q + 1) * near)
        left = spec[:, here].reshape(2 * members * near, width).astype(jnp.bfloat16)
        acc[q] += dot_lanes(left, near_map(own_ref, other_ref, here, width))

    @pl.when(chunk == pl.num_programs(0) - 1)
    def _():
        mask = same_frequency(near, sensors, wide)
        for q in range(freqs // near):
            here = slice(q * near, (q + 1) * near)
            for b in range(members):
                real = acc[q, 2 * b * near : (2 * b + 1) * near]
                imag = acc[q, (2 * b + 1) * near : (2 * b + 2) * near]
                sums = (
                    real[:, :wide] - imag[:, wide:] + picked[2 * b, here],
                    imag[:, :wide] + real[:, wide:] + picked[2 * b + 1, here],
                )
                for part, value in enumerate(sums):
                    line = jnp.sum(jnp.where(mask, value, 0.0), 0, keepdims=True)
                    out_ref[0, part, b, q : q + 1] = line[:, :lanes]
                    out_ref[1, part, b, q : q + 1] = line[:, lanes:]


def map_cost(members, own, other, moved):
    return pl.CostEstimate(
        flops=16 * members * other.size,
        bytes_accessed=2 * moved,
        transcendentals=0,
    )


def observe(core, field, own, other, table, local_cells):
    chips, _, members, rows, steps, lanes = field.shape
    _, freqs, sensors, cells = other.shape
    width = CHUNK_ROWS * lanes
    near = lanes // sensors
    shape = (2, 2, members, freqs // near, lanes)
    block = (chips, 2, members, CHUNK_ROWS, steps, lanes)
    return call(
        observe_kernel,
        core,
        (rows // CHUNK_ROWS,),
        [pl.BlockSpec(block, lambda c, core: (0, 0, 0, c, 0, 0))]
        + [pl.BlockSpec(memory_space=pltpu.VMEM)] * 2
        + [whole_block(table), whole_block(local_cells)],
        pl.BlockSpec(shape, lambda c, core: (0, 0, 0, 0, 0)),
        jax.ShapeDtypeStruct(shape, jnp.float32),
        [
            pltpu.VMEM((2 * members, freqs, width), jnp.float32),
            pltpu.VMEM((freqs // near, 2 * members * near, 4 * lanes), jnp.float32),
            pltpu.VMEM((2 * members, freqs, 2 * lanes), jnp.float32),
        ],
        cost_estimate=map_cost(members, own, other, field.size),
        name="observe",
    )(core, field, *resident(own, other), table, local_cells)


def pull_kernel(core_ref, *refs):
    *sums, noise_ref, own_ref, other_ref, back_ref, cell_ref, out_ref, weights, adjoint = refs
    devices, _, members, rows, steps, lanes = out_ref.shape
    freqs, sensors, _ = own_ref.shape[1:]
    width = rows * lanes
    near = lanes // sensors
    wide = 2 * lanes

    def total(part, b, which):
        values = [ref[which, part, b] for ref in sums]
        while len(values) > 1:
            values = [values[k] + values[k + 1] for k in range(0, len(values), 2)]
        noise = noise_ref[which : which + 1]
        return (noise * values[0]).astype(jnp.bfloat16).astype(jnp.float32)

    @pl.when(pl.program_id(0) == 0)
    def _():
        mask = same_frequency(near, sensors, wide)
        for b in range(members):
            real, imag = (
                jnp.concatenate([total(part, b, 0), total(part, b, 1)], axis=1) for part in range(2)
            )
            for q in range(freqs // near):
                here = slice(q * near, (q + 1) * near)
                w_real = jnp.where(mask, real[q : q + 1], 0.0)
                w_imag = jnp.where(mask, imag[q : q + 1], 0.0)
                weights[2 * b, here, :wide] = w_real
                weights[2 * b, here, wide:] = w_imag
                weights[2 * b + 1, here, :wide] = w_imag
                weights[2 * b + 1, here, wide:] = -w_real

    marks = marks_of(cell_ref, width)
    for m in range(2 * members):
        adjoint[m] = dot(weights[m, :, :wide].astype(jnp.bfloat16), marks)
    for q in range(freqs // near):
        here = slice(q * near, (q + 1) * near)
        left = weights[:, here].reshape(2 * members * near, 2 * wide).astype(jnp.bfloat16)
        part = dot(left, near_map(own_ref, other_ref, here, width))
        adjoint[:, here] += part.reshape(2 * members, near, width)
    for b in range(members):
        whole = adjoint[2 * b : 2 * b + 2].reshape(2 * freqs, width)
        high = whole.astype(jnp.bfloat16)
        low = (whole - high.astype(jnp.float32)).astype(jnp.bfloat16)
        misfit = (dot(back_ref[...], high) + dot(back_ref[...], low)).astype(out_ref.dtype)
        for r in range(rows):
            part = misfit[:, r * lanes : (r + 1) * lanes]
            out_ref[:, :, b, r] = part.reshape(devices, 2, steps, lanes)


def pull_back(core, sums, noise, own, other, back, local_cells, shape):
    devices, _, members, rows, steps, lanes = shape
    _, freqs, sensors, cells = other.shape
    width = CHUNK_ROWS * lanes
    small = [*sums, noise]
    return call(
        pull_kernel,
        core,
        (rows // CHUNK_ROWS,),
        [whole_block(array) for array in small]
        + [pl.BlockSpec(memory_space=pltpu.VMEM)] * 2
        + [whole_block(back), whole_block(local_cells)],
        pl.BlockSpec(
            (devices, 2, members, CHUNK_ROWS, steps, lanes), lambda c, core: (0, 0, 0, c, 0, 0)
        ),
        jax.ShapeDtypeStruct(shape, jnp.bfloat16),
        [
            pltpu.VMEM((2 * members, freqs, 4 * lanes), jnp.float32),
            pltpu.VMEM((2 * members, freqs, width), jnp.float32),
        ],
        cost_estimate=map_cost(members, own, other, math.prod(shape)),
        name="pull_back",
    )(core, *small, *resident(own, other), back, local_cells)


def rims(top, bottom):
    size = lax.axis_size("cells")
    onward = [(k, k + 1) for k in range(size - 1)]
    backward = [(k + 1, k) for k in range(size - 1)]
    return lax.ppermute(bottom, "cells", onward), lax.ppermute(top, "cells", backward)


def misfit_rims(edge):
    size, width = lax.axis_size("cells"), lax.axis_size("sensors")
    same, cross = [], []
    for cell in range(size):
        for sensor in range(width):
            there = cell + 2 * (sensor % 2) - 1
            if 0 <= there < size:
                same.append((cell * width + sensor, there * width + sensor))
                cross.append((cell * width + sensor, there * width + (sensor ^ 1)))
    both = ("cells", "sensors")
    return lax.ppermute(edge, both, same), lax.ppermute(edge, both, cross)


def swap_cores(value):
    size = lax.axis_size("sensors")
    return lax.ppermute(value, "sensors", [(k, k ^ 1) for k in range(size)])


def from_all_cells(value):
    size = lax.axis_size("cells")
    if size & (size - 1):
        return [lax.psum(value, "cells")]
    return [value] + [
        lax.ppermute(value, "cells", [(k, k ^ other) for k in range(size)])
        for other in range(1, size)
    ]


def shards(rhs, forward_map, stiffness, reaction, noise_weight, sensor_cell):
    steps, samples, rows, cols = rhs.shape
    _, freqs, sensors, cells = forward_map.shape
    size = lax.axis_size("sensors")
    chips = size // 2
    cell_index = lax.axis_index("cells")
    sensor_index = lax.axis_index("sensors")
    core = sensor_index % 2
    near = LANES // sensors
    half = cells // 2

    cores = jnp.stack([core, 1 - core])
    offsets = cores[None, :, None] * steps + jnp.arange(steps, dtype=jnp.int32)
    chip_steps = 2 * steps
    places = jnp.arange(chips, dtype=jnp.int32)[:, None, None] * chip_steps
    table = transform_table(freqs, places + offsets)
    back = table.T

    diagonal = reaction + 4.0 * stiffness * stiffness
    local = jnp.stack([stiffness, diagonal])
    up, down = rims(local[:, :HALO], local[:, rows - HALO :])
    stiff, diag = jnp.concatenate([up, local, down], axis=1)
    inside = diag > 0.0
    inverse = jnp.where(inside, 1.0 / jnp.where(inside, diag, 1.0), 0.0)
    unscale = jnp.where(inside, 1.0 / jnp.where(inside, stiff, 1.0), 0.0)
    scaled = DAMPING * inverse * stiff
    coeff = jnp.stack([scaled, scaled * stiff, unscale, stiff, diag])
    coeff = jnp.broadcast_to(coeff[:, :, None, :], coeff.shape[:2] + (SUBLANES, cols))

    def per_lane(values):
        own = lax.dynamic_slice_in_dim(values, sensor_index * sensors, sensors)
        other = lax.dynamic_slice_in_dim(values, (sensor_index ^ 1) * sensors, sensors)
        return jnp.stack([jnp.tile(own, near), jnp.tile(other, near)])

    noise = per_lane(noise_weight)
    local_cells = per_lane(sensor_cell) - (cell_index * cells + core * half)
    local_cells = jnp.broadcast_to(local_cells.reshape(2 * LANES, 1), (2 * LANES, LANES))
    core = core.reshape(1)

    members = samples // GROUPS
    top, bottom = (
        jnp.transpose(rim, (1, 2, 0, 3)).astype(jnp.bfloat16)
        for rim in (rhs[:, :, :HALO], rhs[:, :, rows - HALO :])
    )
    states = []
    for group in range(GROUPS):
        here = slice(group * members, (group + 1) * members)
        up, down = rims(top[here], bottom[here])
        states.append(start(group, members, core, rhs, up, down, coeff))
    there, *states[0] = lax.optimization_barrier(((1 - core[0]) * half, *states[0]))
    away = lax.dynamic_slice_in_dim(forward_map, there, half, axis=3)
    other_map = keep(jnp.zeros_like(there), swap_cores(away), half)
    own_map = keep(half - there, forward_map, half)

    lines = [[k for k in range(size) if k % 2 == parity] for parity in range(2)]
    shape = (chips, 2, members, rows // 2, steps, cols)

    def ready(state):
        iterate, keep, give, rest, top, bottom = state
        above, below = rims(top, bottom)
        return iterate, jnp.stack([keep, swap_cores(give)]), (above, rest, below)

    def edges(misfit):
        first = (rows // 2 - HALO) * core[0]
        edge = lax.dynamic_slice_in_dim(misfit, first, HALO, axis=2)
        same, _ = misfit_rims(edge[0])
        _, cross = misfit_rims(edge[1])
        return misfit[0], swap_cores(misfit[1]), same, cross

    states = [ready(state) for state in states]
    outputs = ()
    for iteration in range(ITERS):
        fields = [lax.all_gather(state[1], "sensors", axis_index_groups=lines) for state in states]
        totals = []
        for field in fields:
            sums = observe(core, field, own_map, other_map, table, local_cells)
            sums = from_all_cells(sums + swap_cores(sums)[::-1])
            misfit = pull_back(core, sums, noise, own_map, other_map, back, local_cells, shape)
            totals.append(
                lax.psum_scatter(
                    misfit, "sensors", scatter_dimension=0, axis_index_groups=lines, tiled=False
                )
            )
        for group in range(GROUPS):
            iterate, _, rests = states[group]
            total = totals[group]
            if iteration < ITERS - 1:
                states[group] = ready(step(core, rests, edges(total), iterate, coeff))
            else:
                if outputs:
                    total, outputs = lax.optimization_barrier((total, outputs))
                outputs = finish(
                    group, samples, core, rests, edges(total), iterate, coeff, outputs
                )
    return tuple(out.reshape(rhs.shape) for out in outputs)


def solution(mesh):
    placed = (
        P("sensors", None, "cells", None),
        P(None, None, "sensors", "cells"),
        P("cells", None),
        P("cells", None),
        P(),
        P(),
    )
    return jax.shard_map(
        shards,
        mesh=mesh,
        in_specs=placed,
        out_specs=(P("sensors", None, "cells", None), P("sensors", None, "cells", None)),
        check_vma=False,
    )
```

```python
import math

import jax
import jax.numpy as jnp
from jax import lax
from jax.experimental import pallas as pl
from jax.experimental.pallas import tpu as pltpu
from jax.sharding import PartitionSpec as P

SWEEPS = 4
ITERS = 2
DAMPING = 0.8
HALO = SWEEPS
LANES = 128
APART = 3
SUBLANES = 8
GROUPS = 2
CHUNK_ROWS = 4
VMEM_BYTES = 40 * 2**20


def transform_table(freqs, moments):
    period = moments.size
    wave = jnp.arange(freqs, dtype=jnp.int32)[:, None]
    moment = moments.reshape(1, period)
    phase = (wave * moment % period).astype(jnp.float32) * (2.0 * math.pi / period)
    factor = 1.0 / math.sqrt(period)
    return jnp.concatenate([jnp.cos(phase) * factor, -jnp.sin(phase) * factor], axis=0).astype(
        jnp.bfloat16
    )


def whole_block(array):
    return pl.BlockSpec(array.shape, lambda *_: (0,) * array.ndim)


def call(kernel, core, grid, in_specs, out_specs, out_shape, scratch=(), aliases=None, **kwargs):
    grid_spec = pltpu.PrefetchScalarGridSpec(
        num_scalar_prefetch=1,
        grid=grid,
        in_specs=in_specs,
        out_specs=out_specs,
        scratch_shapes=list(scratch),
    )
    return pl.pallas_call(
        kernel,
        grid_spec=grid_spec,
        out_shape=out_shape,
        input_output_aliases=aliases or {},
        compiler_params=pltpu.CompilerParams(vmem_limit_bytes=VMEM_BYTES),
        **kwargs,
    )


def dot(left, right):
    return jnp.dot(left, right, preferred_element_type=jnp.float32)


def dot_lanes(left, right):
    return lax.dot_general(left, right, (((1,), (1,)), ((), ())), preferred_element_type=jnp.float32)


def neighbours(field):
    inner = field[1:-1]
    lane = lax.broadcasted_iota(jnp.int32, inner.shape, 2)
    before = jnp.where(lane == 0, 0.0, pltpu.roll(inner, 1, 2))
    after = jnp.where(lane == LANES - 1, 0.0, pltpu.roll(inner, LANES - 1, 2))
    return (field[2:] + field[:-2]) + (before + after)


def trim(array, width):
    return array[width : array.shape[0] - width]


def precondition(residual, coeff_ref):
    extra = (coeff_ref.shape[1] - residual.shape[0]) // 2
    coeff = [trim(coeff_ref[k], extra) for k in range(3)]
    first = coeff[0] * residual
    scaled = first
    for sweep in range(1, SWEEPS):
        scaled = (
            (1.0 - DAMPING) * scaled[1:-1]
            + trim(first, sweep)
            + trim(coeff[1], sweep) * neighbours(scaled)
        )
    return trim(coeff[2], SWEEPS - 1) * scaled


def prior(field, coeff_ref):
    extra = (coeff_ref.shape[1] - field.shape[0]) // 2
    stiffness = trim(coeff_ref[3], extra)
    diagonal = trim(coeff_ref[4], extra + 1)
    return diagonal * field[1:-1] - stiffness[1:-1] * neighbours(stiffness * field)


def time_chunks(steps, body):
    def run(index, carry):
        body(pl.ds(pl.multiple_of(index * SUBLANES, SUBLANES), SUBLANES))
        return carry

    lax.fori_loop(0, steps // SUBLANES, run, 0)


def fields(members, rows, steps, cols):
    field = pl.BlockSpec((1, rows, steps, cols), lambda b, core: (b, 0, 0, 0))
    half = pl.BlockSpec((1, rows // 2, steps, cols), lambda b, core: (b, 0, 0, 0))
    rim = pl.BlockSpec((1, HALO, steps, cols), lambda b, core: (b, 0, 0, 0))

    def shape(count, dtype):
        return jax.ShapeDtypeStruct((members, count, steps, cols), dtype)

    specs = [field, half, half, field, rim, rim]
    shapes = [
        shape(rows, jnp.float32),
        shape(rows // 2, jnp.bfloat16),
        shape(rows // 2, jnp.bfloat16),
        shape(rows, jnp.float32),
        shape(HALO, jnp.bfloat16),
        shape(HALO, jnp.bfloat16),
    ]
    return field, half, rim, specs, shapes


def put_rest(rest, times, rest_ref, top_ref, bottom_ref):
    rest_ref[0, :, times] = rest
    top_ref[0, :, times] = rest[:HALO].astype(top_ref.dtype)
    bottom_ref[0, :, times] = rest[rest.shape[0] - HALO :].astype(bottom_ref.dtype)


def put_low(core, iter_ref, keep_ref, give_ref):
    half = keep_ref.shape[1]
    keep_ref[0] = iter_ref[0, pl.ds(core * half, half)].astype(keep_ref.dtype)
    give_ref[0] = iter_ref[0, pl.ds((1 - core) * half, half)].astype(give_ref.dtype)


def start_kernel(
    core_ref, rhs_ref, up_ref, down_ref, coeff_ref,
    iter_ref, keep_ref, give_ref, rest_ref, top_ref, bottom_ref,
):
    def body(times):
        here = jnp.swapaxes(rhs_ref[times], 0, 1)
        rims_here = [ref[0, :, times].astype(jnp.float32) for ref in (up_ref, down_ref)]
        update = precondition(jnp.concatenate([rims_here[0], here, rims_here[1]], axis=0), coeff_ref)
        iter_ref[0, :, times] = update[1:-1]
        put_rest(here - prior(update, coeff_ref), times, rest_ref, top_ref, bottom_ref)

    time_chunks(iter_ref.shape[2], body)
    put_low(core_ref[0], iter_ref, keep_ref, give_ref)


def start(group, members, core, rhs, up, down, coeff):
    steps, _, rows, cols = rhs.shape
    flat = rhs.reshape(steps, -1, cols)
    field, half, rim, specs, shapes = fields(members, rows, steps, cols)
    return call(
        start_kernel,
        core,
        (members,),
        [
            pl.BlockSpec((steps, rows, cols), lambda b, core: (0, b + group * members, 0)),
            rim,
            rim,
            whole_block(coeff),
        ],
        specs,
        shapes,
        name="start",
    )(core, flat, up, down, coeff)


def residual_of(core, times, rest_refs, misfit_refs, whole_ref):
    own_ref, other_ref, same_ref, cross_ref = misfit_refs
    half = own_ref.shape[1]
    whole_ref[pl.ds(core * half, half)] = own_ref[0, :, times].astype(jnp.float32)
    whole_ref[pl.ds((1 - core) * half, half)] = other_ref[0, :, times].astype(jnp.float32)
    same = same_ref[0, :, times].astype(jnp.float32)
    cross = cross_ref[0, :, times].astype(jnp.float32)
    first = core == 0
    parts = [jnp.where(first, cross, same), whole_ref[...], jnp.where(first, same, cross)]
    rests = [ref[0, :, times].astype(jnp.float32) for ref in rest_refs]
    return jnp.concatenate([rest - part for rest, part in zip(rests, parts)], axis=0)


def step_kernel(
    core_ref, up_ref, rest_ref, down_ref, own_ref, other_ref, same_ref, cross_ref, iter_ref, coeff_ref,
    next_ref, keep_ref, give_ref, later_ref, top_ref, bottom_ref, whole_ref,
):
    def body(times):
        residual = residual_of(
            core_ref[0],
            times,
            (up_ref, rest_ref, down_ref),
            (own_ref, other_ref, same_ref, cross_ref),
            whole_ref,
        )
        update = precondition(residual, coeff_ref)
        next_ref[0, :, times] = iter_ref[0, :, times] + update[1:-1]
        put_rest(rest_ref[0, :, times] - prior(update, coeff_ref), times, later_ref, top_ref, bottom_ref)

    time_chunks(iter_ref.shape[2], body)
    put_low(core_ref[0], next_ref, keep_ref, give_ref)


def step(core, rests, misfits, iterate, coeff):
    members, rows, steps, cols = iterate.shape
    field, half, rim, specs, shapes = fields(members, rows, steps, cols)
    return call(
        step_kernel,
        core,
        (members,),
        [rim, field, rim, half, half, rim, rim, field, whole_block(coeff)],
        specs,
        shapes,
        [pltpu.VMEM((rows, SUBLANES, cols), jnp.float32)],
        name="step",
    )(core, *rests, *misfits, iterate, coeff)


def finish_kernel(
    core_ref, up_ref, rest_ref, down_ref, own_ref, other_ref, same_ref, cross_ref, iter_ref, coeff_ref,
    *refs,
):
    solution_ref, residual_ref, whole_ref = refs[-3:]

    def body(times):
        residual = residual_of(
            core_ref[0],
            times,
            (up_ref, rest_ref, down_ref),
            (own_ref, other_ref, same_ref, cross_ref),
            whole_ref,
        )
        update = precondition(residual, coeff_ref)
        solution_ref[times] = jnp.swapaxes(iter_ref[0, :, times] + update[1:-1], 0, 1)
        residual_ref[times] = jnp.swapaxes(trim(residual, HALO), 0, 1)

    time_chunks(iter_ref.shape[2], body)


def finish(group, samples, core, rests, misfits, iterate, coeff, previous):
    members, rows, steps, cols = iterate.shape
    field, half, rim, _, _ = fields(members, rows, steps, cols)
    result = pl.BlockSpec((steps, rows, cols), lambda b, core: (0, b + group * members, 0))
    shape = jax.ShapeDtypeStruct((steps, samples * rows, cols), jnp.float32)
    in_specs = [rim, field, rim, half, half, rim, rim, field, whole_block(coeff)]
    first = 1 + len(in_specs)
    return call(
        finish_kernel,
        core,
        (members,),
        in_specs + [pl.BlockSpec(memory_space=pl.ANY)] * len(previous),
        [result, result],
        [shape, shape],
        [pltpu.VMEM((rows, SUBLANES, cols), jnp.float32)],
        {first + k: k for k in range(len(previous))},
        name="finish",
    )(core, *rests, *misfits, iterate, coeff, *previous)


def same_frequency(near, sensors, lanes):
    shape = (near, lanes)
    return lax.broadcasted_iota(jnp.int32, shape, 0) == (
        lax.broadcasted_iota(jnp.int32, shape, 1) % LANES // sensors
    )


def marks_of(cell_ref, width):
    first = pl.program_id(0) * width
    parts = []
    for start_lane in range(0, width, LANES):
        lane = lax.broadcasted_iota(jnp.int32, cell_ref.shape, 1) + (first + start_lane)
        parts.append(jnp.where(cell_ref[...] == lane, 1.0, 0.0).astype(jnp.bfloat16))
    return jnp.concatenate(parts, axis=1)


def near_map(own_ref, other_ref, here):
    _, freqs, sensors, width = own_ref.shape
    parts = [
        ref[part, here].reshape(LANES, width) for part in range(2) for ref in (own_ref, other_ref)
    ]
    return jnp.concatenate(parts, axis=0)


def observe_kernel(core_ref, field_ref, *refs):
    *slot_refs, own_ref, other_ref, table_ref, around_ref, cell_ref = refs[:-4]
    out_ref, spec, acc, picked = refs[-4:]
    chips, _, whole, rows, steps, lanes = field_ref.shape
    members = spec.shape[0] // 2
    freqs, sensors, width = own_ref.shape[1:]
    near = lanes // sensors
    wide = 2 * lanes
    chunk = pl.program_id(0)

    @pl.when(chunk == 0)
    def _():
        acc[...] = jnp.zeros_like(acc)
        picked[...] = jnp.zeros_like(picked)

    marks = marks_of(cell_ref, width)

    def history(b, r):
        if b < whole:
            return field_ref[:, :, b, r].reshape(2 * chips * steps, lanes)
        slots = [slot_refs[0][:, b - whole, r]]
        for k in range(1, chips):
            slots.append(slot_refs[k][:, b - whole, r] + slot_refs[2 * chips - 1 - k][:, b - whole, r])
        return jnp.concatenate([slot.reshape(2 * steps, lanes) for slot in slots], axis=0)

    for b in range(members):
        table = table_ref[...] if b < whole else around_ref[...]
        spectrum = dot(table, jnp.concatenate([history(b, r) for r in range(rows)], axis=1))
        spec[2 * b] = spectrum[:freqs]
        spec[2 * b + 1] = spectrum[freqs:]
    for m in range(2 * members):
        picked[m] += dot_lanes(spec[m].astype(jnp.bfloat16), marks)
    for q in range(freqs // near):
        here = slice(q * near, (q + 1) * near)
        left = spec[:, here].reshape(2 * members * near, width).astype(jnp.bfloat16)
        acc[q] += dot_lanes(left, near_map(own_ref, other_ref, here))

    @pl.when(chunk == pl.num_programs(0) - 1)
    def _():
        mask = same_frequency(near, sensors, wide)
        for q in range(freqs // near):
            here = slice(q * near, (q + 1) * near)
            for b in range(members):
                real = acc[q, 2 * b * near : (2 * b + 1) * near]
                imag = acc[q, (2 * b + 1) * near : (2 * b + 2) * near]
                sums = (
                    real[:, :wide] - imag[:, wide:] + picked[2 * b, here],
                    imag[:, :wide] + real[:, wide:] + picked[2 * b + 1, here],
                )
                for part, value in enumerate(sums):
                    line = jnp.sum(jnp.where(mask, value, 0.0), 0, keepdims=True)
                    out_ref[0, part, b, q : q + 1] = line[:, :lanes]
                    out_ref[1, part, b, q : q + 1] = line[:, lanes:]


def map_specs(own, width):
    chunks = own.shape[3] // (2 * width)
    spec = pl.BlockSpec(own.shape[:3] + (width,), lambda c, core: (0, 0, 0, core[0] * chunks + c))
    return [spec, spec]


def map_cost(members, own, moved):
    return pl.CostEstimate(
        flops=8 * members * own.size, bytes_accessed=2 * own.size + 2 * moved, transcendentals=0
    )


def observe(core, field, slots, own, other, table, around, local_cells):
    chips, _, whole, rows, steps, lanes = field.shape
    apart = slots[0].shape[1]
    members = whole + apart
    _, freqs, sensors, cells = own.shape
    width = CHUNK_ROWS * lanes
    near = lanes // sensors
    shape = (2, 2, members, freqs // near, lanes)
    block = (chips, 2, whole, CHUNK_ROWS, steps, lanes)
    slot = pl.BlockSpec((2, apart, CHUNK_ROWS, steps, lanes), lambda c, core: (0, 0, c, 0, 0))
    return call(
        observe_kernel,
        core,
        (rows // CHUNK_ROWS,),
        [pl.BlockSpec(block, lambda c, core: (0, 0, 0, c, 0, 0))]
        + [slot] * len(slots)
        + map_specs(own, width)
        + [whole_block(table), whole_block(around), whole_block(local_cells)],
        pl.BlockSpec(shape, lambda c, core: (0, 0, 0, 0, 0)),
        jax.ShapeDtypeStruct(shape, jnp.float32),
        [
            pltpu.VMEM((2 * members, freqs, width), jnp.float32),
            pltpu.VMEM((freqs // near, 2 * members * near, 4 * lanes), jnp.float32),
            pltpu.VMEM((2 * members, freqs, 2 * lanes), jnp.float32),
        ],
        cost_estimate=map_cost(members, own, field.size),
        name="observe",
    )(core, field, *slots, own, other, table, around, local_cells)


def pull_kernel(core_ref, *refs):
    *sums, noise_ref, own_ref, other_ref, back_ref, cell_ref = refs[:-3]
    out_ref, weights, adjoint = refs[-3:]
    devices, _, members, rows, steps, lanes = out_ref.shape
    freqs, sensors, width = own_ref.shape[1:]
    near = lanes // sensors
    wide = 2 * lanes

    def total(part, b, which):
        values = [ref[which, part, b] for ref in sums]
        while len(values) > 1:
            values = [values[k] + values[k + 1] for k in range(0, len(values), 2)]
        noise = noise_ref[which : which + 1]
        return (noise * values[0]).astype(jnp.bfloat16).astype(jnp.float32)

    @pl.when(pl.program_id(0) == 0)
    def _():
        mask = same_frequency(near, sensors, wide)
        for b in range(members):
            real, imag = (
                jnp.concatenate([total(part, b, 0), total(part, b, 1)], axis=1) for part in range(2)
            )
            for q in range(freqs // near):
                here = slice(q * near, (q + 1) * near)
                w_real = jnp.where(mask, real[q : q + 1], 0.0)
                w_imag = jnp.where(mask, imag[q : q + 1], 0.0)
                weights[2 * b, here, :wide] = w_real
                weights[2 * b, here, wide:] = w_imag
                weights[2 * b + 1, here, :wide] = w_imag
                weights[2 * b + 1, here, wide:] = -w_real

    marks = marks_of(cell_ref, width)
    for m in range(2 * members):
        adjoint[m] = dot(weights[m, :, :wide].astype(jnp.bfloat16), marks)
    for q in range(freqs // near):
        here = slice(q * near, (q + 1) * near)
        left = weights[:, here].reshape(2 * members * near, 2 * wide).astype(jnp.bfloat16)
        part = dot(left, near_map(own_ref, other_ref, here))
        adjoint[:, here] += part.reshape(2 * members, near, width)
    for b in range(members):
        whole = adjoint[2 * b : 2 * b + 2].reshape(2 * freqs, width)
        high = whole.astype(jnp.bfloat16)
        low = (whole - high.astype(jnp.float32)).astype(jnp.bfloat16)
        misfit = (dot(back_ref[...], high) + dot(back_ref[...], low)).astype(out_ref.dtype)
        for r in range(rows):
            part = misfit[:, r * lanes : (r + 1) * lanes]
            out_ref[:, :, b, r] = part.reshape(devices, 2, steps, lanes)


def pull_back(core, sums, noise, own, other, back, local_cells, shape):
    devices, _, members, rows, steps, lanes = shape
    _, freqs, sensors, cells = own.shape
    width = CHUNK_ROWS * lanes
    small = [*sums, noise]
    return call(
        pull_kernel,
        core,
        (rows // CHUNK_ROWS,),
        [whole_block(array) for array in small]
        + map_specs(own, width)
        + [whole_block(back), whole_block(local_cells)],
        pl.BlockSpec(
            (devices, 2, members, CHUNK_ROWS, steps, lanes), lambda c, core: (0, 0, 0, c, 0, 0)
        ),
        jax.ShapeDtypeStruct(shape, jnp.bfloat16),
        [
            pltpu.VMEM((2 * members, freqs, 4 * lanes), jnp.float32),
            pltpu.VMEM((2 * members, freqs, width), jnp.float32),
        ],
        cost_estimate=map_cost(members, own, math.prod(shape)),
        name="pull_back",
    )(core, *small, own, other, back, local_cells)


def rims(top, bottom):
    size = lax.axis_size("cells")
    onward = [(k, k + 1) for k in range(size - 1)]
    backward = [(k + 1, k) for k in range(size - 1)]
    return lax.ppermute(bottom, "cells", onward), lax.ppermute(top, "cells", backward)


def misfit_rims(edge):
    size, width = lax.axis_size("cells"), lax.axis_size("sensors")
    same, cross = [], []
    for cell in range(size):
        for sensor in range(width):
            there = cell + 2 * (sensor % 2) - 1
            if 0 <= there < size:
                same.append((cell * width + sensor, there * width + sensor))
                cross.append((cell * width + sensor, there * width + (sensor ^ 1)))
    both = ("cells", "sensors")
    return lax.ppermute(edge, both, same), lax.ppermute(edge, both, cross)


def swap_cores(value):
    size = lax.axis_size("sensors")
    return lax.ppermute(value, "sensors", [(k, k ^ 1) for k in range(size)])


def from_all_cells(value):
    size = lax.axis_size("cells")
    if size & (size - 1):
        return [lax.psum(value, "cells")]
    return [value] + [
        lax.ppermute(value, "cells", [(k, k ^ other) for k in range(size)])
        for other in range(1, size)
    ]


class Line:
    def __init__(self, value):
        self.size = lax.axis_size("sensors")
        self.value, self.ups, self.downs = value, [], []
        self.ends = (value, value)

    def hop(self, last=False):
        while len(self.ups) < self.size // 2 - 1:
            start = 2 * len(self.ups)
            onward = [(k, k + 2) for k in range(start, self.size - 2)]
            backward = [(self.size - 1 - k, self.size - 1 - there) for k, there in onward]
            up = lax.ppermute(self.ends[0], "sensors", onward)
            down = lax.ppermute(self.ends[1], "sensors", backward)
            self.ups.append(up)
            self.downs.append(down)
            self.ends = (up, down)
            if not last:
                break

    def after(self, other):
        if other is not None and self.ups:
            self.ends, other = lax.optimization_barrier((self.ends, other))
            self.ups[-1], self.downs[-1] = self.ends
        return other

    def slots(self):
        return [self.value, *self.ups, *self.downs]


def shards(rhs, forward_map, stiffness, reaction, noise_weight, sensor_cell):
    steps, samples, rows, cols = rhs.shape
    _, freqs, sensors, cells = forward_map.shape
    size = lax.axis_size("sensors")
    chips = size // 2
    cell_index = lax.axis_index("cells")
    sensor_index = lax.axis_index("sensors")
    core = sensor_index % 2
    near = LANES // sensors
    half = cells // 2
    other_map = swap_cores(forward_map)

    cores = jnp.stack([core, 1 - core])
    offsets = cores[None, :, None] * steps + jnp.arange(steps, dtype=jnp.int32)
    chip_steps = 2 * steps
    places = jnp.arange(chips, dtype=jnp.int32)[:, None, None] * chip_steps
    table = transform_table(freqs, places + offsets)
    back = table.T
    chip = sensor_index // 2
    places = (chip - jnp.arange(chips, dtype=jnp.int32)) % chips
    around = transform_table(freqs, places[:, None, None] * chip_steps + offsets)

    diagonal = reaction + 4.0 * stiffness * stiffness
    local = jnp.stack([stiffness, diagonal])
    up, down = rims(local[:, :HALO], local[:, rows - HALO :])
    stiff, diag = jnp.concatenate([up, local, down], axis=1)
    inside = diag > 0.0
    inverse = jnp.where(inside, 1.0 / jnp.where(inside, diag, 1.0), 0.0)
    unscale = jnp.where(inside, 1.0 / jnp.where(inside, stiff, 1.0), 0.0)
    scaled = DAMPING * inverse * stiff
    coeff = jnp.stack([scaled, scaled * stiff, unscale, stiff, diag])
    coeff = jnp.broadcast_to(coeff[:, :, None, :], coeff.shape[:2] + (SUBLANES, cols))

    def per_lane(values):
        own = lax.dynamic_slice_in_dim(values, sensor_index * sensors, sensors)
        other = lax.dynamic_slice_in_dim(values, (sensor_index ^ 1) * sensors, sensors)
        return jnp.stack([jnp.tile(own, near), jnp.tile(other, near)])

    noise = per_lane(noise_weight)
    local_cells = per_lane(sensor_cell) - (cell_index * cells + core * half)
    local_cells = jnp.broadcast_to(local_cells.reshape(2 * LANES, 1), (2 * LANES, LANES))
    core = core.reshape(1)

    members = samples // GROUPS
    whole = members - members // APART
    edge_rows = lax.optimization_barrier((rhs[:, :, :HALO], rhs[:, :, rows - HALO :]))
    top, bottom = (jnp.transpose(rim, (1, 2, 0, 3)).astype(jnp.bfloat16) for rim in edge_rows)
    lines = [[k for k in range(size) if k % 2 == parity] for parity in range(2)]
    shape = (chips, 2, members, rows // 2, steps, cols)

    def ready(state):
        iterate, keep, give, rest, top, bottom = state
        above, below = rims(top, bottom)
        pair = jnp.stack([keep, swap_cores(give)])
        parts = lax.optimization_barrier((pair[:, :whole], pair[:, whole:]))
        return iterate, *parts, (above, rest, below)

    def edges(misfit):
        first = (rows // 2 - HALO) * core[0]
        edge = lax.dynamic_slice_in_dim(misfit, first, HALO, axis=2)
        same, _ = misfit_rims(edge[0])
        _, cross = misfit_rims(edge[1])
        return misfit[0], swap_cores(misfit[1]), same, cross

    states = []
    for group in range(GROUPS):
        here = slice(group * members, (group + 1) * members)
        ends = (top[here], bottom[here])
        if states:
            iterate, pair, *others = states[0]
            pair, ends = lax.optimization_barrier((pair, ends))
            states[0] = (iterate, pair, *others)
        begun = start(group, members, core, rhs, *rims(*ends), coeff)
        states.append(ready(begun))

    line = Line(states[0][2])
    outputs = ()
    for iteration in range(ITERS):
        fields = [lax.all_gather(state[1], "sensors", axis_index_groups=lines) for state in states]
        line.hop(last=True)
        totals = []
        for group in range(GROUPS):
            iterate, _, _, rests = states[group]
            field, rests = lax.optimization_barrier((fields[group], rests))
            states[group] = iterate, rests
            slots, line = line.slots(), None
            if group + 1 < GROUPS:
                line = Line(states[group + 1][2])
                line.hop()
            sums = observe(
                core, field, slots, forward_map, other_map, table, around, local_cells
            )
            if line is not None:
                sums = line.after(sums)
                line.hop()
            sums = from_all_cells(sums + swap_cores(sums)[::-1])
            misfit = pull_back(core, sums, noise, forward_map, other_map, back, local_cells, shape)
            if line is not None:
                misfit = line.after(misfit)
                line.hop(last=True)
            totals.append(
                lax.psum_scatter(
                    misfit, "sensors", scatter_dimension=0, axis_index_groups=lines, tiled=False
                )
            )
        for group in range(GROUPS):
            iterate, rests = states[group]
            total = totals[group]
            if iteration < ITERS - 1:
                if group == 1:
                    line.hop()
                    total = line.after(total)
                states[group] = ready(step(core, rests, edges(total), iterate, coeff))
                if group == 0:
                    line = Line(states[0][2])
            else:
                if outputs:
                    total, outputs = lax.optimization_barrier((total, outputs))
                outputs = finish(
                    group, samples, core, rests, edges(total), iterate, coeff, outputs
                )
    return tuple(out.reshape(rhs.shape) for out in outputs)


def solution(mesh):
    placed = (
        P("sensors", None, "cells", None),
        P(None, None, "sensors", "cells"),
        P("cells", None),
        P("cells", None),
        P(),
        P(),
    )
    return jax.shard_map(
        shards,
        mesh=mesh,
        in_specs=placed,
        out_specs=(P("sensors", None, "cells", None), P("sensors", None, "cells", None)),
        check_vma=False,
    )
```

```python
import math

import jax
import jax.numpy as jnp
from jax import lax
from jax.experimental import pallas as pl
from jax.experimental.pallas import tpu as pltpu
from jax.sharding import PartitionSpec as P

SWEEPS = 4
ITERS = 2
DAMPING = 0.8
HALO = SWEEPS
LANES = 128
APART = 3
SUBLANES = 8
GROUPS = 2
CHUNK_ROWS = 4
VMEM_BYTES = 40 * 2**20


def transform_table(freqs, moments):
    period = moments.size
    wave = jnp.arange(freqs, dtype=jnp.int32)[:, None]
    moment = moments.reshape(1, period)
    phase = (wave * moment % period).astype(jnp.float32) * (2.0 * math.pi / period)
    factor = 1.0 / math.sqrt(period)
    return jnp.concatenate([jnp.cos(phase) * factor, -jnp.sin(phase) * factor], axis=0).astype(
        jnp.bfloat16
    )


def whole_block(array):
    return pl.BlockSpec(array.shape, lambda *_: (0,) * array.ndim)


def call(kernel, core, grid, in_specs, out_specs, out_shape, scratch=(), aliases=None, **kwargs):
    grid_spec = pltpu.PrefetchScalarGridSpec(
        num_scalar_prefetch=1,
        grid=grid,
        in_specs=in_specs,
        out_specs=out_specs,
        scratch_shapes=list(scratch),
    )
    return pl.pallas_call(
        kernel,
        grid_spec=grid_spec,
        out_shape=out_shape,
        input_output_aliases=aliases or {},
        compiler_params=pltpu.CompilerParams(vmem_limit_bytes=VMEM_BYTES),
        **kwargs,
    )


def dot(left, right):
    return jnp.dot(left, right, preferred_element_type=jnp.float32)


def dot_lanes(left, right):
    return lax.dot_general(left, right, (((1,), (1,)), ((), ())), preferred_element_type=jnp.float32)


def neighbours(field):
    inner = field[1:-1]
    lane = lax.broadcasted_iota(jnp.int32, inner.shape, 2)
    before = jnp.where(lane == 0, 0.0, pltpu.roll(inner, 1, 2))
    after = jnp.where(lane == LANES - 1, 0.0, pltpu.roll(inner, LANES - 1, 2))
    return (field[2:] + field[:-2]) + (before + after)


def trim(array, width):
    return array[width : array.shape[0] - width]


def precondition(residual, coeff_ref):
    extra = (coeff_ref.shape[1] - residual.shape[0]) // 2
    coeff = [trim(coeff_ref[k], extra) for k in range(3)]
    first = coeff[0] * residual
    scaled = first
    for sweep in range(1, SWEEPS):
        scaled = (
            (1.0 - DAMPING) * scaled[1:-1]
            + trim(first, sweep)
            + trim(coeff[1], sweep) * neighbours(scaled)
        )
    return trim(coeff[2], SWEEPS - 1) * scaled


def prior(field, coeff_ref):
    extra = (coeff_ref.shape[1] - field.shape[0]) // 2
    stiffness = trim(coeff_ref[3], extra)
    diagonal = trim(coeff_ref[4], extra + 1)
    return diagonal * field[1:-1] - stiffness[1:-1] * neighbours(stiffness * field)


def time_chunks(steps, body):
    def run(index, carry):
        body(pl.ds(pl.multiple_of(index * SUBLANES, SUBLANES), SUBLANES))
        return carry

    lax.fori_loop(0, steps // SUBLANES, run, 0)


def fields(members, rows, steps, cols):
    field = pl.BlockSpec((1, rows, steps, cols), lambda b, core: (b, 0, 0, 0))
    half = pl.BlockSpec((1, rows // 2, steps, cols), lambda b, core: (b, 0, 0, 0))
    rim = pl.BlockSpec((1, HALO, steps, cols), lambda b, core: (b, 0, 0, 0))

    def shape(count, dtype):
        return jax.ShapeDtypeStruct((members, count, steps, cols), dtype)

    specs = [field, half, half, field, rim, rim]
    shapes = [
        shape(rows, jnp.float32),
        shape(rows // 2, jnp.bfloat16),
        shape(rows // 2, jnp.bfloat16),
        shape(rows, jnp.float32),
        shape(HALO, jnp.bfloat16),
        shape(HALO, jnp.bfloat16),
    ]
    return field, half, rim, specs, shapes


def put_rest(rest, times, rest_ref, top_ref, bottom_ref):
    rest_ref[0, :, times] = rest
    top_ref[0, :, times] = rest[:HALO].astype(top_ref.dtype)
    bottom_ref[0, :, times] = rest[rest.shape[0] - HALO :].astype(bottom_ref.dtype)


def put_low(core, iter_ref, keep_ref, give_ref):
    half = keep_ref.shape[1]
    keep_ref[0] = iter_ref[0, pl.ds(core * half, half)].astype(keep_ref.dtype)
    give_ref[0] = iter_ref[0, pl.ds((1 - core) * half, half)].astype(give_ref.dtype)


def start_kernel(
    core_ref, rhs_ref, up_ref, down_ref, coeff_ref,
    iter_ref, keep_ref, give_ref, rest_ref, top_ref, bottom_ref,
):
    def body(times):
        here = jnp.swapaxes(rhs_ref[times], 0, 1)
        rims_here = [ref[0, :, times].astype(jnp.float32) for ref in (up_ref, down_ref)]
        update = precondition(jnp.concatenate([rims_here[0], here, rims_here[1]], axis=0), coeff_ref)
        iter_ref[0, :, times] = update[1:-1]
        put_rest(here - prior(update, coeff_ref), times, rest_ref, top_ref, bottom_ref)

    time_chunks(iter_ref.shape[2], body)
    put_low(core_ref[0], iter_ref, keep_ref, give_ref)


def start(group, members, core, rhs, up, down, coeff):
    steps, _, rows, cols = rhs.shape
    flat = rhs.reshape(steps, -1, cols)
    field, half, rim, specs, shapes = fields(members, rows, steps, cols)
    return call(
        start_kernel,
        core,
        (members,),
        [
            pl.BlockSpec((steps, rows, cols), lambda b, core: (0, b + group * members, 0)),
            rim,
            rim,
            whole_block(coeff),
        ],
        specs,
        shapes,
        name="start",
    )(core, flat, up, down, coeff)


def residual_of(core, times, rest_refs, misfit_refs, whole_ref):
    own_ref, other_ref, same_ref, cross_ref = misfit_refs
    half = own_ref.shape[1]
    whole_ref[pl.ds(core * half, half)] = own_ref[0, :, times].astype(jnp.float32)
    whole_ref[pl.ds((1 - core) * half, half)] = other_ref[0, :, times].astype(jnp.float32)
    same = same_ref[0, :, times].astype(jnp.float32)
    cross = cross_ref[0, :, times].astype(jnp.float32)
    first = core == 0
    parts = [jnp.where(first, cross, same), whole_ref[...], jnp.where(first, same, cross)]
    rests = [ref[0, :, times].astype(jnp.float32) for ref in rest_refs]
    return jnp.concatenate([rest - part for rest, part in zip(rests, parts)], axis=0)


def step_kernel(
    core_ref, up_ref, rest_ref, down_ref, own_ref, other_ref, same_ref, cross_ref, iter_ref, coeff_ref,
    next_ref, keep_ref, give_ref, later_ref, top_ref, bottom_ref, whole_ref,
):
    def body(times):
        residual = residual_of(
            core_ref[0],
            times,
            (up_ref, rest_ref, down_ref),
            (own_ref, other_ref, same_ref, cross_ref),
            whole_ref,
        )
        update = precondition(residual, coeff_ref)
        next_ref[0, :, times] = iter_ref[0, :, times] + update[1:-1]
        put_rest(rest_ref[0, :, times] - prior(update, coeff_ref), times, later_ref, top_ref, bottom_ref)

    time_chunks(iter_ref.shape[2], body)
    put_low(core_ref[0], next_ref, keep_ref, give_ref)


def step(core, rests, misfits, iterate, coeff):
    members, rows, steps, cols = iterate.shape
    field, half, rim, specs, shapes = fields(members, rows, steps, cols)
    return call(
        step_kernel,
        core,
        (members,),
        [rim, field, rim, half, half, rim, rim, field, whole_block(coeff)],
        specs,
        shapes,
        [pltpu.VMEM((rows, SUBLANES, cols), jnp.float32)],
        name="step",
    )(core, *rests, *misfits, iterate, coeff)


def finish_kernel(
    core_ref, up_ref, rest_ref, down_ref, own_ref, other_ref, same_ref, cross_ref, iter_ref, coeff_ref,
    *refs,
):
    solution_ref, residual_ref, whole_ref = refs[-3:]

    def body(times):
        residual = residual_of(
            core_ref[0],
            times,
            (up_ref, rest_ref, down_ref),
            (own_ref, other_ref, same_ref, cross_ref),
            whole_ref,
        )
        update = precondition(residual, coeff_ref)
        solution_ref[times] = jnp.swapaxes(iter_ref[0, :, times] + update[1:-1], 0, 1)
        residual_ref[times] = jnp.swapaxes(trim(residual, HALO), 0, 1)

    time_chunks(iter_ref.shape[2], body)


def finish(group, samples, core, rests, misfits, iterate, coeff, previous):
    members, rows, steps, cols = iterate.shape
    field, half, rim, _, _ = fields(members, rows, steps, cols)
    result = pl.BlockSpec((steps, rows, cols), lambda b, core: (0, b + group * members, 0))
    shape = jax.ShapeDtypeStruct((steps, samples * rows, cols), jnp.float32)
    in_specs = [rim, field, rim, half, half, rim, rim, field, whole_block(coeff)]
    first = 1 + len(in_specs)
    return call(
        finish_kernel,
        core,
        (members,),
        in_specs + [pl.BlockSpec(memory_space=pl.ANY)] * len(previous),
        [result, result],
        [shape, shape],
        [pltpu.VMEM((rows, SUBLANES, cols), jnp.float32)],
        {first + k: k for k in range(len(previous))},
        name="finish",
    )(core, *rests, *misfits, iterate, coeff, *previous)


def same_frequency(near, sensors, lanes):
    shape = (near, lanes)
    return lax.broadcasted_iota(jnp.int32, shape, 0) == (
        lax.broadcasted_iota(jnp.int32, shape, 1) % LANES // sensors
    )


def marks_of(cell_ref, width):
    first = pl.program_id(0) * width
    parts = []
    for start_lane in range(0, width, LANES):
        lane = lax.broadcasted_iota(jnp.int32, cell_ref.shape, 1) + (first + start_lane)
        parts.append(jnp.where(cell_ref[...] == lane, 1.0, 0.0).astype(jnp.bfloat16))
    return jnp.concatenate(parts, axis=1)


def near_map(own_ref, other_ref, here):
    _, freqs, sensors, width = own_ref.shape
    parts = [
        ref[part, here].reshape(LANES, width) for part in range(2) for ref in (own_ref, other_ref)
    ]
    return jnp.concatenate(parts, axis=0)


def observe_kernel(core_ref, field_ref, *refs):
    *slot_refs, own_ref, other_ref, table_ref, around_ref, cell_ref = refs[:-4]
    out_ref, spec, acc, picked = refs[-4:]
    chips, _, whole, rows, steps, lanes = field_ref.shape
    members = spec.shape[0] // 2
    freqs, sensors, width = own_ref.shape[1:]
    near = lanes // sensors
    wide = 2 * lanes
    chunk = pl.program_id(0)

    @pl.when(chunk == 0)
    def _():
        acc[...] = jnp.zeros_like(acc)
        picked[...] = jnp.zeros_like(picked)

    marks = marks_of(cell_ref, width)

    def history(b, r):
        if b < whole:
            return field_ref[:, :, b, r].reshape(2 * chips * steps, lanes)
        slots = [slot_refs[0][:, b - whole, r]]
        for k in range(1, chips):
            slots.append(slot_refs[k][:, b - whole, r] + slot_refs[2 * chips - 1 - k][:, b - whole, r])
        return jnp.concatenate([slot.reshape(2 * steps, lanes) for slot in slots], axis=0)

    for b in range(members):
        table = table_ref[...] if b < whole else around_ref[...]
        spectrum = dot(table, jnp.concatenate([history(b, r) for r in range(rows)], axis=1))
        spec[2 * b] = spectrum[:freqs]
        spec[2 * b + 1] = spectrum[freqs:]
    for m in range(2 * members):
        picked[m] += dot_lanes(spec[m].astype(jnp.bfloat16), marks)
    for q in range(freqs // near):
        here = slice(q * near, (q + 1) * near)
        left = spec[:, here].reshape(2 * members * near, width).astype(jnp.bfloat16)
        acc[q] += dot_lanes(left, near_map(own_ref, other_ref, here))

    @pl.when(chunk == pl.num_programs(0) - 1)
    def _():
        mask = same_frequency(near, sensors, wide)
        for q in range(freqs // near):
            here = slice(q * near, (q + 1) * near)
            for b in range(members):
                real = acc[q, 2 * b * near : (2 * b + 1) * near]
                imag = acc[q, (2 * b + 1) * near : (2 * b + 2) * near]
                sums = (
                    real[:, :wide] - imag[:, wide:] + picked[2 * b, here],
                    imag[:, :wide] + real[:, wide:] + picked[2 * b + 1, here],
                )
                for part, value in enumerate(sums):
                    line = jnp.sum(jnp.where(mask, value, 0.0), 0, keepdims=True)
                    out_ref[0, part, b, q : q + 1] = line[:, :lanes]
                    out_ref[1, part, b, q : q + 1] = line[:, lanes:]


def map_specs(own, width):
    chunks = own.shape[3] // (2 * width)
    spec = pl.BlockSpec(own.shape[:3] + (width,), lambda c, core: (0, 0, 0, core[0] * chunks + c))
    return [spec, spec]


def map_cost(members, own, moved):
    return pl.CostEstimate(
        flops=8 * members * own.size, bytes_accessed=2 * own.size + 2 * moved, transcendentals=0
    )


def observe(core, field, slots, own, other, table, around, local_cells):
    chips, _, whole, rows, steps, lanes = field.shape
    apart = slots[0].shape[1]
    members = whole + apart
    _, freqs, sensors, cells = own.shape
    width = CHUNK_ROWS * lanes
    near = lanes // sensors
    shape = (2, 2, members, freqs // near, lanes)
    block = (chips, 2, whole, CHUNK_ROWS, steps, lanes)
    slot = pl.BlockSpec((2, apart, CHUNK_ROWS, steps, lanes), lambda c, core: (0, 0, c, 0, 0))
    return call(
        observe_kernel,
        core,
        (rows // CHUNK_ROWS,),
        [pl.BlockSpec(block, lambda c, core: (0, 0, 0, c, 0, 0))]
        + [slot] * len(slots)
        + map_specs(own, width)
        + [whole_block(table), whole_block(around), whole_block(local_cells)],
        pl.BlockSpec(shape, lambda c, core: (0, 0, 0, 0, 0)),
        jax.ShapeDtypeStruct(shape, jnp.float32),
        [
            pltpu.VMEM((2 * members, freqs, width), jnp.float32),
            pltpu.VMEM((freqs // near, 2 * members * near, 4 * lanes), jnp.float32),
            pltpu.VMEM((2 * members, freqs, 2 * lanes), jnp.float32),
        ],
        cost_estimate=map_cost(members, own, field.size),
        name="observe",
    )(core, field, *slots, own, other, table, around, local_cells)


def pull_kernel(core_ref, *refs):
    *sums, noise_ref, own_ref, other_ref, back_ref, cell_ref = refs[:-3]
    out_ref, weights, adjoint = refs[-3:]
    devices, _, members, rows, steps, lanes = out_ref.shape
    freqs, sensors, width = own_ref.shape[1:]
    near = lanes // sensors
    wide = 2 * lanes

    def total(part, b, which):
        values = [ref[which, part, b] for ref in sums]
        while len(values) > 1:
            values = [values[k] + values[k + 1] for k in range(0, len(values), 2)]
        noise = noise_ref[which : which + 1]
        return (noise * values[0]).astype(jnp.bfloat16).astype(jnp.float32)

    @pl.when(pl.program_id(0) == 0)
    def _():
        mask = same_frequency(near, sensors, wide)
        for b in range(members):
            real, imag = (
                jnp.concatenate([total(part, b, 0), total(part, b, 1)], axis=1) for part in range(2)
            )
            for q in range(freqs // near):
                here = slice(q * near, (q + 1) * near)
                w_real = jnp.where(mask, real[q : q + 1], 0.0)
                w_imag = jnp.where(mask, imag[q : q + 1], 0.0)
                weights[2 * b, here, :wide] = w_real
                weights[2 * b, here, wide:] = w_imag
                weights[2 * b + 1, here, :wide] = w_imag
                weights[2 * b + 1, here, wide:] = -w_real

    marks = marks_of(cell_ref, width)
    for m in range(2 * members):
        adjoint[m] = dot(weights[m, :, :wide].astype(jnp.bfloat16), marks)
    for q in range(freqs // near):
        here = slice(q * near, (q + 1) * near)
        left = weights[:, here].reshape(2 * members * near, 2 * wide).astype(jnp.bfloat16)
        part = dot(left, near_map(own_ref, other_ref, here))
        adjoint[:, here] += part.reshape(2 * members, near, width)
    for b in range(members):
        whole = adjoint[2 * b : 2 * b + 2].reshape(2 * freqs, width)
        high = whole.astype(jnp.bfloat16)
        low = (whole - high.astype(jnp.float32)).astype(jnp.bfloat16)
        misfit = (dot(back_ref[...], high) + dot(back_ref[...], low)).astype(out_ref.dtype)
        for r in range(rows):
            part = misfit[:, r * lanes : (r + 1) * lanes]
            out_ref[:, :, b, r] = part.reshape(devices, 2, steps, lanes)


def pull_back(core, sums, noise, own, other, back, local_cells, shape):
    devices, _, members, rows, steps, lanes = shape
    _, freqs, sensors, cells = own.shape
    width = CHUNK_ROWS * lanes
    small = [*sums, noise]
    return call(
        pull_kernel,
        core,
        (rows // CHUNK_ROWS,),
        [whole_block(array) for array in small]
        + map_specs(own, width)
        + [whole_block(back), whole_block(local_cells)],
        pl.BlockSpec(
            (devices, 2, members, CHUNK_ROWS, steps, lanes), lambda c, core: (0, 0, 0, c, 0, 0)
        ),
        jax.ShapeDtypeStruct(shape, jnp.bfloat16),
        [
            pltpu.VMEM((2 * members, freqs, 4 * lanes), jnp.float32),
            pltpu.VMEM((2 * members, freqs, width), jnp.float32),
        ],
        cost_estimate=map_cost(members, own, math.prod(shape)),
        name="pull_back",
    )(core, *small, own, other, back, local_cells)


def rims(top, bottom):
    size = lax.axis_size("cells")
    onward = [(k, k + 1) for k in range(size - 1)]
    backward = [(k + 1, k) for k in range(size - 1)]
    return lax.ppermute(bottom, "cells", onward), lax.ppermute(top, "cells", backward)


def misfit_rims(edge):
    size, width = lax.axis_size("cells"), lax.axis_size("sensors")
    same, cross = [], []
    for cell in range(size):
        for sensor in range(width):
            there = cell + 2 * (sensor % 2) - 1
            if 0 <= there < size:
                same.append((cell * width + sensor, there * width + sensor))
                cross.append((cell * width + sensor, there * width + (sensor ^ 1)))
    both = ("cells", "sensors")
    return lax.ppermute(edge, both, same), lax.ppermute(edge, both, cross)


def swap_cores(value):
    size = lax.axis_size("sensors")
    return lax.ppermute(value, "sensors", [(k, k ^ 1) for k in range(size)])


def from_all_cells(value):
    size = lax.axis_size("cells")
    if size & (size - 1):
        return [lax.psum(value, "cells")]
    return [value] + [
        lax.ppermute(value, "cells", [(k, k ^ other) for k in range(size)])
        for other in range(1, size)
    ]


class Line:
    def __init__(self, value):
        self.size = lax.axis_size("sensors")
        self.value, self.ups, self.downs = value, [], []
        self.ends = (value, value)

    def hop(self, last=False):
        while len(self.ups) < self.size // 2 - 1:
            start = 2 * len(self.ups)
            onward = [(k, k + 2) for k in range(start, self.size - 2)]
            backward = [(self.size - 1 - k, self.size - 1 - there) for k, there in onward]
            up = lax.ppermute(self.ends[0], "sensors", onward)
            down = lax.ppermute(self.ends[1], "sensors", backward)
            self.ups.append(up)
            self.downs.append(down)
            self.ends = (up, down)
            if not last:
                break

    def after(self, other):
        if other is not None and self.ups:
            self.ends, other = lax.optimization_barrier((self.ends, other))
            self.ups[-1], self.downs[-1] = self.ends
        return other

    def slots(self):
        return [self.value, *self.ups, *self.downs]


def shards(rhs, forward_map, stiffness, reaction, noise_weight, sensor_cell):
    steps, samples, rows, cols = rhs.shape
    _, freqs, sensors, cells = forward_map.shape
    size = lax.axis_size("sensors")
    chips = size // 2
    cell_index = lax.axis_index("cells")
    sensor_index = lax.axis_index("sensors")
    core = sensor_index % 2
    near = LANES // sensors
    half = cells // 2

    cores = jnp.stack([core, 1 - core])
    offsets = cores[None, :, None] * steps + jnp.arange(steps, dtype=jnp.int32)
    chip_steps = 2 * steps
    places = jnp.arange(chips, dtype=jnp.int32)[:, None, None] * chip_steps
    table = transform_table(freqs, places + offsets)
    back = table.T
    chip = sensor_index // 2
    places = (chip - jnp.arange(chips, dtype=jnp.int32)) % chips
    around = transform_table(freqs, places[:, None, None] * chip_steps + offsets)

    diagonal = reaction + 4.0 * stiffness * stiffness
    local = jnp.stack([stiffness, diagonal])
    up, down = rims(local[:, :HALO], local[:, rows - HALO :])
    stiff, diag = jnp.concatenate([up, local, down], axis=1)
    inside = diag > 0.0
    inverse = jnp.where(inside, 1.0 / jnp.where(inside, diag, 1.0), 0.0)
    unscale = jnp.where(inside, 1.0 / jnp.where(inside, stiff, 1.0), 0.0)
    scaled = DAMPING * inverse * stiff
    coeff = jnp.stack([scaled, scaled * stiff, unscale, stiff, diag])
    coeff = jnp.broadcast_to(coeff[:, :, None, :], coeff.shape[:2] + (SUBLANES, cols))

    def per_lane(values):
        own = lax.dynamic_slice_in_dim(values, sensor_index * sensors, sensors)
        other = lax.dynamic_slice_in_dim(values, (sensor_index ^ 1) * sensors, sensors)
        return jnp.stack([jnp.tile(own, near), jnp.tile(other, near)])

    noise = per_lane(noise_weight)
    local_cells = per_lane(sensor_cell) - (cell_index * cells + core * half)
    local_cells = jnp.broadcast_to(local_cells.reshape(2 * LANES, 1), (2 * LANES, LANES))
    core = core.reshape(1)

    members = samples // GROUPS
    whole = members - members // APART
    edge_rows = lax.optimization_barrier((rhs[:, :, :HALO], rhs[:, :, rows - HALO :]))
    top, bottom = (jnp.transpose(rim, (1, 2, 0, 3)).astype(jnp.bfloat16) for rim in edge_rows)
    lines = [[k for k in range(size) if k % 2 == parity] for parity in range(2)]
    shape = (chips, 2, members, rows // 2, steps, cols)

    def ready(state):
        iterate, keep, give, rest, top, bottom = state
        above, below = rims(top, bottom)
        pair = jnp.stack([keep, swap_cores(give)])
        parts = lax.optimization_barrier((pair[:, :whole], pair[:, whole:]))
        return iterate, *parts, (above, rest, below)

    def edges(misfit):
        first = (rows // 2 - HALO) * core[0]
        edge = lax.dynamic_slice_in_dim(misfit, first, HALO, axis=2)
        same, _ = misfit_rims(edge[0])
        _, cross = misfit_rims(edge[1])
        return misfit[0], swap_cores(misfit[1]), same, cross

    def begin(group, ends):
        return ready(start(group, members, core, rhs, *rims(*ends), coeff))

    groups = [slice(group * members, (group + 1) * members) for group in range(GROUPS)]
    states = [begin(0, (top[groups[0]], bottom[groups[0]]))]
    iterate, pair, apart, rests = states[0]
    pair, apart, whole_map = lax.optimization_barrier((pair, apart, forward_map))
    other_map = swap_cores(whole_map)
    line = Line(apart)
    line.hop()
    for group in range(1, GROUPS):
        ends = (top[groups[group]], bottom[groups[group]])
        rests, ends = line.after((rests, ends))
        states.append(begin(group, ends))
    states[0] = iterate, pair, apart, rests

    outputs = ()
    for iteration in range(ITERS):
        fields = [lax.all_gather(state[1], "sensors", axis_index_groups=lines) for state in states]
        line.hop(last=True)
        totals = []
        for group in range(GROUPS):
            slots, line = line.slots(), None
            if group + 1 < GROUPS:
                line = Line(states[group + 1][2])
                line.hop()
            sums = observe(
                core, fields[group], slots, forward_map, other_map, table, around, local_cells
            )
            if line is not None:
                iterate, pair, apart, rests = states[group + 1]
                sums, rests = lax.optimization_barrier((sums, rests))
                line.after(sums)
                states[group + 1] = iterate, pair, apart, rests
                line.hop()
            sums = from_all_cells(sums + swap_cores(sums)[::-1])
            misfit = pull_back(core, sums, noise, forward_map, other_map, back, local_cells, shape)
            if line is not None:
                line.after(misfit)
                line.hop(last=True)
            totals.append(
                lax.psum_scatter(
                    misfit, "sensors", scatter_dimension=0, axis_index_groups=lines, tiled=False
                )
            )
        for group in range(GROUPS):
            iterate, _, _, rests = states[group]
            total = totals[group]
            if iteration < ITERS - 1:
                if group == 1:
                    before = states[0]
                    line = Line(before[2])
                    line.hop()
                    line.hop()
                    total, earlier = line.after((total, before[3]))
                    states[0] = (*before[:3], earlier)
                states[group] = ready(step(core, rests, edges(total), iterate, coeff))
            else:
                if outputs:
                    total, outputs = lax.optimization_barrier((total, outputs))
                outputs = finish(
                    group, samples, core, rests, edges(total), iterate, coeff, outputs
                )
    return tuple(out.reshape(rhs.shape) for out in outputs)


def solution(mesh):
    placed = (
        P("sensors", None, "cells", None),
        P(None, None, "sensors", "cells"),
        P("cells", None),
        P("cells", None),
        P(),
        P(),
    )
    return jax.shard_map(
        shards,
        mesh=mesh,
        in_specs=placed,
        out_specs=(P("sensors", None, "cells", None), P("sensors", None, "cells", None)),
        check_vma=False,
    )
```

```python
import math

import jax
import jax.numpy as jnp
from jax import lax
from jax.experimental import pallas as pl
from jax.experimental.pallas import tpu as pltpu
from jax.sharding import PartitionSpec as P

SWEEPS = 4
ITERS = 2
DAMPING = 0.8
HALO = SWEEPS
LANES = 128
APART = 3
SUBLANES = 8
GROUPS = 2
CHUNK_ROWS = 4
VMEM_BYTES = 40 * 2**20


def transform_table(freqs, moments):
    period = moments.size
    wave = jnp.arange(freqs, dtype=jnp.int32)[:, None]
    moment = moments.reshape(1, period)
    phase = (wave * moment % period).astype(jnp.float32) * (2.0 * math.pi / period)
    factor = 1.0 / math.sqrt(period)
    return jnp.concatenate([jnp.cos(phase) * factor, -jnp.sin(phase) * factor], axis=0).astype(
        jnp.bfloat16
    )


def whole_block(array):
    return pl.BlockSpec(array.shape, lambda *_: (0,) * array.ndim)


def call(kernel, core, grid, in_specs, out_specs, out_shape, scratch=(), aliases=None, **kwargs):
    grid_spec = pltpu.PrefetchScalarGridSpec(
        num_scalar_prefetch=1,
        grid=grid,
        in_specs=in_specs,
        out_specs=out_specs,
        scratch_shapes=list(scratch),
    )
    return pl.pallas_call(
        kernel,
        grid_spec=grid_spec,
        out_shape=out_shape,
        input_output_aliases=aliases or {},
        compiler_params=pltpu.CompilerParams(vmem_limit_bytes=VMEM_BYTES),
        **kwargs,
    )


def dot(left, right):
    return jnp.dot(left, right, preferred_element_type=jnp.float32)


def dot_lanes(left, right):
    return lax.dot_general(left, right, (((1,), (1,)), ((), ())), preferred_element_type=jnp.float32)


def neighbours(field):
    inner = field[1:-1]
    lane = lax.broadcasted_iota(jnp.int32, inner.shape, 2)
    before = jnp.where(lane == 0, 0.0, pltpu.roll(inner, 1, 2))
    after = jnp.where(lane == LANES - 1, 0.0, pltpu.roll(inner, LANES - 1, 2))
    return (field[2:] + field[:-2]) + (before + after)


def trim(array, width):
    return array[width : array.shape[0] - width]


def precondition(residual, coeff_ref):
    extra = (coeff_ref.shape[1] - residual.shape[0]) // 2
    coeff = [trim(coeff_ref[k], extra) for k in range(3)]
    first = coeff[0] * residual
    scaled = first
    for sweep in range(1, SWEEPS):
        scaled = (
            (1.0 - DAMPING) * scaled[1:-1]
            + trim(first, sweep)
            + trim(coeff[1], sweep) * neighbours(scaled)
        )
    return trim(coeff[2], SWEEPS - 1) * scaled


def prior(field, coeff_ref):
    extra = (coeff_ref.shape[1] - field.shape[0]) // 2
    stiffness = trim(coeff_ref[3], extra)
    diagonal = trim(coeff_ref[4], extra + 1)
    return diagonal * field[1:-1] - stiffness[1:-1] * neighbours(stiffness * field)


def time_chunks(steps, body):
    def run(index, carry):
        body(pl.ds(pl.multiple_of(index * SUBLANES, SUBLANES), SUBLANES))
        return carry

    lax.fori_loop(0, steps // SUBLANES, run, 0)


def fields(members, rows, steps, cols):
    field = pl.BlockSpec((1, rows, steps, cols), lambda b, core: (b, 0, 0, 0))
    half = pl.BlockSpec((1, rows // 2, steps, cols), lambda b, core: (b, 0, 0, 0))
    rim = pl.BlockSpec((1, HALO, steps, cols), lambda b, core: (b, 0, 0, 0))

    def shape(count, dtype):
        return jax.ShapeDtypeStruct((members, count, steps, cols), dtype)

    specs = [field, half, half, field, rim, rim]
    shapes = [
        shape(rows, jnp.float32),
        shape(rows // 2, jnp.bfloat16),
        shape(rows // 2, jnp.bfloat16),
        shape(rows, jnp.float32),
        shape(HALO, jnp.bfloat16),
        shape(HALO, jnp.bfloat16),
    ]
    return field, half, rim, specs, shapes


def put_rest(rest, times, rest_ref, top_ref, bottom_ref):
    rest_ref[0, :, times] = rest
    top_ref[0, :, times] = rest[:HALO].astype(top_ref.dtype)
    bottom_ref[0, :, times] = rest[rest.shape[0] - HALO :].astype(bottom_ref.dtype)


def put_low(core, iter_ref, keep_ref, give_ref):
    half = keep_ref.shape[1]
    keep_ref[0] = iter_ref[0, pl.ds(core * half, half)].astype(keep_ref.dtype)
    give_ref[0] = iter_ref[0, pl.ds((1 - core) * half, half)].astype(give_ref.dtype)


def start_kernel(
    core_ref, rhs_ref, up_ref, down_ref, coeff_ref,
    iter_ref, keep_ref, give_ref, rest_ref, top_ref, bottom_ref,
):
    def body(times):
        here = jnp.swapaxes(rhs_ref[times], 0, 1)
        rims_here = [ref[0, :, times].astype(jnp.float32) for ref in (up_ref, down_ref)]
        update = precondition(jnp.concatenate([rims_here[0], here, rims_here[1]], axis=0), coeff_ref)
        iter_ref[0, :, times] = update[1:-1]
        put_rest(here - prior(update, coeff_ref), times, rest_ref, top_ref, bottom_ref)

    time_chunks(iter_ref.shape[2], body)
    put_low(core_ref[0], iter_ref, keep_ref, give_ref)


def start(group, members, core, rhs, up, down, coeff):
    steps, _, rows, cols = rhs.shape
    flat = rhs.reshape(steps, -1, cols)
    field, half, rim, specs, shapes = fields(members, rows, steps, cols)
    return call(
        start_kernel,
        core,
        (members,),
        [
            pl.BlockSpec((steps, rows, cols), lambda b, core: (0, b + group * members, 0)),
            rim,
            rim,
            whole_block(coeff),
        ],
        specs,
        shapes,
        name="start",
    )(core, flat, up, down, coeff)


def residual_of(core, times, rest_refs, misfit_refs, whole_ref):
    own_ref, other_ref, same_ref, cross_ref = misfit_refs
    half = own_ref.shape[1]
    whole_ref[pl.ds(core * half, half)] = own_ref[0, :, times].astype(jnp.float32)
    whole_ref[pl.ds((1 - core) * half, half)] = other_ref[0, :, times].astype(jnp.float32)
    same = same_ref[0, :, times].astype(jnp.float32)
    cross = cross_ref[0, :, times].astype(jnp.float32)
    first = core == 0
    parts = [jnp.where(first, cross, same), whole_ref[...], jnp.where(first, same, cross)]
    rests = [ref[0, :, times].astype(jnp.float32) for ref in rest_refs]
    return jnp.concatenate([rest - part for rest, part in zip(rests, parts)], axis=0)


def step_kernel(
    core_ref, up_ref, rest_ref, down_ref, own_ref, other_ref, same_ref, cross_ref, iter_ref, coeff_ref,
    next_ref, keep_ref, give_ref, later_ref, top_ref, bottom_ref, whole_ref,
):
    def body(times):
        residual = residual_of(
            core_ref[0],
            times,
            (up_ref, rest_ref, down_ref),
            (own_ref, other_ref, same_ref, cross_ref),
            whole_ref,
        )
        update = precondition(residual, coeff_ref)
        next_ref[0, :, times] = iter_ref[0, :, times] + update[1:-1]
        put_rest(rest_ref[0, :, times] - prior(update, coeff_ref), times, later_ref, top_ref, bottom_ref)

    time_chunks(iter_ref.shape[2], body)
    put_low(core_ref[0], next_ref, keep_ref, give_ref)


def step(core, rests, misfits, iterate, coeff):
    members, rows, steps, cols = iterate.shape
    field, half, rim, specs, shapes = fields(members, rows, steps, cols)
    return call(
        step_kernel,
        core,
        (members,),
        [rim, field, rim, half, half, rim, rim, field, whole_block(coeff)],
        specs,
        shapes,
        [pltpu.VMEM((rows, SUBLANES, cols), jnp.float32)],
        name="step",
    )(core, *rests, *misfits, iterate, coeff)


def finish_kernel(
    core_ref, up_ref, rest_ref, down_ref, own_ref, other_ref, same_ref, cross_ref, iter_ref, coeff_ref,
    *refs,
):
    solution_ref, residual_ref, whole_ref = refs[-3:]

    def body(times):
        residual = residual_of(
            core_ref[0],
            times,
            (up_ref, rest_ref, down_ref),
            (own_ref, other_ref, same_ref, cross_ref),
            whole_ref,
        )
        update = precondition(residual, coeff_ref)
        solution_ref[times] = jnp.swapaxes(iter_ref[0, :, times] + update[1:-1], 0, 1)
        residual_ref[times] = jnp.swapaxes(trim(residual, HALO), 0, 1)

    time_chunks(iter_ref.shape[2], body)


def finish(group, samples, core, rests, misfits, iterate, coeff, previous):
    members, rows, steps, cols = iterate.shape
    field, half, rim, _, _ = fields(members, rows, steps, cols)
    result = pl.BlockSpec((steps, rows, cols), lambda b, core: (0, b + group * members, 0))
    shape = jax.ShapeDtypeStruct((steps, samples * rows, cols), jnp.float32)
    in_specs = [rim, field, rim, half, half, rim, rim, field, whole_block(coeff)]
    first = 1 + len(in_specs)
    return call(
        finish_kernel,
        core,
        (members,),
        in_specs + [pl.BlockSpec(memory_space=pl.ANY)] * len(previous),
        [result, result],
        [shape, shape],
        [pltpu.VMEM((rows, SUBLANES, cols), jnp.float32)],
        {first + k: k for k in range(len(previous))},
        name="finish",
    )(core, *rests, *misfits, iterate, coeff, *previous)


def same_frequency(near, sensors, lanes):
    shape = (near, lanes)
    return lax.broadcasted_iota(jnp.int32, shape, 0) == (
        lax.broadcasted_iota(jnp.int32, shape, 1) % LANES // sensors
    )


def marks_of(cell_ref, width):
    first = pl.program_id(0) * width
    parts = []
    for start_lane in range(0, width, LANES):
        lane = lax.broadcasted_iota(jnp.int32, cell_ref.shape, 1) + (first + start_lane)
        parts.append(jnp.where(cell_ref[...] == lane, 1.0, 0.0).astype(jnp.bfloat16))
    return jnp.concatenate(parts, axis=1)


def near_map(own_ref, other_ref, here):
    _, freqs, sensors, width = own_ref.shape
    parts = [
        ref[part, here].reshape(LANES, width) for part in range(2) for ref in (own_ref, other_ref)
    ]
    return jnp.concatenate(parts, axis=0)


def observe_kernel(core_ref, field_ref, *refs):
    *slot_refs, own_ref, other_ref, table_ref, around_ref, cell_ref = refs[:-4]
    out_ref, spec, acc, picked = refs[-4:]
    chips, _, whole, rows, steps, lanes = field_ref.shape
    members = spec.shape[0] // 2
    freqs, sensors, width = own_ref.shape[1:]
    near = lanes // sensors
    wide = 2 * lanes
    chunk = pl.program_id(0)

    @pl.when(chunk == 0)
    def _():
        acc[...] = jnp.zeros_like(acc)
        picked[...] = jnp.zeros_like(picked)

    marks = marks_of(cell_ref, width)

    def history(b, r):
        if b < whole:
            return field_ref[:, :, b, r].reshape(2 * chips * steps, lanes)
        slots = [slot_refs[0][:, b - whole, r]]
        for k in range(1, chips):
            slots.append(slot_refs[k][:, b - whole, r] + slot_refs[2 * chips - 1 - k][:, b - whole, r])
        return jnp.concatenate([slot.reshape(2 * steps, lanes) for slot in slots], axis=0)

    for b in range(members):
        table = table_ref[...] if b < whole else around_ref[...]
        spectrum = dot(table, jnp.concatenate([history(b, r) for r in range(rows)], axis=1))
        spec[2 * b] = spectrum[:freqs]
        spec[2 * b + 1] = spectrum[freqs:]
    for m in range(2 * members):
        picked[m] += dot_lanes(spec[m].astype(jnp.bfloat16), marks)
    for q in range(freqs // near):
        here = slice(q * near, (q + 1) * near)
        left = spec[:, here].reshape(2 * members * near, width).astype(jnp.bfloat16)
        acc[q] += dot_lanes(left, near_map(own_ref, other_ref, here))

    @pl.when(chunk == pl.num_programs(0) - 1)
    def _():
        mask = same_frequency(near, sensors, wide)
        for q in range(freqs // near):
            here = slice(q * near, (q + 1) * near)
            for b in range(members):
                real = acc[q, 2 * b * near : (2 * b + 1) * near]
                imag = acc[q, (2 * b + 1) * near : (2 * b + 2) * near]
                sums = (
                    real[:, :wide] - imag[:, wide:] + picked[2 * b, here],
                    imag[:, :wide] + real[:, wide:] + picked[2 * b + 1, here],
                )
                for part, value in enumerate(sums):
                    line = jnp.sum(jnp.where(mask, value, 0.0), 0, keepdims=True)
                    out_ref[0, part, b, q : q + 1] = line[:, :lanes]
                    out_ref[1, part, b, q : q + 1] = line[:, lanes:]


def map_specs(own, width):
    chunks = own.shape[3] // (2 * width)
    spec = pl.BlockSpec(own.shape[:3] + (width,), lambda c, core: (0, 0, 0, core[0] * chunks + c))
    return [spec, spec]


def map_cost(members, own, moved):
    return pl.CostEstimate(
        flops=8 * members * own.size, bytes_accessed=2 * own.size + 2 * moved, transcendentals=0
    )


def observe(core, field, slots, own, other, table, around, local_cells):
    chips, _, whole, rows, steps, lanes = field.shape
    apart = slots[0].shape[1] if slots else 0
    members = whole + apart
    _, freqs, sensors, cells = own.shape
    width = CHUNK_ROWS * lanes
    near = lanes // sensors
    shape = (2, 2, members, freqs // near, lanes)
    block = (chips, 2, whole, CHUNK_ROWS, steps, lanes)
    slot = pl.BlockSpec((2, apart, CHUNK_ROWS, steps, lanes), lambda c, core: (0, 0, c, 0, 0))
    return call(
        observe_kernel,
        core,
        (rows // CHUNK_ROWS,),
        [pl.BlockSpec(block, lambda c, core: (0, 0, 0, c, 0, 0))]
        + [slot] * len(slots)
        + map_specs(own, width)
        + [whole_block(table), whole_block(around), whole_block(local_cells)],
        pl.BlockSpec(shape, lambda c, core: (0, 0, 0, 0, 0)),
        jax.ShapeDtypeStruct(shape, jnp.float32),
        [
            pltpu.VMEM((2 * members, freqs, width), jnp.float32),
            pltpu.VMEM((freqs // near, 2 * members * near, 4 * lanes), jnp.float32),
            pltpu.VMEM((2 * members, freqs, 2 * lanes), jnp.float32),
        ],
        cost_estimate=map_cost(members, own, field.size),
        name="observe",
    )(core, field, *slots, own, other, table, around, local_cells)


def pull_kernel(core_ref, *refs):
    *sums, noise_ref, own_ref, other_ref, back_ref, cell_ref = refs[:-3]
    out_ref, weights, adjoint = refs[-3:]
    devices, _, members, rows, steps, lanes = out_ref.shape
    freqs, sensors, width = own_ref.shape[1:]
    near = lanes // sensors
    wide = 2 * lanes

    def total(part, b, which):
        values = [ref[which, part, b] for ref in sums]
        while len(values) > 1:
            values = [values[k] + values[k + 1] for k in range(0, len(values), 2)]
        noise = noise_ref[which : which + 1]
        return (noise * values[0]).astype(jnp.bfloat16).astype(jnp.float32)

    @pl.when(pl.program_id(0) == 0)
    def _():
        mask = same_frequency(near, sensors, wide)
        for b in range(members):
            real, imag = (
                jnp.concatenate([total(part, b, 0), total(part, b, 1)], axis=1) for part in range(2)
            )
            for q in range(freqs // near):
                here = slice(q * near, (q + 1) * near)
                w_real = jnp.where(mask, real[q : q + 1], 0.0)
                w_imag = jnp.where(mask, imag[q : q + 1], 0.0)
                weights[2 * b, here, :wide] = w_real
                weights[2 * b, here, wide:] = w_imag
                weights[2 * b + 1, here, :wide] = w_imag
                weights[2 * b + 1, here, wide:] = -w_real

    marks = marks_of(cell_ref, width)
    for m in range(2 * members):
        adjoint[m] = dot(weights[m, :, :wide].astype(jnp.bfloat16), marks)
    for q in range(freqs // near):
        here = slice(q * near, (q + 1) * near)
        left = weights[:, here].reshape(2 * members * near, 2 * wide).astype(jnp.bfloat16)
        part = dot(left, near_map(own_ref, other_ref, here))
        adjoint[:, here] += part.reshape(2 * members, near, width)
    for b in range(members):
        whole = adjoint[2 * b : 2 * b + 2].reshape(2 * freqs, width)
        high = whole.astype(jnp.bfloat16)
        low = (whole - high.astype(jnp.float32)).astype(jnp.bfloat16)
        misfit = (dot(back_ref[...], high) + dot(back_ref[...], low)).astype(out_ref.dtype)
        for r in range(rows):
            part = misfit[:, r * lanes : (r + 1) * lanes]
            out_ref[:, :, b, r] = part.reshape(devices, 2, steps, lanes)


def pull_back(core, sums, noise, own, other, back, local_cells, shape):
    devices, _, members, rows, steps, lanes = shape
    _, freqs, sensors, cells = own.shape
    width = CHUNK_ROWS * lanes
    small = [*sums, noise]
    return call(
        pull_kernel,
        core,
        (rows // CHUNK_ROWS,),
        [whole_block(array) for array in small]
        + map_specs(own, width)
        + [whole_block(back), whole_block(local_cells)],
        pl.BlockSpec(
            (devices, 2, members, CHUNK_ROWS, steps, lanes), lambda c, core: (0, 0, 0, c, 0, 0)
        ),
        jax.ShapeDtypeStruct(shape, jnp.bfloat16),
        [
            pltpu.VMEM((2 * members, freqs, 4 * lanes), jnp.float32),
            pltpu.VMEM((2 * members, freqs, width), jnp.float32),
        ],
        cost_estimate=map_cost(members, own, math.prod(shape)),
        name="pull_back",
    )(core, *small, own, other, back, local_cells)


def rims(top, bottom):
    size = lax.axis_size("cells")
    onward = [(k, k + 1) for k in range(size - 1)]
    backward = [(k + 1, k) for k in range(size - 1)]
    return lax.ppermute(bottom, "cells", onward), lax.ppermute(top, "cells", backward)


def misfit_rims(edge):
    size, width = lax.axis_size("cells"), lax.axis_size("sensors")
    same, cross = [], []
    for cell in range(size):
        for sensor in range(width):
            there = cell + 2 * (sensor % 2) - 1
            if 0 <= there < size:
                same.append((cell * width + sensor, there * width + sensor))
                cross.append((cell * width + sensor, there * width + (sensor ^ 1)))
    both = ("cells", "sensors")
    return lax.ppermute(edge, both, same), lax.ppermute(edge, both, cross)


def swap_cores(value):
    size = lax.axis_size("sensors")
    return lax.ppermute(value, "sensors", [(k, k ^ 1) for k in range(size)])


def from_all_cells(value):
    size = lax.axis_size("cells")
    if size & (size - 1):
        return [lax.psum(value, "cells")]
    return [value] + [
        lax.ppermute(value, "cells", [(k, k ^ other) for k in range(size)])
        for other in range(1, size)
    ]


class Line:
    def __init__(self, value):
        self.size = lax.axis_size("sensors")
        self.value, self.ups, self.downs = value, [], []
        self.ends = (value, value)

    def hop(self, last=False):
        while len(self.ups) < self.size // 2 - 1:
            start = 2 * len(self.ups)
            onward = [(k, k + 2) for k in range(start, self.size - 2)]
            backward = [(self.size - 1 - k, self.size - 1 - there) for k, there in onward]
            up = lax.ppermute(self.ends[0], "sensors", onward)
            down = lax.ppermute(self.ends[1], "sensors", backward)
            self.ups.append(up)
            self.downs.append(down)
            self.ends = (up, down)
            if not last:
                break

    def after(self, other):
        if other is not None and self.ups:
            self.ends, other = lax.optimization_barrier((self.ends, other))
            self.ups[-1], self.downs[-1] = self.ends
        return other

    def slots(self):
        return [self.value, *self.ups, *self.downs]


def shards(rhs, forward_map, stiffness, reaction, noise_weight, sensor_cell):
    steps, samples, rows, cols = rhs.shape
    _, freqs, sensors, cells = forward_map.shape
    size = lax.axis_size("sensors")
    chips = size // 2
    cell_index = lax.axis_index("cells")
    sensor_index = lax.axis_index("sensors")
    core = sensor_index % 2
    near = LANES // sensors
    half = cells // 2

    cores = jnp.stack([core, 1 - core])
    offsets = cores[None, :, None] * steps + jnp.arange(steps, dtype=jnp.int32)
    chip_steps = 2 * steps
    places = jnp.arange(chips, dtype=jnp.int32)[:, None, None] * chip_steps
    table = transform_table(freqs, places + offsets)
    back = table.T
    chip = sensor_index // 2
    places = (chip - jnp.arange(chips, dtype=jnp.int32)) % chips
    around = transform_table(freqs, places[:, None, None] * chip_steps + offsets)

    diagonal = reaction + 4.0 * stiffness * stiffness
    local = jnp.stack([stiffness, diagonal])
    up, down = rims(local[:, :HALO], local[:, rows - HALO :])
    stiff, diag = jnp.concatenate([up, local, down], axis=1)
    inside = diag > 0.0
    inverse = jnp.where(inside, 1.0 / jnp.where(inside, diag, 1.0), 0.0)
    unscale = jnp.where(inside, 1.0 / jnp.where(inside, stiff, 1.0), 0.0)
    scaled = DAMPING * inverse * stiff
    coeff = jnp.stack([scaled, scaled * stiff, unscale, stiff, diag])
    coeff = jnp.broadcast_to(coeff[:, :, None, :], coeff.shape[:2] + (SUBLANES, cols))

    def per_lane(values):
        own = lax.dynamic_slice_in_dim(values, sensor_index * sensors, sensors)
        other = lax.dynamic_slice_in_dim(values, (sensor_index ^ 1) * sensors, sensors)
        return jnp.stack([jnp.tile(own, near), jnp.tile(other, near)])

    noise = per_lane(noise_weight)
    local_cells = per_lane(sensor_cell) - (cell_index * cells + core * half)
    local_cells = jnp.broadcast_to(local_cells.reshape(2 * LANES, 1), (2 * LANES, LANES))
    core = core.reshape(1)

    members = samples // GROUPS
    whole = members - members // APART
    edge_rows = lax.optimization_barrier((rhs[:, :, :HALO], rhs[:, :, rows - HALO :]))
    top, bottom = (jnp.transpose(rim, (1, 2, 0, 3)).astype(jnp.bfloat16) for rim in edge_rows)
    lines = [[k for k in range(size) if k % 2 == parity] for parity in range(2)]
    shape = (chips, 2, members, rows // 2, steps, cols)

    def ready(state, whole):
        iterate, keep, give, rest, top, bottom = state
        above, below = rims(top, bottom)
        pair = jnp.stack([keep, swap_cores(give)])
        parts = lax.optimization_barrier((pair[:, :whole], pair[:, whole:]))
        return iterate, *parts, (above, rest, below)

    def edges(misfit):
        first = (rows // 2 - HALO) * core[0]
        edge = lax.dynamic_slice_in_dim(misfit, first, HALO, axis=2)
        same, _ = misfit_rims(edge[0])
        _, cross = misfit_rims(edge[1])
        return misfit[0], swap_cores(misfit[1]), same, cross

    def begin(group, ends, whole):
        return ready(start(group, members, core, rhs, *rims(*ends), coeff), whole)

    groups = [slice(group * members, (group + 1) * members) for group in range(GROUPS)]
    states = [begin(0, (top[groups[0]], bottom[groups[0]]), members)]
    iterate, pair, apart, rests = states[0]
    pair, whole_map = lax.optimization_barrier((pair, forward_map))
    other_map = swap_cores(whole_map)
    for group in range(1, GROUPS):
        ends = (top[groups[group]], bottom[groups[group]])
        _, rests, ends = lax.optimization_barrier((pair, rests, ends))
        states.append(begin(group, ends, whole))
    states[0] = iterate, pair, apart, rests
    line = None

    outputs = ()
    for iteration in range(ITERS):
        fields = [lax.all_gather(state[1], "sensors", axis_index_groups=lines) for state in states]
        if line is not None:
            line.hop(last=True)
        totals = []
        for group in range(GROUPS):
            iterate, _, _, rests = states[group]
            field = fields[group]
            slots, line = (line.slots() if line is not None else []), None
            if group > 0:
                field, rests = lax.optimization_barrier((field, rests))
            states[group] = iterate, rests
            if group + 1 < GROUPS:
                line = Line(states[group + 1][2])
                line.hop()
                field = line.after(field)
                line.hop()
            sums = observe(
                core, field, slots, forward_map, other_map, table, around, local_cells
            )
            if line is not None:
                sums = line.after(sums)
                line.hop(last=True)
            sums = from_all_cells(sums + swap_cores(sums)[::-1])
            misfit = pull_back(core, sums, noise, forward_map, other_map, back, local_cells, shape)
            if line is not None:
                misfit = line.after(misfit)
            totals.append(
                lax.psum_scatter(
                    misfit, "sensors", scatter_dimension=0, axis_index_groups=lines, tiled=False
                )
            )
        for group in range(GROUPS):
            iterate, rests = states[group]
            total = totals[group]
            if iteration < ITERS - 1:
                if group == 1:
                    before = states[0]
                    line = Line(before[2])
                    line.hop()
                    line.hop()
                    total, earlier = line.after((total, before[3]))
                    states[0] = (*before[:3], earlier)
                states[group] = ready(step(core, rests, edges(total), iterate, coeff), whole)
            else:
                if outputs:
                    total, outputs = lax.optimization_barrier((total, outputs))
                outputs = finish(
                    group, samples, core, rests, edges(total), iterate, coeff, outputs
                )
    return tuple(out.reshape(rhs.shape) for out in outputs)


def solution(mesh):
    placed = (
        P("sensors", None, "cells", None),
        P(None, None, "sensors", "cells"),
        P("cells", None),
        P("cells", None),
        P(),
        P(),
    )
    return jax.shard_map(
        shards,
        mesh=mesh,
        in_specs=placed,
        out_specs=(P("sensors", None, "cells", None), P("sensors", None, "cells", None)),
        check_vma=False,
    )
```

```python
import math

import jax
import jax.numpy as jnp
from jax import lax
from jax.experimental import pallas as pl
from jax.experimental.pallas import tpu as pltpu
from jax.sharding import PartitionSpec as P

SWEEPS = 4
ITERS = 2
DAMPING = 0.8
HALO = SWEEPS
LANES = 128
SUBLANES = 8
GROUPS = 2
CHUNK_ROWS = 4
VMEM_BYTES = 40 * 2**20


def transform_table(freqs, moments):
    period = moments.size
    wave = jnp.arange(freqs, dtype=jnp.int32)[:, None]
    moment = moments.reshape(1, period)
    phase = (wave * moment % period).astype(jnp.float32) * (2.0 * math.pi / period)
    factor = 1.0 / math.sqrt(period)
    return jnp.concatenate([jnp.cos(phase) * factor, -jnp.sin(phase) * factor], axis=0).astype(
        jnp.bfloat16
    )


def whole_block(array):
    return pl.BlockSpec(array.shape, lambda *_: (0,) * array.ndim)


def call(kernel, core, grid, in_specs, out_specs, out_shape, scratch=(), aliases=None, **kwargs):
    grid_spec = pltpu.PrefetchScalarGridSpec(
        num_scalar_prefetch=1,
        grid=grid,
        in_specs=in_specs,
        out_specs=out_specs,
        scratch_shapes=list(scratch),
    )
    return pl.pallas_call(
        kernel,
        grid_spec=grid_spec,
        out_shape=out_shape,
        input_output_aliases=aliases or {},
        compiler_params=pltpu.CompilerParams(vmem_limit_bytes=VMEM_BYTES),
        **kwargs,
    )


def dot(left, right):
    return jnp.dot(left, right, preferred_element_type=jnp.float32)


def dot_lanes(left, right):
    return lax.dot_general(left, right, (((1,), (1,)), ((), ())), preferred_element_type=jnp.float32)


def neighbours(field):
    inner = field[1:-1]
    lane = lax.broadcasted_iota(jnp.int32, inner.shape, 2)
    before = jnp.where(lane == 0, 0.0, pltpu.roll(inner, 1, 2))
    after = jnp.where(lane == LANES - 1, 0.0, pltpu.roll(inner, LANES - 1, 2))
    return (field[2:] + field[:-2]) + (before + after)


def trim(array, width):
    return array[width : array.shape[0] - width]


def precondition(residual, coeff_ref):
    extra = (coeff_ref.shape[1] - residual.shape[0]) // 2
    coeff = [trim(coeff_ref[k], extra) for k in range(3)]
    first = coeff[0] * residual
    scaled = first
    for sweep in range(1, SWEEPS):
        scaled = (
            (1.0 - DAMPING) * scaled[1:-1]
            + trim(first, sweep)
            + trim(coeff[1], sweep) * neighbours(scaled)
        )
    return trim(coeff[2], SWEEPS - 1) * scaled


def prior(field, coeff_ref):
    extra = (coeff_ref.shape[1] - field.shape[0]) // 2
    stiffness = trim(coeff_ref[3], extra)
    diagonal = trim(coeff_ref[4], extra + 1)
    return diagonal * field[1:-1] - stiffness[1:-1] * neighbours(stiffness * field)


def time_chunks(steps, body):
    def run(index, carry):
        body(pl.ds(pl.multiple_of(index * SUBLANES, SUBLANES), SUBLANES))
        return carry

    lax.fori_loop(0, steps // SUBLANES, run, 0)


def fields(members, rows, steps, cols):
    field = pl.BlockSpec((1, rows, steps, cols), lambda b, core: (b, 0, 0, 0))
    half = pl.BlockSpec((1, rows // 2, steps, cols), lambda b, core: (b, 0, 0, 0))
    rim = pl.BlockSpec((1, HALO, steps, cols), lambda b, core: (b, 0, 0, 0))

    def shape(count, dtype):
        return jax.ShapeDtypeStruct((members, count, steps, cols), dtype)

    specs = [field, field, field, rim, rim]
    shapes = [
        shape(rows, jnp.float32),
        shape(rows, jnp.bfloat16),
        shape(rows, jnp.float32),
        shape(HALO, jnp.bfloat16),
        shape(HALO, jnp.bfloat16),
    ]
    return field, half, rim, specs, shapes


def put_rest(rest, times, rest_ref, top_ref, bottom_ref):
    rest_ref[0, :, times] = rest
    top_ref[0, :, times] = rest[:HALO].astype(top_ref.dtype)
    bottom_ref[0, :, times] = rest[rest.shape[0] - HALO :].astype(bottom_ref.dtype)


def start_kernel(
    core_ref, rhs_ref, up_ref, down_ref, coeff_ref,
    iter_ref, low_ref, rest_ref, top_ref, bottom_ref,
):
    def body(times):
        here = jnp.swapaxes(rhs_ref[times], 0, 1)
        rims_here = [ref[0, :, times].astype(jnp.float32) for ref in (up_ref, down_ref)]
        update = precondition(jnp.concatenate([rims_here[0], here, rims_here[1]], axis=0), coeff_ref)
        iter_ref[0, :, times] = update[1:-1]
        put_rest(here - prior(update, coeff_ref), times, rest_ref, top_ref, bottom_ref)

    time_chunks(iter_ref.shape[2], body)
    low_ref[...] = iter_ref[...].astype(low_ref.dtype)


def start(group, members, core, rhs, up, down, coeff):
    steps, _, rows, cols = rhs.shape
    flat = rhs.reshape(steps, -1, cols)
    field, half, rim, specs, shapes = fields(members, rows, steps, cols)
    return call(
        start_kernel,
        core,
        (members,),
        [
            pl.BlockSpec((steps, rows, cols), lambda b, core: (0, b + group * members, 0)),
            rim,
            rim,
            whole_block(coeff),
        ],
        specs,
        shapes,
        name="start",
    )(core, flat, up, down, coeff)


def residual_of(core, times, rest_refs, misfit_refs, whole_ref):
    own_ref, other_ref, same_ref, cross_ref = misfit_refs
    half = own_ref.shape[1]
    whole_ref[pl.ds(core * half, half)] = own_ref[0, :, times].astype(jnp.float32)
    whole_ref[pl.ds((1 - core) * half, half)] = other_ref[0, :, times].astype(jnp.float32)
    same = same_ref[0, :, times].astype(jnp.float32)
    cross = cross_ref[0, :, times].astype(jnp.float32)
    first = core == 0
    parts = [jnp.where(first, cross, same), whole_ref[...], jnp.where(first, same, cross)]
    rests = [ref[0, :, times].astype(jnp.float32) for ref in rest_refs]
    return jnp.concatenate([rest - part for rest, part in zip(rests, parts)], axis=0)


def step_kernel(
    core_ref, up_ref, rest_ref, down_ref, own_ref, other_ref, same_ref, cross_ref, iter_ref, coeff_ref,
    next_ref, low_ref, later_ref, top_ref, bottom_ref, whole_ref,
):
    def body(times):
        residual = residual_of(
            core_ref[0],
            times,
            (up_ref, rest_ref, down_ref),
            (own_ref, other_ref, same_ref, cross_ref),
            whole_ref,
        )
        update = precondition(residual, coeff_ref)
        next_ref[0, :, times] = iter_ref[0, :, times] + update[1:-1]
        put_rest(rest_ref[0, :, times] - prior(update, coeff_ref), times, later_ref, top_ref, bottom_ref)

    time_chunks(iter_ref.shape[2], body)
    low_ref[...] = next_ref[...].astype(low_ref.dtype)


def step(core, rests, misfits, iterate, coeff):
    members, rows, steps, cols = iterate.shape
    field, half, rim, specs, shapes = fields(members, rows, steps, cols)
    return call(
        step_kernel,
        core,
        (members,),
        [rim, field, rim, half, half, rim, rim, field, whole_block(coeff)],
        specs,
        shapes,
        [pltpu.VMEM((rows, SUBLANES, cols), jnp.float32)],
        name="step",
    )(core, *rests, *misfits, iterate, coeff)


def finish_kernel(
    core_ref, up_ref, rest_ref, down_ref, own_ref, other_ref, same_ref, cross_ref, iter_ref, coeff_ref,
    *refs,
):
    solution_ref, residual_ref, whole_ref = refs[-3:]

    def body(times):
        residual = residual_of(
            core_ref[0],
            times,
            (up_ref, rest_ref, down_ref),
            (own_ref, other_ref, same_ref, cross_ref),
            whole_ref,
        )
        update = precondition(residual, coeff_ref)
        solution_ref[times] = jnp.swapaxes(iter_ref[0, :, times] + update[1:-1], 0, 1)
        residual_ref[times] = jnp.swapaxes(trim(residual, HALO), 0, 1)

    time_chunks(iter_ref.shape[2], body)


def finish(group, samples, core, rests, misfits, iterate, coeff, previous):
    members, rows, steps, cols = iterate.shape
    field, half, rim, _, _ = fields(members, rows, steps, cols)
    result = pl.BlockSpec((steps, rows, cols), lambda b, core: (0, b + group * members, 0))
    shape = jax.ShapeDtypeStruct((steps, samples * rows, cols), jnp.float32)
    in_specs = [rim, field, rim, half, half, rim, rim, field, whole_block(coeff)]
    first = 1 + len(in_specs)
    return call(
        finish_kernel,
        core,
        (members,),
        in_specs + [pl.BlockSpec(memory_space=pl.ANY)] * len(previous),
        [result, result],
        [shape, shape],
        [pltpu.VMEM((rows, SUBLANES, cols), jnp.float32)],
        {first + k: k for k in range(len(previous))},
        name="finish",
    )(core, *rests, *misfits, iterate, coeff, *previous)


def same_frequency(near, sensors, lanes):
    shape = (near, lanes)
    return lax.broadcasted_iota(jnp.int32, shape, 0) == (
        lax.broadcasted_iota(jnp.int32, shape, 1) % LANES // sensors
    )


def marks_of(cell_ref, width):
    first = pl.program_id(0) * width
    parts = []
    for start_lane in range(0, width, LANES):
        lane = lax.broadcasted_iota(jnp.int32, cell_ref.shape, 1) + (first + start_lane)
        parts.append(jnp.where(cell_ref[...] == lane, 1.0, 0.0).astype(jnp.bfloat16))
    return jnp.concatenate(parts, axis=1)


def near_map(own_ref, other_ref, here):
    _, freqs, sensors, width = own_ref.shape
    parts = [
        ref[part, here].reshape(LANES, width) for part in range(2) for ref in (own_ref, other_ref)
    ]
    return jnp.concatenate(parts, axis=0)


def observe_kernel(core_ref, *refs):
    *field_refs, own_ref, other_ref, table_ref, cell_ref, out_ref, spec, acc, picked = refs
    parts, members, rows, steps, lanes = field_refs[0].shape
    freqs, sensors, width = own_ref.shape[1:]
    near = lanes // sensors
    wide = 2 * lanes
    chunk = pl.program_id(0)

    @pl.when(chunk == 0)
    def _():
        acc[...] = jnp.zeros_like(acc)
        picked[...] = jnp.zeros_like(picked)

    marks = marks_of(cell_ref, width)

    def history(b, r):
        if len(field_refs) == 1:
            return field_refs[0][:, b, r].reshape(parts * steps, lanes)
        chips = (len(field_refs) + 1) // 2
        slots = [field_refs[0][:, b, r]]
        for k in range(1, chips):
            slots.append(field_refs[k][:, b, r] + field_refs[2 * chips - 1 - k][:, b, r])
        return jnp.concatenate([slot.reshape(parts * steps, lanes) for slot in slots], axis=0)

    for b in range(members):
        spectrum = dot(
            table_ref[...], jnp.concatenate([history(b, r) for r in range(rows)], axis=1)
        )
        spec[2 * b] = spectrum[:freqs]
        spec[2 * b + 1] = spectrum[freqs:]
    for m in range(2 * members):
        picked[m] += dot_lanes(spec[m].astype(jnp.bfloat16), marks)
    for q in range(freqs // near):
        here = slice(q * near, (q + 1) * near)
        left = spec[:, here].reshape(2 * members * near, width).astype(jnp.bfloat16)
        acc[q] += dot_lanes(left, near_map(own_ref, other_ref, here))

    @pl.when(chunk == pl.num_programs(0) - 1)
    def _():
        mask = same_frequency(near, sensors, wide)
        for q in range(freqs // near):
            here = slice(q * near, (q + 1) * near)
            for b in range(members):
                real = acc[q, 2 * b * near : (2 * b + 1) * near]
                imag = acc[q, (2 * b + 1) * near : (2 * b + 2) * near]
                sums = (
                    real[:, :wide] - imag[:, wide:] + picked[2 * b, here],
                    imag[:, :wide] + real[:, wide:] + picked[2 * b + 1, here],
                )
                for part, value in enumerate(sums):
                    line = jnp.sum(jnp.where(mask, value, 0.0), 0, keepdims=True)
                    out_ref[0, part, b, q : q + 1] = line[:, :lanes]
                    out_ref[1, part, b, q : q + 1] = line[:, lanes:]


def map_specs(own, width):
    chunks = own.shape[3] // (2 * width)
    spec = pl.BlockSpec(own.shape[:3] + (width,), lambda c, core: (0, 0, 0, core[0] * chunks + c))
    return [spec, spec]


def map_cost(members, own, moved):
    return pl.CostEstimate(
        flops=8 * members * own.size, bytes_accessed=2 * own.size + 2 * moved, transcendentals=0
    )


def observe(core, fields, own, other, table, local_cells):
    parts, members, rows, steps, lanes = fields[0].shape
    _, freqs, sensors, cells = own.shape
    width = CHUNK_ROWS * lanes
    near = lanes // sensors
    chunks = cells // (2 * width)
    first = chunks if len(fields) == 1 else 0
    shape = (2, 2, members, freqs // near, lanes)
    block = pl.BlockSpec(
        (parts, members, CHUNK_ROWS, steps, lanes),
        lambda c, core: (0, 0, core[0] * first + c, 0, 0),
    )
    return call(
        observe_kernel,
        core,
        (chunks,),
        [block] * len(fields)
        + map_specs(own, width)
        + [whole_block(table), whole_block(local_cells)],
        pl.BlockSpec(shape, lambda c, core: (0, 0, 0, 0, 0)),
        jax.ShapeDtypeStruct(shape, jnp.float32),
        [
            pltpu.VMEM((2 * members, freqs, width), jnp.float32),
            pltpu.VMEM((freqs // near, 2 * members * near, 4 * lanes), jnp.float32),
            pltpu.VMEM((2 * members, freqs, 2 * lanes), jnp.float32),
        ],
        cost_estimate=map_cost(members, own, len(fields) * fields[0].size),
        name="observe",
    )(core, *fields, own, other, table, local_cells)


def pull_kernel(core_ref, *refs):
    *sums, noise_ref, own_ref, other_ref, back_ref, cell_ref = refs[:-3]
    out_ref, weights, adjoint = refs[-3:]
    devices, _, members, rows, steps, lanes = out_ref.shape
    freqs, sensors, width = own_ref.shape[1:]
    near = lanes // sensors
    wide = 2 * lanes

    def total(part, b, which):
        values = [ref[which, part, b] for ref in sums]
        while len(values) > 1:
            values = [values[k] + values[k + 1] for k in range(0, len(values), 2)]
        noise = noise_ref[which : which + 1]
        return (noise * values[0]).astype(jnp.bfloat16).astype(jnp.float32)

    @pl.when(pl.program_id(0) == 0)
    def _():
        mask = same_frequency(near, sensors, wide)
        for b in range(members):
            real, imag = (
                jnp.concatenate([total(part, b, 0), total(part, b, 1)], axis=1) for part in range(2)
            )
            for q in range(freqs // near):
                here = slice(q * near, (q + 1) * near)
                w_real = jnp.where(mask, real[q : q + 1], 0.0)
                w_imag = jnp.where(mask, imag[q : q + 1], 0.0)
                weights[2 * b, here, :wide] = w_real
                weights[2 * b, here, wide:] = w_imag
                weights[2 * b + 1, here, :wide] = w_imag
                weights[2 * b + 1, here, wide:] = -w_real

    marks = marks_of(cell_ref, width)
    for m in range(2 * members):
        adjoint[m] = dot(weights[m, :, :wide].astype(jnp.bfloat16), marks)
    for q in range(freqs // near):
        here = slice(q * near, (q + 1) * near)
        left = weights[:, here].reshape(2 * members * near, 2 * wide).astype(jnp.bfloat16)
        part = dot(left, near_map(own_ref, other_ref, here))
        adjoint[:, here] += part.reshape(2 * members, near, width)
    for b in range(members):
        whole = adjoint[2 * b : 2 * b + 2].reshape(2 * freqs, width)
        high = whole.astype(jnp.bfloat16)
        low = (whole - high.astype(jnp.float32)).astype(jnp.bfloat16)
        misfit = (dot(back_ref[...], high) + dot(back_ref[...], low)).astype(out_ref.dtype)
        for r in range(rows):
            part = misfit[:, r * lanes : (r + 1) * lanes]
            out_ref[:, :, b, r] = part.reshape(devices, 2, steps, lanes)


def pull_back(core, sums, noise, own, other, back, local_cells, shape):
    devices, _, members, rows, steps, lanes = shape
    _, freqs, sensors, cells = own.shape
    width = CHUNK_ROWS * lanes
    small = [*sums, noise]
    return call(
        pull_kernel,
        core,
        (rows // CHUNK_ROWS,),
        [whole_block(array) for array in small]
        + map_specs(own, width)
        + [whole_block(back), whole_block(local_cells)],
        pl.BlockSpec(
            (devices, 2, members, CHUNK_ROWS, steps, lanes), lambda c, core: (0, 0, 0, c, 0, 0)
        ),
        jax.ShapeDtypeStruct(shape, jnp.bfloat16),
        [
            pltpu.VMEM((2 * members, freqs, 4 * lanes), jnp.float32),
            pltpu.VMEM((2 * members, freqs, width), jnp.float32),
        ],
        cost_estimate=map_cost(members, own, math.prod(shape)),
        name="pull_back",
    )(core, *small, own, other, back, local_cells)


def rims(top, bottom):
    size = lax.axis_size("cells")
    onward = [(k, k + 1) for k in range(size - 1)]
    backward = [(k + 1, k) for k in range(size - 1)]
    return lax.ppermute(bottom, "cells", onward), lax.ppermute(top, "cells", backward)


def misfit_rims(edge):
    size, width = lax.axis_size("cells"), lax.axis_size("sensors")
    same, cross = [], []
    for cell in range(size):
        for sensor in range(width):
            there = cell + 2 * (sensor % 2) - 1
            if 0 <= there < size:
                same.append((cell * width + sensor, there * width + sensor))
                cross.append((cell * width + sensor, there * width + (sensor ^ 1)))
    both = ("cells", "sensors")
    return lax.ppermute(edge, both, same), lax.ppermute(edge, both, cross)


def swap_cores(value):
    size = lax.axis_size("sensors")
    return lax.ppermute(value, "sensors", [(k, k ^ 1) for k in range(size)])


def from_all_cells(value):
    size = lax.axis_size("cells")
    if size & (size - 1):
        return [lax.psum(value, "cells")]
    return [value] + [
        lax.ppermute(value, "cells", [(k, k ^ other) for k in range(size)])
        for other in range(1, size)
    ]


class Line:
    def __init__(self, value):
        self.size = lax.axis_size("sensors")
        self.value, self.ups, self.downs = value, [], []
        self.ends = (value, value)

    def hop(self, last=False):
        while len(self.ups) < self.size // 2 - 1:
            start = 2 * len(self.ups)
            onward = [(k, k + 2) for k in range(start, self.size - 2)]
            backward = [(self.size - 1 - k, self.size - 1 - there) for k, there in onward]
            up = lax.ppermute(self.ends[0], "sensors", onward)
            down = lax.ppermute(self.ends[1], "sensors", backward)
            self.ups.append(up)
            self.downs.append(down)
            self.ends = (up, down)
            if not last:
                break

    def after(self, other):
        if other is not None and self.ups:
            self.ends, other = lax.optimization_barrier((self.ends, other))
            self.ups[-1], self.downs[-1] = self.ends
        return other

    def slots(self):
        return [self.value, *self.ups, *self.downs]


class Scatter:
    def __init__(self, parts):
        self.size, self.parts = lax.axis_size("sensors"), parts
        self.chip = lax.axis_index("sensors") // 2
        self.hops, self.ends = 0, (None, None)

    def part(self, place, received):
        place = jnp.clip(place, 0, self.parts.shape[0] - 1)
        value = lax.dynamic_index_in_dim(self.parts, place, keepdims=False)
        if received is None:
            return value
        total = value.astype(jnp.float32) + received.astype(jnp.float32)
        return total.astype(value.dtype)

    def hop(self, last=False):
        chips = self.parts.shape[0]
        while self.hops < chips - 1:
            self.hops += 1
            far = chips - self.hops
            onward = [(k, k + 2) for k in range(2 * self.hops)]
            backward = [(self.size - 1 - k, self.size - 1 - there) for k, there in onward]
            up = self.part(self.chip + far, self.ends[0])
            down = self.part(self.chip - far, self.ends[1])
            self.ends = (
                lax.ppermute(up, "sensors", onward),
                lax.ppermute(down, "sensors", backward),
            )
            if not last:
                break

    def after(self, other):
        self.ends, other = lax.optimization_barrier((self.ends, other))
        return other

    def total(self):
        up, down = (end.astype(jnp.float32) for end in self.ends)
        own = lax.dynamic_index_in_dim(self.parts, self.chip, keepdims=False)
        return (own.astype(jnp.float32) + (up + down)).astype(own.dtype)


def shards(rhs, forward_map, stiffness, reaction, noise_weight, sensor_cell):
    steps, samples, rows, cols = rhs.shape
    _, freqs, sensors, cells = forward_map.shape
    size = lax.axis_size("sensors")
    chips = size // 2
    cell_index = lax.axis_index("cells")
    sensor_index = lax.axis_index("sensors")
    core = sensor_index % 2
    near = LANES // sensors
    half = cells // 2

    cores = jnp.stack([core, 1 - core])
    offsets = cores[None, :, None] * steps + jnp.arange(steps, dtype=jnp.int32)
    chip_steps = 2 * steps
    places = jnp.arange(chips, dtype=jnp.int32)[:, None, None] * chip_steps
    back = transform_table(freqs, places + offsets).T
    table = transform_table(freqs, jnp.arange(2 * freqs, dtype=jnp.int32))
    chip = sensor_index // 2
    places = (chip - jnp.arange(chips, dtype=jnp.int32)) % chips
    around = transform_table(freqs, places[:, None, None] * chip_steps + offsets)

    diagonal = reaction + 4.0 * stiffness * stiffness
    local = jnp.stack([stiffness, diagonal])
    up, down = rims(local[:, :HALO], local[:, rows - HALO :])
    stiff, diag = jnp.concatenate([up, local, down], axis=1)
    inside = diag > 0.0
    inverse = jnp.where(inside, 1.0 / jnp.where(inside, diag, 1.0), 0.0)
    unscale = jnp.where(inside, 1.0 / jnp.where(inside, stiff, 1.0), 0.0)
    scaled = DAMPING * inverse * stiff
    coeff = jnp.stack([scaled, scaled * stiff, unscale, stiff, diag])
    coeff = jnp.broadcast_to(coeff[:, :, None, :], coeff.shape[:2] + (SUBLANES, cols))

    def per_lane(values):
        own = lax.dynamic_slice_in_dim(values, sensor_index * sensors, sensors)
        other = lax.dynamic_slice_in_dim(values, (sensor_index ^ 1) * sensors, sensors)
        return jnp.stack([jnp.tile(own, near), jnp.tile(other, near)])

    noise = per_lane(noise_weight)
    local_cells = per_lane(sensor_cell) - (cell_index * cells + core * half)
    local_cells = jnp.broadcast_to(local_cells.reshape(2 * LANES, 1), (2 * LANES, LANES))
    core = core.reshape(1)

    members = samples // GROUPS
    edge_rows = lax.optimization_barrier((rhs[:, :, :HALO], rhs[:, :, rows - HALO :]))
    top, bottom = (jnp.transpose(rim, (1, 2, 0, 3)).astype(jnp.bfloat16) for rim in edge_rows)
    lines = [[k for k in range(size) if k % 2 == parity] for parity in range(2)]
    shape = (chips, 2, members, rows // 2, steps, cols)

    def ready(state):
        iterate, low, rest, top, bottom = state
        above, below = rims(top, bottom)
        return iterate, low, (above, rest, below)

    def begin(group, ends):
        return ready(start(group, members, core, rhs, *rims(*ends), coeff))

    def gather(low):
        return [lax.all_gather(low, "sensors")]

    def both_cores(low):
        keep, give = (
            lax.dynamic_slice_in_dim(low, first * (rows // 2), rows // 2, axis=1)
            for first in (core[0], 1 - core[0])
        )
        return jnp.stack([keep, swap_cores(give)])

    def scatter(misfit):
        return lax.psum_scatter(
            misfit, "sensors", scatter_dimension=0, axis_index_groups=lines, tiled=False
        )

    def edges(misfit):
        first = (rows // 2 - HALO) * core[0]
        edge = lax.dynamic_slice_in_dim(misfit, first, HALO, axis=2)
        same, _ = misfit_rims(edge[0])
        _, cross = misfit_rims(edge[1])
        return misfit[0], swap_cores(misfit[1]), same, cross

    groups = [slice(group * members, (group + 1) * members) for group in range(GROUPS)]
    states = [begin(0, (top[groups[0]], bottom[groups[0]]))]
    iterate, low, rests = states[0]
    low, whole_map = lax.optimization_barrier((low, forward_map))
    other_map = swap_cores(whole_map)
    for group in range(1, GROUPS):
        ends = (top[groups[group]], bottom[groups[group]])
        _, rests, ends = lax.optimization_barrier((low, rests, ends))
        states.append(begin(group, ends))
    states[0] = iterate, low, rests
    fields = [gather(state[1]) for state in states]

    def hessian(fields, table):
        sums = observe(core, fields, forward_map, other_map, table, local_cells)
        sums = from_all_cells(sums + swap_cores(sums)[::-1])
        return pull_back(core, sums, noise, forward_map, other_map, back, local_cells, shape)

    outputs = ()
    for iteration in range(ITERS):
        misfits = []
        for group in range(GROUPS):
            iterate, low, rests = states[group]
            field = fields[group]
            if group > 0:
                field, rests = lax.optimization_barrier((field, rests))
            states[group] = iterate, low, rests
            misfits.append(hessian(field, table if len(field) == 1 else around))
        if iteration == ITERS - 1:
            for group in range(GROUPS):
                iterate, _, rests = states[group]
                total = scatter(misfits[group])
                if outputs:
                    total, outputs = lax.optimization_barrier((total, outputs))
                outputs = finish(
                    group, samples, core, rests, edges(total), iterate, coeff, outputs
                )
            break
        line, back_line = None, Scatter(misfits[-1])
        for group in range(GROUPS):
            iterate, _, rests = states[group]
            if group < GROUPS - 1:
                parts = edges(scatter(misfits[group]))
                if group == 0:
                    back_line.hop()
                    parts = back_line.after(parts)
                    back_line.hop()
            else:
                back_line.hop(last=True)
                ends = back_line.after(line.ends)
                line.ends = ends
                line.ups[-1], line.downs[-1] = ends
                total = back_line.total()
                line.hop()
                before = states[0]
                parts, earlier = line.after((edges(total), before[2]))
                states[0] = (*before[:2], earlier)
                line.hop(last=True)
            states[group] = ready(step(core, rests, parts, iterate, coeff))
            if group == 0:
                pair = back_line.after(both_cores(states[0][1]))
                line = Line(pair)
                line.hop()
        fields = [line.slots()] + [gather(state[1]) for state in states[1:]]
    return tuple(out.reshape(rhs.shape) for out in outputs)


def solution(mesh):
    placed = (
        P("sensors", None, "cells", None),
        P(None, None, "sensors", "cells"),
        P("cells", None),
        P("cells", None),
        P(),
        P(),
    )
    return jax.shard_map(
        shards,
        mesh=mesh,
        in_specs=placed,
        out_specs=(P("sensors", None, "cells", None), P("sensors", None, "cells", None)),
        check_vma=False,
    )
```

```python
import math

import jax
import jax.numpy as jnp
from jax import lax
from jax.experimental import pallas as pl
from jax.experimental.pallas import tpu as pltpu
from jax.sharding import PartitionSpec as P

SWEEPS = 4
ITERS = 2
DAMPING = 0.8
HALO = SWEEPS
LANES = 128
APART = 3
SUBLANES = 8
GROUPS = 2
CHUNK_ROWS = 4
VMEM_BYTES = 40 * 2**20


def transform_table(freqs, moments):
    period = moments.size
    wave = jnp.arange(freqs, dtype=jnp.int32)[:, None]
    moment = moments.reshape(1, period)
    phase = (wave * moment % period).astype(jnp.float32) * (2.0 * math.pi / period)
    factor = 1.0 / math.sqrt(period)
    return jnp.concatenate([jnp.cos(phase) * factor, -jnp.sin(phase) * factor], axis=0).astype(
        jnp.bfloat16
    )


def whole_block(array):
    return pl.BlockSpec(array.shape, lambda *_: (0,) * array.ndim)


def call(kernel, core, grid, in_specs, out_specs, out_shape, scratch=(), aliases=None, **kwargs):
    grid_spec = pltpu.PrefetchScalarGridSpec(
        num_scalar_prefetch=1,
        grid=grid,
        in_specs=in_specs,
        out_specs=out_specs,
        scratch_shapes=list(scratch),
    )
    return pl.pallas_call(
        kernel,
        grid_spec=grid_spec,
        out_shape=out_shape,
        input_output_aliases=aliases or {},
        compiler_params=pltpu.CompilerParams(vmem_limit_bytes=VMEM_BYTES),
        **kwargs,
    )


def dot(left, right):
    return jnp.dot(left, right, preferred_element_type=jnp.float32)


def dot_lanes(left, right):
    return lax.dot_general(left, right, (((1,), (1,)), ((), ())), preferred_element_type=jnp.float32)


def neighbours(field):
    inner = field[1:-1]
    lane = lax.broadcasted_iota(jnp.int32, inner.shape, 2)
    before = jnp.where(lane == 0, 0.0, pltpu.roll(inner, 1, 2))
    after = jnp.where(lane == LANES - 1, 0.0, pltpu.roll(inner, LANES - 1, 2))
    return (field[2:] + field[:-2]) + (before + after)


def trim(array, width):
    return array[width : array.shape[0] - width]


def precondition(residual, coeff_ref):
    extra = (coeff_ref.shape[1] - residual.shape[0]) // 2
    coeff = [trim(coeff_ref[k], extra) for k in range(3)]
    first = coeff[0] * residual
    scaled = first
    for sweep in range(1, SWEEPS):
        scaled = (
            (1.0 - DAMPING) * scaled[1:-1]
            + trim(first, sweep)
            + trim(coeff[1], sweep) * neighbours(scaled)
        )
    return trim(coeff[2], SWEEPS - 1) * scaled


def prior(field, coeff_ref):
    extra = (coeff_ref.shape[1] - field.shape[0]) // 2
    stiffness = trim(coeff_ref[3], extra)
    diagonal = trim(coeff_ref[4], extra + 1)
    return diagonal * field[1:-1] - stiffness[1:-1] * neighbours(stiffness * field)


def time_chunks(steps, body):
    def run(index, carry):
        body(pl.ds(pl.multiple_of(index * SUBLANES, SUBLANES), SUBLANES))
        return carry

    lax.fori_loop(0, steps // SUBLANES, run, 0)


def fields(members, rows, steps, cols):
    field = pl.BlockSpec((1, rows, steps, cols), lambda b, core: (b, 0, 0, 0))
    rim = pl.BlockSpec((1, HALO, steps, cols), lambda b, core: (b, 0, 0, 0))
    misfits = [
        pl.BlockSpec((None, 1, count, steps, cols), lambda b, core, place=place: (place, b, 0, 0, 0))
        for place, count in ((0, rows // 2), (1, rows // 2), (0, HALO), (1, HALO))
    ]

    def shape(count, dtype):
        return jax.ShapeDtypeStruct((members, count, steps, cols), dtype)

    specs = [field, field, field, rim, rim]
    shapes = [
        shape(rows, jnp.float32),
        shape(rows, jnp.bfloat16),
        shape(rows, jnp.float32),
        shape(HALO, jnp.bfloat16),
        shape(HALO, jnp.bfloat16),
    ]
    return field, rim, misfits, specs, shapes


def put_rest(rest, times, rest_ref, top_ref, bottom_ref):
    rest_ref[0, :, times] = rest
    top_ref[0, :, times] = rest[:HALO].astype(top_ref.dtype)
    bottom_ref[0, :, times] = rest[rest.shape[0] - HALO :].astype(bottom_ref.dtype)


def start_kernel(
    core_ref, rhs_ref, up_ref, down_ref, coeff_ref,
    iter_ref, low_ref, rest_ref, top_ref, bottom_ref,
):
    def body(times):
        here = jnp.swapaxes(rhs_ref[times], 0, 1)
        rims_here = [ref[0, :, times].astype(jnp.float32) for ref in (up_ref, down_ref)]
        update = precondition(jnp.concatenate([rims_here[0], here, rims_here[1]], axis=0), coeff_ref)
        iter_ref[0, :, times] = update[1:-1]
        put_rest(here - prior(update, coeff_ref), times, rest_ref, top_ref, bottom_ref)

    time_chunks(iter_ref.shape[2], body)
    low_ref[...] = iter_ref[...].astype(low_ref.dtype)


def start(group, members, core, rhs, up, down, coeff):
    steps, _, rows, cols = rhs.shape
    flat = rhs.reshape(steps, -1, cols)
    _, rim, _, specs, shapes = fields(members, rows, steps, cols)
    return call(
        start_kernel,
        core,
        (members,),
        [
            pl.BlockSpec((steps, rows, cols), lambda b, core: (0, b + group * members, 0)),
            rim,
            rim,
            whole_block(coeff),
        ],
        specs,
        shapes,
        name="start",
    )(core, flat, up, down, coeff)


def residual_of(core, times, rest_refs, misfit_refs, whole_ref):
    own_ref, other_ref, same_ref, cross_ref = misfit_refs
    half = own_ref.shape[1]
    whole_ref[pl.ds(core * half, half)] = own_ref[0, :, times].astype(jnp.float32)
    whole_ref[pl.ds((1 - core) * half, half)] = other_ref[0, :, times].astype(jnp.float32)
    same = same_ref[0, :, times].astype(jnp.float32)
    cross = cross_ref[0, :, times].astype(jnp.float32)
    first = core == 0
    parts = [jnp.where(first, cross, same), whole_ref[...], jnp.where(first, same, cross)]
    rests = [ref[0, :, times].astype(jnp.float32) for ref in rest_refs]
    return jnp.concatenate([rest - part for rest, part in zip(rests, parts)], axis=0)


def step_kernel(
    core_ref, up_ref, rest_ref, down_ref, own_ref, other_ref, same_ref, cross_ref, iter_ref, coeff_ref,
    next_ref, low_ref, later_ref, top_ref, bottom_ref, whole_ref,
):
    def body(times):
        residual = residual_of(
            core_ref[0],
            times,
            (up_ref, rest_ref, down_ref),
            (own_ref, other_ref, same_ref, cross_ref),
            whole_ref,
        )
        update = precondition(residual, coeff_ref)
        next_ref[0, :, times] = iter_ref[0, :, times] + update[1:-1]
        put_rest(rest_ref[0, :, times] - prior(update, coeff_ref), times, later_ref, top_ref, bottom_ref)

    time_chunks(iter_ref.shape[2], body)
    low_ref[...] = next_ref[...].astype(low_ref.dtype)


def step(core, rests, misfits, iterate, coeff):
    members, rows, steps, cols = iterate.shape
    field, rim, parts, specs, shapes = fields(members, rows, steps, cols)
    return call(
        step_kernel,
        core,
        (members,),
        [rim, field, rim, *parts, field, whole_block(coeff)],
        specs,
        shapes,
        [pltpu.VMEM((rows, SUBLANES, cols), jnp.float32)],
        name="step",
    )(core, *rests, *misfits, iterate, coeff)


def finish_kernel(
    core_ref, up_ref, rest_ref, down_ref, own_ref, other_ref, same_ref, cross_ref, iter_ref, coeff_ref,
    *refs,
):
    solution_ref, residual_ref, whole_ref = refs[-3:]

    def body(times):
        residual = residual_of(
            core_ref[0],
            times,
            (up_ref, rest_ref, down_ref),
            (own_ref, other_ref, same_ref, cross_ref),
            whole_ref,
        )
        update = precondition(residual, coeff_ref)
        solution_ref[times] = jnp.swapaxes(iter_ref[0, :, times] + update[1:-1], 0, 1)
        residual_ref[times] = jnp.swapaxes(trim(residual, HALO), 0, 1)

    time_chunks(iter_ref.shape[2], body)


def finish(group, samples, core, rests, misfits, iterate, coeff, previous):
    members, rows, steps, cols = iterate.shape
    field, rim, parts, _, _ = fields(members, rows, steps, cols)
    result = pl.BlockSpec((steps, rows, cols), lambda b, core: (0, b + group * members, 0))
    shape = jax.ShapeDtypeStruct((steps, samples * rows, cols), jnp.float32)
    in_specs = [rim, field, rim, *parts, field, whole_block(coeff)]
    first = 1 + len(in_specs)
    return call(
        finish_kernel,
        core,
        (members,),
        in_specs + [pl.BlockSpec(memory_space=pl.ANY)] * len(previous),
        [result, result],
        [shape, shape],
        [pltpu.VMEM((rows, SUBLANES, cols), jnp.float32)],
        {first + k: k for k in range(len(previous))},
        name="finish",
    )(core, *rests, *misfits, iterate, coeff, *previous)


def same_frequency(near, sensors, lanes):
    shape = (near, lanes)
    return lax.broadcasted_iota(jnp.int32, shape, 0) == (
        lax.broadcasted_iota(jnp.int32, shape, 1) % LANES // sensors
    )


def marks_of(cell_ref, width):
    first = pl.program_id(0) * width
    parts = []
    for start_lane in range(0, width, LANES):
        lane = lax.broadcasted_iota(jnp.int32, cell_ref.shape, 1) + (first + start_lane)
        parts.append(jnp.where(cell_ref[...] == lane, 1.0, 0.0).astype(jnp.bfloat16))
    return jnp.concatenate(parts, axis=1)


def near_map(own_ref, other_ref, here):
    _, freqs, sensors, width = own_ref.shape
    parts = [
        ref[part, here].reshape(LANES, width) for part in range(2) for ref in (own_ref, other_ref)
    ]
    return jnp.concatenate(parts, axis=0)


def observe_kernel(core_ref, field_ref, *refs):
    *slot_refs, own_ref, other_ref, table_ref, around_ref, cell_ref = refs[:-4]
    out_ref, spec, acc, picked = refs[-4:]
    rows, steps, lanes = field_ref.shape[-3:]
    members = spec.shape[0] // 2
    chips = table_ref.shape[1] // (2 * steps)
    whole = field_ref.shape[-4]
    freqs, sensors, width = own_ref.shape[1:]
    near = lanes // sensors
    wide = 2 * lanes
    chunk = pl.program_id(0)

    @pl.when(chunk == 0)
    def _():
        acc[...] = jnp.zeros_like(acc)
        picked[...] = jnp.zeros_like(picked)

    marks = marks_of(cell_ref, width)

    def history(b, r):
        if b < whole:
            here = field_ref[..., b, r, :, :]
            return here.reshape(2 * chips * steps, lanes)
        slots = [slot_refs[0][:, b - whole, r]]
        for k in range(1, chips):
            slots.append(slot_refs[k][:, b - whole, r] + slot_refs[2 * chips - 1 - k][:, b - whole, r])
        return jnp.concatenate([slot.reshape(2 * steps, lanes) for slot in slots], axis=0)

    for b in range(members):
        table = table_ref[...] if b < whole else around_ref[...]
        spectrum = dot(table, jnp.concatenate([history(b, r) for r in range(rows)], axis=1))
        spec[2 * b] = spectrum[:freqs]
        spec[2 * b + 1] = spectrum[freqs:]
    for m in range(2 * members):
        picked[m] += dot_lanes(spec[m].astype(jnp.bfloat16), marks)
    for q in range(freqs // near):
        here = slice(q * near, (q + 1) * near)
        left = spec[:, here].reshape(2 * members * near, width).astype(jnp.bfloat16)
        acc[q] += dot_lanes(left, near_map(own_ref, other_ref, here))

    @pl.when(chunk == pl.num_programs(0) - 1)
    def _():
        mask = same_frequency(near, sensors, wide)
        for q in range(freqs // near):
            here = slice(q * near, (q + 1) * near)
            for b in range(members):
                real = acc[q, 2 * b * near : (2 * b + 1) * near]
                imag = acc[q, (2 * b + 1) * near : (2 * b + 2) * near]
                sums = (
                    real[:, :wide] - imag[:, wide:] + picked[2 * b, here],
                    imag[:, :wide] + real[:, wide:] + picked[2 * b + 1, here],
                )
                for part, value in enumerate(sums):
                    line = jnp.sum(jnp.where(mask, value, 0.0), 0, keepdims=True)
                    out_ref[0, part, b, q : q + 1] = line[:, :lanes]
                    out_ref[1, part, b, q : q + 1] = line[:, lanes:]


def map_specs(own, width):
    chunks = own.shape[3] // (2 * width)
    spec = pl.BlockSpec(own.shape[:3] + (width,), lambda c, core: (0, 0, 0, core[0] * chunks + c))
    return [spec, spec]


def map_cost(members, own, moved):
    return pl.CostEstimate(
        flops=8 * members * own.size, bytes_accessed=2 * own.size + 2 * moved, transcendentals=0
    )


def observe(core, field, slots, own, other, table, around, local_cells):
    *sources, whole, rows, steps, lanes = field.shape
    apart = slots[0].shape[1] if slots else 0
    members = whole + apart
    _, freqs, sensors, cells = own.shape
    width = CHUNK_ROWS * lanes
    near = lanes // sensors
    shape = (2, 2, members, freqs // near, lanes)
    chunks = cells // (2 * width)
    first = chunks if len(sources) == 1 else 0
    block = (*sources, whole, CHUNK_ROWS, steps, lanes)
    lead = (0,) * len(sources) + (0,)
    slot = pl.BlockSpec((2, apart, CHUNK_ROWS, steps, lanes), lambda c, core: (0, 0, c, 0, 0))
    return call(
        observe_kernel,
        core,
        (chunks,),
        [pl.BlockSpec(block, lambda c, core: (*lead, core[0] * first + c, 0, 0))]
        + [slot] * len(slots)
        + map_specs(own, width)
        + [whole_block(table), whole_block(around), whole_block(local_cells)],
        pl.BlockSpec(shape, lambda c, core: (0, 0, 0, 0, 0)),
        jax.ShapeDtypeStruct(shape, jnp.float32),
        [
            pltpu.VMEM((2 * members, freqs, width), jnp.float32),
            pltpu.VMEM((freqs // near, 2 * members * near, 4 * lanes), jnp.float32),
            pltpu.VMEM((2 * members, freqs, 2 * lanes), jnp.float32),
        ],
        cost_estimate=map_cost(members, own, field.size),
        name="observe",
    )(core, field, *slots, own, other, table, around, local_cells)


def pull_kernel(core_ref, *refs):
    *sums, noise_ref, own_ref, other_ref, back_ref, cell_ref = refs[:-3]
    out_ref, weights, adjoint = refs[-3:]
    devices, _, members, rows, steps, lanes = out_ref.shape
    freqs, sensors, width = own_ref.shape[1:]
    near = lanes // sensors
    wide = 2 * lanes

    def total(part, b, which):
        values = [ref[which, part, b] for ref in sums]
        while len(values) > 1:
            values = [values[k] + values[k + 1] for k in range(0, len(values), 2)]
        noise = noise_ref[which : which + 1]
        return (noise * values[0]).astype(jnp.bfloat16).astype(jnp.float32)

    @pl.when(pl.program_id(0) == 0)
    def _():
        mask = same_frequency(near, sensors, wide)
        for b in range(members):
            real, imag = (
                jnp.concatenate([total(part, b, 0), total(part, b, 1)], axis=1) for part in range(2)
            )
            for q in range(freqs // near):
                here = slice(q * near, (q + 1) * near)
                w_real = jnp.where(mask, real[q : q + 1], 0.0)
                w_imag = jnp.where(mask, imag[q : q + 1], 0.0)
                weights[2 * b, here, :wide] = w_real
                weights[2 * b, here, wide:] = w_imag
                weights[2 * b + 1, here, :wide] = w_imag
                weights[2 * b + 1, here, wide:] = -w_real

    marks = marks_of(cell_ref, width)
    for m in range(2 * members):
        adjoint[m] = dot(weights[m, :, :wide].astype(jnp.bfloat16), marks)
    for q in range(freqs // near):
        here = slice(q * near, (q + 1) * near)
        left = weights[:, here].reshape(2 * members * near, 2 * wide).astype(jnp.bfloat16)
        part = dot(left, near_map(own_ref, other_ref, here))
        adjoint[:, here] += part.reshape(2 * members, near, width)
    for b in range(members):
        whole = adjoint[2 * b : 2 * b + 2].reshape(2 * freqs, width)
        high = whole.astype(jnp.bfloat16)
        low = (whole - high.astype(jnp.float32)).astype(jnp.bfloat16)
        misfit = (dot(back_ref[...], high) + dot(back_ref[...], low)).astype(out_ref.dtype)
        for r in range(rows):
            part = misfit[:, r * lanes : (r + 1) * lanes]
            out_ref[:, :, b, r] = part.reshape(devices, 2, steps, lanes)


def pull_back(core, sums, noise, own, other, back, local_cells, shape):
    devices, _, members, rows, steps, lanes = shape
    _, freqs, sensors, cells = own.shape
    width = CHUNK_ROWS * lanes
    small = [*sums, noise]
    return call(
        pull_kernel,
        core,
        (rows // CHUNK_ROWS,),
        [whole_block(array) for array in small]
        + map_specs(own, width)
        + [whole_block(back), whole_block(local_cells)],
        pl.BlockSpec(
            (devices, 2, members, CHUNK_ROWS, steps, lanes), lambda c, core: (0, 0, 0, c, 0, 0)
        ),
        jax.ShapeDtypeStruct(shape, jnp.bfloat16),
        [
            pltpu.VMEM((2 * members, freqs, 4 * lanes), jnp.float32),
            pltpu.VMEM((2 * members, freqs, width), jnp.float32),
        ],
        cost_estimate=map_cost(members, own, math.prod(shape)),
        name="pull_back",
    )(core, *small, own, other, back, local_cells)


def rims(top, bottom):
    size = lax.axis_size("cells")
    onward = [(k, k + 1) for k in range(size - 1)]
    backward = [(k + 1, k) for k in range(size - 1)]
    return lax.ppermute(bottom, "cells", onward), lax.ppermute(top, "cells", backward)


def misfit_rims(edge):
    size, width = lax.axis_size("cells"), lax.axis_size("sensors")
    same, cross = [], []
    for cell in range(size):
        for sensor in range(width):
            there = cell + 2 * (sensor % 2) - 1
            if 0 <= there < size:
                same.append((cell * width + sensor, there * width + sensor))
                cross.append((cell * width + sensor, there * width + (sensor ^ 1)))
    both = ("cells", "sensors")
    return lax.ppermute(edge, both, same), lax.ppermute(edge, both, cross)


def swap_cores(value):
    size = lax.axis_size("sensors")
    return lax.ppermute(value, "sensors", [(k, k ^ 1) for k in range(size)])


def from_all_cells(value):
    size = lax.axis_size("cells")
    if size & (size - 1):
        return [lax.psum(value, "cells")]
    return [value] + [
        lax.ppermute(value, "cells", [(k, k ^ other) for k in range(size)])
        for other in range(1, size)
    ]


class Line:
    def __init__(self, value):
        self.size = lax.axis_size("sensors")
        self.value, self.ups, self.downs = value, [], []
        self.ends = (value, value)

    def hop(self, last=False):
        while len(self.ups) < self.size // 2 - 1:
            start = 2 * len(self.ups)
            onward = [(k, k + 2) for k in range(start, self.size - 2)]
            backward = [(self.size - 1 - k, self.size - 1 - there) for k, there in onward]
            up = lax.ppermute(self.ends[0], "sensors", onward)
            down = lax.ppermute(self.ends[1], "sensors", backward)
            self.ups.append(up)
            self.downs.append(down)
            self.ends = (up, down)
            if not last:
                break

    def after(self, other):
        if other is not None and self.ups:
            self.ends, other = lax.optimization_barrier((self.ends, other))
            self.ups[-1], self.downs[-1] = self.ends
        return other

    def slots(self):
        return [self.value, *self.ups, *self.downs]


def shards(rhs, forward_map, stiffness, reaction, noise_weight, sensor_cell):
    steps, samples, rows, cols = rhs.shape
    _, freqs, sensors, cells = forward_map.shape
    size = lax.axis_size("sensors")
    chips = size // 2
    cell_index = lax.axis_index("cells")
    sensor_index = lax.axis_index("sensors")
    core = sensor_index % 2
    near = LANES // sensors
    half = cells // 2

    cores = jnp.stack([core, 1 - core])
    offsets = cores[None, :, None] * steps + jnp.arange(steps, dtype=jnp.int32)
    chip_steps = 2 * steps
    places = jnp.arange(chips, dtype=jnp.int32)[:, None, None] * chip_steps
    table = transform_table(freqs, places + offsets)
    back = table.T
    in_order = transform_table(freqs, jnp.arange(2 * freqs, dtype=jnp.int32))
    chip = sensor_index // 2
    places = (chip - jnp.arange(chips, dtype=jnp.int32)) % chips
    around = transform_table(freqs, places[:, None, None] * chip_steps + offsets)

    diagonal = reaction + 4.0 * stiffness * stiffness
    local = jnp.stack([stiffness, diagonal])
    members = samples // GROUPS
    groups = [slice(group * members, (group + 1) * members) for group in range(GROUPS)]

    def rim_rows(here, first):
        part = lax.slice_in_dim(rhs[:, here], first, first + HALO, axis=2)
        return jnp.transpose(lax.optimization_barrier(part), (1, 2, 0, 3))

    def packed(first):
        part = rim_rows(groups[0], first).reshape(members * HALO, steps, cols)
        extra = local[:, first : first + HALO].reshape(2 * HALO, cols)
        extra = jnp.pad(extra, ((0, -2 * HALO % steps), (0, 0))).reshape(-1, steps, cols)
        return jnp.concatenate([part, extra], axis=0)

    def unpacked(value):
        part = value[: members * HALO].reshape(members, HALO, steps, cols)
        extra = value[members * HALO :].reshape(-1, cols)[: 2 * HALO].reshape(2, HALO, cols)
        return part, extra

    (up_first, up), (down_first, down) = (
        unpacked(value) for value in rims(packed(0), packed(rows - HALO))
    )
    stiff, diag = jnp.concatenate([up, local, down], axis=1)
    inside = diag > 0.0
    inverse = jnp.where(inside, 1.0 / jnp.where(inside, diag, 1.0), 0.0)
    unscale = jnp.where(inside, 1.0 / jnp.where(inside, stiff, 1.0), 0.0)
    scaled = DAMPING * inverse * stiff
    coeff = jnp.stack([scaled, scaled * stiff, unscale, stiff, diag])
    coeff = jnp.broadcast_to(coeff[:, :, None, :], coeff.shape[:2] + (SUBLANES, cols))

    def per_lane(values):
        own = lax.dynamic_slice_in_dim(values, sensor_index * sensors, sensors)
        other = lax.dynamic_slice_in_dim(values, (sensor_index ^ 1) * sensors, sensors)
        return jnp.stack([jnp.tile(own, near), jnp.tile(other, near)])

    noise = per_lane(noise_weight)
    local_cells = per_lane(sensor_cell) - (cell_index * cells + core * half)
    local_cells = jnp.broadcast_to(local_cells.reshape(2 * LANES, 1), (2 * LANES, LANES))
    core = core.reshape(1)

    whole = members - members // APART
    lines = [[k for k in range(size) if k % 2 == parity] for parity in range(2)]
    shape = (chips, 2, members, rows // 2, steps, cols)

    def both_cores(low):
        keep, give = (
            lax.dynamic_slice_in_dim(low, first * (rows // 2), rows // 2, axis=1)
            for first in (core[0], 1 - core[0])
        )
        return jnp.stack([keep, swap_cores(give)])

    def ready(state):
        iterate, low, rest, top, bottom = state
        above, below = rims(top, bottom)
        pair = both_cores(low)
        parts = lax.optimization_barrier((pair[:, :whole], pair[:, whole:]))
        return iterate, *parts, (above, rest, below)

    def edges(misfit):
        first = (rows // 2 - HALO) * core[0]
        edge = lax.dynamic_slice_in_dim(misfit, first, HALO, axis=2)
        return misfit, swap_cores(misfit), *misfit_rims(edge)

    iterate, low, rest, *ends = start(0, members, core, rhs, up_first, down_first, coeff)
    low, whole_map = lax.optimization_barrier((low, forward_map))
    other_map = swap_cores(whole_map)
    above, below = rims(*ends)
    states = [(iterate, low, None, (above, rest, below))]
    for group in range(1, GROUPS):
        ends = tuple(
            rim_rows(groups[group], first).astype(jnp.bfloat16) for first in (0, rows - HALO)
        )
        _, rests, ends = lax.optimization_barrier((low, states[0][3], ends))
        states[0] = (*states[0][:3], rests)
        states.append(ready(start(group, members, core, rhs, *rims(*ends), coeff)))
    line = None

    outputs = ()
    for iteration in range(ITERS):
        fields = [
            lax.all_gather(state[1], "sensors", axis_index_groups=None if state[2] is None else lines)
            for state in states
        ]
        if line is not None:
            line.hop(last=True)
        totals = []
        for group in range(GROUPS):
            iterate, _, _, rests = states[group]
            field = fields[group]
            slots, line = (line.slots() if line is not None else []), None
            if group > 0:
                field, rests = lax.optimization_barrier((field, rests))
            states[group] = iterate, rests
            if group + 1 < GROUPS:
                line = Line(states[group + 1][2])
                line.hop()
                field = line.after(field)
                line.hop()
            sums = observe(
                core,
                field,
                slots,
                forward_map,
                other_map,
                table if slots else in_order,
                around,
                local_cells,
            )
            if line is not None:
                sums = line.after(sums)
                line.hop(last=True)
            sums = from_all_cells(sums + swap_cores(sums)[::-1])
            misfit = pull_back(core, sums, noise, forward_map, other_map, back, local_cells, shape)
            if line is not None:
                misfit = line.after(misfit)
            totals.append(
                lax.psum_scatter(
                    misfit, "sensors", scatter_dimension=0, axis_index_groups=lines, tiled=False
                )
            )
        for group in range(GROUPS):
            iterate, rests = states[group]
            total = totals[group]
            if iteration < ITERS - 1:
                if group == 1:
                    before = states[0]
                    line = Line(before[2])
                    line.hop()
                    line.hop()
                    total, earlier = line.after((total, before[3]))
                    states[0] = (*before[:3], earlier)
                states[group] = ready(step(core, rests, edges(total), iterate, coeff))
            else:
                if outputs:
                    total, outputs = lax.optimization_barrier((total, outputs))
                outputs = finish(
                    group, samples, core, rests, edges(total), iterate, coeff, outputs
                )
    return tuple(out.reshape(rhs.shape) for out in outputs)


def solution(mesh):
    placed = (
        P("sensors", None, "cells", None),
        P(None, None, "sensors", "cells"),
        P("cells", None),
        P("cells", None),
        P(),
        P(),
    )
    return jax.shard_map(
        shards,
        mesh=mesh,
        in_specs=placed,
        out_specs=(P("sensors", None, "cells", None), P("sensors", None, "cells", None)),
        check_vma=False,
    )
```

```python
import math

import jax
import jax.numpy as jnp
from jax import lax
from jax.experimental import pallas as pl
from jax.experimental.pallas import tpu as pltpu
from jax.sharding import PartitionSpec as P

SWEEPS = 4
ITERS = 2
DAMPING = 0.8
HALO = SWEEPS
LANES = 128
APART = 3
SUBLANES = 8
GROUPS = 2
CHUNK_ROWS = 4
VMEM_BYTES = 40 * 2**20


def transform_table(freqs, moments):
    period = moments.size
    wave = jnp.arange(freqs, dtype=jnp.int32)[:, None]
    moment = moments.reshape(1, period)
    phase = (wave * moment % period).astype(jnp.float32) * (2.0 * math.pi / period)
    factor = 1.0 / math.sqrt(period)
    return jnp.concatenate([jnp.cos(phase) * factor, -jnp.sin(phase) * factor], axis=0).astype(
        jnp.bfloat16
    )


def whole_block(array):
    return pl.BlockSpec(array.shape, lambda *_: (0,) * array.ndim)


def call(kernel, core, grid, in_specs, out_specs, out_shape, scratch=(), aliases=None, **kwargs):
    grid_spec = pltpu.PrefetchScalarGridSpec(
        num_scalar_prefetch=1,
        grid=grid,
        in_specs=in_specs,
        out_specs=out_specs,
        scratch_shapes=list(scratch),
    )
    return pl.pallas_call(
        kernel,
        grid_spec=grid_spec,
        out_shape=out_shape,
        input_output_aliases=aliases or {},
        compiler_params=pltpu.CompilerParams(vmem_limit_bytes=VMEM_BYTES),
        **kwargs,
    )


def dot(left, right):
    return jnp.dot(left, right, preferred_element_type=jnp.float32)


def dot_lanes(left, right):
    return lax.dot_general(left, right, (((1,), (1,)), ((), ())), preferred_element_type=jnp.float32)


def neighbours(field):
    inner = field[1:-1]
    lane = lax.broadcasted_iota(jnp.int32, inner.shape, 2)
    before = jnp.where(lane == 0, 0.0, pltpu.roll(inner, 1, 2))
    after = jnp.where(lane == LANES - 1, 0.0, pltpu.roll(inner, LANES - 1, 2))
    return (field[2:] + field[:-2]) + (before + after)


def trim(array, width):
    return array[width : array.shape[0] - width]


def precondition(residual, coeff_ref):
    extra = (coeff_ref.shape[1] - residual.shape[0]) // 2
    coeff = [trim(coeff_ref[k], extra) for k in range(3)]
    first = coeff[0] * residual
    scaled = first
    for sweep in range(1, SWEEPS):
        scaled = (
            (1.0 - DAMPING) * scaled[1:-1]
            + trim(first, sweep)
            + trim(coeff[1], sweep) * neighbours(scaled)
        )
    return trim(coeff[2], SWEEPS - 1) * scaled


def prior(field, coeff_ref):
    extra = (coeff_ref.shape[1] - field.shape[0]) // 2
    stiffness = trim(coeff_ref[3], extra)
    diagonal = trim(coeff_ref[4], extra + 1)
    return diagonal * field[1:-1] - stiffness[1:-1] * neighbours(stiffness * field)


def time_chunks(steps, body):
    def run(index, carry):
        body(pl.ds(pl.multiple_of(index * SUBLANES, SUBLANES), SUBLANES))
        return carry

    lax.fori_loop(0, steps // SUBLANES, run, 0)


def fields(members, rows, steps, cols):
    field = pl.BlockSpec((1, rows, steps, cols), lambda b, core: (b, 0, 0, 0))
    rim = pl.BlockSpec((1, HALO, steps, cols), lambda b, core: (b, 0, 0, 0))
    misfits = [
        pl.BlockSpec((None, 1, count, steps, cols), lambda b, core: (0, b, 0, 0, 0))
        for count in (rows // 2, rows // 2, HALO, HALO)
    ]

    def shape(count, dtype):
        return jax.ShapeDtypeStruct((members, count, steps, cols), dtype)

    specs = [field, field, field, rim, rim]
    shapes = [
        shape(rows, jnp.float32),
        shape(rows, jnp.bfloat16),
        shape(rows, jnp.float32),
        shape(HALO, jnp.bfloat16),
        shape(HALO, jnp.bfloat16),
    ]
    return field, rim, misfits, specs, shapes


def put_rest(rest, times, rest_ref, top_ref, bottom_ref):
    rest_ref[0, :, times] = rest
    top_ref[0, :, times] = rest[:HALO].astype(top_ref.dtype)
    bottom_ref[0, :, times] = rest[rest.shape[0] - HALO :].astype(bottom_ref.dtype)


def start_kernel(
    core_ref, rhs_ref, up_ref, down_ref, coeff_ref,
    iter_ref, low_ref, rest_ref, top_ref, bottom_ref,
):
    def body(times):
        here = jnp.swapaxes(rhs_ref[times], 0, 1)
        rims_here = [ref[0, :, times].astype(jnp.float32) for ref in (up_ref, down_ref)]
        update = precondition(jnp.concatenate([rims_here[0], here, rims_here[1]], axis=0), coeff_ref)
        iter_ref[0, :, times] = update[1:-1]
        put_rest(here - prior(update, coeff_ref), times, rest_ref, top_ref, bottom_ref)

    time_chunks(iter_ref.shape[2], body)
    low_ref[...] = iter_ref[...].astype(low_ref.dtype)


def start(group, members, core, rhs, up, down, coeff):
    steps, _, rows, cols = rhs.shape
    flat = rhs.reshape(steps, -1, cols)
    _, rim, _, specs, shapes = fields(members, rows, steps, cols)
    return call(
        start_kernel,
        core,
        (members,),
        [
            pl.BlockSpec((steps, rows, cols), lambda b, core: (0, b + group * members, 0)),
            rim,
            rim,
            whole_block(coeff),
        ],
        specs,
        shapes,
        name="start",
    )(core, flat, up, down, coeff)


def residual_of(core, times, rest_refs, misfit_refs, whole_ref):
    own_ref, other_ref, same_ref, cross_ref = misfit_refs
    half = own_ref.shape[1]
    whole_ref[pl.ds(core * half, half)] = own_ref[0, :, times].astype(jnp.float32)
    whole_ref[pl.ds((1 - core) * half, half)] = other_ref[0, :, times].astype(jnp.float32)
    same = same_ref[0, :, times].astype(jnp.float32)
    cross = cross_ref[0, :, times].astype(jnp.float32)
    first = core == 0
    parts = [jnp.where(first, cross, same), whole_ref[...], jnp.where(first, same, cross)]
    rests = [ref[0, :, times].astype(jnp.float32) for ref in rest_refs]
    return jnp.concatenate([rest - part for rest, part in zip(rests, parts)], axis=0)


def step_kernel(
    core_ref, up_ref, rest_ref, down_ref, own_ref, other_ref, same_ref, cross_ref, iter_ref, coeff_ref,
    next_ref, low_ref, later_ref, top_ref, bottom_ref, whole_ref,
):
    def body(times):
        residual = residual_of(
            core_ref[0],
            times,
            (up_ref, rest_ref, down_ref),
            (own_ref, other_ref, same_ref, cross_ref),
            whole_ref,
        )
        update = precondition(residual, coeff_ref)
        next_ref[0, :, times] = iter_ref[0, :, times] + update[1:-1]
        put_rest(rest_ref[0, :, times] - prior(update, coeff_ref), times, later_ref, top_ref, bottom_ref)

    time_chunks(iter_ref.shape[2], body)
    low_ref[...] = next_ref[...].astype(low_ref.dtype)


def step(core, rests, misfits, iterate, coeff):
    members, rows, steps, cols = iterate.shape
    field, rim, parts, specs, shapes = fields(members, rows, steps, cols)
    return call(
        step_kernel,
        core,
        (members,),
        [rim, field, rim, *parts, field, whole_block(coeff)],
        specs,
        shapes,
        [pltpu.VMEM((rows, SUBLANES, cols), jnp.float32)],
        name="step",
    )(core, *rests, *misfits, iterate, coeff)


def finish_kernel(
    core_ref, up_ref, rest_ref, down_ref, own_ref, other_ref, same_ref, cross_ref, iter_ref, coeff_ref,
    *refs,
):
    solution_ref, residual_ref, whole_ref = refs[-3:]

    def body(times):
        residual = residual_of(
            core_ref[0],
            times,
            (up_ref, rest_ref, down_ref),
            (own_ref, other_ref, same_ref, cross_ref),
            whole_ref,
        )
        update = precondition(residual, coeff_ref)
        solution_ref[times] = jnp.swapaxes(iter_ref[0, :, times] + update[1:-1], 0, 1)
        residual_ref[times] = jnp.swapaxes(trim(residual, HALO), 0, 1)

    time_chunks(iter_ref.shape[2], body)


def finish(group, samples, core, rests, misfits, iterate, coeff, previous):
    members, rows, steps, cols = iterate.shape
    field, rim, parts, _, _ = fields(members, rows, steps, cols)
    result = pl.BlockSpec((steps, rows, cols), lambda b, core: (0, b + group * members, 0))
    shape = jax.ShapeDtypeStruct((steps, samples * rows, cols), jnp.float32)
    in_specs = [rim, field, rim, *parts, field, whole_block(coeff)]
    first = 1 + len(in_specs)
    return call(
        finish_kernel,
        core,
        (members,),
        in_specs + [pl.BlockSpec(memory_space=pl.ANY)] * len(previous),
        [result, result],
        [shape, shape],
        [pltpu.VMEM((rows, SUBLANES, cols), jnp.float32)],
        {first + k: k for k in range(len(previous))},
        name="finish",
    )(core, *rests, *misfits, iterate, coeff, *previous)


def same_frequency(near, sensors, lanes):
    shape = (near, lanes)
    return lax.broadcasted_iota(jnp.int32, shape, 0) == (
        lax.broadcasted_iota(jnp.int32, shape, 1) % LANES // sensors
    )


def marks_of(cell_ref, width):
    first = pl.program_id(0) * width
    parts = []
    for start_lane in range(0, width, LANES):
        lane = lax.broadcasted_iota(jnp.int32, cell_ref.shape, 1) + (first + start_lane)
        parts.append(jnp.where(cell_ref[...] == lane, 1.0, 0.0).astype(jnp.bfloat16))
    return jnp.concatenate(parts, axis=1)


def near_map(own_ref, other_ref, here):
    _, freqs, sensors, width = own_ref.shape
    parts = [
        ref[part, here].reshape(LANES, width) for part in range(2) for ref in (own_ref, other_ref)
    ]
    return jnp.concatenate(parts, axis=0)


def observe_kernel(core_ref, field_ref, *refs):
    *slot_refs, own_ref, other_ref, table_ref, around_ref, cell_ref = refs[:-4]
    out_ref, spec, acc, picked = refs[-4:]
    rows, steps, lanes = field_ref.shape[-3:]
    members = spec.shape[0] // 2
    chips = table_ref.shape[1] // (2 * steps)
    whole = field_ref.shape[-4]
    freqs, sensors, width = own_ref.shape[1:]
    near = lanes // sensors
    wide = 2 * lanes
    chunk = pl.program_id(0)

    @pl.when(chunk == 0)
    def _():
        acc[...] = jnp.zeros_like(acc)
        picked[...] = jnp.zeros_like(picked)

    marks = marks_of(cell_ref, width)

    def history(b, r):
        if b < whole:
            here = field_ref[..., b, r, :, :]
            return here.reshape(2 * chips * steps, lanes)
        slots = [slot_refs[0][:, b - whole, r]]
        for k in range(1, chips):
            slots.append(slot_refs[k][:, b - whole, r] + slot_refs[2 * chips - 1 - k][:, b - whole, r])
        return jnp.concatenate([slot.reshape(2 * steps, lanes) for slot in slots], axis=0)

    for b in range(members):
        table = table_ref[...] if b < whole else around_ref[...]
        spectrum = dot(table, jnp.concatenate([history(b, r) for r in range(rows)], axis=1))
        spec[2 * b] = spectrum[:freqs]
        spec[2 * b + 1] = spectrum[freqs:]
    for m in range(2 * members):
        picked[m] += dot_lanes(spec[m].astype(jnp.bfloat16), marks)
    for q in range(freqs // near):
        here = slice(q * near, (q + 1) * near)
        left = spec[:, here].reshape(2 * members * near, width).astype(jnp.bfloat16)
        acc[q] += dot_lanes(left, near_map(own_ref, other_ref, here))

    @pl.when(chunk == pl.num_programs(0) - 1)
    def _():
        mask = same_frequency(near, sensors, wide)
        for q in range(freqs // near):
            here = slice(q * near, (q + 1) * near)
            for b in range(members):
                real = acc[q, 2 * b * near : (2 * b + 1) * near]
                imag = acc[q, (2 * b + 1) * near : (2 * b + 2) * near]
                sums = (
                    real[:, :wide] - imag[:, wide:] + picked[2 * b, here],
                    imag[:, :wide] + real[:, wide:] + picked[2 * b + 1, here],
                )
                for part, value in enumerate(sums):
                    line = jnp.sum(jnp.where(mask, value, 0.0), 0, keepdims=True)
                    out_ref[0, part, b, q : q + 1] = line[:, :lanes]
                    out_ref[1, part, b, q : q + 1] = line[:, lanes:]


def map_specs(own, width):
    chunks = own.shape[3] // (2 * width)
    spec = pl.BlockSpec(own.shape[:3] + (width,), lambda c, core: (0, 0, 0, core[0] * chunks + c))
    return [spec, spec]


def map_cost(members, own, moved):
    return pl.CostEstimate(
        flops=8 * members * own.size, bytes_accessed=2 * own.size + 2 * moved, transcendentals=0
    )


def observe(core, field, slots, own, other, table, around, local_cells):
    *sources, whole, rows, steps, lanes = field.shape
    apart = slots[0].shape[1] if slots else 0
    members = whole + apart
    _, freqs, sensors, cells = own.shape
    width = CHUNK_ROWS * lanes
    near = lanes // sensors
    shape = (2, 2, members, freqs // near, lanes)
    chunks = cells // (2 * width)
    first = chunks if len(sources) == 1 else 0
    block = (*sources, whole, CHUNK_ROWS, steps, lanes)
    lead = (0,) * len(sources) + (0,)
    slot = pl.BlockSpec((2, apart, CHUNK_ROWS, steps, lanes), lambda c, core: (0, 0, c, 0, 0))
    return call(
        observe_kernel,
        core,
        (chunks,),
        [pl.BlockSpec(block, lambda c, core: (*lead, core[0] * first + c, 0, 0))]
        + [slot] * len(slots)
        + map_specs(own, width)
        + [whole_block(table), whole_block(around), whole_block(local_cells)],
        pl.BlockSpec(shape, lambda c, core: (0, 0, 0, 0, 0)),
        jax.ShapeDtypeStruct(shape, jnp.float32),
        [
            pltpu.VMEM((2 * members, freqs, width), jnp.float32),
            pltpu.VMEM((freqs // near, 2 * members * near, 4 * lanes), jnp.float32),
            pltpu.VMEM((2 * members, freqs, 2 * lanes), jnp.float32),
        ],
        cost_estimate=map_cost(members, own, field.size),
        name="observe",
    )(core, field, *slots, own, other, table, around, local_cells)


def pull_kernel(core_ref, *refs):
    *sums, noise_ref, own_ref, other_ref, back_ref, cell_ref = refs[:-3]
    out_ref, weights, adjoint = refs[-3:]
    devices, _, members, rows, steps, lanes = out_ref.shape
    freqs, sensors, width = own_ref.shape[1:]
    near = lanes // sensors
    wide = 2 * lanes

    def total(part, b, which):
        values = [ref[which, part, b] for ref in sums]
        while len(values) > 1:
            values = [values[k] + values[k + 1] for k in range(0, len(values), 2)]
        noise = noise_ref[which : which + 1]
        return (noise * values[0]).astype(jnp.bfloat16).astype(jnp.float32)

    @pl.when(pl.program_id(0) == 0)
    def _():
        mask = same_frequency(near, sensors, wide)
        for b in range(members):
            real, imag = (
                jnp.concatenate([total(part, b, 0), total(part, b, 1)], axis=1) for part in range(2)
            )
            for q in range(freqs // near):
                here = slice(q * near, (q + 1) * near)
                w_real = jnp.where(mask, real[q : q + 1], 0.0)
                w_imag = jnp.where(mask, imag[q : q + 1], 0.0)
                weights[2 * b, here, :wide] = w_real
                weights[2 * b, here, wide:] = w_imag
                weights[2 * b + 1, here, :wide] = w_imag
                weights[2 * b + 1, here, wide:] = -w_real

    marks = marks_of(cell_ref, width)
    for m in range(2 * members):
        adjoint[m] = dot(weights[m, :, :wide].astype(jnp.bfloat16), marks)
    for q in range(freqs // near):
        here = slice(q * near, (q + 1) * near)
        left = weights[:, here].reshape(2 * members * near, 2 * wide).astype(jnp.bfloat16)
        part = dot(left, near_map(own_ref, other_ref, here))
        adjoint[:, here] += part.reshape(2 * members, near, width)
    for b in range(members):
        whole = adjoint[2 * b : 2 * b + 2].reshape(2 * freqs, width)
        high = whole.astype(jnp.bfloat16)
        low = (whole - high.astype(jnp.float32)).astype(jnp.bfloat16)
        misfit = (dot(back_ref[...], high) + dot(back_ref[...], low)).astype(out_ref.dtype)
        for r in range(rows):
            part = misfit[:, r * lanes : (r + 1) * lanes]
            out_ref[:, :, b, r] = part.reshape(devices, 2, steps, lanes)


def pull_back(core, sums, noise, own, other, back, local_cells, shape):
    devices, _, members, rows, steps, lanes = shape
    _, freqs, sensors, cells = own.shape
    width = CHUNK_ROWS * lanes
    small = [*sums, noise]
    return call(
        pull_kernel,
        core,
        (rows // CHUNK_ROWS,),
        [whole_block(array) for array in small]
        + map_specs(own, width)
        + [whole_block(back), whole_block(local_cells)],
        pl.BlockSpec(
            (devices, 2, members, CHUNK_ROWS, steps, lanes), lambda c, core: (0, 0, 0, c, 0, 0)
        ),
        jax.ShapeDtypeStruct(shape, jnp.bfloat16),
        [
            pltpu.VMEM((2 * members, freqs, 4 * lanes), jnp.float32),
            pltpu.VMEM((2 * members, freqs, width), jnp.float32),
        ],
        cost_estimate=map_cost(members, own, math.prod(shape)),
        name="pull_back",
    )(core, *small, own, other, back, local_cells)


def rims(top, bottom):
    size = lax.axis_size("cells")
    onward = [(k, k + 1) for k in range(size - 1)]
    backward = [(k + 1, k) for k in range(size - 1)]
    return lax.ppermute(bottom, "cells", onward), lax.ppermute(top, "cells", backward)


def misfit_rims(edge):
    size, width = lax.axis_size("cells"), lax.axis_size("sensors")
    same, cross = [], []
    for cell in range(size):
        for sensor in range(width):
            there = cell + 2 * (sensor % 2) - 1
            if 0 <= there < size:
                same.append((cell * width + sensor, there * width + sensor))
                cross.append((cell * width + sensor, there * width + (sensor ^ 1)))
    both = ("cells", "sensors")
    return lax.ppermute(edge, both, same), lax.ppermute(edge, both, cross)


def swap_cores(value):
    size = lax.axis_size("sensors")
    return lax.ppermute(value, "sensors", [(k, k ^ 1) for k in range(size)])


def from_all_cells(value):
    size = lax.axis_size("cells")
    if size & (size - 1):
        return [lax.psum(value, "cells")]
    return [value] + [
        lax.ppermute(value, "cells", [(k, k ^ other) for k in range(size)])
        for other in range(1, size)
    ]


class Line:
    def __init__(self, value):
        self.size = lax.axis_size("sensors")
        self.value, self.ups, self.downs = value, [], []
        self.ends = (value, value)

    def hop(self, last=False):
        while len(self.ups) < self.size // 2 - 1:
            start = 2 * len(self.ups)
            onward = [(k, k + 2) for k in range(start, self.size - 2)]
            backward = [(self.size - 1 - k, self.size - 1 - there) for k, there in onward]
            up = lax.ppermute(self.ends[0], "sensors", onward)
            down = lax.ppermute(self.ends[1], "sensors", backward)
            self.ups.append(up)
            self.downs.append(down)
            self.ends = (up, down)
            if not last:
                break

    def after(self, other):
        if other is not None and self.ups:
            self.ends, other = lax.optimization_barrier((self.ends, other))
            self.ups[-1], self.downs[-1] = self.ends
        return other

    def slots(self):
        return [self.value, *self.ups, *self.downs]


def shards(rhs, forward_map, stiffness, reaction, noise_weight, sensor_cell):
    steps, samples, rows, cols = rhs.shape
    _, freqs, sensors, cells = forward_map.shape
    size = lax.axis_size("sensors")
    chips = size // 2
    cell_index = lax.axis_index("cells")
    sensor_index = lax.axis_index("sensors")
    core = sensor_index % 2
    near = LANES // sensors
    half = cells // 2
    other_map = swap_cores(forward_map)

    cores = jnp.stack([core, 1 - core])
    offsets = cores[None, :, None] * steps + jnp.arange(steps, dtype=jnp.int32)
    chip_steps = 2 * steps
    places = jnp.arange(chips, dtype=jnp.int32)[:, None, None] * chip_steps
    table = transform_table(freqs, places + offsets)
    back = table.T
    in_order = transform_table(freqs, jnp.arange(2 * freqs, dtype=jnp.int32))
    chip = sensor_index // 2
    places = (chip - jnp.arange(chips, dtype=jnp.int32)) % chips
    around = transform_table(freqs, places[:, None, None] * chip_steps + offsets)

    diagonal = reaction + 4.0 * stiffness * stiffness
    local = jnp.stack([stiffness, diagonal])
    members = samples // GROUPS
    groups = [slice(group * members, (group + 1) * members) for group in range(GROUPS)]

    def rim_rows(here, first):
        part = lax.slice_in_dim(rhs[:, here], first, first + HALO, axis=2)
        return jnp.transpose(lax.optimization_barrier(part), (1, 2, 0, 3))

    def packed(first):
        part = rim_rows(groups[0], first).astype(jnp.bfloat16).reshape(members * HALO, steps, cols)
        value, terms = local[:, first : first + HALO].reshape(2 * HALO, cols), []
        for _ in range(3):
            terms.append(lax.optimization_barrier(value.astype(jnp.bfloat16)))
            value = value - terms[-1].astype(jnp.float32)
        extra = jnp.concatenate(terms, axis=0)
        extra = jnp.pad(extra, ((0, -6 * HALO % steps), (0, 0))).reshape(-1, steps, cols)
        return jnp.concatenate([part, extra], axis=0)

    def unpacked(value):
        part = value[: members * HALO].reshape(members, HALO, steps, cols)
        extra = value[members * HALO :].reshape(-1, cols)[: 6 * HALO].astype(jnp.float32)
        high, middle, low = extra.reshape(3, 2, HALO, cols)
        return part, high + (middle + low)

    (up_first, up), (down_first, down) = (
        unpacked(value) for value in rims(packed(0), packed(rows - HALO))
    )
    stiff, diag = jnp.concatenate([up, local, down], axis=1)
    inside = diag > 0.0
    inverse = jnp.where(inside, 1.0 / jnp.where(inside, diag, 1.0), 0.0)
    unscale = jnp.where(inside, 1.0 / jnp.where(inside, stiff, 1.0), 0.0)
    scaled = DAMPING * inverse * stiff
    coeff = jnp.stack([scaled, scaled * stiff, unscale, stiff, diag])
    coeff = jnp.broadcast_to(coeff[:, :, None, :], coeff.shape[:2] + (SUBLANES, cols))

    def per_lane(values):
        own = lax.dynamic_slice_in_dim(values, sensor_index * sensors, sensors)
        other = lax.dynamic_slice_in_dim(values, (sensor_index ^ 1) * sensors, sensors)
        return jnp.stack([jnp.tile(own, near), jnp.tile(other, near)])

    noise = per_lane(noise_weight)
    local_cells = per_lane(sensor_cell) - (cell_index * cells + core * half)
    local_cells = jnp.broadcast_to(local_cells.reshape(2 * LANES, 1), (2 * LANES, LANES))
    core = core.reshape(1)

    whole = members - members // APART
    lines = [[k for k in range(size) if k % 2 == parity] for parity in range(2)]
    shape = (chips, 2, members, rows // 2, steps, cols)

    def both_cores(low):
        keep, give = (
            lax.dynamic_slice_in_dim(low, first * (rows // 2), rows // 2, axis=1)
            for first in (core[0], 1 - core[0])
        )
        return jnp.stack([keep, swap_cores(give)])

    def ready(state):
        iterate, low, rest, top, bottom = state
        above, below = rims(top, bottom)
        pair = both_cores(low)
        parts = lax.optimization_barrier((pair[:, :whole], pair[:, whole:]))
        return iterate, *parts, (above, rest, below)

    def edges(misfit):
        first = (rows // 2 - HALO) * core[0]
        edge = lax.dynamic_slice_in_dim(misfit, first, HALO, axis=2)
        same, _ = misfit_rims(edge[:1])
        _, cross = misfit_rims(edge[1:])
        return misfit, swap_cores(misfit[1:]), same, cross

    iterate, low, rest, *ends = start(0, members, core, rhs, up_first, down_first, coeff)
    above, below = rims(*ends)
    states = [(iterate, low, None, (above, rest, below))]
    for group in range(1, GROUPS):
        ends = tuple(
            rim_rows(groups[group], first).astype(jnp.bfloat16) for first in (0, rows - HALO)
        )
        _, rests, ends = lax.optimization_barrier((low, states[0][3], ends))
        states[0] = (*states[0][:3], rests)
        states.append(ready(start(group, members, core, rhs, *rims(*ends), coeff)))
    line = None

    outputs = ()
    for iteration in range(ITERS):
        fields = [
            lax.all_gather(state[1], "sensors", axis_index_groups=None if state[2] is None else lines)
            for state in states
        ]
        if line is not None:
            line.hop(last=True)
        totals = []
        for group in range(GROUPS):
            iterate, _, _, rests = states[group]
            field = fields[group]
            slots, line = (line.slots() if line is not None else []), None
            if group > 0:
                field, rests = lax.optimization_barrier((field, rests))
            states[group] = iterate, rests
            if group + 1 < GROUPS:
                line = Line(states[group + 1][2])
                line.hop()
                field = line.after(field)
                line.hop()
            sums = observe(
                core,
                field,
                slots,
                forward_map,
                other_map,
                table if slots else in_order,
                around,
                local_cells,
            )
            if line is not None:
                sums = line.after(sums)
                line.hop(last=True)
            sums = from_all_cells(sums + swap_cores(sums)[::-1])
            misfit = pull_back(core, sums, noise, forward_map, other_map, back, local_cells, shape)
            if line is not None:
                misfit = line.after(misfit)
            totals.append(
                lax.psum_scatter(
                    misfit, "sensors", scatter_dimension=0, axis_index_groups=lines, tiled=False
                )
            )
        for group in range(GROUPS):
            iterate, rests = states[group]
            total = totals[group]
            if iteration < ITERS - 1:
                if group == 1:
                    before = states[0]
                    line = Line(before[2])
                    line.hop()
                    line.hop()
                    total, earlier = line.after((total, before[3]))
                    states[0] = (*before[:3], earlier)
                states[group] = ready(step(core, rests, edges(total), iterate, coeff))
            else:
                if outputs:
                    total, outputs = lax.optimization_barrier((total, outputs))
                outputs = finish(
                    group, samples, core, rests, edges(total), iterate, coeff, outputs
                )
    return tuple(out.reshape(rhs.shape) for out in outputs)


def solution(mesh):
    placed = (
        P("sensors", None, "cells", None),
        P(None, None, "sensors", "cells"),
        P("cells", None),
        P("cells", None),
        P(),
        P(),
    )
    return jax.shard_map(
        shards,
        mesh=mesh,
        in_specs=placed,
        out_specs=(P("sensors", None, "cells", None), P("sensors", None, "cells", None)),
        check_vma=False,
    )
```

```python
import math

import jax
import jax.numpy as jnp
from jax import lax
from jax.experimental import pallas as pl
from jax.experimental.pallas import tpu as pltpu
from jax.sharding import PartitionSpec as P

SWEEPS = 4
ITERS = 2
DAMPING = 0.8
HALO = SWEEPS
LANES = 128
APART = 3
SUBLANES = 8
GROUPS = 2
CHUNK_ROWS = 4
VMEM_BYTES = 40 * 2**20


def transform_table(freqs, moments):
    period = moments.size
    wave = jnp.arange(freqs, dtype=jnp.int32)[:, None]
    moment = moments.reshape(1, period)
    phase = (wave * moment % period).astype(jnp.float32) * (2.0 * math.pi / period)
    factor = 1.0 / math.sqrt(period)
    return jnp.concatenate([jnp.cos(phase) * factor, -jnp.sin(phase) * factor], axis=0).astype(
        jnp.bfloat16
    )


def whole_block(array):
    return pl.BlockSpec(array.shape, lambda *_: (0,) * array.ndim)


def in_hbm(*arrays):
    return [pltpu.with_memory_space_constraint(array, pltpu.HBM) for array in arrays]


def call(kernel, core, grid, in_specs, out_specs, out_shape, scratch=(), aliases=None, **kwargs):
    grid_spec = pltpu.PrefetchScalarGridSpec(
        num_scalar_prefetch=1,
        grid=grid,
        in_specs=in_specs,
        out_specs=out_specs,
        scratch_shapes=list(scratch),
    )
    return pl.pallas_call(
        kernel,
        grid_spec=grid_spec,
        out_shape=out_shape,
        input_output_aliases=aliases or {},
        compiler_params=pltpu.CompilerParams(vmem_limit_bytes=VMEM_BYTES),
        **kwargs,
    )


def dot(left, right):
    return jnp.dot(left, right, preferred_element_type=jnp.float32)


def dot_lanes(left, right):
    return lax.dot_general(left, right, (((1,), (1,)), ((), ())), preferred_element_type=jnp.float32)


def neighbours(field):
    inner = field[1:-1]
    lane = lax.broadcasted_iota(jnp.int32, inner.shape, 2)
    before = jnp.where(lane == 0, 0.0, pltpu.roll(inner, 1, 2))
    after = jnp.where(lane == LANES - 1, 0.0, pltpu.roll(inner, LANES - 1, 2))
    return (field[2:] + field[:-2]) + (before + after)


def trim(array, width):
    return array[width : array.shape[0] - width]


def precondition(residual, coeff_ref):
    extra = (coeff_ref.shape[1] - residual.shape[0]) // 2
    coeff = [trim(coeff_ref[k], extra) for k in range(3)]
    first = coeff[0] * residual
    scaled = first
    for sweep in range(1, SWEEPS):
        scaled = (
            (1.0 - DAMPING) * scaled[1:-1]
            + trim(first, sweep)
            + trim(coeff[1], sweep) * neighbours(scaled)
        )
    return trim(coeff[2], SWEEPS - 1) * scaled


def prior(field, coeff_ref):
    extra = (coeff_ref.shape[1] - field.shape[0]) // 2
    stiffness = trim(coeff_ref[3], extra)
    diagonal = trim(coeff_ref[4], extra + 1)
    return diagonal * field[1:-1] - stiffness[1:-1] * neighbours(stiffness * field)


def time_chunks(steps, body):
    def run(index, carry):
        body(pl.ds(pl.multiple_of(index * SUBLANES, SUBLANES), SUBLANES))
        return carry

    lax.fori_loop(0, steps // SUBLANES, run, 0)


def fields(members, rows, steps, cols):
    field = pl.BlockSpec((1, rows, steps, cols), lambda b, core: (b, 0, 0, 0))
    rim = pl.BlockSpec((1, HALO, steps, cols), lambda b, core: (b, 0, 0, 0))
    misfits = [
        pl.BlockSpec((None, 1, count, steps, cols), lambda b, core: (0, b, 0, 0, 0))
        for count in (rows // 2, rows // 2, HALO, HALO)
    ]

    def shape(count, dtype):
        return jax.ShapeDtypeStruct((members, count, steps, cols), dtype)

    specs = [field, field, field, rim, rim]
    shapes = [
        pltpu.HBM((members, rows, steps, cols), jnp.float32),
        pltpu.HBM((members, rows, steps, cols), jnp.bfloat16),
        pltpu.HBM((members, rows, steps, cols), jnp.float32),
        shape(HALO, jnp.bfloat16),
        shape(HALO, jnp.bfloat16),
    ]
    return field, rim, misfits, specs, shapes


def put_rest(rest, times, rest_ref, top_ref, bottom_ref):
    rest_ref[0, :, times] = rest
    top_ref[0, :, times] = rest[:HALO].astype(top_ref.dtype)
    bottom_ref[0, :, times] = rest[rest.shape[0] - HALO :].astype(bottom_ref.dtype)


def start_kernel(
    core_ref, rhs_ref, up_ref, down_ref, coeff_ref,
    iter_ref, low_ref, rest_ref, top_ref, bottom_ref,
):
    def body(times):
        here = jnp.swapaxes(rhs_ref[times], 0, 1)
        rims_here = [ref[0, :, times].astype(jnp.float32) for ref in (up_ref, down_ref)]
        update = precondition(jnp.concatenate([rims_here[0], here, rims_here[1]], axis=0), coeff_ref)
        iter_ref[0, :, times] = update[1:-1]
        put_rest(here - prior(update, coeff_ref), times, rest_ref, top_ref, bottom_ref)

    time_chunks(iter_ref.shape[2], body)
    low_ref[...] = iter_ref[...].astype(low_ref.dtype)


def start(group, members, core, rhs, up, down, coeff):
    steps, _, rows, cols = rhs.shape
    flat = rhs.reshape(steps, -1, cols)
    _, rim, _, specs, shapes = fields(members, rows, steps, cols)
    return call(
        start_kernel,
        core,
        (members,),
        [
            pl.BlockSpec((steps, rows, cols), lambda b, core: (0, b + group * members, 0)),
            rim,
            rim,
            whole_block(coeff),
        ],
        specs,
        shapes,
        name="start",
    )(core, *in_hbm(flat), up, down, coeff)


def residual_of(core, times, rest_refs, misfit_refs, whole_ref):
    own_ref, other_ref, same_ref, cross_ref = misfit_refs
    half = own_ref.shape[1]
    whole_ref[pl.ds(core * half, half)] = own_ref[0, :, times].astype(jnp.float32)
    whole_ref[pl.ds((1 - core) * half, half)] = other_ref[0, :, times].astype(jnp.float32)
    same = same_ref[0, :, times].astype(jnp.float32)
    cross = cross_ref[0, :, times].astype(jnp.float32)
    first = core == 0
    parts = [jnp.where(first, cross, same), whole_ref[...], jnp.where(first, same, cross)]
    rests = [ref[0, :, times].astype(jnp.float32) for ref in rest_refs]
    return jnp.concatenate([rest - part for rest, part in zip(rests, parts)], axis=0)


def held(rests, misfits, iterate):
    above, rest, below = rests
    own, other, same, cross = misfits
    rest, own, iterate = in_hbm(rest, own, iterate)
    return above, rest, below, own, other, same, cross, iterate


def step_kernel(
    core_ref, up_ref, rest_ref, down_ref, own_ref, other_ref, same_ref, cross_ref, iter_ref, coeff_ref,
    next_ref, low_ref, later_ref, top_ref, bottom_ref, whole_ref,
):
    def body(times):
        residual = residual_of(
            core_ref[0],
            times,
            (up_ref, rest_ref, down_ref),
            (own_ref, other_ref, same_ref, cross_ref),
            whole_ref,
        )
        update = precondition(residual, coeff_ref)
        next_ref[0, :, times] = iter_ref[0, :, times] + update[1:-1]
        put_rest(rest_ref[0, :, times] - prior(update, coeff_ref), times, later_ref, top_ref, bottom_ref)

    time_chunks(iter_ref.shape[2], body)
    low_ref[...] = next_ref[...].astype(low_ref.dtype)


def step(core, rests, misfits, iterate, coeff):
    members, rows, steps, cols = iterate.shape
    field, rim, parts, specs, shapes = fields(members, rows, steps, cols)
    return call(
        step_kernel,
        core,
        (members,),
        [rim, field, rim, *parts, field, whole_block(coeff)],
        specs,
        shapes,
        [pltpu.VMEM((rows, SUBLANES, cols), jnp.float32)],
        name="step",
    )(core, *held(rests, misfits, iterate), coeff)


def finish_kernel(
    core_ref, up_ref, rest_ref, down_ref, own_ref, other_ref, same_ref, cross_ref, iter_ref, coeff_ref,
    *refs,
):
    solution_ref, residual_ref, whole_ref = refs[-3:]

    def body(times):
        residual = residual_of(
            core_ref[0],
            times,
            (up_ref, rest_ref, down_ref),
            (own_ref, other_ref, same_ref, cross_ref),
            whole_ref,
        )
        update = precondition(residual, coeff_ref)
        solution_ref[times] = jnp.swapaxes(iter_ref[0, :, times] + update[1:-1], 0, 1)
        residual_ref[times] = jnp.swapaxes(trim(residual, HALO), 0, 1)

    time_chunks(iter_ref.shape[2], body)


def finish(group, samples, core, rests, misfits, iterate, coeff, previous):
    members, rows, steps, cols = iterate.shape
    field, rim, parts, _, _ = fields(members, rows, steps, cols)
    result = pl.BlockSpec((steps, rows, cols), lambda b, core: (0, b + group * members, 0))
    shape = jax.ShapeDtypeStruct((steps, samples * rows, cols), jnp.float32)
    in_specs = [rim, field, rim, *parts, field, whole_block(coeff)]
    first = 1 + len(in_specs)
    return call(
        finish_kernel,
        core,
        (members,),
        in_specs + [pl.BlockSpec(memory_space=pl.ANY)] * len(previous),
        [result, result],
        [shape, shape],
        [pltpu.VMEM((rows, SUBLANES, cols), jnp.float32)],
        {first + k: k for k in range(len(previous))},
        name="finish",
    )(core, *held(rests, misfits, iterate), coeff, *previous)


def same_frequency(near, sensors, lanes):
    shape = (near, lanes)
    return lax.broadcasted_iota(jnp.int32, shape, 0) == (
        lax.broadcasted_iota(jnp.int32, shape, 1) % LANES // sensors
    )


def marks_of(cell_ref, width):
    first = pl.program_id(0) * width
    parts = []
    for start_lane in range(0, width, LANES):
        lane = lax.broadcasted_iota(jnp.int32, cell_ref.shape, 1) + (first + start_lane)
        parts.append(jnp.where(cell_ref[...] == lane, 1.0, 0.0).astype(jnp.bfloat16))
    return jnp.concatenate(parts, axis=1)


def near_map(own_ref, other_ref, here):
    _, freqs, sensors, width = own_ref.shape
    parts = [
        ref[part, here].reshape(LANES, width) for part in range(2) for ref in (own_ref, other_ref)
    ]
    return jnp.concatenate(parts, axis=0)


def observe_kernel(core_ref, field_ref, *refs):
    *slot_refs, own_ref, other_ref, table_ref, around_ref, cell_ref = refs[:-4]
    out_ref, spec, acc, picked = refs[-4:]
    rows, steps, lanes = field_ref.shape[-3:]
    members = spec.shape[0] // 2
    chips = table_ref.shape[1] // (2 * steps)
    whole = field_ref.shape[-4]
    freqs, sensors, width = own_ref.shape[1:]
    near = lanes // sensors
    wide = 2 * lanes
    chunk = pl.program_id(0)

    @pl.when(chunk == 0)
    def _():
        acc[...] = jnp.zeros_like(acc)
        picked[...] = jnp.zeros_like(picked)

    marks = marks_of(cell_ref, width)

    def history(b, r):
        if b < whole:
            here = field_ref[..., b, r, :, :]
            return here.reshape(2 * chips * steps, lanes)
        slots = [slot_refs[0][:, b - whole, r]]
        for k in range(1, chips):
            slots.append(slot_refs[k][:, b - whole, r] + slot_refs[2 * chips - 1 - k][:, b - whole, r])
        return jnp.concatenate([slot.reshape(2 * steps, lanes) for slot in slots], axis=0)

    for b in range(members):
        table = table_ref[...] if b < whole else around_ref[...]
        spectrum = dot(table, jnp.concatenate([history(b, r) for r in range(rows)], axis=1))
        spec[2 * b] = spectrum[:freqs]
        spec[2 * b + 1] = spectrum[freqs:]
    for m in range(2 * members):
        picked[m] += dot_lanes(spec[m].astype(jnp.bfloat16), marks)
    for q in range(freqs // near):
        here = slice(q * near, (q + 1) * near)
        left = spec[:, here].reshape(2 * members * near, width).astype(jnp.bfloat16)
        acc[q] += dot_lanes(left, near_map(own_ref, other_ref, here))

    @pl.when(chunk == pl.num_programs(0) - 1)
    def _():
        mask = same_frequency(near, sensors, wide)
        for q in range(freqs // near):
            here = slice(q * near, (q + 1) * near)
            for b in range(members):
                real = acc[q, 2 * b * near : (2 * b + 1) * near]
                imag = acc[q, (2 * b + 1) * near : (2 * b + 2) * near]
                sums = (
                    real[:, :wide] - imag[:, wide:] + picked[2 * b, here],
                    imag[:, :wide] + real[:, wide:] + picked[2 * b + 1, here],
                )
                for part, value in enumerate(sums):
                    line = jnp.sum(jnp.where(mask, value, 0.0), 0, keepdims=True)
                    out_ref[0, part, b, q : q + 1] = line[:, :lanes]
                    out_ref[1, part, b, q : q + 1] = line[:, lanes:]


def map_specs(own, width):
    chunks = own.shape[3] // (2 * width)
    spec = pl.BlockSpec(own.shape[:3] + (width,), lambda c, core: (0, 0, 0, core[0] * chunks + c))
    return [spec, spec]


def map_cost(members, own, moved):
    return pl.CostEstimate(
        flops=8 * members * own.size, bytes_accessed=2 * own.size + 2 * moved, transcendentals=0
    )


def observe(core, field, slots, own, other, table, around, local_cells):
    *sources, whole, rows, steps, lanes = field.shape
    apart = slots[0].shape[1] if slots else 0
    members = whole + apart
    _, freqs, sensors, cells = own.shape
    width = CHUNK_ROWS * lanes
    near = lanes // sensors
    shape = (2, 2, members, freqs // near, lanes)
    chunks = cells // (2 * width)
    first = chunks if len(sources) == 1 else 0
    block = (*sources, whole, CHUNK_ROWS, steps, lanes)
    lead = (0,) * len(sources) + (0,)
    slot = pl.BlockSpec((2, apart, CHUNK_ROWS, steps, lanes), lambda c, core: (0, 0, c, 0, 0))
    return call(
        observe_kernel,
        core,
        (chunks,),
        [pl.BlockSpec(block, lambda c, core: (*lead, core[0] * first + c, 0, 0))]
        + [slot] * len(slots)
        + map_specs(own, width)
        + [whole_block(table), whole_block(around), whole_block(local_cells)],
        pl.BlockSpec(shape, lambda c, core: (0, 0, 0, 0, 0)),
        jax.ShapeDtypeStruct(shape, jnp.float32),
        [
            pltpu.VMEM((2 * members, freqs, width), jnp.float32),
            pltpu.VMEM((freqs // near, 2 * members * near, 4 * lanes), jnp.float32),
            pltpu.VMEM((2 * members, freqs, 2 * lanes), jnp.float32),
        ],
        cost_estimate=map_cost(members, own, field.size),
        name="observe",
    )(core, *in_hbm(field), *slots, *in_hbm(own, other), table, around, local_cells)


def pull_kernel(core_ref, *refs):
    *sums, noise_ref, own_ref, other_ref, back_ref, cell_ref = refs[:-3]
    out_ref, weights, adjoint = refs[-3:]
    devices, _, members, rows, steps, lanes = out_ref.shape
    freqs, sensors, width = own_ref.shape[1:]
    near = lanes // sensors
    wide = 2 * lanes

    def total(part, b, which):
        values = [ref[which, part, b] for ref in sums]
        while len(values) > 1:
            values = [values[k] + values[k + 1] for k in range(0, len(values), 2)]
        noise = noise_ref[which : which + 1]
        return (noise * values[0]).astype(jnp.bfloat16).astype(jnp.float32)

    @pl.when(pl.program_id(0) == 0)
    def _():
        mask = same_frequency(near, sensors, wide)
        for b in range(members):
            real, imag = (
                jnp.concatenate([total(part, b, 0), total(part, b, 1)], axis=1) for part in range(2)
            )
            for q in range(freqs // near):
                here = slice(q * near, (q + 1) * near)
                w_real = jnp.where(mask, real[q : q + 1], 0.0)
                w_imag = jnp.where(mask, imag[q : q + 1], 0.0)
                weights[2 * b, here, :wide] = w_real
                weights[2 * b, here, wide:] = w_imag
                weights[2 * b + 1, here, :wide] = w_imag
                weights[2 * b + 1, here, wide:] = -w_real

    marks = marks_of(cell_ref, width)
    for m in range(2 * members):
        adjoint[m] = dot(weights[m, :, :wide].astype(jnp.bfloat16), marks)
    for q in range(freqs // near):
        here = slice(q * near, (q + 1) * near)
        left = weights[:, here].reshape(2 * members * near, 2 * wide).astype(jnp.bfloat16)
        part = dot(left, near_map(own_ref, other_ref, here))
        adjoint[:, here] += part.reshape(2 * members, near, width)
    for b in range(members):
        whole = adjoint[2 * b : 2 * b + 2].reshape(2 * freqs, width)
        high = whole.astype(jnp.bfloat16)
        low = (whole - high.astype(jnp.float32)).astype(jnp.bfloat16)
        misfit = (dot(back_ref[...], high) + dot(back_ref[...], low)).astype(out_ref.dtype)
        for r in range(rows):
            part = misfit[:, r * lanes : (r + 1) * lanes]
            out_ref[:, :, b, r] = part.reshape(devices, 2, steps, lanes)


def pull_back(core, sums, noise, own, other, back, local_cells, shape):
    devices, _, members, rows, steps, lanes = shape
    _, freqs, sensors, cells = own.shape
    width = CHUNK_ROWS * lanes
    small = [*sums, noise]
    return call(
        pull_kernel,
        core,
        (rows // CHUNK_ROWS,),
        [whole_block(array) for array in small]
        + map_specs(own, width)
        + [whole_block(back), whole_block(local_cells)],
        pl.BlockSpec(
            (devices, 2, members, CHUNK_ROWS, steps, lanes), lambda c, core: (0, 0, 0, c, 0, 0)
        ),
        pltpu.HBM(shape, jnp.bfloat16),
        [
            pltpu.VMEM((2 * members, freqs, 4 * lanes), jnp.float32),
            pltpu.VMEM((2 * members, freqs, width), jnp.float32),
        ],
        cost_estimate=map_cost(members, own, math.prod(shape)),
        name="pull_back",
    )(core, *small, *in_hbm(own, other), back, local_cells)


def rims(top, bottom):
    size = lax.axis_size("cells")
    onward = [(k, k + 1) for k in range(size - 1)]
    backward = [(k + 1, k) for k in range(size - 1)]
    return lax.ppermute(bottom, "cells", onward), lax.ppermute(top, "cells", backward)


def misfit_rims(edge):
    size, width = lax.axis_size("cells"), lax.axis_size("sensors")
    same, cross = [], []
    for cell in range(size):
        for sensor in range(width):
            there = cell + 2 * (sensor % 2) - 1
            if 0 <= there < size:
                same.append((cell * width + sensor, there * width + sensor))
                cross.append((cell * width + sensor, there * width + (sensor ^ 1)))
    both = ("cells", "sensors")
    return lax.ppermute(edge, both, same), lax.ppermute(edge, both, cross)


def swap_cores(value):
    size = lax.axis_size("sensors")
    return lax.ppermute(value, "sensors", [(k, k ^ 1) for k in range(size)])


def from_all_cells(value):
    size = lax.axis_size("cells")
    if size & (size - 1):
        return [lax.psum(value, "cells")]
    return [value] + [
        lax.ppermute(value, "cells", [(k, k ^ other) for k in range(size)])
        for other in range(1, size)
    ]


class Line:
    def __init__(self, value):
        self.size = lax.axis_size("sensors")
        self.value, self.ups, self.downs = value, [], []
        self.ends = (value, value)

    def hop(self, last=False):
        while len(self.ups) < self.size // 2 - 1:
            start = 2 * len(self.ups)
            onward = [(k, k + 2) for k in range(start, self.size - 2)]
            backward = [(self.size - 1 - k, self.size - 1 - there) for k, there in onward]
            up = lax.ppermute(self.ends[0], "sensors", onward)
            down = lax.ppermute(self.ends[1], "sensors", backward)
            self.ups.append(up)
            self.downs.append(down)
            self.ends = (up, down)
            if not last:
                break

    def after(self, other):
        if other is not None and self.ups:
            self.ends, other = lax.optimization_barrier((self.ends, other))
            self.ups[-1], self.downs[-1] = self.ends
        return other

    def slots(self):
        return [self.value, *self.ups, *self.downs]


def shards(rhs, forward_map, stiffness, reaction, noise_weight, sensor_cell):
    steps, samples, rows, cols = rhs.shape
    _, freqs, sensors, cells = forward_map.shape
    size = lax.axis_size("sensors")
    chips = size // 2
    cell_index = lax.axis_index("cells")
    sensor_index = lax.axis_index("sensors")
    core = sensor_index % 2
    near = LANES // sensors
    half = cells // 2
    other_map = swap_cores(forward_map)

    cores = jnp.stack([core, 1 - core])
    offsets = cores[None, :, None] * steps + jnp.arange(steps, dtype=jnp.int32)
    chip_steps = 2 * steps
    places = jnp.arange(chips, dtype=jnp.int32)[:, None, None] * chip_steps
    table = transform_table(freqs, places + offsets)
    back = table.T
    in_order = transform_table(freqs, jnp.arange(2 * freqs, dtype=jnp.int32))
    chip = sensor_index // 2
    places = (chip - jnp.arange(chips, dtype=jnp.int32)) % chips
    around = transform_table(freqs, places[:, None, None] * chip_steps + offsets)

    diagonal = reaction + 4.0 * stiffness * stiffness
    local = jnp.stack([stiffness, diagonal])
    members = samples // GROUPS
    groups = [slice(group * members, (group + 1) * members) for group in range(GROUPS)]

    def rim_rows(here, first):
        part = lax.slice_in_dim(rhs[:, here], first, first + HALO, axis=2)
        return jnp.transpose(lax.optimization_barrier(part), (1, 2, 0, 3))

    def packed(first):
        part = rim_rows(groups[0], first).astype(jnp.bfloat16).reshape(members * HALO, steps, cols)
        value, terms = local[:, first : first + HALO].reshape(2 * HALO, cols), []
        for _ in range(3):
            terms.append(lax.optimization_barrier(value.astype(jnp.bfloat16)))
            value = value - terms[-1].astype(jnp.float32)
        extra = jnp.concatenate(terms, axis=0)
        extra = jnp.pad(extra, ((0, -6 * HALO % steps), (0, 0))).reshape(-1, steps, cols)
        return jnp.concatenate([part, extra], axis=0)

    def unpacked(value):
        part = value[: members * HALO].reshape(members, HALO, steps, cols)
        extra = value[members * HALO :].reshape(-1, cols)[: 6 * HALO].astype(jnp.float32)
        high, middle, low = extra.reshape(3, 2, HALO, cols)
        return part, high + (middle + low)

    (up_first, up), (down_first, down) = (
        unpacked(value) for value in rims(packed(0), packed(rows - HALO))
    )
    stiff, diag = jnp.concatenate([up, local, down], axis=1)
    inside = diag > 0.0
    inverse = jnp.where(inside, 1.0 / jnp.where(inside, diag, 1.0), 0.0)
    unscale = jnp.where(inside, 1.0 / jnp.where(inside, stiff, 1.0), 0.0)
    scaled = DAMPING * inverse * stiff
    coeff = jnp.stack([scaled, scaled * stiff, unscale, stiff, diag])
    coeff = jnp.broadcast_to(coeff[:, :, None, :], coeff.shape[:2] + (SUBLANES, cols))

    def per_lane(values):
        own = lax.dynamic_slice_in_dim(values, sensor_index * sensors, sensors)
        other = lax.dynamic_slice_in_dim(values, (sensor_index ^ 1) * sensors, sensors)
        return jnp.stack([jnp.tile(own, near), jnp.tile(other, near)])

    noise = per_lane(noise_weight)
    local_cells = per_lane(sensor_cell) - (cell_index * cells + core * half)
    local_cells = jnp.broadcast_to(local_cells.reshape(2 * LANES, 1), (2 * LANES, LANES))
    core = core.reshape(1)

    whole = members - members // APART
    lines = [[k for k in range(size) if k % 2 == parity] for parity in range(2)]
    shape = (chips, 2, members, rows // 2, steps, cols)

    def both_cores(low):
        keep, give = (
            lax.dynamic_slice_in_dim(low, first * (rows // 2), rows // 2, axis=1)
            for first in (core[0], 1 - core[0])
        )
        return jnp.stack([keep, swap_cores(give)])

    def ready(state):
        iterate, low, rest, top, bottom = state
        above, below = rims(top, bottom)
        pair = both_cores(low)
        parts = lax.optimization_barrier((pair[:, :whole], pair[:, whole:]))
        return iterate, *parts, (above, rest, below)

    def edges(misfit):
        first = (rows // 2 - HALO) * core[0]
        edge = lax.dynamic_slice_in_dim(misfit, first, HALO, axis=2)
        same, _ = misfit_rims(edge[:1])
        _, cross = misfit_rims(edge[1:])
        return misfit, swap_cores(misfit[1:]), same, cross

    iterate, low, rest, *ends = start(0, members, core, rhs, up_first, down_first, coeff)
    above, below = rims(*ends)
    states = [(iterate, low, None, (above, rest, below))]
    for group in range(1, GROUPS):
        ends = tuple(
            rim_rows(groups[group], first).astype(jnp.bfloat16) for first in (0, rows - HALO)
        )
        _, rests, ends = lax.optimization_barrier((low, states[0][3], ends))
        states[0] = (*states[0][:3], rests)
        states.append(ready(start(group, members, core, rhs, *rims(*ends), coeff)))
    line = None

    outputs = ()
    for iteration in range(ITERS):
        fields = [
            lax.all_gather(state[1], "sensors", axis_index_groups=None if state[2] is None else lines)
            for state in states
        ]
        if line is not None:
            line.hop(last=True)
        totals = []
        for group in range(GROUPS):
            iterate, _, _, rests = states[group]
            field = fields[group]
            slots, line = (line.slots() if line is not None else []), None
            if group > 0:
                field, rests = lax.optimization_barrier((field, rests))
            states[group] = iterate, rests
            if group + 1 < GROUPS:
                line = Line(states[group + 1][2])
                line.hop()
                field = line.after(field)
                line.hop()
            sums = observe(
                core,
                field,
                slots,
                forward_map,
                other_map,
                table if slots else in_order,
                around,
                local_cells,
            )
            if line is not None:
                sums = line.after(sums)
                line.hop(last=True)
            sums = from_all_cells(sums + swap_cores(sums)[::-1])
            misfit = pull_back(core, sums, noise, forward_map, other_map, back, local_cells, shape)
            if line is not None:
                misfit = line.after(misfit)
            totals.append(
                lax.psum_scatter(
                    misfit, "sensors", scatter_dimension=0, axis_index_groups=lines, tiled=False
                )
            )
        for group in range(GROUPS):
            iterate, rests = states[group]
            total = totals[group]
            if iteration < ITERS - 1:
                if group == 1:
                    before = states[0]
                    line = Line(before[2])
                    line.hop()
                    line.hop()
                    total, earlier = line.after((total, before[3]))
                    states[0] = (*before[:3], earlier)
                states[group] = ready(step(core, rests, edges(total), iterate, coeff))
            else:
                if outputs:
                    total, outputs = lax.optimization_barrier((total, outputs))
                outputs = finish(
                    group, samples, core, rests, edges(total), iterate, coeff, outputs
                )
    return tuple(out.reshape(rhs.shape) for out in outputs)


def solution(mesh):
    placed = (
        P("sensors", None, "cells", None),
        P(None, None, "sensors", "cells"),
        P("cells", None),
        P("cells", None),
        P(),
        P(),
    )
    return jax.shard_map(
        shards,
        mesh=mesh,
        in_specs=placed,
        out_specs=(P("sensors", None, "cells", None), P("sensors", None, "cells", None)),
        check_vma=False,
    )
```

```python
import math

import jax
import jax.numpy as jnp
from jax import lax
from jax.experimental import pallas as pl
from jax.experimental.pallas import tpu as pltpu
from jax.sharding import PartitionSpec as P

SWEEPS = 4
ITERS = 2
DAMPING = 0.8
HALO = SWEEPS
LANES = 128
APART = 3
SUBLANES = 8
GROUPS = 2
CHUNK_ROWS = 4
VMEM_BYTES = 40 * 2**20


def transform_table(freqs, moments):
    period = moments.size
    wave = jnp.arange(freqs, dtype=jnp.int32)[:, None]
    moment = moments.reshape(1, period)
    phase = (wave * moment % period).astype(jnp.float32) * (2.0 * math.pi / period)
    factor = 1.0 / math.sqrt(period)
    return jnp.concatenate([jnp.cos(phase) * factor, -jnp.sin(phase) * factor], axis=0).astype(
        jnp.bfloat16
    )


def whole_block(array):
    return pl.BlockSpec(array.shape, lambda *_: (0,) * array.ndim)


def in_hbm(*arrays):
    return [pltpu.with_memory_space_constraint(array, pltpu.HBM) for array in arrays]


def call(kernel, core, grid, in_specs, out_specs, out_shape, scratch=(), aliases=None, **kwargs):
    grid_spec = pltpu.PrefetchScalarGridSpec(
        num_scalar_prefetch=1,
        grid=grid,
        in_specs=in_specs,
        out_specs=out_specs,
        scratch_shapes=list(scratch),
    )
    return pl.pallas_call(
        kernel,
        grid_spec=grid_spec,
        out_shape=out_shape,
        input_output_aliases=aliases or {},
        compiler_params=pltpu.CompilerParams(vmem_limit_bytes=VMEM_BYTES),
        **kwargs,
    )


def dot(left, right):
    return jnp.dot(left, right, preferred_element_type=jnp.float32)


def dot_lanes(left, right):
    return lax.dot_general(left, right, (((1,), (1,)), ((), ())), preferred_element_type=jnp.float32)


def neighbours(field):
    inner = field[1:-1]
    lane = lax.broadcasted_iota(jnp.int32, inner.shape, 2)
    before = jnp.where(lane == 0, 0.0, pltpu.roll(inner, 1, 2))
    after = jnp.where(lane == LANES - 1, 0.0, pltpu.roll(inner, LANES - 1, 2))
    return (field[2:] + field[:-2]) + (before + after)


def trim(array, width):
    return array[width : array.shape[0] - width]


def precondition(residual, coeff_ref):
    extra = (coeff_ref.shape[1] - residual.shape[0]) // 2
    coeff = [trim(coeff_ref[k], extra) for k in range(3)]
    first = coeff[0] * residual
    scaled = first
    for sweep in range(1, SWEEPS):
        scaled = (
            (1.0 - DAMPING) * scaled[1:-1]
            + trim(first, sweep)
            + trim(coeff[1], sweep) * neighbours(scaled)
        )
    return trim(coeff[2], SWEEPS - 1) * scaled


def prior(field, coeff_ref):
    extra = (coeff_ref.shape[1] - field.shape[0]) // 2
    stiffness = trim(coeff_ref[3], extra)
    diagonal = trim(coeff_ref[4], extra + 1)
    return diagonal * field[1:-1] - stiffness[1:-1] * neighbours(stiffness * field)


def time_chunks(steps, body):
    def run(index, carry):
        body(pl.ds(pl.multiple_of(index * SUBLANES, SUBLANES), SUBLANES))
        return carry

    lax.fori_loop(0, steps // SUBLANES, run, 0)


def fields(members, rows, steps, cols):
    field = pl.BlockSpec((1, rows, steps, cols), lambda b, core: (b, 0, 0, 0))
    rim = pl.BlockSpec((1, HALO, steps, cols), lambda b, core: (b, 0, 0, 0))
    misfits = [
        pl.BlockSpec((None, 1, count, steps, cols), lambda b, core: (0, b, 0, 0, 0))
        for count in (rows // 2, rows // 2, HALO, HALO)
    ]

    def shape(count, dtype):
        return jax.ShapeDtypeStruct((members, count, steps, cols), dtype)

    specs = [field, field, field, rim, rim]
    shapes = [
        pltpu.HBM((members, rows, steps, cols), jnp.float32),
        pltpu.HBM((members, rows, steps, cols), jnp.bfloat16),
        pltpu.HBM((members, rows, steps, cols), jnp.float32),
        shape(HALO, jnp.bfloat16),
        shape(HALO, jnp.bfloat16),
    ]
    return field, rim, misfits, specs, shapes


def put_rest(rest, times, rest_ref, top_ref, bottom_ref):
    rest_ref[0, :, times] = rest
    top_ref[0, :, times] = rest[:HALO].astype(top_ref.dtype)
    bottom_ref[0, :, times] = rest[rest.shape[0] - HALO :].astype(bottom_ref.dtype)


def start_kernel(
    core_ref, rhs_ref, up_ref, down_ref, coeff_ref,
    iter_ref, low_ref, rest_ref, top_ref, bottom_ref,
):
    def body(times):
        here = jnp.swapaxes(rhs_ref[times], 0, 1)
        rims_here = [ref[0, :, times].astype(jnp.float32) for ref in (up_ref, down_ref)]
        update = precondition(jnp.concatenate([rims_here[0], here, rims_here[1]], axis=0), coeff_ref)
        iter_ref[0, :, times] = update[1:-1]
        put_rest(here - prior(update, coeff_ref), times, rest_ref, top_ref, bottom_ref)

    time_chunks(iter_ref.shape[2], body)
    low_ref[...] = iter_ref[...].astype(low_ref.dtype)


def start(group, members, core, rhs, up, down, coeff):
    steps, _, rows, cols = rhs.shape
    flat = rhs.reshape(steps, -1, cols)
    _, rim, _, specs, shapes = fields(members, rows, steps, cols)
    return call(
        start_kernel,
        core,
        (members,),
        [
            pl.BlockSpec((steps, rows, cols), lambda b, core: (0, b + group * members, 0)),
            rim,
            rim,
            whole_block(coeff),
        ],
        specs,
        shapes,
        name="start",
    )(core, *in_hbm(flat), up, down, coeff)


def residual_of(core, times, rest_refs, misfit_refs, whole_ref):
    own_ref, other_ref, same_ref, cross_ref = misfit_refs
    half = own_ref.shape[1]
    whole_ref[pl.ds(core * half, half)] = own_ref[0, :, times].astype(jnp.float32)
    whole_ref[pl.ds((1 - core) * half, half)] = other_ref[0, :, times].astype(jnp.float32)
    same = same_ref[0, :, times].astype(jnp.float32)
    cross = cross_ref[0, :, times].astype(jnp.float32)
    first = core == 0
    parts = [jnp.where(first, cross, same), whole_ref[...], jnp.where(first, same, cross)]
    rests = [ref[0, :, times].astype(jnp.float32) for ref in rest_refs]
    return jnp.concatenate([rest - part for rest, part in zip(rests, parts)], axis=0)


def inner_kernel(core_ref, rhs_ref, coeff_ref, low_ref, wide_ref):
    def body(times):
        update = precondition(jnp.swapaxes(rhs_ref[times], 0, 1), coeff_ref)
        wide_ref[:, times] = update[1:-1]

    time_chunks(wide_ref.shape[1], body)
    low_ref[0] = wide_ref[...].astype(low_ref.dtype)


def inner(group, members, core, rhs, coeff):
    steps, _, rows, cols = rhs.shape
    flat = rhs.reshape(steps, -1, cols)
    inside = rows - 2 * HALO
    return call(
        inner_kernel,
        core,
        (members,),
        [
            pl.BlockSpec((steps, rows, cols), lambda b, core: (0, b + group * members, 0)),
            whole_block(coeff),
        ],
        pl.BlockSpec((1, inside, steps, cols), lambda b, core: (b, 0, 0, 0)),
        pltpu.HBM((members, inside, steps, cols), jnp.bfloat16),
        [pltpu.VMEM((inside, steps, cols), jnp.float32)],
        name="inner",
    )(core, *in_hbm(flat), coeff)


def held(rests, misfits, iterate):
    above, rest, below = rests
    own, other, same, cross = misfits
    rest, own, iterate = in_hbm(rest, own, iterate)
    return above, rest, below, own, other, same, cross, iterate


def step_kernel(
    core_ref, up_ref, rest_ref, down_ref, own_ref, other_ref, same_ref, cross_ref, iter_ref, coeff_ref,
    next_ref, low_ref, later_ref, top_ref, bottom_ref, whole_ref,
):
    def body(times):
        residual = residual_of(
            core_ref[0],
            times,
            (up_ref, rest_ref, down_ref),
            (own_ref, other_ref, same_ref, cross_ref),
            whole_ref,
        )
        update = precondition(residual, coeff_ref)
        next_ref[0, :, times] = iter_ref[0, :, times] + update[1:-1]
        put_rest(rest_ref[0, :, times] - prior(update, coeff_ref), times, later_ref, top_ref, bottom_ref)

    time_chunks(iter_ref.shape[2], body)
    low_ref[...] = next_ref[...].astype(low_ref.dtype)


def step(core, rests, misfits, iterate, coeff):
    members, rows, steps, cols = iterate.shape
    field, rim, parts, specs, shapes = fields(members, rows, steps, cols)
    return call(
        step_kernel,
        core,
        (members,),
        [rim, field, rim, *parts, field, whole_block(coeff)],
        specs,
        shapes,
        [pltpu.VMEM((rows, SUBLANES, cols), jnp.float32)],
        name="step",
    )(core, *held(rests, misfits, iterate), coeff)


def finish_kernel(
    core_ref, up_ref, rest_ref, down_ref, own_ref, other_ref, same_ref, cross_ref, iter_ref, coeff_ref,
    *refs,
):
    solution_ref, residual_ref, whole_ref = refs[-3:]

    def body(times):
        residual = residual_of(
            core_ref[0],
            times,
            (up_ref, rest_ref, down_ref),
            (own_ref, other_ref, same_ref, cross_ref),
            whole_ref,
        )
        update = precondition(residual, coeff_ref)
        solution_ref[times] = jnp.swapaxes(iter_ref[0, :, times] + update[1:-1], 0, 1)
        residual_ref[times] = jnp.swapaxes(trim(residual, HALO), 0, 1)

    time_chunks(iter_ref.shape[2], body)


def finish(group, samples, core, rests, misfits, iterate, coeff, previous):
    members, rows, steps, cols = iterate.shape
    field, rim, parts, _, _ = fields(members, rows, steps, cols)
    result = pl.BlockSpec((steps, rows, cols), lambda b, core: (0, b + group * members, 0))
    shape = jax.ShapeDtypeStruct((steps, samples * rows, cols), jnp.float32)
    in_specs = [rim, field, rim, *parts, field, whole_block(coeff)]
    first = 1 + len(in_specs)
    return call(
        finish_kernel,
        core,
        (members,),
        in_specs + [pl.BlockSpec(memory_space=pl.ANY)] * len(previous),
        [result, result],
        [shape, shape],
        [pltpu.VMEM((rows, SUBLANES, cols), jnp.float32)],
        {first + k: k for k in range(len(previous))},
        name="finish",
    )(core, *held(rests, misfits, iterate), coeff, *previous)


def same_frequency(near, sensors, lanes):
    shape = (near, lanes)
    return lax.broadcasted_iota(jnp.int32, shape, 0) == (
        lax.broadcasted_iota(jnp.int32, shape, 1) % LANES // sensors
    )


def marks_of(cell_ref, width, chunk):
    first = chunk * width
    parts = []
    for start_lane in range(0, width, LANES):
        lane = lax.broadcasted_iota(jnp.int32, cell_ref.shape, 1) + (first + start_lane)
        parts.append(jnp.where(cell_ref[...] == lane, 1.0, 0.0).astype(jnp.bfloat16))
    return jnp.concatenate(parts, axis=1)


def near_map(own_ref, other_ref, here):
    _, freqs, sensors, width = own_ref.shape
    parts = [
        ref[part, here].reshape(LANES, width) for part in range(2) for ref in (own_ref, other_ref)
    ]
    return jnp.concatenate(parts, axis=0)


def place_of(chunk, core_ref, split):
    chunks = pl.num_programs(0)
    return jnp.where(core_ref[0] == 1, chunk, (chunk + 1) % chunks) if split else chunk


def observe_kernel(core_ref, field_ref, *refs):
    *slot_refs, own_ref, other_ref, table_ref, around_ref, cell_ref = refs[:-4]
    out_ref, spec, acc, picked = refs[-4:]
    rows, steps, lanes = field_ref.shape[-3:]
    members = spec.shape[0] // 2
    chips = table_ref.shape[1] // (2 * steps)
    whole = field_ref.shape[-4]
    freqs, sensors, width = own_ref.shape[1:]
    near = lanes // sensors
    wide = 2 * lanes
    chunk = pl.program_id(0)

    @pl.when(chunk == 0)
    def _():
        acc[...] = jnp.zeros_like(acc)
        picked[...] = jnp.zeros_like(picked)

    split = len(slot_refs) > 0 and len(field_ref.shape) == 5
    marks = marks_of(cell_ref, width, place_of(chunk, core_ref, split))

    def gathered(b, r):
        return field_ref[..., b, r, :, :].reshape(2 * chips * steps, lanes)

    def along(b, r):
        slots = [slot_refs[0][:, b, r]]
        for k in range(1, chips):
            slots.append(slot_refs[k][:, b, r] + slot_refs[2 * chips - 1 - k][:, b, r])
        return jnp.concatenate([slot.reshape(2 * steps, lanes) for slot in slots], axis=0)

    def transform(b, table, history, first):
        times = jnp.concatenate([history(b - first, r) for r in range(rows)], axis=1)
        spectrum = dot(table[...], times)
        spec[2 * b] = spectrum[:freqs]
        spec[2 * b + 1] = spectrum[freqs:]

    if split:

        @pl.when(chunk < pl.num_programs(0) - 1)
        def _():
            for b in range(members):
                transform(b, table_ref, gathered, 0)

        @pl.when(chunk == pl.num_programs(0) - 1)
        def _():
            for b in range(members):
                transform(b, around_ref, along, 0)

    else:
        for b in range(members):
            if b < whole:
                transform(b, table_ref, gathered, 0)
            else:
                transform(b, around_ref, along, whole)
    for m in range(2 * members):
        picked[m] += dot_lanes(spec[m].astype(jnp.bfloat16), marks)
    for q in range(freqs // near):
        here = slice(q * near, (q + 1) * near)
        left = spec[:, here].reshape(2 * members * near, width).astype(jnp.bfloat16)
        acc[q] += dot_lanes(left, near_map(own_ref, other_ref, here))

    @pl.when(chunk == pl.num_programs(0) - 1)
    def _():
        mask = same_frequency(near, sensors, wide)
        for q in range(freqs // near):
            here = slice(q * near, (q + 1) * near)
            for b in range(members):
                real = acc[q, 2 * b * near : (2 * b + 1) * near]
                imag = acc[q, (2 * b + 1) * near : (2 * b + 2) * near]
                sums = (
                    real[:, :wide] - imag[:, wide:] + picked[2 * b, here],
                    imag[:, :wide] + real[:, wide:] + picked[2 * b + 1, here],
                )
                for part, value in enumerate(sums):
                    line = jnp.sum(jnp.where(mask, value, 0.0), 0, keepdims=True)
                    out_ref[0, part, b, q : q + 1] = line[:, :lanes]
                    out_ref[1, part, b, q : q + 1] = line[:, lanes:]


def map_specs(own, width):
    chunks = own.shape[3] // (2 * width)
    spec = pl.BlockSpec(own.shape[:3] + (width,), lambda c, core: (0, 0, 0, core[0] * chunks + c))
    return [spec, spec]


def map_cost(members, own, moved):
    return pl.CostEstimate(
        flops=8 * members * own.size, bytes_accessed=2 * own.size + 2 * moved, transcendentals=0
    )


def observe(core, field, slots, own, other, table, around, local_cells):
    *sources, whole, rows, steps, lanes = field.shape
    split = len(sources) == 1
    apart = slots[0].shape[1]
    members = whole if split else whole + apart
    _, freqs, sensors, cells = own.shape
    width = CHUNK_ROWS * lanes
    near = lanes // sensors
    shape = (2, 2, members, freqs // near, lanes)
    chunks = cells // (2 * width)
    block = (*sources, whole, CHUNK_ROWS, steps, lanes)
    lead = (0,) * len(sources) + (0,)

    def field_place(c, core):
        return (*lead, core[0] * (chunks - 1) + jnp.minimum(c, chunks - 2) if split else c, 0, 0)

    def map_place(c, core):
        here = jnp.where(core[0] == 1, c, (c + 1) % chunks) if split else c
        return (0, 0, 0, core[0] * chunks + here)

    slot = pl.BlockSpec(
        (2, apart, CHUNK_ROWS, steps, lanes), lambda c, core: (0, 0, 0 if split else c, 0, 0)
    )
    map_block = pl.BlockSpec(own.shape[:3] + (width,), map_place)
    return call(
        observe_kernel,
        core,
        (chunks,),
        [pl.BlockSpec(block, field_place)]
        + [slot] * len(slots)
        + [map_block] * 2
        + [whole_block(table), whole_block(around), whole_block(local_cells)],
        pl.BlockSpec(shape, lambda c, core: (0, 0, 0, 0, 0)),
        jax.ShapeDtypeStruct(shape, jnp.float32),
        [
            pltpu.VMEM((2 * members, freqs, width), jnp.float32),
            pltpu.VMEM((freqs // near, 2 * members * near, 4 * lanes), jnp.float32),
            pltpu.VMEM((2 * members, freqs, 2 * lanes), jnp.float32),
        ],
        cost_estimate=map_cost(members, own, field.size),
        name="observe",
    )(core, *in_hbm(field), *slots, *in_hbm(own, other), table, around, local_cells)


def pull_kernel(core_ref, *refs):
    *sums, noise_ref, own_ref, other_ref, back_ref, cell_ref = refs[:-3]
    out_ref, weights, adjoint = refs[-3:]
    devices, _, members, rows, steps, lanes = out_ref.shape
    freqs, sensors, width = own_ref.shape[1:]
    near = lanes // sensors
    wide = 2 * lanes

    def total(part, b, which):
        values = [ref[which, part, b] for ref in sums]
        while len(values) > 1:
            values = [values[k] + values[k + 1] for k in range(0, len(values), 2)]
        noise = noise_ref[which : which + 1]
        return (noise * values[0]).astype(jnp.bfloat16).astype(jnp.float32)

    @pl.when(pl.program_id(0) == 0)
    def _():
        mask = same_frequency(near, sensors, wide)
        for b in range(members):
            real, imag = (
                jnp.concatenate([total(part, b, 0), total(part, b, 1)], axis=1) for part in range(2)
            )
            for q in range(freqs // near):
                here = slice(q * near, (q + 1) * near)
                w_real = jnp.where(mask, real[q : q + 1], 0.0)
                w_imag = jnp.where(mask, imag[q : q + 1], 0.0)
                weights[2 * b, here, :wide] = w_real
                weights[2 * b, here, wide:] = w_imag
                weights[2 * b + 1, here, :wide] = w_imag
                weights[2 * b + 1, here, wide:] = -w_real

    marks = marks_of(cell_ref, width, pl.program_id(0))
    for m in range(2 * members):
        adjoint[m] = dot(weights[m, :, :wide].astype(jnp.bfloat16), marks)
    for q in range(freqs // near):
        here = slice(q * near, (q + 1) * near)
        left = weights[:, here].reshape(2 * members * near, 2 * wide).astype(jnp.bfloat16)
        part = dot(left, near_map(own_ref, other_ref, here))
        adjoint[:, here] += part.reshape(2 * members, near, width)
    for b in range(members):
        whole = adjoint[2 * b : 2 * b + 2].reshape(2 * freqs, width)
        high = whole.astype(jnp.bfloat16)
        low = (whole - high.astype(jnp.float32)).astype(jnp.bfloat16)
        misfit = (dot(back_ref[...], high) + dot(back_ref[...], low)).astype(out_ref.dtype)
        for r in range(rows):
            part = misfit[:, r * lanes : (r + 1) * lanes]
            out_ref[:, :, b, r] = part.reshape(devices, 2, steps, lanes)


def pull_back(core, sums, noise, own, other, back, local_cells, shape):
    devices, _, members, rows, steps, lanes = shape
    _, freqs, sensors, cells = own.shape
    width = CHUNK_ROWS * lanes
    small = [*sums, noise]
    return call(
        pull_kernel,
        core,
        (rows // CHUNK_ROWS,),
        [whole_block(array) for array in small]
        + map_specs(own, width)
        + [whole_block(back), whole_block(local_cells)],
        pl.BlockSpec(
            (devices, 2, members, CHUNK_ROWS, steps, lanes), lambda c, core: (0, 0, 0, c, 0, 0)
        ),
        pltpu.HBM(shape, jnp.bfloat16),
        [
            pltpu.VMEM((2 * members, freqs, 4 * lanes), jnp.float32),
            pltpu.VMEM((2 * members, freqs, width), jnp.float32),
        ],
        cost_estimate=map_cost(members, own, math.prod(shape)),
        name="pull_back",
    )(core, *small, *in_hbm(own, other), back, local_cells)


def rims(top, bottom):
    size = lax.axis_size("cells")
    onward = [(k, k + 1) for k in range(size - 1)]
    backward = [(k + 1, k) for k in range(size - 1)]
    return lax.ppermute(bottom, "cells", onward), lax.ppermute(top, "cells", backward)


def misfit_rims(edge):
    size, width = lax.axis_size("cells"), lax.axis_size("sensors")
    same, cross = [], []
    for cell in range(size):
        for sensor in range(width):
            there = cell + 2 * (sensor % 2) - 1
            if 0 <= there < size:
                same.append((cell * width + sensor, there * width + sensor))
                cross.append((cell * width + sensor, there * width + (sensor ^ 1)))
    both = ("cells", "sensors")
    return lax.ppermute(edge, both, same), lax.ppermute(edge, both, cross)


def swap_cores(value):
    size = lax.axis_size("sensors")
    return lax.ppermute(value, "sensors", [(k, k ^ 1) for k in range(size)])


def from_all_cells(value):
    size = lax.axis_size("cells")
    if size & (size - 1):
        return [lax.psum(value, "cells")]
    return [value] + [
        lax.ppermute(value, "cells", [(k, k ^ other) for k in range(size)])
        for other in range(1, size)
    ]


class Line:
    def __init__(self, value):
        self.size = lax.axis_size("sensors")
        self.value, self.ups, self.downs = value, [], []
        self.ends = (value, value)

    def hop(self, last=False):
        while len(self.ups) < self.size // 2 - 1:
            start = 2 * len(self.ups)
            onward = [(k, k + 2) for k in range(start, self.size - 2)]
            backward = [(self.size - 1 - k, self.size - 1 - there) for k, there in onward]
            up = lax.ppermute(self.ends[0], "sensors", onward)
            down = lax.ppermute(self.ends[1], "sensors", backward)
            self.ups.append(up)
            self.downs.append(down)
            self.ends = (up, down)
            if not last:
                break

    def after(self, other):
        if other is not None and self.ups:
            self.ends, other = lax.optimization_barrier((self.ends, other))
            self.ups[-1], self.downs[-1] = self.ends
        return other

    def slots(self):
        return [self.value, *self.ups, *self.downs]


def coefficients(stiff, diag):
    inside = diag > 0.0
    inverse = jnp.where(inside, 1.0 / jnp.where(inside, diag, 1.0), 0.0)
    unscale = jnp.where(inside, 1.0 / jnp.where(inside, stiff, 1.0), 0.0)
    scaled = DAMPING * inverse * stiff
    coeff = jnp.stack([scaled, scaled * stiff, unscale, stiff, diag])
    return jnp.broadcast_to(coeff[:, :, None, :], (*coeff.shape[:2], SUBLANES, coeff.shape[2]))


def shards(rhs, forward_map, stiffness, reaction, noise_weight, sensor_cell):
    steps, samples, rows, cols = rhs.shape
    _, freqs, sensors, cells = forward_map.shape
    size = lax.axis_size("sensors")
    chips = size // 2
    cell_index = lax.axis_index("cells")
    sensor_index = lax.axis_index("sensors")
    core = sensor_index % 2
    near = LANES // sensors
    half = cells // 2
    other_map = swap_cores(forward_map)

    cores = jnp.stack([core, 1 - core])
    offsets = cores[None, :, None] * steps + jnp.arange(steps, dtype=jnp.int32)
    chip_steps = 2 * steps
    places = jnp.arange(chips, dtype=jnp.int32)[:, None, None] * chip_steps
    table = transform_table(freqs, places + offsets)
    back = table.T
    in_order = transform_table(freqs, jnp.arange(2 * freqs, dtype=jnp.int32))
    chip = sensor_index // 2
    places = (chip - jnp.arange(chips, dtype=jnp.int32)) % chips
    around = transform_table(freqs, places[:, None, None] * chip_steps + offsets)

    diagonal = reaction + 4.0 * stiffness * stiffness
    local = jnp.stack([stiffness, diagonal])
    members = samples // GROUPS
    groups = [slice(group * members, (group + 1) * members) for group in range(GROUPS)]

    def rim_rows(here, first):
        part = lax.slice_in_dim(rhs[:, here], first, first + HALO, axis=2)
        return jnp.transpose(lax.optimization_barrier(part), (1, 2, 0, 3))

    def packed(first):
        part = rim_rows(groups[0], first).astype(jnp.bfloat16).reshape(members * HALO, steps, cols)
        value, terms = local[:, first : first + HALO].reshape(2 * HALO, cols), []
        for _ in range(3):
            terms.append(lax.optimization_barrier(value.astype(jnp.bfloat16)))
            value = value - terms[-1].astype(jnp.float32)
        extra = jnp.concatenate(terms, axis=0)
        extra = jnp.pad(extra, ((0, -6 * HALO % steps), (0, 0))).reshape(-1, steps, cols)
        return jnp.concatenate([part, extra], axis=0)

    def unpacked(value):
        part = value[: members * HALO].reshape(members, HALO, steps, cols)
        extra = value[members * HALO :].reshape(-1, cols)[: 6 * HALO].astype(jnp.float32)
        high, middle, low = extra.reshape(3, 2, HALO, cols)
        return part, high + (middle + low)

    (up_first, up), (down_first, down) = (
        unpacked(value) for value in rims(packed(0), packed(rows - HALO))
    )
    stiff, diag = jnp.concatenate([up, local, down], axis=1)
    coeff = coefficients(stiff, diag)
    local_coeff = coefficients(stiffness, diagonal)

    def per_lane(values):
        own = lax.dynamic_slice_in_dim(values, sensor_index * sensors, sensors)
        other = lax.dynamic_slice_in_dim(values, (sensor_index ^ 1) * sensors, sensors)
        return jnp.stack([jnp.tile(own, near), jnp.tile(other, near)])

    noise = per_lane(noise_weight)
    local_cells = per_lane(sensor_cell) - (cell_index * cells + core * half)
    local_cells = jnp.broadcast_to(local_cells.reshape(2 * LANES, 1), (2 * LANES, LANES))
    core = core.reshape(1)

    whole = members - members // APART
    lines = [[k for k in range(size) if k % 2 == parity] for parity in range(2)]
    shape = (chips, 2, members, rows // 2, steps, cols)

    def both_cores(low, first, last, count):
        here = first + (last - first) * core[0]
        keep = lax.dynamic_slice_in_dim(low, here, count, axis=1)
        give = lax.dynamic_slice_in_dim(low, first + last - here, count, axis=1)
        return jnp.stack([keep, swap_cores(give)])

    def ready(state):
        iterate, low, rest, top, bottom = state
        above, below = rims(top, bottom)
        pair = both_cores(low, 0, rows // 2, rows // 2)
        parts = lax.optimization_barrier((pair[:, :whole], pair[:, whole:]))
        return iterate, *parts, (above, rest, below)

    def edges(misfit):
        first = (rows // 2 - HALO) * core[0]
        edge = lax.dynamic_slice_in_dim(misfit, first, HALO, axis=2)
        same, _ = misfit_rims(edge[:1])
        _, cross = misfit_rims(edge[1:])
        return misfit, swap_cores(misfit[1:]), same, cross

    inside = inner(0, members, core, rhs, local_coeff)
    iterate, low, rest, *ends = start(0, members, core, rhs, up_first, down_first, coeff)
    above, below = rims(*ends)
    states = [(iterate, inside, None, (above, rest, below))]
    line = Line(both_cores(low, 0, rows - CHUNK_ROWS, CHUNK_ROWS))
    line.hop()
    for group in range(1, GROUPS):
        ends = tuple(
            rim_rows(groups[group], first).astype(jnp.bfloat16) for first in (0, rows - HALO)
        )
        rests, ends = line.after((states[0][3], ends))
        states[0] = (*states[0][:3], rests)
        states.append(ready(start(group, members, core, rhs, *rims(*ends), coeff)))

    outputs = ()
    for iteration in range(ITERS):
        fields = [
            lax.all_gather(state[1], "sensors", axis_index_groups=None if state[2] is None else lines)
            for state in states
        ]
        line.hop(last=True)
        totals = []
        for group in range(GROUPS):
            iterate, sent, _, rests = states[group]
            field = fields[group]
            slots, line = line.slots(), None
            if group > 0:
                field, rests = lax.optimization_barrier((field, rests))
            states[group] = iterate, rests
            if group + 1 < GROUPS:
                line = Line(states[group + 1][2])
                line.hop()
                field = line.after(field)
                line.hop()
            sums = observe(
                core,
                field,
                slots,
                forward_map,
                other_map,
                in_order if sent.ndim == 4 else table,
                around,
                local_cells,
            )
            if line is not None:
                sums = line.after(sums)
                line.hop(last=True)
            sums = from_all_cells(sums + swap_cores(sums)[::-1])
            misfit = pull_back(core, sums, noise, forward_map, other_map, back, local_cells, shape)
            if line is not None:
                misfit = line.after(misfit)
            totals.append(
                lax.psum_scatter(
                    misfit, "sensors", scatter_dimension=0, axis_index_groups=lines, tiled=False
                )
            )
        for group in range(GROUPS):
            iterate, rests = states[group]
            total = totals[group]
            if iteration < ITERS - 1:
                if group == 1:
                    before = states[0]
                    line = Line(before[2])
                    line.hop()
                    line.hop()
                    total, earlier = line.after((total, before[3]))
                    states[0] = (*before[:3], earlier)
                states[group] = ready(step(core, rests, edges(total), iterate, coeff))
            else:
                if outputs:
                    total, outputs = lax.optimization_barrier((total, outputs))
                outputs = finish(
                    group, samples, core, rests, edges(total), iterate, coeff, outputs
                )
    return tuple(out.reshape(rhs.shape) for out in outputs)


def solution(mesh):
    placed = (
        P("sensors", None, "cells", None),
        P(None, None, "sensors", "cells"),
        P("cells", None),
        P("cells", None),
        P(),
        P(),
    )
    return jax.shard_map(
        shards,
        mesh=mesh,
        in_specs=placed,
        out_specs=(P("sensors", None, "cells", None), P("sensors", None, "cells", None)),
        check_vma=False,
    )
```

```python
import math

import jax
import jax.numpy as jnp
from jax import lax
from jax.experimental import pallas as pl
from jax.experimental.pallas import tpu as pltpu
from jax.sharding import PartitionSpec as P

SWEEPS = 4
ITERS = 2
DAMPING = 0.8
HALO = SWEEPS
LANES = 128
APART = 3
SUBLANES = 8
GROUPS = 2
CHUNK_ROWS = 4
VMEM_BYTES = 40 * 2**20


def transform_table(freqs, moments):
    period = moments.size
    wave = jnp.arange(freqs, dtype=jnp.int32)[:, None]
    moment = moments.reshape(1, period)
    phase = (wave * moment % period).astype(jnp.float32) * (2.0 * math.pi / period)
    factor = 1.0 / math.sqrt(period)
    return jnp.concatenate([jnp.cos(phase) * factor, -jnp.sin(phase) * factor], axis=0).astype(
        jnp.bfloat16
    )


def whole_block(array):
    return pl.BlockSpec(array.shape, lambda *_: (0,) * array.ndim)


def in_hbm(*arrays):
    return [pltpu.with_memory_space_constraint(array, pltpu.HBM) for array in arrays]


def call(kernel, core, grid, in_specs, out_specs, out_shape, scratch=(), aliases=None, **kwargs):
    grid_spec = pltpu.PrefetchScalarGridSpec(
        num_scalar_prefetch=1,
        grid=grid,
        in_specs=in_specs,
        out_specs=out_specs,
        scratch_shapes=list(scratch),
    )
    return pl.pallas_call(
        kernel,
        grid_spec=grid_spec,
        out_shape=out_shape,
        input_output_aliases=aliases or {},
        compiler_params=pltpu.CompilerParams(vmem_limit_bytes=VMEM_BYTES),
        **kwargs,
    )


def dot(left, right):
    return jnp.dot(left, right, preferred_element_type=jnp.float32)


def dot_lanes(left, right):
    return lax.dot_general(left, right, (((1,), (1,)), ((), ())), preferred_element_type=jnp.float32)


def neighbours(field):
    inner = field[1:-1]
    lane = lax.broadcasted_iota(jnp.int32, inner.shape, 2)
    before = jnp.where(lane == 0, 0.0, pltpu.roll(inner, 1, 2))
    after = jnp.where(lane == LANES - 1, 0.0, pltpu.roll(inner, LANES - 1, 2))
    return (field[2:] + field[:-2]) + (before + after)


def trim(array, width):
    return array[width : array.shape[0] - width]


def precondition(residual, coeff_ref):
    extra = (coeff_ref.shape[1] - residual.shape[0]) // 2
    coeff = [trim(coeff_ref[k], extra) for k in range(3)]
    first = coeff[0] * residual
    scaled = first
    for sweep in range(1, SWEEPS):
        scaled = (
            (1.0 - DAMPING) * scaled[1:-1]
            + trim(first, sweep)
            + trim(coeff[1], sweep) * neighbours(scaled)
        )
    return trim(coeff[2], SWEEPS - 1) * scaled


def prior(field, coeff_ref):
    extra = (coeff_ref.shape[1] - field.shape[0]) // 2
    stiffness = trim(coeff_ref[3], extra)
    diagonal = trim(coeff_ref[4], extra + 1)
    return diagonal * field[1:-1] - stiffness[1:-1] * neighbours(stiffness * field)


def time_chunks(steps, body):
    def run(index, carry):
        body(pl.ds(pl.multiple_of(index * SUBLANES, SUBLANES), SUBLANES))
        return carry

    lax.fori_loop(0, steps // SUBLANES, run, 0)


def fields(members, rows, steps, cols):
    field = pl.BlockSpec((1, rows, steps, cols), lambda b, core: (b, 0, 0, 0))
    rim = pl.BlockSpec((1, HALO, steps, cols), lambda b, core: (b, 0, 0, 0))
    misfits = [
        pl.BlockSpec((None, 1, count, steps, cols), lambda b, core: (0, b, 0, 0, 0))
        for count in (rows // 2, rows // 2, HALO, HALO)
    ]

    def shape(count, dtype):
        return jax.ShapeDtypeStruct((members, count, steps, cols), dtype)

    specs = [field, field, field, rim, rim]
    shapes = [
        pltpu.HBM((members, rows, steps, cols), jnp.float32),
        pltpu.HBM((members, rows, steps, cols), jnp.bfloat16),
        pltpu.HBM((members, rows, steps, cols), jnp.float32),
        shape(HALO, jnp.bfloat16),
        shape(HALO, jnp.bfloat16),
    ]
    return field, rim, misfits, specs, shapes


def put_rest(rest, times, rest_ref, top_ref, bottom_ref):
    rest_ref[0, :, times] = rest
    top_ref[0, :, times] = rest[:HALO].astype(top_ref.dtype)
    bottom_ref[0, :, times] = rest[rest.shape[0] - HALO :].astype(bottom_ref.dtype)


def start_kernel(
    core_ref, rhs_ref, up_ref, down_ref, coeff_ref,
    iter_ref, low_ref, rest_ref, top_ref, bottom_ref,
):
    def body(times):
        here = jnp.swapaxes(rhs_ref[times], 0, 1)
        rims_here = [ref[0, :, times].astype(jnp.float32) for ref in (up_ref, down_ref)]
        update = precondition(jnp.concatenate([rims_here[0], here, rims_here[1]], axis=0), coeff_ref)
        iter_ref[0, :, times] = update[1:-1]
        put_rest(here - prior(update, coeff_ref), times, rest_ref, top_ref, bottom_ref)

    time_chunks(iter_ref.shape[2], body)
    low_ref[...] = iter_ref[...].astype(low_ref.dtype)


def start(group, members, core, rhs, up, down, coeff):
    steps, _, rows, cols = rhs.shape
    flat = rhs.reshape(steps, -1, cols)
    _, rim, _, specs, shapes = fields(members, rows, steps, cols)
    return call(
        start_kernel,
        core,
        (members,),
        [
            pl.BlockSpec((steps, rows, cols), lambda b, core: (0, b + group * members, 0)),
            rim,
            rim,
            whole_block(coeff),
        ],
        specs,
        shapes,
        name="start",
    )(core, *in_hbm(flat), up, down, coeff)


def residual_of(core, times, rest_refs, misfit_refs, whole_ref):
    own_ref, other_ref, same_ref, cross_ref = misfit_refs
    half = own_ref.shape[1]
    whole_ref[pl.ds(core * half, half)] = own_ref[0, :, times].astype(jnp.float32)
    whole_ref[pl.ds((1 - core) * half, half)] = other_ref[0, :, times].astype(jnp.float32)
    same = same_ref[0, :, times].astype(jnp.float32)
    cross = cross_ref[0, :, times].astype(jnp.float32)
    first = core == 0
    parts = [jnp.where(first, cross, same), whole_ref[...], jnp.where(first, same, cross)]
    rests = [ref[0, :, times].astype(jnp.float32) for ref in rest_refs]
    return jnp.concatenate([rest - part for rest, part in zip(rests, parts)], axis=0)


def inner_kernel(core_ref, rhs_ref, coeff_ref, low_ref, wide_ref):
    def body(times):
        update = precondition(jnp.swapaxes(rhs_ref[times], 0, 1), coeff_ref)
        wide_ref[:, times] = update[1:-1]

    time_chunks(wide_ref.shape[1], body)
    low_ref[0] = wide_ref[...].astype(low_ref.dtype)


def inner(group, members, core, rhs, coeff):
    steps, _, rows, cols = rhs.shape
    flat = rhs.reshape(steps, -1, cols)
    inside = rows - 2 * HALO
    return call(
        inner_kernel,
        core,
        (members,),
        [
            pl.BlockSpec((steps, rows, cols), lambda b, core: (0, b + group * members, 0)),
            whole_block(coeff),
        ],
        pl.BlockSpec((1, inside, steps, cols), lambda b, core: (b, 0, 0, 0)),
        pltpu.HBM((members, inside, steps, cols), jnp.bfloat16),
        [pltpu.VMEM((inside, steps, cols), jnp.float32)],
        name="inner",
    )(core, *in_hbm(flat), coeff)


def held(rests, misfits, iterate):
    above, rest, below = rests
    own, other, same, cross = misfits
    rest, own, iterate = in_hbm(rest, own, iterate)
    return above, rest, below, own, other, same, cross, iterate


def step_kernel(
    core_ref, up_ref, rest_ref, down_ref, own_ref, other_ref, same_ref, cross_ref, iter_ref, coeff_ref,
    next_ref, low_ref, later_ref, top_ref, bottom_ref, whole_ref,
):
    def body(times):
        residual = residual_of(
            core_ref[0],
            times,
            (up_ref, rest_ref, down_ref),
            (own_ref, other_ref, same_ref, cross_ref),
            whole_ref,
        )
        update = precondition(residual, coeff_ref)
        next_ref[0, :, times] = iter_ref[0, :, times] + update[1:-1]
        put_rest(rest_ref[0, :, times] - prior(update, coeff_ref), times, later_ref, top_ref, bottom_ref)

    time_chunks(iter_ref.shape[2], body)
    low_ref[...] = next_ref[...].astype(low_ref.dtype)


def step(core, rests, misfits, iterate, coeff):
    members, rows, steps, cols = iterate.shape
    field, rim, parts, specs, shapes = fields(members, rows, steps, cols)
    return call(
        step_kernel,
        core,
        (members,),
        [rim, field, rim, *parts, field, whole_block(coeff)],
        specs,
        shapes,
        [pltpu.VMEM((rows, SUBLANES, cols), jnp.float32)],
        name="step",
    )(core, *held(rests, misfits, iterate), coeff)


def finish_kernel(
    core_ref, up_ref, rest_ref, down_ref, own_ref, other_ref, same_ref, cross_ref, iter_ref, coeff_ref,
    *refs,
):
    solution_ref, residual_ref, whole_ref = refs[-3:]

    def body(times):
        residual = residual_of(
            core_ref[0],
            times,
            (up_ref, rest_ref, down_ref),
            (own_ref, other_ref, same_ref, cross_ref),
            whole_ref,
        )
        update = precondition(residual, coeff_ref)
        solution_ref[times] = jnp.swapaxes(iter_ref[0, :, times] + update[1:-1], 0, 1)
        residual_ref[times] = jnp.swapaxes(trim(residual, HALO), 0, 1)

    time_chunks(iter_ref.shape[2], body)


def finish(group, samples, core, rests, misfits, iterate, coeff, previous):
    members, rows, steps, cols = iterate.shape
    field, rim, parts, _, _ = fields(members, rows, steps, cols)
    result = pl.BlockSpec((steps, rows, cols), lambda b, core: (0, b + group * members, 0))
    shape = jax.ShapeDtypeStruct((steps, samples * rows, cols), jnp.float32)
    in_specs = [rim, field, rim, *parts, field, whole_block(coeff)]
    first = 1 + len(in_specs)
    return call(
        finish_kernel,
        core,
        (members,),
        in_specs + [pl.BlockSpec(memory_space=pl.ANY)] * len(previous),
        [result, result],
        [shape, shape],
        [pltpu.VMEM((rows, SUBLANES, cols), jnp.float32)],
        {first + k: k for k in range(len(previous))},
        name="finish",
    )(core, *held(rests, misfits, iterate), coeff, *previous)


def same_frequency(near, sensors, lanes):
    shape = (near, lanes)
    return lax.broadcasted_iota(jnp.int32, shape, 0) == (
        lax.broadcasted_iota(jnp.int32, shape, 1) % LANES // sensors
    )


def marks_of(cell_ref, width, chunk):
    first = chunk * width
    parts = []
    for start_lane in range(0, width, LANES):
        lane = lax.broadcasted_iota(jnp.int32, cell_ref.shape, 1) + (first + start_lane)
        parts.append(jnp.where(cell_ref[...] == lane, 1.0, 0.0).astype(jnp.bfloat16))
    return jnp.concatenate(parts, axis=1)


def near_map(own_ref, other_ref, here):
    _, freqs, sensors, width = own_ref.shape
    parts = [
        ref[part, here].reshape(LANES, width) for part in range(2) for ref in (own_ref, other_ref)
    ]
    return jnp.concatenate(parts, axis=0)


def place_of(chunk, core_ref, split):
    chunks = pl.num_programs(0)
    return jnp.where(core_ref[0] == 1, chunk, (chunk + 1) % chunks) if split else chunk


def observe_kernel(core_ref, field_ref, *refs):
    *slot_refs, own_ref, other_ref, table_ref, around_ref, cell_ref = refs[:-4]
    out_ref, spec, acc, picked = refs[-4:]
    rows, steps, lanes = field_ref.shape[-3:]
    members = spec.shape[0] // 2
    chips = table_ref.shape[1] // (2 * steps)
    whole = field_ref.shape[-4]
    freqs, sensors, width = own_ref.shape[1:]
    near = lanes // sensors
    wide = 2 * lanes
    chunk = pl.program_id(0)

    @pl.when(chunk == 0)
    def _():
        acc[...] = jnp.zeros_like(acc)
        picked[...] = jnp.zeros_like(picked)

    split = len(slot_refs) > 0 and len(field_ref.shape) == 5
    marks = marks_of(cell_ref, width, place_of(chunk, core_ref, split))

    def gathered(b, r):
        return field_ref[..., b, r, :, :].reshape(2 * chips * steps, lanes)

    def along(b, r):
        slots = [slot_refs[0][:, b, r]]
        for k in range(1, chips):
            slots.append(slot_refs[k][:, b, r] + slot_refs[2 * chips - 1 - k][:, b, r])
        return jnp.concatenate([slot.reshape(2 * steps, lanes) for slot in slots], axis=0)

    def transform(b, table, history, first):
        times = jnp.concatenate([history(b - first, r) for r in range(rows)], axis=1)
        spectrum = dot(table[...], times)
        spec[2 * b] = spectrum[:freqs]
        spec[2 * b + 1] = spectrum[freqs:]

    if split:

        @pl.when(chunk < pl.num_programs(0) - 1)
        def _():
            for b in range(members):
                transform(b, table_ref, gathered, 0)

        @pl.when(chunk == pl.num_programs(0) - 1)
        def _():
            for b in range(members):
                transform(b, around_ref, along, 0)

    else:
        for b in range(members):
            if b < whole:
                transform(b, table_ref, gathered, 0)
            else:
                transform(b, around_ref, along, whole)
    for m in range(2 * members):
        picked[m] += dot_lanes(spec[m].astype(jnp.bfloat16), marks)
    for q in range(freqs // near):
        here = slice(q * near, (q + 1) * near)
        left = spec[:, here].reshape(2 * members * near, width).astype(jnp.bfloat16)
        acc[q] += dot_lanes(left, near_map(own_ref, other_ref, here))

    @pl.when(chunk == pl.num_programs(0) - 1)
    def _():
        mask = same_frequency(near, sensors, wide)
        for q in range(freqs // near):
            here = slice(q * near, (q + 1) * near)
            for b in range(members):
                real = acc[q, 2 * b * near : (2 * b + 1) * near]
                imag = acc[q, (2 * b + 1) * near : (2 * b + 2) * near]
                sums = (
                    real[:, :wide] - imag[:, wide:] + picked[2 * b, here],
                    imag[:, :wide] + real[:, wide:] + picked[2 * b + 1, here],
                )
                for part, value in enumerate(sums):
                    line = jnp.sum(jnp.where(mask, value, 0.0), 0, keepdims=True)
                    out_ref[0, part, b, q : q + 1] = line[:, :lanes]
                    out_ref[1, part, b, q : q + 1] = line[:, lanes:]


def map_specs(own, width):
    chunks = own.shape[3] // (2 * width)
    spec = pl.BlockSpec(own.shape[:3] + (width,), lambda c, core: (0, 0, 0, core[0] * chunks + c))
    return [spec, spec]


def map_cost(members, own, moved):
    return pl.CostEstimate(
        flops=8 * members * own.size, bytes_accessed=2 * own.size + 2 * moved, transcendentals=0
    )


def observe(core, field, slots, own, other, table, around, local_cells):
    *sources, whole, rows, steps, lanes = field.shape
    split = len(sources) == 1
    apart = slots[0].shape[1]
    members = whole if split else whole + apart
    _, freqs, sensors, cells = own.shape
    width = CHUNK_ROWS * lanes
    near = lanes // sensors
    shape = (2, 2, members, freqs // near, lanes)
    chunks = cells // (2 * width)
    block = (*sources, whole, CHUNK_ROWS, steps, lanes)
    lead = (0,) * len(sources) + (0,)

    def field_place(c, core):
        return (*lead, core[0] * (chunks - 1) + jnp.minimum(c, chunks - 2) if split else c, 0, 0)

    def map_place(c, core):
        here = jnp.where(core[0] == 1, c, (c + 1) % chunks) if split else c
        return (0, 0, 0, core[0] * chunks + here)

    slot = pl.BlockSpec(
        (2, apart, CHUNK_ROWS, steps, lanes), lambda c, core: (0, 0, 0 if split else c, 0, 0)
    )
    map_block = pl.BlockSpec(own.shape[:3] + (width,), map_place)
    return call(
        observe_kernel,
        core,
        (chunks,),
        [pl.BlockSpec(block, field_place)]
        + [slot] * len(slots)
        + [map_block] * 2
        + [whole_block(table), whole_block(around), whole_block(local_cells)],
        pl.BlockSpec(shape, lambda c, core: (0, 0, 0, 0, 0)),
        jax.ShapeDtypeStruct(shape, jnp.float32),
        [
            pltpu.VMEM((2 * members, freqs, width), jnp.float32),
            pltpu.VMEM((freqs // near, 2 * members * near, 4 * lanes), jnp.float32),
            pltpu.VMEM((2 * members, freqs, 2 * lanes), jnp.float32),
        ],
        cost_estimate=map_cost(members, own, field.size),
        name="observe",
    )(core, *in_hbm(field), *slots, *in_hbm(own, other), table, around, local_cells)


def pull_kernel(core_ref, *refs):
    *sums, noise_ref, own_ref, other_ref, back_ref, cell_ref = refs[:-3]
    out_ref, weights, adjoint = refs[-3:]
    devices, _, members, rows, steps, lanes = out_ref.shape
    freqs, sensors, width = own_ref.shape[1:]
    near = lanes // sensors
    wide = 2 * lanes

    def total(part, b, which):
        values = [ref[which, part, b] for ref in sums]
        while len(values) > 1:
            values = [values[k] + values[k + 1] for k in range(0, len(values), 2)]
        noise = noise_ref[which : which + 1]
        return (noise * values[0]).astype(jnp.bfloat16).astype(jnp.float32)

    @pl.when(pl.program_id(0) == 0)
    def _():
        mask = same_frequency(near, sensors, wide)
        for b in range(members):
            real, imag = (
                jnp.concatenate([total(part, b, 0), total(part, b, 1)], axis=1) for part in range(2)
            )
            for q in range(freqs // near):
                here = slice(q * near, (q + 1) * near)
                w_real = jnp.where(mask, real[q : q + 1], 0.0)
                w_imag = jnp.where(mask, imag[q : q + 1], 0.0)
                weights[2 * b, here, :wide] = w_real
                weights[2 * b, here, wide:] = w_imag
                weights[2 * b + 1, here, :wide] = w_imag
                weights[2 * b + 1, here, wide:] = -w_real

    marks = marks_of(cell_ref, width, pl.program_id(0))
    for m in range(2 * members):
        adjoint[m] = dot(weights[m, :, :wide].astype(jnp.bfloat16), marks)
    for q in range(freqs // near):
        here = slice(q * near, (q + 1) * near)
        left = weights[:, here].reshape(2 * members * near, 2 * wide).astype(jnp.bfloat16)
        part = dot(left, near_map(own_ref, other_ref, here))
        adjoint[:, here] += part.reshape(2 * members, near, width)
    for b in range(members):
        whole = adjoint[2 * b : 2 * b + 2].reshape(2 * freqs, width)
        high = whole.astype(jnp.bfloat16)
        low = (whole - high.astype(jnp.float32)).astype(jnp.bfloat16)
        misfit = (dot(back_ref[...], high) + dot(back_ref[...], low)).astype(out_ref.dtype)
        for r in range(rows):
            part = misfit[:, r * lanes : (r + 1) * lanes]
            out_ref[:, :, b, r] = part.reshape(devices, 2, steps, lanes)


def pull_back(core, sums, noise, own, other, back, local_cells, shape):
    devices, _, members, rows, steps, lanes = shape
    _, freqs, sensors, cells = own.shape
    width = CHUNK_ROWS * lanes
    small = [*sums, noise]
    return call(
        pull_kernel,
        core,
        (rows // CHUNK_ROWS,),
        [whole_block(array) for array in small]
        + map_specs(own, width)
        + [whole_block(back), whole_block(local_cells)],
        pl.BlockSpec(
            (devices, 2, members, CHUNK_ROWS, steps, lanes), lambda c, core: (0, 0, 0, c, 0, 0)
        ),
        pltpu.HBM(shape, jnp.bfloat16),
        [
            pltpu.VMEM((2 * members, freqs, 4 * lanes), jnp.float32),
            pltpu.VMEM((2 * members, freqs, width), jnp.float32),
        ],
        cost_estimate=map_cost(members, own, math.prod(shape)),
        name="pull_back",
    )(core, *small, *in_hbm(own, other), back, local_cells)


def rims(top, bottom):
    size = lax.axis_size("cells")
    onward = [(k, k + 1) for k in range(size - 1)]
    backward = [(k + 1, k) for k in range(size - 1)]
    return lax.ppermute(bottom, "cells", onward), lax.ppermute(top, "cells", backward)


def misfit_rims(edge):
    size, width = lax.axis_size("cells"), lax.axis_size("sensors")
    same, cross = [], []
    for cell in range(size):
        for sensor in range(width):
            there = cell + 2 * (sensor % 2) - 1
            if 0 <= there < size:
                same.append((cell * width + sensor, there * width + sensor))
                cross.append((cell * width + sensor, there * width + (sensor ^ 1)))
    both = ("cells", "sensors")
    return lax.ppermute(edge, both, same), lax.ppermute(edge, both, cross)


def swap_cores(value):
    size = lax.axis_size("sensors")
    return lax.ppermute(value, "sensors", [(k, k ^ 1) for k in range(size)])


def from_all_cells(value):
    size = lax.axis_size("cells")
    if size & (size - 1):
        return [lax.psum(value, "cells")]
    return [value] + [
        lax.ppermute(value, "cells", [(k, k ^ other) for k in range(size)])
        for other in range(1, size)
    ]


class Line:
    def __init__(self, value):
        self.size = lax.axis_size("sensors")
        self.value, self.ups, self.downs = value, [], []
        self.ends = (value, value)

    def hop(self, last=False):
        while len(self.ups) < self.size // 2 - 1:
            start = 2 * len(self.ups)
            onward = [(k, k + 2) for k in range(start, self.size - 2)]
            backward = [(self.size - 1 - k, self.size - 1 - there) for k, there in onward]
            up = lax.ppermute(self.ends[0], "sensors", onward)
            down = lax.ppermute(self.ends[1], "sensors", backward)
            self.ups.append(up)
            self.downs.append(down)
            self.ends = (up, down)
            if not last:
                break

    def after(self, other):
        if other is not None and self.ups:
            self.ends, other = lax.optimization_barrier((self.ends, other))
            self.ups[-1], self.downs[-1] = self.ends
        return other

    def slots(self):
        return [self.value, *self.ups, *self.downs]


def coefficients(stiff, diag):
    inside = diag > 0.0
    inverse = jnp.where(inside, 1.0 / jnp.where(inside, diag, 1.0), 0.0)
    unscale = jnp.where(inside, 1.0 / jnp.where(inside, stiff, 1.0), 0.0)
    scaled = DAMPING * inverse * stiff
    coeff = jnp.stack([scaled, scaled * stiff, unscale, stiff, diag])
    return jnp.broadcast_to(coeff[:, :, None, :], (*coeff.shape[:2], SUBLANES, coeff.shape[2]))


def shards(rhs, forward_map, stiffness, reaction, noise_weight, sensor_cell):
    steps, samples, rows, cols = rhs.shape
    _, freqs, sensors, cells = forward_map.shape
    size = lax.axis_size("sensors")
    chips = size // 2
    cell_index = lax.axis_index("cells")
    sensor_index = lax.axis_index("sensors")
    core = sensor_index % 2
    near = LANES // sensors
    half = cells // 2
    other_map = swap_cores(forward_map)

    cores = jnp.stack([core, 1 - core])
    offsets = cores[None, :, None] * steps + jnp.arange(steps, dtype=jnp.int32)
    chip_steps = 2 * steps
    places = jnp.arange(chips, dtype=jnp.int32)[:, None, None] * chip_steps
    table = transform_table(freqs, places + offsets)
    back = table.T
    in_order = transform_table(freqs, jnp.arange(2 * freqs, dtype=jnp.int32))
    chip = sensor_index // 2
    places = (chip - jnp.arange(chips, dtype=jnp.int32)) % chips
    around = transform_table(freqs, places[:, None, None] * chip_steps + offsets)

    diagonal = reaction + 4.0 * stiffness * stiffness
    local = jnp.stack([stiffness, diagonal])
    members = samples // GROUPS
    groups = [slice(group * members, (group + 1) * members) for group in range(GROUPS)]

    def rim_rows(here, first):
        part = lax.slice_in_dim(rhs[:, here], first, first + HALO, axis=2)
        return jnp.transpose(lax.optimization_barrier(part), (1, 2, 0, 3))

    def packed(first):
        part = rim_rows(groups[0], first).astype(jnp.bfloat16).reshape(members * HALO, steps, cols)
        value, terms = local[:, first : first + HALO].reshape(2 * HALO, cols), []
        for _ in range(3):
            terms.append(lax.optimization_barrier(value.astype(jnp.bfloat16)))
            value = value - terms[-1].astype(jnp.float32)
        extra = jnp.concatenate(terms, axis=0)
        extra = jnp.pad(extra, ((0, -6 * HALO % steps), (0, 0))).reshape(-1, steps, cols)
        return jnp.concatenate([part, extra], axis=0)

    def unpacked(value):
        part = value[: members * HALO].reshape(members, HALO, steps, cols)
        extra = value[members * HALO :].reshape(-1, cols)[: 6 * HALO].astype(jnp.float32)
        high, middle, low = extra.reshape(3, 2, HALO, cols)
        return part, high + (middle + low)

    (up_first, up), (down_first, down) = (
        unpacked(value) for value in rims(packed(0), packed(rows - HALO))
    )
    stiff, diag = jnp.concatenate([up, local, down], axis=1)
    coeff = coefficients(stiff, diag)
    local_coeff = coefficients(stiffness, diagonal)

    def per_lane(values):
        own = lax.dynamic_slice_in_dim(values, sensor_index * sensors, sensors)
        other = lax.dynamic_slice_in_dim(values, (sensor_index ^ 1) * sensors, sensors)
        return jnp.stack([jnp.tile(own, near), jnp.tile(other, near)])

    noise = per_lane(noise_weight)
    local_cells = per_lane(sensor_cell) - (cell_index * cells + core * half)
    local_cells = jnp.broadcast_to(local_cells.reshape(2 * LANES, 1), (2 * LANES, LANES))
    core = core.reshape(1)

    whole = members - members // APART
    lines = [[k for k in range(size) if k % 2 == parity] for parity in range(2)]
    shape = (chips, 2, members, rows // 2, steps, cols)

    def both_cores(low, first, last, count):
        here = first + (last - first) * core[0]
        keep = lax.dynamic_slice_in_dim(low, here, count, axis=1)
        give = lax.dynamic_slice_in_dim(low, first + last - here, count, axis=1)
        return jnp.stack([keep, swap_cores(give)])

    def ready(state):
        iterate, low, rest, top, bottom = state
        above, below = rims(top, bottom)
        pair = both_cores(low, 0, rows // 2, rows // 2)
        parts = lax.optimization_barrier((pair[:, :whole], pair[:, whole:]))
        return iterate, *parts, (above, rest, below)

    def edges(misfit):
        first = (rows // 2 - HALO) * core[0]
        edge = lax.dynamic_slice_in_dim(misfit, first, HALO, axis=2)
        same, _ = misfit_rims(edge[:1])
        _, cross = misfit_rims(edge[1:])
        return misfit, swap_cores(misfit[1:]), same, cross

    inside = inner(0, members, core, rhs, local_coeff)
    iterate, low, rest, *ends = start(0, members, core, rhs, up_first, down_first, coeff)
    above, below = rims(*ends)
    states = [(iterate, inside, None, (above, rest, below))]
    line = Line(both_cores(low, 0, rows - CHUNK_ROWS, CHUNK_ROWS))
    for group in range(1, GROUPS):
        ends = tuple(
            rim_rows(groups[group], first).astype(jnp.bfloat16) for first in (0, rows - HALO)
        )
        _, rests, ends = lax.optimization_barrier((low, states[0][3], ends))
        states[0] = (*states[0][:3], rests)
        states.append(ready(start(group, members, core, rhs, *rims(*ends), coeff)))

    outputs = ()
    for iteration in range(ITERS):
        fields = [
            lax.all_gather(state[1], "sensors", axis_index_groups=None if state[2] is None else lines)
            for state in states
        ]
        line.hop(last=True)
        totals = []
        for group in range(GROUPS):
            iterate, sent, _, rests = states[group]
            field = fields[group]
            slots, line = line.slots(), None
            if group > 0:
                field, rests = lax.optimization_barrier((field, rests))
            states[group] = iterate, rests
            if group + 1 < GROUPS:
                value = states[group + 1][2]
                if iteration == 0:
                    slots, value = lax.optimization_barrier((slots, value))
                line = Line(value)
                line.hop()
                if iteration > 0:
                    field = line.after(field)
                    line.hop()
            sums = observe(
                core,
                field,
                slots,
                forward_map,
                other_map,
                in_order if sent.ndim == 4 else table,
                around,
                local_cells,
            )
            if line is not None:
                sums = line.after(sums)
                line.hop(last=True)
            sums = from_all_cells(sums + swap_cores(sums)[::-1])
            misfit = pull_back(core, sums, noise, forward_map, other_map, back, local_cells, shape)
            if line is not None:
                misfit = line.after(misfit)
            totals.append(
                lax.psum_scatter(
                    misfit, "sensors", scatter_dimension=0, axis_index_groups=lines, tiled=False
                )
            )
        for group in range(GROUPS):
            iterate, rests = states[group]
            total = totals[group]
            if iteration < ITERS - 1:
                if group == 1:
                    before = states[0]
                    line = Line(before[2])
                    line.hop()
                    line.hop()
                    total, earlier = line.after((total, before[3]))
                    states[0] = (*before[:3], earlier)
                states[group] = ready(step(core, rests, edges(total), iterate, coeff))
            else:
                if outputs:
                    total, outputs = lax.optimization_barrier((total, outputs))
                outputs = finish(
                    group, samples, core, rests, edges(total), iterate, coeff, outputs
                )
    return tuple(out.reshape(rhs.shape) for out in outputs)


def solution(mesh):
    placed = (
        P("sensors", None, "cells", None),
        P(None, None, "sensors", "cells"),
        P("cells", None),
        P("cells", None),
        P(),
        P(),
    )
    return jax.shard_map(
        shards,
        mesh=mesh,
        in_specs=placed,
        out_specs=(P("sensors", None, "cells", None), P("sensors", None, "cells", None)),
        check_vma=False,
    )
```

```python
import math

import jax
import jax.numpy as jnp
from jax import lax
from jax.experimental import pallas as pl
from jax.experimental.pallas import tpu as pltpu
from jax.sharding import PartitionSpec as P

SWEEPS = 4
ITERS = 2
DAMPING = 0.8
HALO = SWEEPS
LANES = 128
APART = 3
SUBLANES = 8
GROUPS = 2
CHUNK_ROWS = 4
SPAN = 16
VMEM_BYTES = 40 * 2**20


def transform_table(freqs, moments):
    period = moments.size
    wave = jnp.arange(freqs, dtype=jnp.int32)[:, None]
    moment = moments.reshape(1, period)
    phase = (wave * moment % period).astype(jnp.float32) * (2.0 * math.pi / period)
    factor = 1.0 / math.sqrt(period)
    return jnp.concatenate([jnp.cos(phase) * factor, -jnp.sin(phase) * factor], axis=0).astype(
        jnp.bfloat16
    )


def whole_block(array):
    return pl.BlockSpec(array.shape, lambda *_: (0,) * array.ndim)


def in_hbm(*arrays):
    return [pltpu.with_memory_space_constraint(array, pltpu.HBM) for array in arrays]


def call(kernel, core, grid, in_specs, out_specs, out_shape, scratch=(), aliases=None, **kwargs):
    grid_spec = pltpu.PrefetchScalarGridSpec(
        num_scalar_prefetch=1,
        grid=grid,
        in_specs=in_specs,
        out_specs=out_specs,
        scratch_shapes=list(scratch),
    )
    return pl.pallas_call(
        kernel,
        grid_spec=grid_spec,
        out_shape=out_shape,
        input_output_aliases=aliases or {},
        compiler_params=pltpu.CompilerParams(vmem_limit_bytes=VMEM_BYTES),
        **kwargs,
    )


def dot(left, right):
    return jnp.dot(left, right, preferred_element_type=jnp.float32)


def dot_lanes(left, right):
    return lax.dot_general(left, right, (((1,), (1,)), ((), ())), preferred_element_type=jnp.float32)


def neighbours(field):
    inner = field[1:-1]
    lane = lax.broadcasted_iota(jnp.int32, inner.shape, 2)
    before = jnp.where(lane == 0, 0.0, pltpu.roll(inner, 1, 2))
    after = jnp.where(lane == LANES - 1, 0.0, pltpu.roll(inner, LANES - 1, 2))
    return (field[2:] + field[:-2]) + (before + after)


def trim(array, width):
    return array[width : array.shape[0] - width]


def precondition(residual, coeff_ref):
    extra = (coeff_ref.shape[1] - residual.shape[0]) // 2
    coeff = [trim(coeff_ref[k], extra) for k in range(3)]
    first = coeff[0] * residual
    scaled = first
    for sweep in range(1, SWEEPS):
        scaled = (
            (1.0 - DAMPING) * scaled[1:-1]
            + trim(first, sweep)
            + trim(coeff[1], sweep) * neighbours(scaled)
        )
    return trim(coeff[2], SWEEPS - 1) * scaled


def prior(field, coeff_ref):
    extra = (coeff_ref.shape[1] - field.shape[0]) // 2
    stiffness = trim(coeff_ref[3], extra)
    diagonal = trim(coeff_ref[4], extra + 1)
    return diagonal * field[1:-1] - stiffness[1:-1] * neighbours(stiffness * field)


def time_chunks(steps, body):
    def run(index, carry):
        body(pl.ds(pl.multiple_of(index * SUBLANES, SUBLANES), SUBLANES))
        return carry

    lax.fori_loop(0, steps // SUBLANES, run, 0)


def fields(members, rows, steps, cols):
    span = min(steps, SPAN)
    field = pl.BlockSpec((1, rows, span, cols), lambda b, t, core: (b, 0, t, 0))
    rim = pl.BlockSpec((1, HALO, span, cols), lambda b, t, core: (b, 0, t, 0))
    misfits = [
        pl.BlockSpec((None, 1, count, span, cols), lambda b, t, core: (0, b, 0, t, 0))
        for count in (rows // 2, rows // 2, HALO, HALO)
    ]

    def shape(count, dtype):
        return jax.ShapeDtypeStruct((members, count, steps, cols), dtype)

    specs = [field, field, field, rim, rim]
    shapes = [
        pltpu.HBM((members, rows, steps, cols), jnp.float32),
        pltpu.HBM((members, rows, steps, cols), jnp.bfloat16),
        pltpu.HBM((members, rows, steps, cols), jnp.float32),
        shape(HALO, jnp.bfloat16),
        shape(HALO, jnp.bfloat16),
    ]
    return field, rim, misfits, specs, shapes


def put_rest(rest, times, rest_ref, top_ref, bottom_ref):
    rest_ref[0, :, times] = rest
    top_ref[0, :, times] = rest[:HALO].astype(top_ref.dtype)
    bottom_ref[0, :, times] = rest[rest.shape[0] - HALO :].astype(bottom_ref.dtype)


def start_kernel(
    core_ref, rhs_ref, up_ref, down_ref, coeff_ref,
    iter_ref, low_ref, rest_ref, top_ref, bottom_ref,
):
    def body(times):
        here = jnp.swapaxes(rhs_ref[times], 0, 1)
        rims_here = [ref[0, :, times].astype(jnp.float32) for ref in (up_ref, down_ref)]
        update = precondition(jnp.concatenate([rims_here[0], here, rims_here[1]], axis=0), coeff_ref)
        iter_ref[0, :, times] = update[1:-1]
        put_rest(here - prior(update, coeff_ref), times, rest_ref, top_ref, bottom_ref)

    time_chunks(iter_ref.shape[2], body)
    low_ref[...] = iter_ref[...].astype(low_ref.dtype)


def start(group, members, core, rhs, up, down, coeff):
    steps, _, rows, cols = rhs.shape
    flat = rhs.reshape(steps, -1, cols)
    _, rim, _, specs, shapes = fields(members, rows, steps, cols)
    return call(
        start_kernel,
        core,
        (members, steps // min(steps, SPAN)),
        [
            pl.BlockSpec(
        (min(steps, SPAN), rows, cols), lambda b, t, core: (t, b + group * members, 0)
    ),
            rim,
            rim,
            whole_block(coeff),
        ],
        specs,
        shapes,
        name="start",
    )(core, *in_hbm(flat), up, down, coeff)


def residual_of(core, times, rest_refs, misfit_refs, whole_ref):
    own_ref, other_ref, same_ref, cross_ref = misfit_refs
    half = own_ref.shape[1]
    whole_ref[pl.ds(core * half, half)] = own_ref[0, :, times].astype(jnp.float32)
    whole_ref[pl.ds((1 - core) * half, half)] = other_ref[0, :, times].astype(jnp.float32)
    same = same_ref[0, :, times].astype(jnp.float32)
    cross = cross_ref[0, :, times].astype(jnp.float32)
    first = core == 0
    parts = [jnp.where(first, cross, same), whole_ref[...], jnp.where(first, same, cross)]
    rests = [ref[0, :, times].astype(jnp.float32) for ref in rest_refs]
    return jnp.concatenate([rest - part for rest, part in zip(rests, parts)], axis=0)


def held(rests, misfits, iterate):
    above, rest, below = rests
    own, other, same, cross = misfits
    rest, own, iterate = in_hbm(rest, own, iterate)
    return above, rest, below, own, other, same, cross, iterate


def step_kernel(
    core_ref, up_ref, rest_ref, down_ref, own_ref, other_ref, same_ref, cross_ref, iter_ref, coeff_ref,
    next_ref, low_ref, later_ref, top_ref, bottom_ref, whole_ref,
):
    def body(times):
        residual = residual_of(
            core_ref[0],
            times,
            (up_ref, rest_ref, down_ref),
            (own_ref, other_ref, same_ref, cross_ref),
            whole_ref,
        )
        update = precondition(residual, coeff_ref)
        next_ref[0, :, times] = iter_ref[0, :, times] + update[1:-1]
        put_rest(rest_ref[0, :, times] - prior(update, coeff_ref), times, later_ref, top_ref, bottom_ref)

    time_chunks(iter_ref.shape[2], body)
    low_ref[...] = next_ref[...].astype(low_ref.dtype)


def step(core, rests, misfits, iterate, coeff):
    members, rows, steps, cols = iterate.shape
    field, rim, parts, specs, shapes = fields(members, rows, steps, cols)
    return call(
        step_kernel,
        core,
        (members, steps // min(steps, SPAN)),
        [rim, field, rim, *parts, field, whole_block(coeff)],
        specs,
        shapes,
        [pltpu.VMEM((rows, SUBLANES, cols), jnp.float32)],
        name="step",
    )(core, *held(rests, misfits, iterate), coeff)


def finish_kernel(
    core_ref, up_ref, rest_ref, down_ref, own_ref, other_ref, same_ref, cross_ref, iter_ref, coeff_ref,
    *refs,
):
    solution_ref, residual_ref, whole_ref = refs[-3:]

    def body(times):
        residual = residual_of(
            core_ref[0],
            times,
            (up_ref, rest_ref, down_ref),
            (own_ref, other_ref, same_ref, cross_ref),
            whole_ref,
        )
        update = precondition(residual, coeff_ref)
        solution_ref[times] = jnp.swapaxes(iter_ref[0, :, times] + update[1:-1], 0, 1)
        residual_ref[times] = jnp.swapaxes(trim(residual, HALO), 0, 1)

    time_chunks(iter_ref.shape[2], body)


def finish(group, samples, core, rests, misfits, iterate, coeff, previous):
    members, rows, steps, cols = iterate.shape
    field, rim, parts, _, _ = fields(members, rows, steps, cols)
    result = pl.BlockSpec(
        (min(steps, SPAN), rows, cols), lambda b, t, core: (t, b + group * members, 0)
    )
    shape = jax.ShapeDtypeStruct((steps, samples * rows, cols), jnp.float32)
    in_specs = [rim, field, rim, *parts, field, whole_block(coeff)]
    first = 1 + len(in_specs)
    return call(
        finish_kernel,
        core,
        (members, steps // min(steps, SPAN)),
        in_specs + [pl.BlockSpec(memory_space=pl.ANY)] * len(previous),
        [result, result],
        [shape, shape],
        [pltpu.VMEM((rows, SUBLANES, cols), jnp.float32)],
        {first + k: k for k in range(len(previous))},
        name="finish",
    )(core, *held(rests, misfits, iterate), coeff, *previous)


def same_frequency(near, sensors, lanes):
    shape = (near, lanes)
    return lax.broadcasted_iota(jnp.int32, shape, 0) == (
        lax.broadcasted_iota(jnp.int32, shape, 1) % LANES // sensors
    )


def marks_of(cell_ref, width):
    first = pl.program_id(0) * width
    parts = []
    for start_lane in range(0, width, LANES):
        lane = lax.broadcasted_iota(jnp.int32, cell_ref.shape, 1) + (first + start_lane)
        parts.append(jnp.where(cell_ref[...] == lane, 1.0, 0.0).astype(jnp.bfloat16))
    return jnp.concatenate(parts, axis=1)


def near_map(own_ref, other_ref, here):
    _, freqs, sensors, width = own_ref.shape
    parts = [
        ref[part, here].reshape(LANES, width) for part in range(2) for ref in (own_ref, other_ref)
    ]
    return jnp.concatenate(parts, axis=0)


def observe_kernel(core_ref, field_ref, *refs):
    *slot_refs, own_ref, other_ref, table_ref, around_ref, cell_ref = refs[:-4]
    out_ref, spec, acc, picked = refs[-4:]
    rows, steps, lanes = field_ref.shape[-3:]
    members = spec.shape[0] // 2
    chips = table_ref.shape[1] // (2 * steps)
    whole = field_ref.shape[-4]
    freqs, sensors, width = own_ref.shape[1:]
    near = lanes // sensors
    wide = 2 * lanes
    chunk = pl.program_id(0)

    @pl.when(chunk == 0)
    def _():
        acc[...] = jnp.zeros_like(acc)
        picked[...] = jnp.zeros_like(picked)

    marks = marks_of(cell_ref, width)

    def history(b, r):
        if b < whole:
            here = field_ref[..., b, r, :, :]
            return here.reshape(2 * chips * steps, lanes)
        slots = [slot_refs[0][:, b - whole, r]]
        for k in range(1, chips):
            slots.append(slot_refs[k][:, b - whole, r] + slot_refs[2 * chips - 1 - k][:, b - whole, r])
        return jnp.concatenate([slot.reshape(2 * steps, lanes) for slot in slots], axis=0)

    for b in range(members):
        table = table_ref[...] if b < whole else around_ref[...]
        spectrum = dot(table, jnp.concatenate([history(b, r) for r in range(rows)], axis=1))
        spec[2 * b] = spectrum[:freqs]
        spec[2 * b + 1] = spectrum[freqs:]
    for m in range(2 * members):
        picked[m] += dot_lanes(spec[m].astype(jnp.bfloat16), marks)
    for q in range(freqs // near):
        here = slice(q * near, (q + 1) * near)
        left = spec[:, here].reshape(2 * members * near, width).astype(jnp.bfloat16)
        acc[q] += dot_lanes(left, near_map(own_ref, other_ref, here))

    @pl.when(chunk == pl.num_programs(0) - 1)
    def _():
        mask = same_frequency(near, sensors, wide)
        for q in range(freqs // near):
            here = slice(q * near, (q + 1) * near)
            for b in range(members):
                real = acc[q, 2 * b * near : (2 * b + 1) * near]
                imag = acc[q, (2 * b + 1) * near : (2 * b + 2) * near]
                sums = (
                    real[:, :wide] - imag[:, wide:] + picked[2 * b, here],
                    imag[:, :wide] + real[:, wide:] + picked[2 * b + 1, here],
                )
                for part, value in enumerate(sums):
                    line = jnp.sum(jnp.where(mask, value, 0.0), 0, keepdims=True)
                    out_ref[0, part, b, q : q + 1] = line[:, :lanes]
                    out_ref[1, part, b, q : q + 1] = line[:, lanes:]


def map_specs(own, width):
    chunks = own.shape[3] // (2 * width)
    spec = pl.BlockSpec(own.shape[:3] + (width,), lambda c, core: (0, 0, 0, core[0] * chunks + c))
    return [spec, spec]


def map_cost(members, own, moved):
    return pl.CostEstimate(
        flops=8 * members * own.size, bytes_accessed=2 * own.size + 2 * moved, transcendentals=0
    )


def observe(core, field, slots, own, other, table, around, local_cells):
    *sources, whole, rows, steps, lanes = field.shape
    apart = slots[0].shape[1] if slots else 0
    members = whole + apart
    _, freqs, sensors, cells = own.shape
    width = CHUNK_ROWS * lanes
    near = lanes // sensors
    shape = (2, 2, members, freqs // near, lanes)
    chunks = cells // (2 * width)
    first = chunks if len(sources) == 1 else 0
    block = (*sources, whole, CHUNK_ROWS, steps, lanes)
    lead = (0,) * len(sources) + (0,)
    slot = pl.BlockSpec((2, apart, CHUNK_ROWS, steps, lanes), lambda c, core: (0, 0, c, 0, 0))
    return call(
        observe_kernel,
        core,
        (chunks,),
        [pl.BlockSpec(block, lambda c, core: (*lead, core[0] * first + c, 0, 0))]
        + [slot] * len(slots)
        + map_specs(own, width)
        + [whole_block(table), whole_block(around), whole_block(local_cells)],
        pl.BlockSpec(shape, lambda c, core: (0, 0, 0, 0, 0)),
        jax.ShapeDtypeStruct(shape, jnp.float32),
        [
            pltpu.VMEM((2 * members, freqs, width), jnp.float32),
            pltpu.VMEM((freqs // near, 2 * members * near, 4 * lanes), jnp.float32),
            pltpu.VMEM((2 * members, freqs, 2 * lanes), jnp.float32),
        ],
        cost_estimate=map_cost(members, own, field.size),
        name="observe",
    )(core, *in_hbm(field), *slots, *in_hbm(own, other), table, around, local_cells)


def pull_kernel(core_ref, *refs):
    *sums, noise_ref, own_ref, other_ref, back_ref, cell_ref = refs[:-3]
    out_ref, weights, adjoint = refs[-3:]
    devices, _, members, rows, steps, lanes = out_ref.shape
    freqs, sensors, width = own_ref.shape[1:]
    near = lanes // sensors
    wide = 2 * lanes

    def total(part, b, which):
        values = [ref[which, part, b] for ref in sums]
        while len(values) > 1:
            values = [values[k] + values[k + 1] for k in range(0, len(values), 2)]
        noise = noise_ref[which : which + 1]
        return (noise * values[0]).astype(jnp.bfloat16).astype(jnp.float32)

    @pl.when(pl.program_id(0) == 0)
    def _():
        mask = same_frequency(near, sensors, wide)
        for b in range(members):
            real, imag = (
                jnp.concatenate([total(part, b, 0), total(part, b, 1)], axis=1) for part in range(2)
            )
            for q in range(freqs // near):
                here = slice(q * near, (q + 1) * near)
                w_real = jnp.where(mask, real[q : q + 1], 0.0)
                w_imag = jnp.where(mask, imag[q : q + 1], 0.0)
                weights[2 * b, here, :wide] = w_real
                weights[2 * b, here, wide:] = w_imag
                weights[2 * b + 1, here, :wide] = w_imag
                weights[2 * b + 1, here, wide:] = -w_real

    marks = marks_of(cell_ref, width)
    for m in range(2 * members):
        adjoint[m] = dot(weights[m, :, :wide].astype(jnp.bfloat16), marks)
    for q in range(freqs // near):
        here = slice(q * near, (q + 1) * near)
        left = weights[:, here].reshape(2 * members * near, 2 * wide).astype(jnp.bfloat16)
        part = dot(left, near_map(own_ref, other_ref, here))
        adjoint[:, here] += part.reshape(2 * members, near, width)
    for b in range(members):
        whole = adjoint[2 * b : 2 * b + 2].reshape(2 * freqs, width)
        high = whole.astype(jnp.bfloat16)
        low = (whole - high.astype(jnp.float32)).astype(jnp.bfloat16)
        misfit = (dot(back_ref[...], high) + dot(back_ref[...], low)).astype(out_ref.dtype)
        for r in range(rows):
            part = misfit[:, r * lanes : (r + 1) * lanes]
            out_ref[:, :, b, r] = part.reshape(devices, 2, steps, lanes)


def pull_back(core, sums, noise, own, other, back, local_cells, shape):
    devices, _, members, rows, steps, lanes = shape
    _, freqs, sensors, cells = own.shape
    width = CHUNK_ROWS * lanes
    small = [*sums, noise]
    return call(
        pull_kernel,
        core,
        (rows // CHUNK_ROWS,),
        [whole_block(array) for array in small]
        + map_specs(own, width)
        + [whole_block(back), whole_block(local_cells)],
        pl.BlockSpec(
            (devices, 2, members, CHUNK_ROWS, steps, lanes), lambda c, core: (0, 0, 0, c, 0, 0)
        ),
        pltpu.HBM(shape, jnp.bfloat16),
        [
            pltpu.VMEM((2 * members, freqs, 4 * lanes), jnp.float32),
            pltpu.VMEM((2 * members, freqs, width), jnp.float32),
        ],
        cost_estimate=map_cost(members, own, math.prod(shape)),
        name="pull_back",
    )(core, *small, *in_hbm(own, other), back, local_cells)


def rims(top, bottom):
    size = lax.axis_size("cells")
    onward = [(k, k + 1) for k in range(size - 1)]
    backward = [(k + 1, k) for k in range(size - 1)]
    return lax.ppermute(bottom, "cells", onward), lax.ppermute(top, "cells", backward)


def misfit_rims(edge):
    size, width = lax.axis_size("cells"), lax.axis_size("sensors")
    same, cross = [], []
    for cell in range(size):
        for sensor in range(width):
            there = cell + 2 * (sensor % 2) - 1
            if 0 <= there < size:
                same.append((cell * width + sensor, there * width + sensor))
                cross.append((cell * width + sensor, there * width + (sensor ^ 1)))
    both = ("cells", "sensors")
    return lax.ppermute(edge, both, same), lax.ppermute(edge, both, cross)


def swap_cores(value):
    size = lax.axis_size("sensors")
    return lax.ppermute(value, "sensors", [(k, k ^ 1) for k in range(size)])


def from_all_cells(value):
    size = lax.axis_size("cells")
    if size & (size - 1):
        return [lax.psum(value, "cells")]
    return [value] + [
        lax.ppermute(value, "cells", [(k, k ^ other) for k in range(size)])
        for other in range(1, size)
    ]


class Line:
    def __init__(self, value):
        self.size = lax.axis_size("sensors")
        self.value, self.ups, self.downs = value, [], []
        self.ends = (value, value)

    def hop(self, last=False):
        while len(self.ups) < self.size // 2 - 1:
            start = 2 * len(self.ups)
            onward = [(k, k + 2) for k in range(start, self.size - 2)]
            backward = [(self.size - 1 - k, self.size - 1 - there) for k, there in onward]
            up = lax.ppermute(self.ends[0], "sensors", onward)
            down = lax.ppermute(self.ends[1], "sensors", backward)
            self.ups.append(up)
            self.downs.append(down)
            self.ends = (up, down)
            if not last:
                break

    def after(self, other):
        if other is not None and self.ups:
            self.ends, other = lax.optimization_barrier((self.ends, other))
            self.ups[-1], self.downs[-1] = self.ends
        return other

    def slots(self):
        return [self.value, *self.ups, *self.downs]


def shards(rhs, forward_map, stiffness, reaction, noise_weight, sensor_cell):
    steps, samples, rows, cols = rhs.shape
    _, freqs, sensors, cells = forward_map.shape
    size = lax.axis_size("sensors")
    chips = size // 2
    cell_index = lax.axis_index("cells")
    sensor_index = lax.axis_index("sensors")
    core = sensor_index % 2
    near = LANES // sensors
    half = cells // 2
    other_map = swap_cores(forward_map)

    cores = jnp.stack([core, 1 - core])
    offsets = cores[None, :, None] * steps + jnp.arange(steps, dtype=jnp.int32)
    chip_steps = 2 * steps
    places = jnp.arange(chips, dtype=jnp.int32)[:, None, None] * chip_steps
    table = transform_table(freqs, places + offsets)
    back = table.T
    in_order = transform_table(freqs, jnp.arange(2 * freqs, dtype=jnp.int32))
    chip = sensor_index // 2
    places = (chip - jnp.arange(chips, dtype=jnp.int32)) % chips
    around = transform_table(freqs, places[:, None, None] * chip_steps + offsets)

    diagonal = reaction + 4.0 * stiffness * stiffness
    local = jnp.stack([stiffness, diagonal])
    members = samples // GROUPS
    groups = [slice(group * members, (group + 1) * members) for group in range(GROUPS)]

    def rim_rows(here, first):
        part = lax.slice_in_dim(rhs[:, here], first, first + HALO, axis=2)
        return jnp.transpose(lax.optimization_barrier(part), (1, 2, 0, 3))

    def packed(first):
        part = rim_rows(groups[0], first).astype(jnp.bfloat16).reshape(members * HALO, steps, cols)
        value, terms = local[:, first : first + HALO].reshape(2 * HALO, cols), []
        for _ in range(3):
            terms.append(lax.optimization_barrier(value.astype(jnp.bfloat16)))
            value = value - terms[-1].astype(jnp.float32)
        extra = jnp.concatenate(terms, axis=0)
        extra = jnp.pad(extra, ((0, -6 * HALO % steps), (0, 0))).reshape(-1, steps, cols)
        return jnp.concatenate([part, extra], axis=0)

    def unpacked(value):
        part = value[: members * HALO].reshape(members, HALO, steps, cols)
        extra = value[members * HALO :].reshape(-1, cols)[: 6 * HALO].astype(jnp.float32)
        high, middle, low = extra.reshape(3, 2, HALO, cols)
        return part, high + (middle + low)

    (up_first, up), (down_first, down) = (
        unpacked(value) for value in rims(packed(0), packed(rows - HALO))
    )
    stiff, diag = jnp.concatenate([up, local, down], axis=1)
    inside = diag > 0.0
    inverse = jnp.where(inside, 1.0 / jnp.where(inside, diag, 1.0), 0.0)
    unscale = jnp.where(inside, 1.0 / jnp.where(inside, stiff, 1.0), 0.0)
    scaled = DAMPING * inverse * stiff
    coeff = jnp.stack([scaled, scaled * stiff, unscale, stiff, diag])
    coeff = jnp.broadcast_to(coeff[:, :, None, :], coeff.shape[:2] + (SUBLANES, cols))

    def per_lane(values):
        own = lax.dynamic_slice_in_dim(values, sensor_index * sensors, sensors)
        other = lax.dynamic_slice_in_dim(values, (sensor_index ^ 1) * sensors, sensors)
        return jnp.stack([jnp.tile(own, near), jnp.tile(other, near)])

    noise = per_lane(noise_weight)
    local_cells = per_lane(sensor_cell) - (cell_index * cells + core * half)
    local_cells = jnp.broadcast_to(local_cells.reshape(2 * LANES, 1), (2 * LANES, LANES))
    core = core.reshape(1)

    whole = members - members // APART
    lines = [[k for k in range(size) if k % 2 == parity] for parity in range(2)]
    shape = (chips, 2, members, rows // 2, steps, cols)

    def both_cores(low):
        keep, give = (
            lax.dynamic_slice_in_dim(low, first * (rows // 2), rows // 2, axis=1)
            for first in (core[0], 1 - core[0])
        )
        return jnp.stack([keep, swap_cores(give)])

    def ready(state):
        iterate, low, rest, top, bottom = state
        above, below = rims(top, bottom)
        pair = both_cores(low)
        parts = lax.optimization_barrier((pair[:, :whole], pair[:, whole:]))
        return iterate, *parts, (above, rest, below)

    def edges(misfit):
        first = (rows // 2 - HALO) * core[0]
        edge = lax.dynamic_slice_in_dim(misfit, first, HALO, axis=2)
        same, _ = misfit_rims(edge[:1])
        _, cross = misfit_rims(edge[1:])
        return misfit, swap_cores(misfit[1:]), same, cross

    iterate, low, rest, *ends = start(0, members, core, rhs, up_first, down_first, coeff)
    above, below = rims(*ends)
    states = [(iterate, low, None, (above, rest, below))]
    for group in range(1, GROUPS):
        ends = tuple(
            rim_rows(groups[group], first).astype(jnp.bfloat16) for first in (0, rows - HALO)
        )
        _, rests, ends = lax.optimization_barrier((low, states[0][3], ends))
        states[0] = (*states[0][:3], rests)
        states.append(ready(start(group, members, core, rhs, *rims(*ends), coeff)))
    line = None

    outputs = ()
    for iteration in range(ITERS):
        fields = [
            lax.all_gather(state[1], "sensors", axis_index_groups=None if state[2] is None else lines)
            for state in states
        ]
        if line is not None:
            line.hop(last=True)
        totals = []
        for group in range(GROUPS):
            iterate, _, _, rests = states[group]
            field = fields[group]
            slots, line = (line.slots() if line is not None else []), None
            if group > 0:
                field, rests = lax.optimization_barrier((field, rests))
            states[group] = iterate, rests
            if group + 1 < GROUPS:
                line = Line(states[group + 1][2])
                line.hop()
                field = line.after(field)
                line.hop()
            sums = observe(
                core,
                field,
                slots,
                forward_map,
                other_map,
                table if slots else in_order,
                around,
                local_cells,
            )
            if line is not None:
                sums = line.after(sums)
                line.hop(last=True)
            sums = from_all_cells(sums + swap_cores(sums)[::-1])
            misfit = pull_back(core, sums, noise, forward_map, other_map, back, local_cells, shape)
            if line is not None:
                misfit = line.after(misfit)
            totals.append(
                lax.psum_scatter(
                    misfit, "sensors", scatter_dimension=0, axis_index_groups=lines, tiled=False
                )
            )
        for group in range(GROUPS):
            iterate, rests = states[group]
            total = totals[group]
            if iteration < ITERS - 1:
                if group == 1:
                    before = states[0]
                    line = Line(before[2])
                    line.hop()
                    line.hop()
                    total, earlier = line.after((total, before[3]))
                    states[0] = (*before[:3], earlier)
                states[group] = ready(step(core, rests, edges(total), iterate, coeff))
            else:
                if outputs:
                    total, outputs = lax.optimization_barrier((total, outputs))
                outputs = finish(
                    group, samples, core, rests, edges(total), iterate, coeff, outputs
                )
    return tuple(out.reshape(rhs.shape) for out in outputs)


def solution(mesh):
    placed = (
        P("sensors", None, "cells", None),
        P(None, None, "sensors", "cells"),
        P("cells", None),
        P("cells", None),
        P(),
        P(),
    )
    return jax.shard_map(
        shards,
        mesh=mesh,
        in_specs=placed,
        out_specs=(P("sensors", None, "cells", None), P("sensors", None, "cells", None)),
        check_vma=False,
    )
```
